32 devices in a mesh: gx: 4 (over y, x), gy: 8 (over z, core).
Axes of the slice: x: 2, y: 2, z: 4, core: 2. Of those that a mesh axis runs over, the one named last changes fastest.
Arguments:
- saved_conc: float32 [3, 2, 64, 64, 512], P(None, None, None, 'gy', 'gx'), may hold values from 0.15 to 0.85
- adjoint_end: float32 [2, 64, 64, 512], P(None, None, 'gy', 'gx'), may hold values from -6 to 6
- rate_field: float32 [64, 64, 512], P(None, 'gy', 'gx'), may hold values from 0.5 to 5
Outputs:
- adjoint_start: float32 [2, 64, 64, 512], P(None, None, 'gy', 'gx')
- rate_grad: float32 [64, 64, 512], P(None, 'gy', 'gx')
The draws below stay inside these ranges and needn't reach their ends.
All inputs are finite; a program needn't handle non-finite values.
Results may differ from the reference program's by a relative error of at most 0.00023.
Values sent between devices are 32-bit elements; how exact they have to be, the bound alone decides.
No kernel may reach another device: no remote copies, remote signals or barrier semaphores. Data moves between devices by JAX's collectives and lax.ppermute only.
A program may use at most 128 MiB of HBM per device.

```python
import math
import jax
import jax.numpy as jnp

NZ = 64
FRAMES = 2
STEPS = 3
NX = 512
NY = 64


def steps_of(rng, shape, shards, low, high):
    loudness, own = 1.0, jax.random.fold_in(rng, 6)
    for dim, blocks in shards:
        draws = jnp.exp(jax.random.uniform(jax.random.fold_in(own, dim), (blocks,), jnp.float32, low / len(shards), high / len(shards)))
        loudness = loudness * jnp.repeat(draws, shape[dim] // blocks).reshape([-1 if axis == dim else 1 for axis in range(len(shape))])
    return loudness


def centred(key, shape, deviation, most, pieces=(), held_as=jnp.bfloat16):
    entries = jax.random.normal(key, shape, jnp.float32) * deviation
    if len(pieces) > 0:
        entries = steps_of(key, shape, pieces, -0.22, 0.18) * entries
    return jnp.clip(entries, min=-most, max=most).astype(held_as)


def setup_inputs(seed: int = 0) -> dict:
    splits = jax.random.split(jax.random.key(seed), 4)
    return {
        "saved_conc": jnp.clip(0.15 + 0.70000002 * jax.random.uniform(splits[0], (STEPS, FRAMES, NZ, NY, NX), jnp.float32) ** steps_of(splits[0], (STEPS, FRAMES, NZ, NY, NX), ((3, 8), (4, 4)), -0.2, 0.2), 0.15, 0.85),
        "adjoint_end": centred(splits[1], (FRAMES, NZ, NY, NX), 1.0, 6.0, ((2, 8), (3, 4)), jnp.float32),
        "rate_field": jnp.clip(jnp.exp(math.log(5.0) - 2.3025851 * jax.random.uniform(splits[2], (NZ, NY, NX), jnp.float32) ** steps_of(splits[2], (NZ, NY, NX), ((1, 8), (2, 4)), -0.2, 0.2)), 0.5, 5.0),
    }


mix_energy = 2.5
grad_energy = 1.0
time_step = 0.1
diff_step = 0.03
bath_potential = 0.5


def laplace_z(field):
    diffs = field[..., 1:, :, :] - field[..., :-1, :, :]
    zeros = jnp.zeros_like(field[..., :1, :, :])
    return jnp.concatenate([diffs, zeros], axis=-3) - jnp.concatenate([zeros, diffs], axis=-3)


def laplace(field):
    total = jnp.roll(field, 1, -1) + jnp.roll(field, -1, -1) + jnp.roll(field, 1, -2) + jnp.roll(field, -1, -2)
    return total - 4.0 * field + laplace_z(field)


def potential(conc):
    return jnp.log(conc / (1.0 - conc)) + mix_energy * (1.0 - 2.0 * conc) - grad_energy * laplace(conc)


def flux_div(mobility, scaled):
    total = jnp.zeros_like(scaled)
    for axis in (-1, -2):
        flux = 0.5 * (mobility + jnp.roll(mobility, -1, axis)) * (jnp.roll(scaled, -1, axis) - scaled)
        total = total + flux - jnp.roll(flux, 1, axis)
    flux_z = 0.5 * (mobility[..., 1:, :, :] + mobility[..., :-1, :, :]) * (scaled[..., 1:, :, :] - scaled[..., :-1, :, :])
    zeros = jnp.zeros_like(scaled[..., :1, :, :])
    return total + jnp.concatenate([flux_z, zeros], axis=-3) - jnp.concatenate([zeros, flux_z], axis=-3)


def face_terms(chem, scaled):
    total = jnp.zeros_like(scaled)
    for axis in (-1, -2):
        term = -0.5 * (jnp.roll(chem, -1, axis) - chem) * (jnp.roll(scaled, -1, axis) - scaled)
        total = total + term + jnp.roll(term, 1, axis)
    term_z = -0.5 * (chem[..., 1:, :, :] - chem[..., :-1, :, :]) * (scaled[..., 1:, :, :] - scaled[..., :-1, :, :])
    zeros = jnp.zeros_like(scaled[..., :1, :, :])
    return total + jnp.concatenate([term_z, zeros], axis=-3) + jnp.concatenate([zeros, term_z], axis=-3)


def reference(saved_conc, adjoint_end, rate_field):
    adjoint = adjoint_end
    rate_grad = jnp.zeros(rate_field.shape, jnp.float32)
    for back in range(STEPS):
        conc = saved_conc[STEPS - 1 - back]
        chem = potential(conc)
        scaled = diff_step * adjoint
        g_pot = flux_div(conc * (1.0 - conc), scaled) - time_step * rate_field * adjoint
        faces = face_terms(chem, scaled)
        rate_grad = rate_grad + time_step * jnp.sum(adjoint * (bath_potential - chem), axis=0)
        curve = 1.0 / (conc * (1.0 - conc)) - 2.0 * mix_energy
        adjoint = adjoint + (1.0 - 2.0 * conc) * faces + curve * g_pot - grad_energy * laplace(g_pot)
    return adjoint, rate_grad
```

```python
import functools

import jax
import jax.numpy as jnp
from jax import lax
from jax.experimental import pallas as pl
from jax.experimental.pallas import tpu as pltpu
from jax.sharding import PartitionSpec as P

mix_energy = 2.5
grad_energy = 1.0
time_step = 0.1
diff_step = 0.03
bath_potential = 0.5

pad = 16
chunk = 24
depth = 2
vmem_limit = 48 * 1024 * 1024
f32 = jnp.float32


def slots(steps):
    widths = [2 * steps] + [2 * steps - 2 * back for back in range(steps)] + [2 * steps - 1]
    starts = [sum(widths[:i]) for i in range(len(widths))]
    total = -(-sum(widths) // 8) * 8
    return list(zip(starts, widths)), total


def chunks(low, high):
    return [(at, min(chunk, high - at)) for at in range(low, high, chunk)]


def face_mask(shape, depth_z):
    lane = lax.broadcasted_iota(jnp.int32, shape, 1)
    return jnp.where(lane % depth_z == depth_z - 1, 0.0, 1.0).astype(f32)


def up(value):
    return pltpu.roll(value, value.shape[1] - 1, 1)


def down(value):
    return pltpu.roll(value, 1, 1)


def pack_kernel(steps, rows, cols, nz, conc_ref, adj_ref, rate_ref, conc_out, adj_out, rate_out,
                main_up, main_dn, late_up, late_dn, x_right, x_left):
    places, _ = slots(steps)
    lanes = adj_out.shape[2]
    half = cols // 2
    lower = lax.broadcasted_iota(jnp.int32, (half, lanes), 1) < nz

    def to_x(y, value, place):
        start, width = place
        x_right[y, start : start + width, :] = value[cols - width :, :]
        x_left[y, start : start + width, :] = value[:width, :]

    for y in range(rows):
        adj = adj_ref[pl.ds(y, lanes, stride=rows), :].T
        adj_out[y] = adj
        to_x(y, adj, places[0])
        rate = rate_ref[pl.ds(y, nz, stride=rows), :]
        rate = jnp.concatenate([rate] * (lanes // nz), axis=0).T
        rate_out[y] = rate
        to_x(y, rate, places[steps + 1])
        x_right[y, sum(places[-1]) :, :] = jnp.zeros((x_right.shape[1] - sum(places[-1]), lanes), f32)
        x_left[y, sum(places[-1]) :, :] = jnp.zeros((x_left.shape[1] - sum(places[-1]), lanes), f32)
        for side, at in ((main_dn, y), (main_up, y - rows + depth)):
            if 0 <= at < depth:
                side[pl.ds((depth + at) * cols, cols), :] = adj
        for side, edge in ((main_dn, 0), (main_up, rows - 1)):
            if y == edge:
                side[pl.ds(2 * depth * cols, half), :] = jnp.where(lower, rate[:half], rate[half:])
        for back in range(steps):
            conc = conc_ref[steps - 1 - back, pl.ds(y, lanes, stride=rows), :].T
            conc_out[back, y] = conc
            to_x(y, conc, places[1 + back])
            for main, late, at in ((main_dn, late_dn, y), (main_up, late_up, y - rows + depth)):
                if 0 <= at < depth:
                    if back == 0:
                        main[pl.ds(at * cols, cols), :] = conc
                    else:
                        late[pl.ds(((back - 1) * depth + at) * cols, cols), :] = conc


def gather_rows(out, place, rows, cols, own, low, high, x_low, x_high, c_low, c_high, rim):
    start, width = place
    right = pad + cols
    for y in range(rows):
        out[rim + y, pad:right, :] = own(y)
        out[rim + y, pad - width : pad, :] = x_low[y, start : start + width, :]
        out[rim + y, right : right + width, :] = x_high[y, start : start + width, :]
    for at in range(rim):
        for row, halo, corner, from_row in (
            (at, low, c_low, depth - rim + at),
            (rim + rows + at, high, c_high, at),
        ):
            out[row, pad:right, :] = halo(from_row)
            out[row, pad - width : pad, :] = corner[0, from_row, start : start + width, :]
            out[row, right : right + width, :] = corner[1, from_row, start : start + width, :]


def potentials(conc, mob, chem, curve, rows, cols, nz):
    low, high = pad - 8, pad + cols + 8
    lanes = conc.shape[2]

    def mob_row(y, _):
        for at, size in chunks(low - 8, high + 8):
            c = conc[y, at : at + size, :]
            mob[y, at : at + size, :] = c * (1.0 - c)
        return 0

    lax.fori_loop(0, rows + 2 * depth, mob_row, 0)

    def chem_row(y, _):
        for at, size in chunks(low, high):
            mask = face_mask((size, lanes), nz)
            c = conc[y + 1, at : at + size, :]
            inv = 1.0 / mob[y + 1, at : at + size, :]
            step_z = (up(c) - c) * mask
            lap = (
                (conc[y + 1, at + 1 : at + size + 1, :] + conc[y + 1, at - 1 : at + size - 1, :])
                + (conc[y, at : at + size, :] + conc[y + 2, at : at + size, :])
                - 4.0 * c
                + (step_z - down(step_z))
            )
            chem[y, at : at + size, :] = (
                jnp.log(c * c * inv) + mix_energy * (1.0 - 2.0 * c) - grad_energy * lap
            )
            curve[y, at : at + size, :] = inv - 2.0 * mix_energy
        return 0

    lax.fori_loop(0, rows + 2, chem_row, 0)


def advance(conc, mob, chem, curve, adj, rate, pot, part, grad, grad_in, rows, cols, nz):
    low, high = pad - 8, pad + cols + 8
    lanes = conc.shape[2]

    def work(y, at, size, own):
        mask = face_mask((size, lanes), nz)
        span = slice(at, at + size)
        a = adj[y + 1, span, :]
        m = mob[y + 1, span, :]
        total = None
        faces = None
        if own:
            mu = chem[y, span, :]
        sides = (
            (0, slice(at + 1, at + size + 1)),
            (0, slice(at - 1, at + size - 1)),
            (1, span),
            (-1, span),
        )
        for dy, cut in sides:
            diff = adj[y + 1 + dy, cut, :] - a
            flux = (mob[y + 1 + dy, cut, :] + m) * diff
            total = flux if total is None else total + flux
            if own:
                term = (chem[y + dy, cut, :] - mu) * diff
                faces = term if faces is None else faces + term
        diff = (up(a) - a) * mask
        flux = (up(m) + m) * diff
        total = total + (flux - down(flux))
        g = (0.5 * diff_step) * total - time_step * rate[y, span, :] * a
        pot[y, span, :] = g
        if own:
            term = (up(mu) - mu) * diff
            faces = faces + (term + down(term))
            c = conc[y + 1, span, :]
            part[y - 1, span, :] = (
                a + (1.0 - 2.0 * c) * ((-0.5 * diff_step) * faces) + curve[y, span, :] * g
            )
            gain = time_step * a * (bath_potential - mu)
            if grad_in is not None:
                gain = gain + grad_in[y - 1, span, :]
            grad[y - 1, span, :] = gain

    def own_row(y, _):
        for at, size in chunks(low, high):
            work(y + 1, at, size, True)
        return 0

    def edge_row(i, _):
        for at, size in chunks(low, high):
            work(i * (rows + 1), at, size, False)
        return 0

    lax.fori_loop(0, rows, own_row, 0)
    lax.fori_loop(0, 2, edge_row, 0)


def finish(pot, part, store, rows, low, high, nz):
    lanes = pot.shape[2]

    def row(y, _):
        for at, size in chunks(low, high):
            mask = face_mask((size, lanes), nz)
            span = slice(at, at + size)
            g = pot[y + 1, span, :]
            step_z = (up(g) - g) * mask
            lap = (
                (pot[y + 1, at + 1 : at + size + 1, :] + pot[y + 1, at - 1 : at + size - 1, :])
                + (pot[y, span, :] + pot[y + 2, span, :])
                - 4.0 * g
                + (step_z - down(step_z))
            )
            store(y, at, size, part[y, span, :] - grad_energy * lap)
        return 0

    lax.fori_loop(0, rows, row, 0)


def send_rows(adj_out, to_up, to_dn, rows, cols):
    low, high = pad - 8, pad + cols + 8
    for at in range(depth):
        to_dn[at] = adj_out[at, low:high, :]
        to_up[at] = adj_out[rows - depth + at, low:high, :]


def first_kernel(steps, rows, cols, nz, conc_own, adj_own, rate_own, from_dn, from_up, x_low, x_high,
                 c_low, c_high, adj_out, rate_ext, grad, to_up, to_dn,
                 conc, mob, chem, curve, adj, pot, part):
    places, _ = slots(steps)
    half = cols // 2
    lanes = conc.shape[2]
    lower = lax.broadcasted_iota(jnp.int32, (half, lanes), 1) < nz

    def rows_of(side, base):
        return lambda at: side[pl.ds((base + at) * cols, cols), :]

    def rate_of(side):
        def one(_):
            packed = side[pl.ds(2 * depth * cols, half), :]
            turned = pltpu.roll(packed, lanes // 2, 1)
            return jnp.concatenate(
                [jnp.where(lower, packed, turned), jnp.where(lower, turned, packed)], axis=0
            )

        return one

    sides = (x_low, x_high, c_low, c_high)
    gather_rows(conc, places[1], rows, cols, lambda y: conc_own[0, y], rows_of(from_dn, 0),
                rows_of(from_up, 0), *sides, depth)
    gather_rows(adj, places[0], rows, cols, lambda y: adj_own[y], rows_of(from_dn, depth),
                rows_of(from_up, depth), *sides, depth)
    gather_rows(rate_ext, places[steps + 1], rows, cols, lambda y: rate_own[y], rate_of(from_dn),
                rate_of(from_up), *sides, 1)
    potentials(conc, mob, chem, curve, rows, cols, nz)
    advance(conc, mob, chem, curve, adj, rate_ext, pot, part, grad, None, rows, cols, nz)

    def store(y, at, size, value):
        adj_out[y, at : at + size, :] = value

    finish(pot, part, store, rows, pad - 8, pad + cols + 8, nz)
    send_rows(adj_out, to_up, to_dn, rows, cols)


def prepare_kernel(steps, rows, cols, nz, back, conc_own, from_dn, from_up, x_low, x_high, c_low,
                   c_high, conc, mob, chem, curve):
    places, _ = slots(steps)

    def rows_of(side):
        return lambda at: side[pl.ds(((back - 1) * depth + at) * cols, cols), :]

    gather_rows(conc, places[1 + back], rows, cols, lambda y: conc_own[back, y], rows_of(from_dn),
                rows_of(from_up), x_low, x_high, c_low, c_high, depth)
    potentials(conc, mob, chem, curve, rows, cols, nz)


def extend(adj, own, from_dn, from_up, rows, cols):
    low, high = pad - 8, pad + cols + 8
    for y in range(rows):
        adj[depth + y, low:high, :] = own[y, low:high, :]
    for at in range(depth):
        adj[at, low:high, :] = from_dn[at]
        adj[depth + rows + at, low:high, :] = from_up[at]


def step_kernel(rows, cols, nz, conc, mob, chem, curve, own, from_dn, from_up, rate, grad_in,
                adj_out, grad, to_up, to_dn, adj, pot, part):
    extend(adj, own, from_dn, from_up, rows, cols)
    advance(conc, mob, chem, curve, adj, rate, pot, part, grad, grad_in, rows, cols, nz)

    def store(y, at, size, value):
        adj_out[y, at : at + size, :] = value

    finish(pot, part, store, rows, pad - 8, pad + cols + 8, nz)
    send_rows(adj_out, to_up, to_dn, rows, cols)


def last_kernel(rows, cols, nz, conc, mob, chem, curve, own, from_dn, from_up, rate, grad_in,
                adj_out, grad_out, adj, pot, part, grad, result):
    lanes = conc.shape[2]
    extend(adj, own, from_dn, from_up, rows, cols)
    advance(conc, mob, chem, curve, adj, rate, pot, part, grad, grad_in, rows, cols, nz)

    def store(y, at, size, value):
        result[y, at : at + size, :] = value

    finish(pot, part, store, rows, pad, pad + cols, nz)
    for y in range(rows):
        adj_out[pl.ds(y, lanes, stride=rows), :] = result[y, pad : pad + cols, :].T
        turned = grad[y, pad : pad + cols, :].T
        total = turned[:nz]
        for frame in range(1, lanes // nz):
            total = total + turned[frame * nz : (frame + 1) * nz]
        grad_out[pl.ds(y, nz, stride=rows), :] = total


def call(kernel, outs, scratch, *operands, cost=0):
    return pl.pallas_call(
        kernel,
        out_shape=[jax.ShapeDtypeStruct(shape, f32) for shape in outs],
        in_specs=[pl.BlockSpec(memory_space=pltpu.VMEM)] * len(operands),
        out_specs=[pl.BlockSpec(memory_space=pltpu.VMEM)] * len(outs),
        scratch_shapes=[pltpu.VMEM(shape, f32) for shape in scratch],
        compiler_params=pltpu.CompilerParams(vmem_limit_bytes=vmem_limit),
        cost_estimate=pl.CostEstimate(flops=cost, bytes_accessed=cost // 32, transcendentals=0),
    )(*operands)


def shift(value, axis, by):
    count = lax.axis_size(axis)
    return lax.ppermute(value, axis, [(i, (i + by) % count) for i in range(count)])


def shards(saved_conc, adjoint_end, rate_field):
    steps, frames, nz, rows, cols = saved_conc.shape
    lanes = frames * nz
    _, total = slots(steps)
    width = cols + 2 * pad
    sent = cols + 16
    flat = lanes * rows
    conc_own, adj_own, rate_own, main_up, main_dn, late_up, late_dn, x_right, x_left = call(
        functools.partial(pack_kernel, steps, rows, cols, nz),
        [(steps, rows, cols, lanes), (rows, cols, lanes), (rows, cols, lanes)]
        + [(2 * depth * cols + cols // 2, lanes)] * 2
        + [((steps - 1) * depth * cols, lanes)] * 2
        + [(rows, total, lanes)] * 2,
        [],
        saved_conc.reshape(steps, flat, cols),
        adjoint_end.reshape(flat, cols),
        rate_field.reshape(nz * rows, cols),
    )
    x_low = shift(x_right, "gx", 1)
    x_high = shift(x_left, "gx", -1)
    from_dn = shift(main_up, "gy", 1)
    from_up = shift(main_dn, "gy", -1)
    corner_up = jnp.stack([x_low[rows - depth :], x_high[rows - depth :]])
    corner_dn = jnp.stack([x_low[:depth], x_high[:depth]])
    c_low = shift(corner_up, "gy", 1)
    c_high = shift(corner_dn, "gy", -1)
    late_from_dn = shift(late_up, "gy", 1)
    late_from_up = shift(late_dn, "gy", -1)
    sides = (x_low, x_high, c_low, c_high)

    ext = (rows + 2 * depth, width, lanes)
    rim = (rows + 2, width, lanes)
    own = (rows, width, lanes)
    edge = (depth, sent, lanes)
    adj, rate, grad, to_up, to_dn = call(
        functools.partial(first_kernel, steps, rows, cols, nz),
        [own, rim, own, edge, edge],
        [ext, ext, rim, rim, ext, rim, own],
        conc_own, adj_own, rate_own, from_dn, from_up, *sides,
    )
    for back in range(1, steps):
        low, high = shift(to_up, "gy", 1), shift(to_dn, "gy", -1)
        fields = call(
            functools.partial(prepare_kernel, steps, rows, cols, nz, back),
            [ext, ext, rim, rim],
            [],
            conc_own, late_from_dn, late_from_up, *sides,
        )
        if back < steps - 1:
            adj, grad, to_up, to_dn = call(
                functools.partial(step_kernel, rows, cols, nz),
                [own, own, edge, edge],
                [ext, rim, own],
                *fields, adj, low, high, rate, grad,
            )
        else:
            adj, grad = call(
                functools.partial(last_kernel, rows, cols, nz),
                [(flat, cols), (nz * rows, cols)],
                [ext, rim, own, own, own],
                *fields, adj, low, high, rate, grad,
            )
    return adj.reshape(adjoint_end.shape), grad.reshape(rate_field.shape)


def solution(mesh):
    return jax.shard_map(
        shards,
        mesh=mesh,
        in_specs=(P(None, None, None, "gy", "gx"), P(None, None, "gy", "gx"), P(None, "gy", "gx")),
        out_specs=(P(None, None, "gy", "gx"), P(None, "gy", "gx")),
        check_vma=False,
    )
```

```python
import functools

import jax
import jax.numpy as jnp
from jax import lax
from jax.experimental import pallas as pl
from jax.experimental.pallas import tpu as pltpu
from jax.sharding import PartitionSpec as P

mix_energy = 2.5
grad_energy = 1.0
time_step = 0.1
diff_step = 0.03
bath_potential = 0.5

pad = 16
chunk = 24
depth = 2
vmem_limit = 20 * 1024 * 1024
far_limit = 20 * 1024 * 1024
f32 = jnp.float32


def slots(steps):
    widths = [2 * steps] + [2 * steps - 2 * back for back in range(steps)] + [2 * steps - 1]
    starts = [sum(widths[:i]) for i in range(len(widths))]
    total = -(-sum(widths) // 8) * 8
    return list(zip(starts, widths)), total


def early(steps):
    return (1 + min(steps, 2)) * depth


def chunks(low, high):
    return [(at, min(chunk, high - at)) for at in range(low, high, chunk)]


def reach(cols):
    return pad - 8, pad + cols + 8


def up(value):
    return pltpu.roll(value, value.shape[1] - 1, 1)


def down(value):
    return pltpu.roll(value, 1, 1)


def face_mask(size, lanes, nz):
    lane = lax.broadcasted_iota(jnp.int32, (size, lanes), 1)
    return jnp.where(lane % nz == nz - 1, 0.0, 1.0).astype(f32)


def row_of(ref, y):
    return lambda dy, cut: ref[y + dy, cut, :]


def laplace(field, at, size, mask):
    span = slice(at, at + size)
    here = field(0, span)
    step_z = (up(here) - here) * mask
    sides = field(0, slice(at + 1, at + size + 1)) + field(0, slice(at - 1, at + size - 1))
    return here, (
        (sides + (field(-1, span) + field(1, span))) - 4.0 * here + (step_z - down(step_z))
    )


def chem_row(conc, chem, curve, at, size, mask):
    c, lap = laplace(conc, at, size, mask)
    inv = 1.0 / (c * (1.0 - c))
    span = slice(at, at + size)
    chem(span, jnp.log(c * c * inv) + mix_energy * (1.0 - 2.0 * c) - grad_energy * lap)
    curve(span, inv - 2.0 * mix_energy)


def face_sums(adj, mob, chem, at, size, mask):
    span = slice(at, at + size)
    a = adj(0, span)
    m = None if mob is None else mob(0, span)
    mu = None if chem is None else chem(0, span)
    flow = pair = None
    for dy, cut in (
        (0, slice(at + 1, at + size + 1)),
        (0, slice(at - 1, at + size - 1)),
        (1, span),
        (-1, span),
    ):
        diff = adj(dy, cut) - a
        if mob is not None:
            term = (mob(dy, cut) + m) * diff
            flow = term if flow is None else flow + term
        if chem is not None:
            term = (chem(dy, cut) - mu) * diff
            pair = term if pair is None else pair + term
    diff = (up(a) - a) * mask
    if mob is not None:
        term = (up(m) + m) * diff
        flow = flow + (term - down(term))
    if chem is not None:
        term = (up(mu) - mu) * diff
        pair = pair + (term + down(term))
    return a, mu, flow, pair


def source(flow, rate, a):
    return (0.5 * diff_step) * flow - time_step * rate * a


def partial(a, c, pair, curve, g):
    return a + (1.0 - 2.0 * c) * ((-0.5 * diff_step) * pair) + curve * g


def gain(a, mu, before):
    value = time_step * a * (bath_potential - mu)
    return value if before is None else before + value


def set_row(ref, y):
    def put(span, value):
        ref[y, span, :] = value

    return put


def interior(rows, cols, nz, conc, mob, chem, curve, adj, rate, pot, part, grad, before, store):
    low, high = reach(cols)
    lanes = adj[0].shape[-1]

    def at_row(field, y):
        return row_of(field[0], field[1] + y)

    def body(y, _):
        for at, size in chunks(low, high):
            mask = face_mask(size, lanes, nz)
            span = slice(at, at + size)
            a, mu, flow, pair = face_sums(
                at_row(adj, y), at_row(mob, y), at_row(chem, y), at, size, mask
            )
            g = source(flow, at_row(rate, y)(0, span), a)
            pot[y - 1, span, :] = g
            part[y - depth, span, :] = partial(
                a, at_row(conc, y)(0, span), pair, at_row(curve, y)(0, span), g
            )
            old = None if before is None else before[y - depth, span, :]
            grad[y - depth, span, :] = gain(a, mu, old)
        return 0

    def edge(i, _):
        y = 1 + i * (rows - 3)
        for at, size in chunks(low, high):
            mask = face_mask(size, lanes, nz)
            a, _mu, flow, _pair = face_sums(at_row(adj, y), at_row(mob, y), None, at, size, mask)
            span = slice(at, at + size)
            pot[y - 1, span, :] = source(flow, at_row(rate, y)(0, span), a)
        return 0

    def close(y, _):
        for at, size in chunks(low, high):
            mask = face_mask(size, lanes, nz)
            span = slice(at, at + size)
            _g, lap = laplace(row_of(pot, y - 1), at, size, mask)
            store(y - depth, span, part[y - depth, span, :] - grad_energy * lap)
        return 0

    lax.fori_loop(depth, rows - depth, body, 0)
    lax.fori_loop(0, 2, edge, 0)
    lax.fori_loop(depth, rows - depth, close, 0)


def boundary(rows, cols, nz, conc, mob, chem, curve, adj, rate, pot, part, grad, before, store,
             fresh):
    low, high = reach(cols)
    lanes = adj[0].shape[-1]
    last = rows - 1

    def at_row(field, y):
        return row_of(field[0], field[1] + y)

    def mirror(s, y):
        return y + s * (last - 2 * y)

    if fresh:

        def mu_side(i, _):
            s, k = i // 2, i % 2
            y = mirror(s, k - 1)
            for at, size in chunks(low, high):
                chem_row(at_row(conc, y), set_row(chem[0], chem[1] + y),
                         set_row(curve[0], curve[1] + y), at, size, face_mask(size, lanes, nz))
            return 0

        lax.fori_loop(0, 4, mu_side, 0)

    def side(s, _):
        y = mirror(s, -1)
        for at, size in chunks(low, high):
            mask = face_mask(size, lanes, nz)
            span = slice(at, at + size)
            a, _mu, flow, _pair = face_sums(at_row(adj, y), at_row(mob, y), None, at, size, mask)
            pot[1 + y, span, :] = source(flow, rate[3 * s, span, :], a)
        y0 = mirror(s, 0)
        for at, size in chunks(low, high):
            mask = face_mask(size, lanes, nz)
            span = slice(at, at + size)
            a, mu, flow, pair = face_sums(
                at_row(adj, y0), at_row(mob, y0), at_row(chem, y0), at, size, mask
            )
            g = source(flow, rate[1 + s, span, :], a)
            pot[1 + y0, span, :] = g
            part[s, 0, span, :] = partial(
                a, at_row(conc, y0)(0, span), pair, at_row(curve, y0)(0, span), g
            )
            old = None if before is None else before[s, 0, span, :]
            grad[s, 0, span, :] = gain(a, mu, old)
        y1 = mirror(s, 1)
        for at, size in chunks(low, high):
            mask = face_mask(size, lanes, nz)
            span = slice(at, at + size)
            a, mu, _flow, pair = face_sums(at_row(adj, y1), None, at_row(chem, y1), at, size, mask)
            part[s, 1, span, :] = partial(
                a, at_row(conc, y1)(0, span), pair, at_row(curve, y1)(0, span), pot[1 + y1, span, :]
            )
            old = None if before is None else before[s, 1, span, :]
            grad[s, 1, span, :] = gain(a, mu, old)
        return 0

    lax.fori_loop(0, 2, side, 0)

    def close(i, _):
        s, k = i // 2, i % 2
        y = mirror(s, k)
        for at, size in chunks(low, high):
            mask = face_mask(size, lanes, nz)
            span = slice(at, at + size)
            _g, lap = laplace(row_of(pot, 1 + y), at, size, mask)
            store(s, k, span, part[s, k, span, :] - grad_energy * lap)
        return 0

    lax.fori_loop(0, 4, close, 0)


def sides_of(rows):
    return [(0, 0, 0), (0, 1, 1), (1, 0, rows - 1), (1, 1, rows - 2)]


def pack_kernel(steps, rows, cols, nz, conc_hbm, adj_hbm, rate_hbm, conc_out, adj_out, rate_out,
                main_up, main_dn, x_right, x_left, conc_in, adj_in, rate_in, sems):
    places, total = slots(steps)
    lanes = adj_out.shape[2]
    half = cols // 2
    lower = lax.broadcasted_iota(jnp.int32, (half, lanes), 1) < nz
    copies = [
        pltpu.make_async_copy(adj_hbm, adj_in, sems.at[0]),
        pltpu.make_async_copy(rate_hbm, rate_in, sems.at[1]),
    ] + [
        pltpu.make_async_copy(conc_hbm.at[steps - 1 - back], conc_in.at[back], sems.at[2 + back])
        for back in range(steps)
    ]
    for copy in copies:
        copy.start()

    def to_x(y, value, place):
        start, width = place
        x_right[y, start : start + width, :] = value[cols - width :, :]
        x_left[y, start : start + width, :] = value[:width, :]

    used = sum(places[-1])
    copies[0].wait()
    for y in range(rows):
        adj = adj_in[pl.ds(y, lanes, stride=rows), :].T
        adj_out[y] = adj
        to_x(y, adj, places[0])
        for side, at in ((main_dn, y), (main_up, y - rows + depth)):
            if 0 <= at < depth:
                side[pl.ds(at * cols, cols), :] = adj
    copies[1].wait()
    for y in range(rows):
        rate = rate_in[pl.ds(y, nz, stride=rows), :]
        rate = jnp.concatenate([rate] * (lanes // nz), axis=0).T
        rate_out[y] = rate
        to_x(y, rate, places[steps + 1])
        if used < total:
            x_right[y, used:, :] = jnp.zeros((total - used, lanes), f32)
            x_left[y, used:, :] = jnp.zeros((total - used, lanes), f32)
        for side, edge in ((main_dn, 0), (main_up, rows - 1)):
            if y == edge:
                side[pl.ds(early(steps) * cols, half), :] = jnp.where(
                    lower, rate[:half], rate[half:]
                )
    for back in range(steps):
        copies[2 + back].wait()
        for y in range(rows):
            conc = conc_in[back, pl.ds(y, lanes, stride=rows), :].T
            conc_out[back, y] = conc
            to_x(y, conc, places[1 + back])
            if back < 2:
                for side, at in ((main_dn, y), (main_up, y - rows + depth)):
                    if 0 <= at < depth:
                        side[pl.ds(((1 + back) * depth + at) * cols, cols), :] = conc


def put_own(out, row, value, y, place, cols, x_low, x_high):
    start, width = place
    right = pad + cols
    out[row, pad:right, :] = value
    out[row, pad - width : pad, :] = x_low[y, start : start + width, :]
    out[row, right : right + width, :] = x_high[y, start : start + width, :]


def put_halo(out, row, value, from_row, place, cols, corner):
    start, width = place
    right = pad + cols
    out[row, pad:right, :] = value
    out[row, pad - width : pad, :] = corner[0, from_row, start : start + width, :]
    out[row, right : right + width, :] = corner[1, from_row, start : start + width, :]


def corner_kernel(rows, x_low, x_high, to_up, to_dn):
    for i, side in enumerate((x_low, x_high)):
        to_up[i] = side[rows - depth :]
        to_dn[i] = side[:depth]


def first_interior(steps, rows, cols, nz, conc_own, adj_own, rate_own, x_low, x_high, edge_up,
                   edge_dn,
                   conc, adj, rate, chem, curve, pot, out, grad, mob, part):
    places, _ = slots(steps)
    low, high = reach(cols)
    lanes = adj.shape[2]
    for y in range(rows):
        at, low_x, high_x = y, x_low, x_high
        if y < depth:
            low_x, high_x = edge_dn.at[0], edge_dn.at[1]
        elif y >= rows - depth:
            at, low_x, high_x = y - rows + depth, edge_up.at[0], edge_up.at[1]
        put_own(conc, y, conc_own[0, y], at, places[1], cols, low_x, high_x)
        put_own(adj, y, adj_own[y], at, places[0], cols, low_x, high_x)
        put_own(rate, y, rate_own[y], at, places[steps + 1], cols, low_x, high_x)
    def mob_row(y, _):
        for at, size in chunks(low - 8, high + 8):
            c = conc[y, at : at + size, :]
            mob[y, at : at + size, :] = c * (1.0 - c)
        return 0

    def mu_row(y, _):
        for at, size in chunks(low, high):
            chem_row(row_of(conc, y), set_row(chem, y - 1), set_row(curve, y - 1), at, size,
                     face_mask(size, lanes, nz))
        return 0

    lax.fori_loop(0, rows, mob_row, 0)
    lax.fori_loop(1, rows - 1, mu_row, 0)

    def store(k, span, value):
        out[k, span, :] = value

    interior(rows, cols, nz, (conc, 0), (mob, 0), (chem, -1), (curve, -1), (adj, 0), (rate, 0),
             pot, part, grad, None, store)


def copy_rows(pairs):
    for out, to, ref, at in pairs:
        out[to] = ref[at]


def send_rows(out, to_up, to_dn, cols):
    low, high = reach(cols)
    for k in range(depth):
        to_dn[k] = out[0, k, low:high, :]
        to_up[depth - 1 - k] = out[1, k, low:high, :]


def first_boundary(steps, rows, cols, nz, conc_in, adj_in, rate_in, chem_in, curve_in, pot_in,
                   from_dn, from_up, c_low, c_high,
                   out, grad, rate, to_up, to_dn, conc, adj, mob, chem, curve, pot, part):
    places, _ = slots(steps)
    low, high = reach(cols)
    half = cols // 2
    lanes = conc.shape[2]
    lower = lax.broadcasted_iota(jnp.int32, (half, lanes), 1) < nz

    def unpack(side):
        packed = side[pl.ds(early(steps) * cols, half), :]
        turned = pltpu.roll(packed, lanes // 2, 1)
        return jnp.concatenate(
            [jnp.where(lower, packed, turned), jnp.where(lower, turned, packed)], axis=0
        )

    near = [0, 1, 2, rows - 3, rows - 2, rows - 1]
    for y in near:
        conc[depth + y] = conc_in[y]
        adj[depth + y] = adj_in[y]
    for y in (1, 2, rows - 3, rows - 2):
        chem[1 + y] = chem_in[y - 1]
        pot[1 + y] = pot_in[y - 1]
    for y in (1, rows - 2):
        curve[1 + y] = curve_in[y - 1]
    for at in range(depth):
        for ref, place, base in ((conc, places[1], depth), (adj, places[0], 0)):
            rows_in = pl.ds((base + at) * cols, cols)
            put_halo(ref, at, from_dn[rows_in, :], at, place, cols, c_low)
            put_halo(ref, depth + rows + at, from_up[rows_in, :], at, place, cols, c_high)
    put_halo(rate, 0, unpack(from_dn), depth - 1, places[steps + 1], cols, c_low)
    rate[1] = rate_in[0]
    rate[2] = rate_in[rows - 1]
    put_halo(rate, 3, unpack(from_up), 0, places[steps + 1], cols, c_high)
    for row in [0, 1, 2, 3, rows, rows + 1, rows + 2, rows + 3]:
        for at, size in chunks(low - 8, high + 8):
            c = conc[row, at : at + size, :]
            mob[row, at : at + size, :] = c * (1.0 - c)

    def store(s, k, span, value):
        out[s, k, span, :] = value

    boundary(rows, cols, nz, (conc, depth), (mob, depth), (chem, 1), (curve, 1), (adj, depth),
             rate, pot, part, grad, None, store, True)
    send_rows(out, to_up, to_dn, cols)


def prepare_kernel(steps, rows, cols, nz, back, conc_own, from_dn, from_up, x_low, x_high, c_low,
                   c_high, conc, mob, chem, curve, *late):
    places, _ = slots(steps)
    low, high = reach(cols)
    lanes = conc.shape[2]
    place = places[1 + back]
    for y in range(rows):
        put_own(conc, depth + y, conc_own[back, y], y, place, cols, x_low, x_high)
    for at in range(depth):
        rows_in = pl.ds((((1 + back) if back < 2 else (back - 2)) * depth + at) * cols, cols)
        put_halo(conc, at, from_dn[rows_in, :], at, place, cols, c_low)
        put_halo(conc, depth + rows + at, from_up[rows_in, :], at, place, cols, c_high)

    if late:
        late_up, late_dn = late
        for after in range(2, steps):
            for at in range(depth):
                span = pl.ds(((after - 2) * depth + at) * cols, cols)
                late_dn[span, :] = conc_own[after, at]
                late_up[span, :] = conc_own[after, rows - depth + at]

    def mob_row(row, _):
        for at, size in chunks(low - 8, high + 8):
            c = conc[row, at : at + size, :]
            mob[row, at : at + size, :] = c * (1.0 - c)
        return 0

    def mu_row(row, _):
        for at, size in chunks(low, high):
            chem_row(row_of(conc, row + 1), set_row(chem, row), set_row(curve, row), at, size,
                     face_mask(size, lanes, nz))
        return 0

    lax.fori_loop(0, rows + 2 * depth, mob_row, 0)
    lax.fori_loop(0, rows + 2, mu_row, 0)


def next_interior(rows, cols, nz, final, conc, mob, chem, curve, rate, inner, outer, before,
                  *rest):
    if final:
        out, grad_out, pot, adj, part, grad, result = rest
    else:
        result, grad, pot, adj, part = rest
    for k in range(rows - 2 * depth):
        adj[depth + k] = inner[k]
    for s, k, y in sides_of(rows):
        adj[y] = outer[s, k]

    def store(k, span, value):
        result[k, span, :] = value

    interior(rows, cols, nz, (conc, depth), (mob, depth), (chem, 1), (curve, 1), (adj, 0),
             (rate, 0), pot, part, grad, before, store)
    if final:
        for k in range(rows - 2 * depth):
            out[k] = result[k, pad : pad + cols, :].T
            grad_out[k] = fold(grad[k, pad : pad + cols, :].T, nz)


def fold(value, nz):
    total = value[:nz]
    for frame in range(1, value.shape[0] // nz):
        total = total + value[frame * nz : (frame + 1) * nz]
    return total


def next_boundary(rows, cols, nz, final, conc, mob, chem, curve, rate, inner, outer, pot_in,
                  before, from_dn, from_up, *rest):
    low, high = reach(cols)
    if final:
        inner_out, inner_grad, out, grad_out, adj, pot, part, grad, result = rest
    else:
        _conc_low, _conc_high, result, grad, to_up, to_dn, adj, pot, part = rest
    adj[2 * depth] = inner[0]
    adj[rows - 1] = inner[rows - 2 * depth - 1]
    for s, k, y in sides_of(rows):
        adj[depth + y] = outer[s, k]
    for at in range(depth):
        adj[at, low:high, :] = from_dn[at]
        adj[depth + rows + at, low:high, :] = from_up[at]
    for y in (1, 2, rows - 3, rows - 2):
        pot[1 + y] = pot_in[y - 1]

    def store(s, k, span, value):
        result[s, k, span, :] = value

    boundary(rows, cols, nz, (conc, depth), (mob, depth), (chem, 1), (curve, 1), (adj, depth),
             rate, pot, part, grad, before, store, False)
    if final:
        lanes = conc.shape[2]
        for k in range(rows - 2 * depth):
            out[pl.ds(depth + k, lanes, stride=rows), :] = inner_out[k]
            grad_out[pl.ds(depth + k, nz, stride=rows), :] = inner_grad[k]
        for s, k, y in sides_of(rows):
            out[pl.ds(y, lanes, stride=rows), :] = result[s, k, pad : pad + cols, :].T
            grad_out[pl.ds(y, nz, stride=rows), :] = fold(grad[s, k, pad : pad + cols, :].T, nz)
    else:
        send_rows(result, to_up, to_dn, cols)


def call(kernel, outs, scratch, *operands, cost=0, far=False):
    space = pltpu.HBM if far else pltpu.VMEM
    limit = far_limit if far else vmem_limit
    return pl.pallas_call(
        kernel,
        out_shape=[jax.ShapeDtypeStruct(shape, f32) for shape in outs],
        in_specs=[pl.BlockSpec(memory_space=space)] * len(operands),
        out_specs=[pl.BlockSpec(memory_space=pltpu.VMEM)] * len(outs),
        scratch_shapes=[pltpu.VMEM(s, f32) if isinstance(s, tuple) else s for s in scratch],
        compiler_params=pltpu.CompilerParams(vmem_limit_bytes=limit),
        cost_estimate=pl.CostEstimate(
            flops=cost * 1_000_000, bytes_accessed=cost * 2_000_000, transcendentals=0
        ),
    )(*operands)


def shift(value, axis, by):
    count = lax.axis_size(axis)
    return lax.ppermute(value, axis, [(i, (i + by) % count) for i in range(count)])


def shards(saved_conc, adjoint_end, rate_field):
    steps, frames, nz, rows, cols = saved_conc.shape
    lanes = frames * nz
    _, total = slots(steps)
    width = cols + 2 * pad
    flat = lanes * rows
    inside = rows - 2 * depth

    def field(count):
        return (count, width, lanes)

    conc_own, adj_own, rate_own, main_up, main_dn, x_right, x_left = call(
        functools.partial(pack_kernel, steps, rows, cols, nz),
        [(steps, rows, cols, lanes), (rows, cols, lanes), (rows, cols, lanes)]
        + [(early(steps) * cols + cols // 2, lanes)] * 2
        + [(rows, total, lanes)] * 2,
        [(steps, flat, cols), (flat, cols), (nz * rows, cols)]
        + [pltpu.SemaphoreType.DMA((2 + steps,))],
        saved_conc.reshape(steps, flat, cols),
        adjoint_end.reshape(flat, cols),
        rate_field.reshape(nz * rows, cols),
        cost=3,
        far=True,
    )
    x_low = shift(x_right, "gx", 1)
    x_high = shift(x_left, "gx", -1)
    from_dn = shift(main_up, "gy", 1)
    from_up = shift(main_dn, "gy", -1)
    corner_up, corner_dn = call(
        functools.partial(corner_kernel, rows), [(2, depth, total, lanes)] * 2, [], x_low, x_high
    )
    c_low = shift(corner_up, "gy", 1)
    c_high = shift(corner_dn, "gy", -1)

    conc, adj, rate_in, chem, curve, pot, inner, inner_grad = call(
        functools.partial(first_interior, steps, rows, cols, nz),
        [field(rows)] * 3 + [field(rows - 2)] * 3 + [field(inside)] * 2,
        [field(rows), field(inside)],
        conc_own, adj_own, rate_own, x_low, x_high, corner_up, corner_dn,
        cost=3,
    )

    both = (2, depth, width, lanes)
    edge = (depth, cols + 16, lanes)
    outer, outer_grad, rate, to_up, to_dn = call(
        functools.partial(first_boundary, steps, rows, cols, nz),
        [both, both, field(4), edge, edge],
        [field(rows + 2 * depth)] * 3 + [field(rows + 2)] * 3 + [both],
        conc, adj, rate_in, chem, curve, pot, from_dn, from_up, c_low, c_high,
        cost=2,
    )
    conc_low, conc_high = from_dn, from_up
    for back in range(1, steps):
        low, high = shift(to_up, "gy", 1), shift(to_dn, "gy", -1)
        final = back == steps - 1
        late = [((steps - 2) * depth * cols, lanes)] * 2 if back == 1 and steps > 2 else []
        fields = call(
            functools.partial(prepare_kernel, steps, rows, cols, nz, back),
            [field(rows + 2 * depth)] * 2 + [field(rows + 2)] * 2 + late,
            [],
            conc_own, conc_low, conc_high, x_low, x_high, c_low, c_high,
            cost=2,
        )
        if late:
            conc_low, conc_high = shift(fields[4], "gy", 1), shift(fields[5], "gy", -1)
            fields = fields[:4]
        tiles = [(inside, lanes, cols), (inside, nz, cols)]
        results = call(
            functools.partial(next_interior, rows, cols, nz, final),
            (tiles if final else [field(inside)] * 2) + [field(rows - 2)],
            [field(rows), field(inside)] + ([field(inside)] * 2 if final else []),
            *fields, rate_in, inner, outer, inner_grad,
            cost=3,
        )
        pot = results[2]
        if final:
            adj, grad = call(
                functools.partial(next_boundary, rows, cols, nz, final),
                [(flat, cols), (nz * rows, cols)],
                [field(rows + 2 * depth), field(rows + 2), both, both, both],
                *fields, rate, inner, outer, pot, outer_grad, low, high, results[0], results[1],
                cost=3,
            )
        else:
            new_outer, outer_grad, to_up, to_dn = call(
                functools.partial(next_boundary, rows, cols, nz, final),
                [both, both, edge, edge],
                [field(rows + 2 * depth), field(rows + 2), both],
                *fields, rate, inner, outer, pot, outer_grad, low, high, conc_low, conc_high,
                cost=2,
            )
            inner, inner_grad, outer = results[0], results[1], new_outer
    return adj.reshape(adjoint_end.shape), grad.reshape(rate_field.shape)


def solution(mesh):
    return jax.shard_map(
        shards,
        mesh=mesh,
        in_specs=(P(None, None, None, "gy", "gx"), P(None, None, "gy", "gx"), P(None, "gy", "gx")),
        out_specs=(P(None, None, "gy", "gx"), P(None, "gy", "gx")),
        check_vma=False,
    )
```

```python
import functools

import jax
import jax.numpy as jnp
from jax import lax
from jax.experimental import pallas as pl
from jax.experimental.pallas import tpu as pltpu
from jax.sharding import PartitionSpec as P

mix_energy = 2.5
grad_energy = 1.0
time_step = 0.1
diff_step = 0.03
bath_potential = 0.5

pad = 16
chunk = 24
depth = 2
early = 1
vmem_limit = 20 * 1024 * 1024
far_limit = 20 * 1024 * 1024
f32 = jnp.float32


def slots(steps):
    widths = [2 * steps] + [2 * steps - 2 * back for back in range(steps)] + [2 * steps - 1]
    starts = [sum(widths[:i]) for i in range(len(widths))]
    total = -(-sum(widths) // 8) * 8
    return list(zip(starts, widths)), total


def chunks(low, high):
    return [(at, min(chunk, high - at)) for at in range(low, high, chunk)]


def reach(cols):
    return pad - 8, pad + cols + 8


def up(value):
    return pltpu.roll(value, value.shape[1] - 1, 1)


def down(value):
    return pltpu.roll(value, 1, 1)


def face_mask(size, lanes, nz):
    lane = lax.broadcasted_iota(jnp.int32, (size, lanes), 1)
    return jnp.where(lane % nz == nz - 1, 0.0, 1.0).astype(f32)


def row_of(ref, y):
    return lambda dy, cut: ref[y + dy, cut, :]


def laplace(field, at, size, mask):
    span = slice(at, at + size)
    here = field(0, span)
    step_z = (up(here) - here) * mask
    sides = field(0, slice(at + 1, at + size + 1)) + field(0, slice(at - 1, at + size - 1))
    return here, (
        (sides + (field(-1, span) + field(1, span))) - 4.0 * here + (step_z - down(step_z))
    )


def chem_row(conc, chem, curve, at, size, mask):
    c, lap = laplace(conc, at, size, mask)
    inv = 1.0 / (c * (1.0 - c))
    span = slice(at, at + size)
    chem(span, jnp.log(c * c * inv) + mix_energy * (1.0 - 2.0 * c) - grad_energy * lap)
    curve(span, inv - 2.0 * mix_energy)


def face_sums(adj, mob, chem, at, size, mask):
    span = slice(at, at + size)
    a = adj(0, span)
    m = None if mob is None else mob(0, span)
    mu = None if chem is None else chem(0, span)
    flow = pair = None
    for dy, cut in (
        (0, slice(at + 1, at + size + 1)),
        (0, slice(at - 1, at + size - 1)),
        (1, span),
        (-1, span),
    ):
        diff = adj(dy, cut) - a
        if mob is not None:
            term = (mob(dy, cut) + m) * diff
            flow = term if flow is None else flow + term
        if chem is not None:
            term = (chem(dy, cut) - mu) * diff
            pair = term if pair is None else pair + term
    diff = (up(a) - a) * mask
    if mob is not None:
        term = (up(m) + m) * diff
        flow = flow + (term - down(term))
    if chem is not None:
        term = (up(mu) - mu) * diff
        pair = pair + (term + down(term))
    return a, mu, flow, pair


def source(flow, rate, a):
    return (0.5 * diff_step) * flow - time_step * rate * a


def partial(a, c, pair, curve, g):
    return a + (1.0 - 2.0 * c) * ((-0.5 * diff_step) * pair) + curve * g


def gain(a, mu, before):
    value = time_step * a * (bath_potential - mu)
    return value if before is None else before + value


def set_row(ref, y):
    def put(span, value):
        ref[y, span, :] = value

    return put


def interior(rows, cols, nz, conc, mob, chem, curve, adj, rate, pot, part, grad, before, store):
    low, high = reach(cols)
    lanes = adj[0].shape[-1]

    def at_row(field, y):
        return row_of(field[0], field[1] + y)

    def body(y, _):
        for at, size in chunks(low, high):
            mask = face_mask(size, lanes, nz)
            span = slice(at, at + size)
            a, mu, flow, pair = face_sums(
                at_row(adj, y), at_row(mob, y), at_row(chem, y), at, size, mask
            )
            g = source(flow, at_row(rate, y)(0, span), a)
            pot[y - 1, span, :] = g
            part[y - depth, span, :] = partial(
                a, at_row(conc, y)(0, span), pair, at_row(curve, y)(0, span), g
            )
            old = None if before is None else before[y - depth, span, :]
            grad[y - depth, span, :] = gain(a, mu, old)
        return 0

    def edge(i, _):
        y = 1 + i * (rows - 3)
        for at, size in chunks(low, high):
            mask = face_mask(size, lanes, nz)
            a, _mu, flow, _pair = face_sums(at_row(adj, y), at_row(mob, y), None, at, size, mask)
            span = slice(at, at + size)
            pot[y - 1, span, :] = source(flow, at_row(rate, y)(0, span), a)
        return 0

    def close(y, _):
        for at, size in chunks(low, high):
            mask = face_mask(size, lanes, nz)
            span = slice(at, at + size)
            _g, lap = laplace(row_of(pot, y - 1), at, size, mask)
            store(y - depth, span, part[y - depth, span, :] - grad_energy * lap)
        return 0

    lax.fori_loop(depth, rows - depth, body, 0)
    lax.fori_loop(0, 2, edge, 0)
    lax.fori_loop(depth, rows - depth, close, 0)


def boundary(rows, cols, nz, conc, mob, chem, curve, adj, rate, pot, part, grad, before, store,
             fresh):
    low, high = reach(cols)
    lanes = adj[0].shape[-1]
    last = rows - 1

    def at_row(field, y):
        return row_of(field[0], field[1] + y)

    def mirror(s, y):
        return y + s * (last - 2 * y)

    if fresh:

        def mu_side(i, _):
            s, k = i // 2, i % 2
            y = mirror(s, k - 1)
            for at, size in chunks(low, high):
                chem_row(at_row(conc, y), set_row(chem[0], chem[1] + y),
                         set_row(curve[0], curve[1] + y), at, size, face_mask(size, lanes, nz))
            return 0

        lax.fori_loop(0, 4, mu_side, 0)

    def side(s, _):
        y = mirror(s, -1)
        for at, size in chunks(low, high):
            mask = face_mask(size, lanes, nz)
            span = slice(at, at + size)
            a, _mu, flow, _pair = face_sums(at_row(adj, y), at_row(mob, y), None, at, size, mask)
            pot[1 + y, span, :] = source(flow, rate[3 * s, span, :], a)
        y0 = mirror(s, 0)
        for at, size in chunks(low, high):
            mask = face_mask(size, lanes, nz)
            span = slice(at, at + size)
            a, mu, flow, pair = face_sums(
                at_row(adj, y0), at_row(mob, y0), at_row(chem, y0), at, size, mask
            )
            g = source(flow, rate[1 + s, span, :], a)
            pot[1 + y0, span, :] = g
            part[s, 0, span, :] = partial(
                a, at_row(conc, y0)(0, span), pair, at_row(curve, y0)(0, span), g
            )
            old = None if before is None else before[s, 0, span, :]
            grad[s, 0, span, :] = gain(a, mu, old)
        y1 = mirror(s, 1)
        for at, size in chunks(low, high):
            mask = face_mask(size, lanes, nz)
            span = slice(at, at + size)
            a, mu, _flow, pair = face_sums(at_row(adj, y1), None, at_row(chem, y1), at, size, mask)
            part[s, 1, span, :] = partial(
                a, at_row(conc, y1)(0, span), pair, at_row(curve, y1)(0, span), pot[1 + y1, span, :]
            )
            old = None if before is None else before[s, 1, span, :]
            grad[s, 1, span, :] = gain(a, mu, old)
        return 0

    lax.fori_loop(0, 2, side, 0)

    def close(i, _):
        s, k = i // 2, i % 2
        y = mirror(s, k)
        for at, size in chunks(low, high):
            mask = face_mask(size, lanes, nz)
            span = slice(at, at + size)
            _g, lap = laplace(row_of(pot, 1 + y), at, size, mask)
            store(s, k, span, part[s, k, span, :] - grad_energy * lap)
        return 0

    lax.fori_loop(0, 4, close, 0)


def is_even(axis):
    return lax.rem(lax.axis_index(axis), 2) == 0


def bases(rows):
    even = is_even("gy")
    top = rows - depth
    return jnp.where(even, top, 0), jnp.where(even, 0, top)


def landings(rows):
    even = is_even("gy")
    top = rows + depth
    return jnp.where(even, top, 0), jnp.where(even, 0, top)


def sides_of(rows):
    return [(0, 0, 0), (0, 1, 1), (1, 0, rows - 1), (1, 1, rows - 2)]


def pack_kernel(steps, rows, cols, nz, conc_hbm, adj_hbm, rate_hbm, conc_out, adj_out, rate_out,
                main_a, main_b, x_a, x_b, conc_in, adj_in, rate_in, sems):
    places, total = slots(steps)
    lanes = adj_out.shape[2]
    half = cols // 2
    lower = lax.broadcasted_iota(jnp.int32, (half, lanes), 1) < nz
    copies = [
        pltpu.make_async_copy(adj_hbm, adj_in, sems.at[0]),
        pltpu.make_async_copy(rate_hbm, rate_in, sems.at[1]),
    ] + [
        pltpu.make_async_copy(conc_hbm.at[steps - 1 - back], conc_in.at[back], sems.at[2 + back])
        for back in range(steps)
    ]
    for copy in copies:
        copy.start()

    even_x = is_even("gx")

    def to_x(y, value, place):
        start, width = place
        last, first = value[cols - width :, :], value[:width, :]
        x_a[y, start : start + width, :] = jnp.where(even_x, last, first)
        x_b[y, start : start + width, :] = jnp.where(even_x, first, last)

    used = sum(places[-1])
    copies[0].wait()
    for y in range(rows):
        adj = adj_in[pl.ds(y, lanes, stride=rows), :].T
        adj_out[y] = adj
        to_x(y, adj, places[0])
    copies[1].wait()
    for y in range(rows):
        rate = rate_in[pl.ds(y, nz, stride=rows), :]
        rate = jnp.concatenate([rate] * (lanes // nz), axis=0).T
        rate_out[y] = rate
        to_x(y, rate, places[steps + 1])
        if used < total:
            x_a[y, used:, :] = jnp.zeros((total - used, lanes), f32)
            x_b[y, used:, :] = jnp.zeros((total - used, lanes), f32)
    for back in range(steps):
        copies[2 + back].wait()
        for y in range(rows):
            conc = conc_in[back, pl.ds(y, lanes, stride=rows), :].T
            conc_out[back, y] = conc
            to_x(y, conc, places[1 + back])
    for side, base in zip((main_a, main_b), bases(rows)):
        for at in range(depth):
            side[pl.ds(at * cols, cols), :] = adj_out[base + at]
            for back in range(early):
                side[pl.ds(((1 + back) * depth + at) * cols, cols), :] = conc_out[back, base + at]
        edge = jnp.where(base == 0, 0, rows - 1)
        side[pl.ds((1 + early) * depth * cols, half), :] = jnp.where(
            lower, rate_out[edge, :half, :], rate_out[edge, half:, :]
        )


def put_own(out, row, value, y, place, cols, x_low, x_high):
    start, width = place
    right = pad + cols
    out[row, pad:right, :] = value
    out[row, pad - width : pad, :] = x_low[y, start : start + width, :]
    out[row, right : right + width, :] = x_high[y, start : start + width, :]


def put_halo(out, row, value, from_row, place, cols, corner):
    start, width = place
    right = pad + cols
    out[row, pad:right, :] = value
    out[row, pad - width : pad, :] = corner[0, from_row, start : start + width, :]
    out[row, right : right + width, :] = corner[1, from_row, start : start + width, :]


def corner_kernel(steps, rows, cols, got_a, got_b, conc_own, main_a,
                  x_low, x_high, corner_a, corner_b, *late):
    even_x = is_even("gx")
    x_low[...] = jnp.where(even_x, got_b[...], got_a[...])
    x_high[...] = jnp.where(even_x, got_a[...], got_b[...])
    for out, base in zip((corner_a, corner_b), bases(rows)):
        for at in range(depth):
            out[0, at] = x_low[base + at]
            out[1, at] = x_high[base + at]
    for out, base in zip(late, bases(rows)):
        for back in range(early, steps):
            for at in range(depth):
                span = pl.ds(((back - early) * depth + at) * cols, cols)
                out[span, :] = conc_own[back, base + at]


def first_interior(steps, rows, cols, nz, conc_own, adj_own, rate_own, x_low, x_high,
                   conc, adj, rate, chem, curve, pot, out, grad, mob, part):
    places, _ = slots(steps)
    low, high = reach(cols)
    lanes = adj.shape[2]
    for y in range(rows):
        put_own(conc, y, conc_own[0, y], y, places[1], cols, x_low, x_high)
        put_own(adj, y, adj_own[y], y, places[0], cols, x_low, x_high)
        put_own(rate, y, rate_own[y], y, places[steps + 1], cols, x_low, x_high)
    def mob_row(y, _):
        for at, size in chunks(low - 8, high + 8):
            c = conc[y, at : at + size, :]
            mob[y, at : at + size, :] = c * (1.0 - c)
        return 0

    def mu_row(y, _):
        for at, size in chunks(low, high):
            chem_row(row_of(conc, y), set_row(chem, y - 1), set_row(curve, y - 1), at, size,
                     face_mask(size, lanes, nz))
        return 0

    lax.fori_loop(0, rows, mob_row, 0)
    lax.fori_loop(1, rows - 1, mu_row, 0)

    def store(k, span, value):
        out[k, span, :] = value

    interior(rows, cols, nz, (conc, 0), (mob, 0), (chem, -1), (curve, -1), (adj, 0), (rate, 0),
             pot, part, grad, None, store)


def copy_rows(pairs):
    for out, to, ref, at in pairs:
        out[to] = ref[at]


def send_rows(out, to_a, to_b, cols):
    low, high = reach(cols)
    even = is_even("gy")
    for k in range(depth):
        for to, side in ((to_a, jnp.where(even, 1, 0)), (to_b, jnp.where(even, 0, 1))):
            to[k] = out[side, jnp.where(side == 1, depth - 1 - k, k), low:high, :]


def first_boundary(steps, rows, cols, nz, conc_in, adj_in, rate_in, chem_in, curve_in, pot_in,
                   from_a, from_b, corner_a, corner_b,
                   out, grad, rate, to_a, to_b, conc, adj, mob, chem, curve, pot, part):
    places, _ = slots(steps)
    low, high = reach(cols)
    half = cols // 2
    lanes = conc.shape[2]
    lower = lax.broadcasted_iota(jnp.int32, (half, lanes), 1) < nz

    def unpack(side):
        packed = side[pl.ds((1 + early) * depth * cols, half), :]
        turned = pltpu.roll(packed, lanes // 2, 1)
        return jnp.concatenate(
            [jnp.where(lower, packed, turned), jnp.where(lower, turned, packed)], axis=0
        )

    near = [0, 1, 2, rows - 3, rows - 2, rows - 1]
    for y in near:
        conc[depth + y] = conc_in[y]
        adj[depth + y] = adj_in[y]
    for y in (1, 2, rows - 3, rows - 2):
        chem[1 + y] = chem_in[y - 1]
        pot[1 + y] = pot_in[y - 1]
    for y in (1, rows - 2):
        curve[1 + y] = curve_in[y - 1]
    rate[1] = rate_in[0]
    rate[2] = rate_in[rows - 1]
    for halo, corner, base in zip((from_a, from_b), (corner_a, corner_b), landings(rows)):
        for at in range(depth):
            for ref, place, first in ((adj, places[0], 0), (conc, places[1], depth)):
                span = pl.ds((first + at) * cols, cols)
                put_halo(ref, base + at, halo[span, :], at, place, cols, corner)
        below = base == 0
        put_halo(rate, jnp.where(below, 0, 3), unpack(halo), jnp.where(below, depth - 1, 0),
                 places[steps + 1], cols, corner)
    for row in [0, 1, 2, 3, rows, rows + 1, rows + 2, rows + 3]:
        for at, size in chunks(low - 8, high + 8):
            c = conc[row, at : at + size, :]
            mob[row, at : at + size, :] = c * (1.0 - c)

    def store(s, k, span, value):
        out[s, k, span, :] = value

    boundary(rows, cols, nz, (conc, depth), (mob, depth), (chem, 1), (curve, 1), (adj, depth),
             rate, pot, part, grad, None, store, True)
    send_rows(out, to_a, to_b, cols)


def prepare_kernel(steps, rows, cols, nz, back, conc_own, from_a, from_b, x_low, x_high,
                   corner_a, corner_b, conc, mob, chem, curve):
    places, _ = slots(steps)
    low, high = reach(cols)
    lanes = conc.shape[2]
    place = places[1 + back]
    for y in range(rows):
        put_own(conc, depth + y, conc_own[back, y], y, place, cols, x_low, x_high)
    for halo, corner, base in zip((from_a, from_b), (corner_a, corner_b), landings(rows)):
        for at in range(depth):
            span = pl.ds(((back - early) * depth + at) * cols, cols)
            put_halo(conc, base + at, halo[span, :], at, place, cols, corner)

    def mob_row(row, _):
        for at, size in chunks(low - 8, high + 8):
            c = conc[row, at : at + size, :]
            mob[row, at : at + size, :] = c * (1.0 - c)
        return 0

    def mu_row(row, _):
        for at, size in chunks(low, high):
            chem_row(row_of(conc, row + 1), set_row(chem, row), set_row(curve, row), at, size,
                     face_mask(size, lanes, nz))
        return 0

    lax.fori_loop(0, rows + 2 * depth, mob_row, 0)
    lax.fori_loop(0, rows + 2, mu_row, 0)


def next_interior(rows, cols, nz, final, conc, mob, chem, curve, rate, inner, outer, before,
                  *rest):
    if final:
        out, grad_out, pot, adj, part, grad, result = rest
    else:
        result, grad, pot, adj, part = rest
    for k in range(rows - 2 * depth):
        adj[depth + k] = inner[k]
    for s, k, y in sides_of(rows):
        adj[y] = outer[s, k]

    def store(k, span, value):
        result[k, span, :] = value

    interior(rows, cols, nz, (conc, depth), (mob, depth), (chem, 1), (curve, 1), (adj, 0),
             (rate, 0), pot, part, grad, before, store)
    if final:
        for k in range(rows - 2 * depth):
            out[k] = result[k, pad : pad + cols, :].T
            grad_out[k] = fold(grad[k, pad : pad + cols, :].T, nz)


def fold(value, nz):
    total = value[:nz]
    for frame in range(1, value.shape[0] // nz):
        total = total + value[frame * nz : (frame + 1) * nz]
    return total


def next_boundary(rows, cols, nz, final, conc, mob, chem, curve, rate, inner, outer, pot_in,
                  before, from_a, from_b, *rest):
    low, high = reach(cols)
    if final:
        inner_out, inner_grad, out, grad_out, adj, pot, part, grad, result = rest
    else:
        result, grad, to_a, to_b, adj, pot, part = rest
    adj[2 * depth] = inner[0]
    adj[rows - 1] = inner[rows - 2 * depth - 1]
    for s, k, y in sides_of(rows):
        adj[depth + y] = outer[s, k]
    for halo, base in zip((from_a, from_b), landings(rows)):
        for at in range(depth):
            adj[base + at, low:high, :] = halo[at]
    for y in (1, 2, rows - 3, rows - 2):
        pot[1 + y] = pot_in[y - 1]

    def store(s, k, span, value):
        result[s, k, span, :] = value

    boundary(rows, cols, nz, (conc, depth), (mob, depth), (chem, 1), (curve, 1), (adj, depth),
             rate, pot, part, grad, before, store, False)
    if final:
        lanes = conc.shape[2]
        for k in range(rows - 2 * depth):
            out[pl.ds(depth + k, lanes, stride=rows), :] = inner_out[k]
            grad_out[pl.ds(depth + k, nz, stride=rows), :] = inner_grad[k]
        for s, k, y in sides_of(rows):
            out[pl.ds(y, lanes, stride=rows), :] = result[s, k, pad : pad + cols, :].T
            grad_out[pl.ds(y, nz, stride=rows), :] = fold(grad[s, k, pad : pad + cols, :].T, nz)
    else:
        send_rows(result, to_a, to_b, cols)


def call(kernel, outs, scratch, *operands, cost=0, far=False):
    space = pltpu.HBM if far else pltpu.VMEM
    limit = far_limit if far else vmem_limit
    return pl.pallas_call(
        kernel,
        out_shape=[jax.ShapeDtypeStruct(shape, f32) for shape in outs],
        in_specs=[pl.BlockSpec(memory_space=space)] * len(operands),
        out_specs=[pl.BlockSpec(memory_space=pltpu.VMEM)] * len(outs),
        scratch_shapes=[pltpu.VMEM(s, f32) if isinstance(s, tuple) else s for s in scratch],
        compiler_params=pltpu.CompilerParams(vmem_limit_bytes=limit),
        cost_estimate=pl.CostEstimate(
            flops=cost * 1_000_000, bytes_accessed=cost * 2_000_000, transcendentals=0
        ),
    )(*operands)


def swap(value_a, value_b, axis):
    count = lax.axis_size(axis)
    pairs_a = [(i, i + 1 - 2 * (i % 2)) for i in range(count)]
    pairs_b = [(i, (i - 1 + 2 * (i % 2)) % count) for i in range(count)]
    return lax.ppermute(value_a, axis, pairs_a), lax.ppermute(value_b, axis, pairs_b)


def shards(saved_conc, adjoint_end, rate_field):
    steps, frames, nz, rows, cols = saved_conc.shape
    lanes = frames * nz
    _, total = slots(steps)
    width = cols + 2 * pad
    flat = lanes * rows
    inside = rows - 2 * depth

    def field(count):
        return (count, width, lanes)

    conc_own, adj_own, rate_own, main_a, main_b, x_a, x_b = call(
        functools.partial(pack_kernel, steps, rows, cols, nz),
        [(steps, rows, cols, lanes), (rows, cols, lanes), (rows, cols, lanes)]
        + [((1 + early) * depth * cols + cols // 2, lanes)] * 2
        + [(rows, total, lanes)] * 2,
        [(steps, flat, cols), (flat, cols), (nz * rows, cols)]
        + [pltpu.SemaphoreType.DMA((2 + steps,))],
        saved_conc.reshape(steps, flat, cols),
        adjoint_end.reshape(flat, cols),
        rate_field.reshape(nz * rows, cols),
        cost=3,
        far=True,
    )
    main_a, main_b = swap(main_a, main_b, "gy")
    x_a, x_b = swap(x_a, x_b, "gx")
    x_low, x_high, corner_a, corner_b, late_a, late_b = call(
        functools.partial(corner_kernel, steps, rows, cols),
        [(rows, total, lanes)] * 2 + [(2, depth, total, lanes)] * 2
        + [((steps - early) * depth * cols, lanes)] * 2,
        [],
        x_a, x_b, conc_own, main_a,
    )
    late_a, late_b = swap(late_a, late_b, "gy")
    corner_a, corner_b = swap(corner_a, corner_b, "gy")

    conc, adj, rate_in, chem, curve, pot, inner, inner_grad = call(
        functools.partial(first_interior, steps, rows, cols, nz),
        [field(rows)] * 3 + [field(rows - 2)] * 3 + [field(inside)] * 2,
        [field(rows), field(inside)],
        conc_own, adj_own, rate_own, x_low, x_high,
        cost=3,
    )
    both = (2, depth, width, lanes)
    edge = (depth, cols + 16, lanes)
    outer, outer_grad, rate, to_a, to_b = call(
        functools.partial(first_boundary, steps, rows, cols, nz),
        [both, both, field(4), edge, edge],
        [field(rows + 2 * depth)] * 3 + [field(rows + 2)] * 3 + [both],
        conc, adj, rate_in, chem, curve, pot, main_a, main_b, corner_a, corner_b,
        cost=2,
    )
    for back in range(1, steps):
        adj_a, adj_b = swap(to_a, to_b, "gy")
        final = back == steps - 1
        fields = call(
            functools.partial(prepare_kernel, steps, rows, cols, nz, back),
            [field(rows + 2 * depth)] * 2 + [field(rows + 2)] * 2,
            [],
            conc_own, late_a, late_b, x_low, x_high, corner_a, corner_b,
            cost=2,
        )
        tiles = [(inside, lanes, cols), (inside, nz, cols)]
        results = call(
            functools.partial(next_interior, rows, cols, nz, final),
            (tiles if final else [field(inside)] * 2) + [field(rows - 2)],
            [field(rows), field(inside)] + ([field(inside)] * 2 if final else []),
            *fields, rate_in, inner, outer, inner_grad,
            cost=3,
        )
        pot = results[2]
        if final:
            adj, grad = call(
                functools.partial(next_boundary, rows, cols, nz, final),
                [(flat, cols), (nz * rows, cols)],
                [field(rows + 2 * depth), field(rows + 2), both, both, both],
                *fields, rate, inner, outer, pot, outer_grad, adj_a, adj_b, results[0], results[1],
                cost=3,
            )
        else:
            new_outer, outer_grad, to_a, to_b = call(
                functools.partial(next_boundary, rows, cols, nz, final),
                [both, both, edge, edge],
                [field(rows + 2 * depth), field(rows + 2), both],
                *fields, rate, inner, outer, pot, outer_grad, adj_a, adj_b,
                cost=2,
            )
            inner, inner_grad, outer = results[0], results[1], new_outer
    return adj.reshape(adjoint_end.shape), grad.reshape(rate_field.shape)


def solution(mesh):
    return jax.shard_map(
        shards,
        mesh=mesh,
        in_specs=(P(None, None, None, "gy", "gx"), P(None, None, "gy", "gx"), P(None, "gy", "gx")),
        out_specs=(P(None, None, "gy", "gx"), P(None, "gy", "gx")),
        check_vma=False,
    )
```

```python
import functools

import jax
import jax.numpy as jnp
from jax import lax
from jax.experimental import pallas as pl
from jax.experimental.pallas import tpu as pltpu
from jax.sharding import PartitionSpec as P

mix_energy = 2.5
grad_energy = 1.0
time_step = 0.1
diff_step = 0.03
bath_potential = 0.5

pad = 16
chunk = 24
depth = 2
vmem_limit = 20 * 1024 * 1024
f32 = jnp.float32


def slots(steps):
    widths = [2 * steps] + [2 * steps - 2 * back for back in range(steps)] + [2 * steps - 1]
    starts = [sum(widths[:i]) for i in range(len(widths))]
    total = -(-sum(widths) // 8) * 8
    return list(zip(starts, widths)), total


def chunks(low, high):
    return [(at, min(chunk, high - at)) for at in range(low, high, chunk)]


def reach(cols):
    return pad - 8, pad + cols + 8


def up(value):
    return pltpu.roll(value, value.shape[1] - 1, 1)


def down(value):
    return pltpu.roll(value, 1, 1)


def face_mask(size, lanes, nz):
    lane = lax.broadcasted_iota(jnp.int32, (size, lanes), 1)
    return jnp.where(lane % nz == nz - 1, 0.0, 1.0).astype(f32)


def row_of(ref, y):
    return lambda dy, cut: ref[y + dy, cut, :]


def laplace(field, at, size, mask):
    span = slice(at, at + size)
    here = field(0, span)
    step_z = (up(here) - here) * mask
    sides = field(0, slice(at + 1, at + size + 1)) + field(0, slice(at - 1, at + size - 1))
    return here, (
        (sides + (field(-1, span) + field(1, span))) - 4.0 * here + (step_z - down(step_z))
    )


def chem_row(conc, chem, curve, at, size, mask):
    c, lap = laplace(conc, at, size, mask)
    inv = 1.0 / (c * (1.0 - c))
    span = slice(at, at + size)
    chem(span, jnp.log(c * c * inv) + mix_energy * (1.0 - 2.0 * c) - grad_energy * lap)
    curve(span, inv - 2.0 * mix_energy)


def face_sums(adj, mob, chem, at, size, mask):
    span = slice(at, at + size)
    a = adj(0, span)
    m = None if mob is None else mob(0, span)
    mu = None if chem is None else chem(0, span)
    flow = pair = None
    for dy, cut in (
        (0, slice(at + 1, at + size + 1)),
        (0, slice(at - 1, at + size - 1)),
        (1, span),
        (-1, span),
    ):
        diff = adj(dy, cut) - a
        if mob is not None:
            term = (mob(dy, cut) + m) * diff
            flow = term if flow is None else flow + term
        if chem is not None:
            term = (chem(dy, cut) - mu) * diff
            pair = term if pair is None else pair + term
    diff = (up(a) - a) * mask
    if mob is not None:
        term = (up(m) + m) * diff
        flow = flow + (term - down(term))
    if chem is not None:
        term = (up(mu) - mu) * diff
        pair = pair + (term + down(term))
    return a, mu, flow, pair


def source(flow, rate, a):
    return (0.5 * diff_step) * flow - time_step * rate * a


def partial(a, c, pair, curve, g):
    return a + (1.0 - 2.0 * c) * ((-0.5 * diff_step) * pair) + curve * g


def gain(a, mu, before):
    value = time_step * a * (bath_potential - mu)
    return value if before is None else before + value


def set_row(ref, y):
    def put(span, value):
        ref[y, span, :] = value

    return put


def interior(rows, cols, nz, conc, mob, chem, curve, adj, rate, pot, part, grad, before, store):
    low, high = reach(cols)
    lanes = adj[0].shape[-1]

    def at_row(field, y):
        return row_of(field[0], field[1] + y)

    def body(y, _):
        for at, size in chunks(low, high):
            mask = face_mask(size, lanes, nz)
            span = slice(at, at + size)
            a, mu, flow, pair = face_sums(
                at_row(adj, y), at_row(mob, y), at_row(chem, y), at, size, mask
            )
            g = source(flow, at_row(rate, y)(0, span), a)
            pot[y - 1, span, :] = g
            part[y - depth, span, :] = partial(
                a, at_row(conc, y)(0, span), pair, at_row(curve, y)(0, span), g
            )
            old = None if before is None else before[y - depth, span, :]
            grad[y - depth, span, :] = gain(a, mu, old)
        return 0

    def edge(i, _):
        y = 1 + i * (rows - 3)
        for at, size in chunks(low, high):
            mask = face_mask(size, lanes, nz)
            a, _mu, flow, _pair = face_sums(at_row(adj, y), at_row(mob, y), None, at, size, mask)
            span = slice(at, at + size)
            pot[y - 1, span, :] = source(flow, at_row(rate, y)(0, span), a)
        return 0

    def close(y, _):
        for at, size in chunks(low, high):
            mask = face_mask(size, lanes, nz)
            span = slice(at, at + size)
            _g, lap = laplace(row_of(pot, y - 1), at, size, mask)
            store(y - depth, span, part[y - depth, span, :] - grad_energy * lap)
        return 0

    lax.fori_loop(depth, rows - depth, body, 0)
    lax.fori_loop(0, 2, edge, 0)
    lax.fori_loop(depth, rows - depth, close, 0)


def boundary(rows, cols, nz, conc, mob, chem, curve, adj, rate, pot, part, grad, before, store,
             fresh):
    low, high = reach(cols)
    lanes = adj[0].shape[-1]
    last = rows - 1

    def at_row(field, y):
        return row_of(field[0], field[1] + y)

    def mirror(s, y):
        return y + s * (last - 2 * y)

    if fresh:

        def mu_side(i, _):
            s, k = i // 2, i % 2
            y = mirror(s, k - 1)
            for at, size in chunks(low, high):
                chem_row(at_row(conc, y), set_row(chem[0], chem[1] + y),
                         set_row(curve[0], curve[1] + y), at, size, face_mask(size, lanes, nz))
            return 0

        lax.fori_loop(0, 4, mu_side, 0)

    def side(s, _):
        y = mirror(s, -1)
        for at, size in chunks(low, high):
            mask = face_mask(size, lanes, nz)
            span = slice(at, at + size)
            a, _mu, flow, _pair = face_sums(at_row(adj, y), at_row(mob, y), None, at, size, mask)
            pot[1 + y, span, :] = source(flow, rate[3 * s, span, :], a)
        y0 = mirror(s, 0)
        for at, size in chunks(low, high):
            mask = face_mask(size, lanes, nz)
            span = slice(at, at + size)
            a, mu, flow, pair = face_sums(
                at_row(adj, y0), at_row(mob, y0), at_row(chem, y0), at, size, mask
            )
            g = source(flow, rate[1 + s, span, :], a)
            pot[1 + y0, span, :] = g
            part[s, 0, span, :] = partial(
                a, at_row(conc, y0)(0, span), pair, at_row(curve, y0)(0, span), g
            )
            old = None if before is None else before[s, 0, span, :]
            grad[s, 0, span, :] = gain(a, mu, old)
        y1 = mirror(s, 1)
        for at, size in chunks(low, high):
            mask = face_mask(size, lanes, nz)
            span = slice(at, at + size)
            a, mu, _flow, pair = face_sums(at_row(adj, y1), None, at_row(chem, y1), at, size, mask)
            part[s, 1, span, :] = partial(
                a, at_row(conc, y1)(0, span), pair, at_row(curve, y1)(0, span), pot[1 + y1, span, :]
            )
            old = None if before is None else before[s, 1, span, :]
            grad[s, 1, span, :] = gain(a, mu, old)
        return 0

    lax.fori_loop(0, 2, side, 0)

    def close(i, _):
        s, k = i // 2, i % 2
        y = mirror(s, k)
        for at, size in chunks(low, high):
            mask = face_mask(size, lanes, nz)
            span = slice(at, at + size)
            _g, lap = laplace(row_of(pot, 1 + y), at, size, mask)
            store(s, k, span, part[s, k, span, :] - grad_energy * lap)
        return 0

    lax.fori_loop(0, 4, close, 0)


def is_even(axis):
    return lax.rem(lax.axis_index(axis), 2) == 0


def bases(rows):
    even = is_even("gy")
    top = rows - depth
    return jnp.where(even, top, 0), jnp.where(even, 0, top)


def landings(rows):
    even = is_even("gy")
    top = rows + depth
    return jnp.where(even, top, 0), jnp.where(even, 0, top)


def sides_of(rows):
    return [(0, 0, 0), (0, 1, 1), (1, 0, rows - 1), (1, 1, rows - 2)]


def edge_kernel(steps, rows, cols, nz, conc_hbm, adj_hbm, rate_hbm, conc_in, adj_in, rate_in,
                main_a, main_b, sems):
    lanes = main_a.shape[1]
    half = cols // 2
    lower = lax.broadcasted_iota(jnp.int32, (half, lanes), 1) < nz
    copies = [
        pltpu.make_async_copy(adj_hbm, adj_in, sems.at[0]),
        pltpu.make_async_copy(rate_hbm, rate_in, sems.at[1]),
    ] + [
        pltpu.make_async_copy(conc_hbm.at[steps - 1 - back], conc_in.at[back], sems.at[2 + back])
        for back in range(steps)
    ]
    for copy in copies:
        copy.start()
    copies[0].wait()
    for side, base in zip((main_a, main_b), bases(rows)):
        for at in range(depth):
            side[pl.ds(at * cols, cols), :] = adj_in[pl.ds(base + at, lanes, stride=rows), :].T
    copies[1].wait()
    for side, base in zip((main_a, main_b), bases(rows)):
        edge = jnp.where(base == 0, 0, rows - 1)
        rate = turned_rate(rate_in, edge, rows, nz, lanes)
        side[pl.ds((1 + steps) * depth * cols, half), :] = jnp.where(
            lower, rate[:half], rate[half:]
        )
    for back in range(steps):
        copies[2 + back].wait()
        for side, base in zip((main_a, main_b), bases(rows)):
            for at in range(depth):
                side[pl.ds(((1 + back) * depth + at) * cols, cols), :] = conc_in[
                    back, pl.ds(base + at, lanes, stride=rows), :
                ].T


def turned_rate(rate, y, rows, nz, lanes):
    value = rate[pl.ds(y, nz, stride=rows), :]
    return jnp.concatenate([value] * (lanes // nz), axis=0).T


def turn_kernel(steps, rows, cols, nz, conc_in, adj_in, rate_in, conc_out, adj_out, rate_out,
                x_a, x_b):
    places, total = slots(steps)
    lanes = adj_out.shape[2]
    even_x = is_even("gx")

    def to_x(y, value, place):
        start, width = place
        last, first = value[cols - width :, :], value[:width, :]
        x_a[y, start : start + width, :] = jnp.where(even_x, last, first)
        x_b[y, start : start + width, :] = jnp.where(even_x, first, last)

    used = sum(places[-1])
    for y in range(rows):
        adj = adj_in[pl.ds(y, lanes, stride=rows), :].T
        adj_out[y] = adj
        to_x(y, adj, places[0])
        rate = turned_rate(rate_in, y, rows, nz, lanes)
        rate_out[y] = rate
        to_x(y, rate, places[steps + 1])
        if used < total:
            x_a[y, used:, :] = jnp.zeros((total - used, lanes), f32)
            x_b[y, used:, :] = jnp.zeros((total - used, lanes), f32)
        for back in range(steps):
            conc = conc_in[back, pl.ds(y, lanes, stride=rows), :].T
            conc_out[back, y] = conc
            to_x(y, conc, places[1 + back])


def put_own(out, row, value, y, place, cols, x_low, x_high):
    start, width = place
    right = pad + cols
    out[row, pad:right, :] = value
    out[row, pad - width : pad, :] = x_low[y, start : start + width, :]
    out[row, right : right + width, :] = x_high[y, start : start + width, :]


def put_halo(out, row, value, from_row, place, cols, corner):
    start, width = place
    right = pad + cols
    out[row, pad:right, :] = value
    out[row, pad - width : pad, :] = corner[0, from_row, start : start + width, :]
    out[row, right : right + width, :] = corner[1, from_row, start : start + width, :]


def corner_kernel(rows, got_a, got_b, x_low, x_high, corner_a, corner_b):
    even_x = is_even("gx")
    x_low[...] = jnp.where(even_x, got_b[...], got_a[...])
    x_high[...] = jnp.where(even_x, got_a[...], got_b[...])
    for out, base in zip((corner_a, corner_b), bases(rows)):
        for at in range(depth):
            out[0, at] = x_low[base + at]
            out[1, at] = x_high[base + at]


def first_interior(steps, rows, cols, nz, conc_own, adj_own, rate_own, x_low, x_high,
                   conc, adj, rate, chem, curve, pot, out, grad, mob, part):
    places, _ = slots(steps)
    low, high = reach(cols)
    lanes = adj.shape[2]
    for y in range(rows):
        put_own(conc, y, conc_own[0, y], y, places[1], cols, x_low, x_high)
        put_own(adj, y, adj_own[y], y, places[0], cols, x_low, x_high)
        put_own(rate, y, rate_own[y], y, places[steps + 1], cols, x_low, x_high)
    def mob_row(y, _):
        for at, size in chunks(low - 8, high + 8):
            c = conc[y, at : at + size, :]
            mob[y, at : at + size, :] = c * (1.0 - c)
        return 0

    def mu_row(y, _):
        for at, size in chunks(low, high):
            chem_row(row_of(conc, y), set_row(chem, y - 1), set_row(curve, y - 1), at, size,
                     face_mask(size, lanes, nz))
        return 0

    lax.fori_loop(0, rows, mob_row, 0)
    lax.fori_loop(1, rows - 1, mu_row, 0)

    def store(k, span, value):
        out[k, span, :] = value

    interior(rows, cols, nz, (conc, 0), (mob, 0), (chem, -1), (curve, -1), (adj, 0), (rate, 0),
             pot, part, grad, None, store)


def copy_rows(pairs):
    for out, to, ref, at in pairs:
        out[to] = ref[at]


def send_rows(out, to_a, to_b, cols):
    low, high = reach(cols)
    even = is_even("gy")
    for k in range(depth):
        for to, side in ((to_a, jnp.where(even, 1, 0)), (to_b, jnp.where(even, 0, 1))):
            to[k] = out[side, jnp.where(side == 1, depth - 1 - k, k), low:high, :]


def first_boundary(steps, rows, cols, nz, conc_in, adj_in, rate_in, chem_in, curve_in, pot_in,
                   from_a, from_b, corner_a, corner_b,
                   out, grad, rate, to_a, to_b, conc, adj, mob, chem, curve, pot, part):
    places, _ = slots(steps)
    low, high = reach(cols)
    half = cols // 2
    lanes = conc.shape[2]
    lower = lax.broadcasted_iota(jnp.int32, (half, lanes), 1) < nz

    def unpack(side):
        packed = side[pl.ds((1 + steps) * depth * cols, half), :]
        turned = pltpu.roll(packed, lanes // 2, 1)
        return jnp.concatenate(
            [jnp.where(lower, packed, turned), jnp.where(lower, turned, packed)], axis=0
        )

    near = [0, 1, 2, rows - 3, rows - 2, rows - 1]
    for y in near:
        conc[depth + y] = conc_in[y]
        adj[depth + y] = adj_in[y]
    for y in (1, 2, rows - 3, rows - 2):
        chem[1 + y] = chem_in[y - 1]
        pot[1 + y] = pot_in[y - 1]
    for y in (1, rows - 2):
        curve[1 + y] = curve_in[y - 1]
    rate[1] = rate_in[0]
    rate[2] = rate_in[rows - 1]
    for halo, corner, base in zip((from_a, from_b), (corner_a, corner_b), landings(rows)):
        for at in range(depth):
            for ref, place, first in ((adj, places[0], 0), (conc, places[1], depth)):
                span = pl.ds((first + at) * cols, cols)
                put_halo(ref, base + at, halo[span, :], at, place, cols, corner)
        below = base == 0
        put_halo(rate, jnp.where(below, 0, 3), unpack(halo), jnp.where(below, depth - 1, 0),
                 places[steps + 1], cols, corner)
    for row in [0, 1, 2, 3, rows, rows + 1, rows + 2, rows + 3]:
        for at, size in chunks(low - 8, high + 8):
            c = conc[row, at : at + size, :]
            mob[row, at : at + size, :] = c * (1.0 - c)

    def store(s, k, span, value):
        out[s, k, span, :] = value

    boundary(rows, cols, nz, (conc, depth), (mob, depth), (chem, 1), (curve, 1), (adj, depth),
             rate, pot, part, grad, None, store, True)
    send_rows(out, to_a, to_b, cols)


def prepare_kernel(steps, rows, cols, nz, back, conc_own, from_a, from_b, x_low, x_high,
                   corner_a, corner_b, conc, mob, chem, curve):
    places, _ = slots(steps)
    low, high = reach(cols)
    lanes = conc.shape[2]
    place = places[1 + back]
    for y in range(rows):
        put_own(conc, depth + y, conc_own[back, y], y, place, cols, x_low, x_high)
    for halo, corner, base in zip((from_a, from_b), (corner_a, corner_b), landings(rows)):
        for at in range(depth):
            span = pl.ds(((1 + back) * depth + at) * cols, cols)
            put_halo(conc, base + at, halo[span, :], at, place, cols, corner)

    def mob_row(row, _):
        for at, size in chunks(low - 8, high + 8):
            c = conc[row, at : at + size, :]
            mob[row, at : at + size, :] = c * (1.0 - c)
        return 0

    def mu_row(row, _):
        for at, size in chunks(low, high):
            chem_row(row_of(conc, row + 1), set_row(chem, row), set_row(curve, row), at, size,
                     face_mask(size, lanes, nz))
        return 0

    lax.fori_loop(0, rows + 2 * depth, mob_row, 0)
    lax.fori_loop(0, rows + 2, mu_row, 0)


def next_interior(rows, cols, nz, final, conc, mob, chem, curve, rate, inner, outer, before,
                  *rest):
    if final:
        out, grad_out, pot, adj, part, grad, result = rest
    else:
        result, grad, pot, adj, part = rest
    for k in range(rows - 2 * depth):
        adj[depth + k] = inner[k]
    for s, k, y in sides_of(rows):
        adj[y] = outer[s, k]

    def store(k, span, value):
        result[k, span, :] = value

    interior(rows, cols, nz, (conc, depth), (mob, depth), (chem, 1), (curve, 1), (adj, 0),
             (rate, 0), pot, part, grad, before, store)
    if final:
        for k in range(rows - 2 * depth):
            out[k] = result[k, pad : pad + cols, :].T
            grad_out[k] = fold(grad[k, pad : pad + cols, :].T, nz)


def fold(value, nz):
    total = value[:nz]
    for frame in range(1, value.shape[0] // nz):
        total = total + value[frame * nz : (frame + 1) * nz]
    return total


def next_boundary(rows, cols, nz, final, conc, mob, chem, curve, rate, inner, outer, pot_in,
                  before, from_a, from_b, *rest):
    low, high = reach(cols)
    if final:
        inner_out, inner_grad, out, grad_out, adj, pot, part, grad, result = rest
    else:
        result, grad, to_a, to_b, adj, pot, part = rest
    adj[2 * depth] = inner[0]
    adj[rows - 1] = inner[rows - 2 * depth - 1]
    for s, k, y in sides_of(rows):
        adj[depth + y] = outer[s, k]
    for halo, base in zip((from_a, from_b), landings(rows)):
        for at in range(depth):
            adj[base + at, low:high, :] = halo[at]
    for y in (1, 2, rows - 3, rows - 2):
        pot[1 + y] = pot_in[y - 1]

    def store(s, k, span, value):
        result[s, k, span, :] = value

    boundary(rows, cols, nz, (conc, depth), (mob, depth), (chem, 1), (curve, 1), (adj, depth),
             rate, pot, part, grad, before, store, False)
    if final:
        lanes = conc.shape[2]
        for k in range(rows - 2 * depth):
            out[pl.ds(depth + k, lanes, stride=rows), :] = inner_out[k]
            grad_out[pl.ds(depth + k, nz, stride=rows), :] = inner_grad[k]
        for s, k, y in sides_of(rows):
            out[pl.ds(y, lanes, stride=rows), :] = result[s, k, pad : pad + cols, :].T
            grad_out[pl.ds(y, nz, stride=rows), :] = fold(grad[s, k, pad : pad + cols, :].T, nz)
    else:
        send_rows(result, to_a, to_b, cols)


def call(kernel, outs, scratch, *operands, cost=0, far=False):
    if far:
        operands = [pltpu.with_memory_space_constraint(value, pltpu.HBM) for value in operands]
    space = pl.ANY if far else pltpu.VMEM
    return pl.pallas_call(
        kernel,
        out_shape=[jax.ShapeDtypeStruct(shape, f32) for shape in outs],
        in_specs=[pl.BlockSpec(memory_space=space)] * len(operands),
        out_specs=[pl.BlockSpec(memory_space=pltpu.VMEM)] * len(outs),
        scratch_shapes=[pltpu.VMEM(s, f32) if isinstance(s, tuple) else s for s in scratch],
        compiler_params=pltpu.CompilerParams(vmem_limit_bytes=vmem_limit),
        cost_estimate=pl.CostEstimate(
            flops=cost * 1_000_000, bytes_accessed=cost * 2_000_000, transcendentals=0
        ),
    )(*operands)


def swap(value_a, value_b, axis):
    count = lax.axis_size(axis)
    pairs_a = [(i, i + 1 - 2 * (i % 2)) for i in range(count)]
    pairs_b = [(i, (i - 1 + 2 * (i % 2)) % count) for i in range(count)]
    return lax.ppermute(value_a, axis, pairs_a), lax.ppermute(value_b, axis, pairs_b)


def shards(saved_conc, adjoint_end, rate_field):
    steps, frames, nz, rows, cols = saved_conc.shape
    lanes = frames * nz
    _, total = slots(steps)
    width = cols + 2 * pad
    flat = lanes * rows
    inside = rows - 2 * depth

    def field(count):
        return (count, width, lanes)

    raw = [(steps, flat, cols), (flat, cols), (nz * rows, cols)]
    conc_raw, adj_raw, rate_raw, main_a, main_b = call(
        functools.partial(edge_kernel, steps, rows, cols, nz),
        raw + [((1 + steps) * depth * cols + cols // 2, lanes)] * 2,
        [pltpu.SemaphoreType.DMA((2 + steps,))],
        saved_conc.reshape(raw[0]), adjoint_end.reshape(raw[1]), rate_field.reshape(raw[2]),
        cost=2,
        far=True,
    )
    main_a, main_b = swap(main_a, main_b, "gy")
    conc_own, adj_own, rate_own, x_a, x_b = call(
        functools.partial(turn_kernel, steps, rows, cols, nz),
        [(steps, rows, cols, lanes), (rows, cols, lanes), (rows, cols, lanes)]
        + [(rows, total, lanes)] * 2,
        [],
        conc_raw, adj_raw, rate_raw,
        cost=1,
    )
    x_a, x_b = swap(x_a, x_b, "gx")
    x_low, x_high, corner_a, corner_b = call(
        functools.partial(corner_kernel, rows),
        [(rows, total, lanes)] * 2 + [(2, depth, total, lanes)] * 2,
        [],
        x_a, x_b,
    )
    corner_a, corner_b = swap(corner_a, corner_b, "gy")

    conc, adj, rate_in, chem, curve, pot, inner, inner_grad = call(
        functools.partial(first_interior, steps, rows, cols, nz),
        [field(rows)] * 3 + [field(rows - 2)] * 3 + [field(inside)] * 2,
        [field(rows), field(inside)],
        conc_own, adj_own, rate_own, x_low, x_high,
        cost=3,
    )
    both = (2, depth, width, lanes)
    edge = (depth, cols + 16, lanes)
    outer, outer_grad, rate, to_a, to_b = call(
        functools.partial(first_boundary, steps, rows, cols, nz),
        [both, both, field(4), edge, edge],
        [field(rows + 2 * depth)] * 3 + [field(rows + 2)] * 3 + [both],
        conc, adj, rate_in, chem, curve, pot, main_a, main_b, corner_a, corner_b,
        cost=2,
    )
    for back in range(1, steps):
        adj_a, adj_b = swap(to_a, to_b, "gy")
        final = back == steps - 1
        fields = call(
            functools.partial(prepare_kernel, steps, rows, cols, nz, back),
            [field(rows + 2 * depth)] * 2 + [field(rows + 2)] * 2,
            [],
            conc_own, main_a, main_b, x_low, x_high, corner_a, corner_b,
            cost=2,
        )
        tiles = [(inside, lanes, cols), (inside, nz, cols)]
        results = call(
            functools.partial(next_interior, rows, cols, nz, final),
            (tiles if final else [field(inside)] * 2) + [field(rows - 2)],
            [field(rows), field(inside)] + ([field(inside)] * 2 if final else []),
            *fields, rate_in, inner, outer, inner_grad,
            cost=3,
        )
        pot = results[2]
        if final:
            adj, grad = call(
                functools.partial(next_boundary, rows, cols, nz, final),
                [(flat, cols), (nz * rows, cols)],
                [field(rows + 2 * depth), field(rows + 2), both, both, both],
                *fields, rate, inner, outer, pot, outer_grad, adj_a, adj_b, results[0], results[1],
                cost=3,
            )
        else:
            new_outer, outer_grad, to_a, to_b = call(
                functools.partial(next_boundary, rows, cols, nz, final),
                [both, both, edge, edge],
                [field(rows + 2 * depth), field(rows + 2), both],
                *fields, rate, inner, outer, pot, outer_grad, adj_a, adj_b,
                cost=2,
            )
            inner, inner_grad, outer = results[0], results[1], new_outer
    return adj.reshape(adjoint_end.shape), grad.reshape(rate_field.shape)


def solution(mesh):
    return jax.shard_map(
        shards,
        mesh=mesh,
        in_specs=(P(None, None, None, "gy", "gx"), P(None, None, "gy", "gx"), P(None, "gy", "gx")),
        out_specs=(P(None, None, "gy", "gx"), P(None, "gy", "gx")),
        check_vma=False,
    )
```

```python
import functools

import jax
import jax.numpy as jnp
from jax import lax
from jax.experimental import pallas as pl
from jax.experimental.pallas import tpu as pltpu
from jax.sharding import PartitionSpec as P

mix_energy = 2.5
grad_energy = 1.0
time_step = 0.1
diff_step = 0.03
bath_potential = 0.5

pad = 16
chunk = 72
depth = 2
vmem_limit = 20 * 1024 * 1024
f32 = jnp.float32


def slots(steps):
    widths = [2 * steps] + [2 * steps - 2 * back for back in range(steps)] + [2 * steps - 1]
    starts = [sum(widths[:i]) for i in range(len(widths))]
    total = -(-sum(widths) // 8) * 8
    return list(zip(starts, widths)), total


def chunks(low, high):
    return [(at, min(chunk, high - at)) for at in range(low, high, chunk)]


def reach(cols):
    return pad - 8, pad + cols + 8


def up(value):
    return pltpu.roll(value, value.shape[1] - 1, 1)


def down(value):
    return pltpu.roll(value, 1, 1)


def face_mask(size, lanes, nz):
    lane = lax.broadcasted_iota(jnp.int32, (size, lanes), 1)
    return jnp.where(lane % nz == nz - 1, 0.0, 1.0).astype(f32)


def row_of(ref, y):
    return lambda dy, cut: ref[y + dy, cut, :]


def laplace(field, at, size, mask):
    span = slice(at, at + size)
    here = field(0, span)
    step_z = (up(here) - here) * mask
    sides = field(0, slice(at + 1, at + size + 1)) + field(0, slice(at - 1, at + size - 1))
    return here, (
        (sides + (field(-1, span) + field(1, span))) - 4.0 * here + (step_z - down(step_z))
    )


def chem_row(conc, chem, curve, at, size, mask):
    c, lap = laplace(conc, at, size, mask)
    inv = 1.0 / (c * (1.0 - c))
    span = slice(at, at + size)
    chem(span, jnp.log(c * c * inv) + mix_energy * (1.0 - 2.0 * c) - grad_energy * lap)
    curve(span, inv - 2.0 * mix_energy)


def face_sums(adj, mob, chem, at, size, mask):
    span = slice(at, at + size)
    a = adj(0, span)
    m = None if mob is None else mob(0, span)
    mu = None if chem is None else chem(0, span)
    flow = pair = None
    for dy, cut in (
        (0, slice(at + 1, at + size + 1)),
        (0, slice(at - 1, at + size - 1)),
        (1, span),
        (-1, span),
    ):
        diff = adj(dy, cut) - a
        if mob is not None:
            term = (mob(dy, cut) + m) * diff
            flow = term if flow is None else flow + term
        if chem is not None:
            term = (chem(dy, cut) - mu) * diff
            pair = term if pair is None else pair + term
    diff = (up(a) - a) * mask
    if mob is not None:
        term = (up(m) + m) * diff
        flow = flow + (term - down(term))
    if chem is not None:
        term = (up(mu) - mu) * diff
        pair = pair + (term + down(term))
    return a, mu, flow, pair


def source(flow, rate, a):
    return (0.5 * diff_step) * flow - time_step * rate * a


def partial(a, c, pair, curve, g):
    return a + (1.0 - 2.0 * c) * ((-0.5 * diff_step) * pair) + curve * g


def gain(a, mu, before):
    value = time_step * a * (bath_potential - mu)
    return value if before is None else before + value


def set_row(ref, y):
    def put(span, value):
        ref[y, span, :] = value

    return put


def interior(rows, cols, nz, conc, mob, chem, curve, adj, rate, pot, part, grad, before, store):
    low, high = reach(cols)
    lanes = adj[0].shape[-1]

    def at_row(field, y):
        return row_of(field[0], field[1] + y)

    def body(y, _):
        for at, size in chunks(low, high):
            mask = face_mask(size, lanes, nz)
            span = slice(at, at + size)
            a, mu, flow, pair = face_sums(
                at_row(adj, y), at_row(mob, y), at_row(chem, y), at, size, mask
            )
            g = source(flow, at_row(rate, y)(0, span), a)
            pot[y - 1, span, :] = g
            part[y - depth, span, :] = partial(
                a, at_row(conc, y)(0, span), pair, at_row(curve, y)(0, span), g
            )
            old = None if before is None else before[y - depth, span, :]
            grad[y - depth, span, :] = gain(a, mu, old)
        return 0

    def edge(i, _):
        y = 1 + i * (rows - 3)
        for at, size in chunks(low, high):
            mask = face_mask(size, lanes, nz)
            a, _mu, flow, _pair = face_sums(at_row(adj, y), at_row(mob, y), None, at, size, mask)
            span = slice(at, at + size)
            pot[y - 1, span, :] = source(flow, at_row(rate, y)(0, span), a)
        return 0

    def close(y, _):
        for at, size in chunks(low, high):
            mask = face_mask(size, lanes, nz)
            span = slice(at, at + size)
            _g, lap = laplace(row_of(pot, y - 1), at, size, mask)
            store(y - depth, span, part[y - depth, span, :] - grad_energy * lap)
        return 0

    lax.fori_loop(depth, rows - depth, body, 0)
    lax.fori_loop(0, 2, edge, 0)
    lax.fori_loop(depth, rows - depth, close, 0)


def boundary(rows, cols, nz, conc, mob, chem, curve, adj, rate, pot, part, grad, before, store,
             fresh):
    low, high = reach(cols)
    lanes = adj[0].shape[-1]
    last = rows - 1

    def at_row(field, y):
        return row_of(field[0], field[1] + y)

    def mirror(s, y):
        return y + s * (last - 2 * y)

    if fresh:

        def mu_side(i, _):
            s, k = i // 2, i % 2
            y = mirror(s, k - 1)
            for at, size in chunks(low, high):
                chem_row(at_row(conc, y), set_row(chem[0], chem[1] + y),
                         set_row(curve[0], curve[1] + y), at, size, face_mask(size, lanes, nz))
            return 0

        lax.fori_loop(0, 4, mu_side, 0)

    def side(s, _):
        y = mirror(s, -1)
        for at, size in chunks(low, high):
            mask = face_mask(size, lanes, nz)
            span = slice(at, at + size)
            a, _mu, flow, _pair = face_sums(at_row(adj, y), at_row(mob, y), None, at, size, mask)
            pot[1 + y, span, :] = source(flow, rate[3 * s, span, :], a)
        y0 = mirror(s, 0)
        for at, size in chunks(low, high):
            mask = face_mask(size, lanes, nz)
            span = slice(at, at + size)
            a, mu, flow, pair = face_sums(
                at_row(adj, y0), at_row(mob, y0), at_row(chem, y0), at, size, mask
            )
            g = source(flow, rate[1 + s, span, :], a)
            pot[1 + y0, span, :] = g
            part[s, 0, span, :] = partial(
                a, at_row(conc, y0)(0, span), pair, at_row(curve, y0)(0, span), g
            )
            old = None if before is None else before[s, 0, span, :]
            grad[s, 0, span, :] = gain(a, mu, old)
        y1 = mirror(s, 1)
        for at, size in chunks(low, high):
            mask = face_mask(size, lanes, nz)
            span = slice(at, at + size)
            a, mu, _flow, pair = face_sums(at_row(adj, y1), None, at_row(chem, y1), at, size, mask)
            part[s, 1, span, :] = partial(
                a, at_row(conc, y1)(0, span), pair, at_row(curve, y1)(0, span), pot[1 + y1, span, :]
            )
            old = None if before is None else before[s, 1, span, :]
            grad[s, 1, span, :] = gain(a, mu, old)
        return 0

    lax.fori_loop(0, 2, side, 0)

    def close(i, _):
        s, k = i // 2, i % 2
        y = mirror(s, k)
        for at, size in chunks(low, high):
            mask = face_mask(size, lanes, nz)
            span = slice(at, at + size)
            _g, lap = laplace(row_of(pot, 1 + y), at, size, mask)
            store(s, k, span, part[s, k, span, :] - grad_energy * lap)
        return 0

    lax.fori_loop(0, 4, close, 0)


def is_even(axis):
    return lax.rem(lax.axis_index(axis), 2) == 0


def bases(rows):
    even = is_even("gy")
    top = rows - depth
    return jnp.where(even, top, 0), jnp.where(even, 0, top)


def landings(rows):
    even = is_even("gy")
    top = rows + depth
    return jnp.where(even, top, 0), jnp.where(even, 0, top)


def sides_of(rows):
    return [(0, 0, 0), (0, 1, 1), (1, 0, rows - 1), (1, 1, rows - 2)]


def edge_kernel(steps, rows, cols, nz, conc_hbm, adj_hbm, rate_hbm, conc_in, adj_in, rate_in,
                main_a, main_b, sems):
    lanes = main_a.shape[1]
    half = cols // 2
    lower = lax.broadcasted_iota(jnp.int32, (half, lanes), 1) < nz
    copies = [
        pltpu.make_async_copy(adj_hbm, adj_in, sems.at[0]),
        pltpu.make_async_copy(rate_hbm, rate_in, sems.at[1]),
    ] + [
        pltpu.make_async_copy(conc_hbm.at[steps - 1 - back], conc_in.at[back], sems.at[2 + back])
        for back in range(steps)
    ]
    for copy in copies:
        copy.start()
    copies[0].wait()
    for side, base in zip((main_a, main_b), bases(rows)):
        for at in range(depth):
            side[pl.ds(at * cols, cols), :] = adj_in[pl.ds(base + at, lanes, stride=rows), :].T
    copies[1].wait()
    for side, base in zip((main_a, main_b), bases(rows)):
        edge = jnp.where(base == 0, 0, rows - 1)
        rate = turned_rate(rate_in, edge, rows, nz, lanes)
        side[pl.ds((1 + steps) * depth * cols, half), :] = jnp.where(
            lower, rate[:half], rate[half:]
        )
    for back in range(steps):
        copies[2 + back].wait()
        for side, base in zip((main_a, main_b), bases(rows)):
            for at in range(depth):
                side[pl.ds(((1 + back) * depth + at) * cols, cols), :] = conc_in[
                    back, pl.ds(base + at, lanes, stride=rows), :
                ].T


def turned_rate(rate, y, rows, nz, lanes):
    value = rate[pl.ds(y, nz, stride=rows), :]
    return jnp.concatenate([value] * (lanes // nz), axis=0).T


def turn_kernel(steps, rows, cols, nz, conc_in, adj_in, rate_in, conc_out, adj_out, rate_out,
                x_a, x_b):
    places, total = slots(steps)
    lanes = adj_out.shape[2]
    even_x = is_even("gx")

    def to_x(y, value, place):
        start, width = place
        last, first = value[cols - width :, :], value[:width, :]
        x_a[y, start : start + width, :] = jnp.where(even_x, last, first)
        x_b[y, start : start + width, :] = jnp.where(even_x, first, last)

    used = sum(places[-1])
    for y in range(rows):
        adj = adj_in[pl.ds(y, lanes, stride=rows), :].T
        adj_out[y] = adj
        to_x(y, adj, places[0])
        rate = turned_rate(rate_in, y, rows, nz, lanes)
        rate_out[y] = rate
        to_x(y, rate, places[steps + 1])
        if used < total:
            x_a[y, used:, :] = jnp.zeros((total - used, lanes), f32)
            x_b[y, used:, :] = jnp.zeros((total - used, lanes), f32)
        for back in range(steps):
            conc = conc_in[back, pl.ds(y, lanes, stride=rows), :].T
            conc_out[back, y] = conc
            to_x(y, conc, places[1 + back])


def put_own(out, row, value, y, place, cols, x_low, x_high):
    start, width = place
    right = pad + cols
    out[row, pad:right, :] = value
    out[row, pad - width : pad, :] = x_low[y, start : start + width, :]
    out[row, right : right + width, :] = x_high[y, start : start + width, :]


def put_halo(out, row, value, from_row, place, cols, corner):
    start, width = place
    right = pad + cols
    out[row, pad:right, :] = value
    out[row, pad - width : pad, :] = corner[0, from_row, start : start + width, :]
    out[row, right : right + width, :] = corner[1, from_row, start : start + width, :]


def corner_kernel(rows, got_a, got_b, x_low, x_high, corner_a, corner_b):
    even_x = is_even("gx")
    x_low[...] = jnp.where(even_x, got_b[...], got_a[...])
    x_high[...] = jnp.where(even_x, got_a[...], got_b[...])
    for out, base in zip((corner_a, corner_b), bases(rows)):
        for at in range(depth):
            out[0, at] = x_low[base + at]
            out[1, at] = x_high[base + at]


def first_interior(steps, rows, cols, nz, conc_own, adj_own, rate_own, x_low, x_high,
                   conc, adj, rate, chem, curve, pot, out, grad, mob, part):
    places, _ = slots(steps)
    low, high = reach(cols)
    lanes = adj.shape[2]
    for y in range(rows):
        put_own(conc, y, conc_own[0, y], y, places[1], cols, x_low, x_high)
        put_own(adj, y, adj_own[y], y, places[0], cols, x_low, x_high)
        put_own(rate, y, rate_own[y], y, places[steps + 1], cols, x_low, x_high)
    def mob_row(y, _):
        for at, size in chunks(low - 8, high + 8):
            c = conc[y, at : at + size, :]
            mob[y, at : at + size, :] = c * (1.0 - c)
        return 0

    def mu_row(y, _):
        for at, size in chunks(low, high):
            chem_row(row_of(conc, y), set_row(chem, y - 1), set_row(curve, y - 1), at, size,
                     face_mask(size, lanes, nz))
        return 0

    lax.fori_loop(0, rows, mob_row, 0)
    lax.fori_loop(1, rows - 1, mu_row, 0)

    def store(k, span, value):
        out[k, span, :] = value

    interior(rows, cols, nz, (conc, 0), (mob, 0), (chem, -1), (curve, -1), (adj, 0), (rate, 0),
             pot, part, grad, None, store)


def copy_rows(pairs):
    for out, to, ref, at in pairs:
        out[to] = ref[at]


def send_rows(out, to_a, to_b, cols):
    low, high = reach(cols)
    even = is_even("gy")
    for k in range(depth):
        for to, side in ((to_a, jnp.where(even, 1, 0)), (to_b, jnp.where(even, 0, 1))):
            to[k] = out[side, jnp.where(side == 1, depth - 1 - k, k), low:high, :]


def first_boundary(steps, rows, cols, nz, conc_in, adj_in, rate_in, chem_in, curve_in, pot_in,
                   from_a, from_b, corner_a, corner_b,
                   out, grad, rate, to_a, to_b, conc, adj, mob, chem, curve, pot, part):
    places, _ = slots(steps)
    low, high = reach(cols)
    half = cols // 2
    lanes = conc.shape[2]
    lower = lax.broadcasted_iota(jnp.int32, (half, lanes), 1) < nz

    def unpack(side):
        packed = side[pl.ds((1 + steps) * depth * cols, half), :]
        turned = pltpu.roll(packed, lanes // 2, 1)
        return jnp.concatenate(
            [jnp.where(lower, packed, turned), jnp.where(lower, turned, packed)], axis=0
        )

    near = [0, 1, 2, rows - 3, rows - 2, rows - 1]
    for y in near:
        conc[depth + y] = conc_in[y]
        adj[depth + y] = adj_in[y]
    for y in (1, 2, rows - 3, rows - 2):
        chem[1 + y] = chem_in[y - 1]
        pot[1 + y] = pot_in[y - 1]
    for y in (1, rows - 2):
        curve[1 + y] = curve_in[y - 1]
    rate[1] = rate_in[0]
    rate[2] = rate_in[rows - 1]
    for halo, corner, base in zip((from_a, from_b), (corner_a, corner_b), landings(rows)):
        for at in range(depth):
            for ref, place, first in ((adj, places[0], 0), (conc, places[1], depth)):
                span = pl.ds((first + at) * cols, cols)
                put_halo(ref, base + at, halo[span, :], at, place, cols, corner)
        below = base == 0
        put_halo(rate, jnp.where(below, 0, 3), unpack(halo), jnp.where(below, depth - 1, 0),
                 places[steps + 1], cols, corner)
    for row in [0, 1, 2, 3, rows, rows + 1, rows + 2, rows + 3]:
        for at, size in chunks(low - 8, high + 8):
            c = conc[row, at : at + size, :]
            mob[row, at : at + size, :] = c * (1.0 - c)

    def store(s, k, span, value):
        out[s, k, span, :] = value

    boundary(rows, cols, nz, (conc, depth), (mob, depth), (chem, 1), (curve, 1), (adj, depth),
             rate, pot, part, grad, None, store, True)
    send_rows(out, to_a, to_b, cols)


def prepare_kernel(steps, rows, cols, nz, back, conc_own, from_a, from_b, x_low, x_high,
                   corner_a, corner_b, conc, mob, chem, curve):
    places, _ = slots(steps)
    low, high = reach(cols)
    lanes = conc.shape[2]
    place = places[1 + back]
    for y in range(rows):
        put_own(conc, depth + y, conc_own[back, y], y, place, cols, x_low, x_high)
    for halo, corner, base in zip((from_a, from_b), (corner_a, corner_b), landings(rows)):
        for at in range(depth):
            span = pl.ds(((1 + back) * depth + at) * cols, cols)
            put_halo(conc, base + at, halo[span, :], at, place, cols, corner)

    def mob_row(row, _):
        for at, size in chunks(low - 8, high + 8):
            c = conc[row, at : at + size, :]
            mob[row, at : at + size, :] = c * (1.0 - c)
        return 0

    def mu_row(row, _):
        for at, size in chunks(low, high):
            chem_row(row_of(conc, row + 1), set_row(chem, row), set_row(curve, row), at, size,
                     face_mask(size, lanes, nz))
        return 0

    lax.fori_loop(0, rows + 2 * depth, mob_row, 0)
    lax.fori_loop(0, rows + 2, mu_row, 0)


def next_interior(rows, cols, nz, final, conc, mob, chem, curve, rate, inner, outer, before,
                  *rest):
    if final:
        out, grad_out, pot, adj, part, grad, result = rest
    else:
        result, grad, pot, adj, part = rest
    for k in range(rows - 2 * depth):
        adj[depth + k] = inner[k]
    for s, k, y in sides_of(rows):
        adj[y] = outer[s, k]

    def store(k, span, value):
        result[k, span, :] = value

    interior(rows, cols, nz, (conc, depth), (mob, depth), (chem, 1), (curve, 1), (adj, 0),
             (rate, 0), pot, part, grad, before, store)
    if final:
        for k in range(rows - 2 * depth):
            out[k] = result[k, pad : pad + cols, :].T
            grad_out[k] = fold(grad[k, pad : pad + cols, :].T, nz)


def fold(value, nz):
    total = value[:nz]
    for frame in range(1, value.shape[0] // nz):
        total = total + value[frame * nz : (frame + 1) * nz]
    return total


def next_boundary(rows, cols, nz, final, conc, mob, chem, curve, rate, inner, outer, pot_in,
                  before, from_a, from_b, *rest):
    low, high = reach(cols)
    if final:
        inner_out, inner_grad, out, grad_out, adj, pot, part, grad, result = rest
    else:
        result, grad, to_a, to_b, adj, pot, part = rest
    adj[2 * depth] = inner[0]
    adj[rows - 1] = inner[rows - 2 * depth - 1]
    for s, k, y in sides_of(rows):
        adj[depth + y] = outer[s, k]
    for halo, base in zip((from_a, from_b), landings(rows)):
        for at in range(depth):
            adj[base + at, low:high, :] = halo[at]
    for y in (1, 2, rows - 3, rows - 2):
        pot[1 + y] = pot_in[y - 1]

    def store(s, k, span, value):
        result[s, k, span, :] = value

    boundary(rows, cols, nz, (conc, depth), (mob, depth), (chem, 1), (curve, 1), (adj, depth),
             rate, pot, part, grad, before, store, False)
    if final:
        lanes = conc.shape[2]
        for k in range(rows - 2 * depth):
            out[pl.ds(depth + k, lanes, stride=rows), :] = inner_out[k]
            grad_out[pl.ds(depth + k, nz, stride=rows), :] = inner_grad[k]
        for s, k, y in sides_of(rows):
            out[pl.ds(y, lanes, stride=rows), :] = result[s, k, pad : pad + cols, :].T
            grad_out[pl.ds(y, nz, stride=rows), :] = fold(grad[s, k, pad : pad + cols, :].T, nz)
    else:
        send_rows(result, to_a, to_b, cols)


def call(kernel, outs, scratch, *operands, cost=0, far=False):
    if far:
        operands = [pltpu.with_memory_space_constraint(value, pltpu.HBM) for value in operands]
    space = pl.ANY if far else pltpu.VMEM
    return pl.pallas_call(
        kernel,
        out_shape=[jax.ShapeDtypeStruct(shape, f32) for shape in outs],
        in_specs=[pl.BlockSpec(memory_space=space)] * len(operands),
        out_specs=[pl.BlockSpec(memory_space=pltpu.VMEM)] * len(outs),
        scratch_shapes=[pltpu.VMEM(s, f32) if isinstance(s, tuple) else s for s in scratch],
        compiler_params=pltpu.CompilerParams(vmem_limit_bytes=vmem_limit),
        cost_estimate=pl.CostEstimate(
            flops=cost * 1_000_000, bytes_accessed=cost * 2_000_000, transcendentals=0
        ),
    )(*operands)


def swap(value_a, value_b, axis):
    count = lax.axis_size(axis)
    pairs_a = [(i, i + 1 - 2 * (i % 2)) for i in range(count)]
    pairs_b = [(i, (i - 1 + 2 * (i % 2)) % count) for i in range(count)]
    return lax.ppermute(value_a, axis, pairs_a), lax.ppermute(value_b, axis, pairs_b)


def shards(saved_conc, adjoint_end, rate_field):
    steps, frames, nz, rows, cols = saved_conc.shape
    lanes = frames * nz
    _, total = slots(steps)
    width = cols + 2 * pad
    flat = lanes * rows
    inside = rows - 2 * depth

    def field(count):
        return (count, width, lanes)

    raw = [(steps, flat, cols), (flat, cols), (nz * rows, cols)]
    conc_raw, adj_raw, rate_raw, main_a, main_b = call(
        functools.partial(edge_kernel, steps, rows, cols, nz),
        raw + [((1 + steps) * depth * cols + cols // 2, lanes)] * 2,
        [pltpu.SemaphoreType.DMA((2 + steps,))],
        saved_conc.reshape(raw[0]), adjoint_end.reshape(raw[1]), rate_field.reshape(raw[2]),
        cost=2,
        far=True,
    )
    main_a, main_b = swap(main_a, main_b, "gy")
    conc_own, adj_own, rate_own, x_a, x_b = call(
        functools.partial(turn_kernel, steps, rows, cols, nz),
        [(steps, rows, cols, lanes), (rows, cols, lanes), (rows, cols, lanes)]
        + [(rows, total, lanes)] * 2,
        [],
        conc_raw, adj_raw, rate_raw,
        cost=1,
    )
    x_a, x_b = swap(x_a, x_b, "gx")
    x_low, x_high, corner_a, corner_b = call(
        functools.partial(corner_kernel, rows),
        [(rows, total, lanes)] * 2 + [(2, depth, total, lanes)] * 2,
        [],
        x_a, x_b,
    )
    corner_a, corner_b = swap(corner_a, corner_b, "gy")

    conc, adj, rate_in, chem, curve, pot, inner, inner_grad = call(
        functools.partial(first_interior, steps, rows, cols, nz),
        [field(rows)] * 3 + [field(rows - 2)] * 3 + [field(inside)] * 2,
        [field(rows), field(inside)],
        conc_own, adj_own, rate_own, x_low, x_high,
        cost=3,
    )
    both = (2, depth, width, lanes)
    edge = (depth, cols + 16, lanes)
    outer, outer_grad, rate, to_a, to_b = call(
        functools.partial(first_boundary, steps, rows, cols, nz),
        [both, both, field(4), edge, edge],
        [field(rows + 2 * depth)] * 3 + [field(rows + 2)] * 3 + [both],
        conc, adj, rate_in, chem, curve, pot, main_a, main_b, corner_a, corner_b,
        cost=2,
    )
    for back in range(1, steps):
        adj_a, adj_b = swap(to_a, to_b, "gy")
        final = back == steps - 1
        fields = call(
            functools.partial(prepare_kernel, steps, rows, cols, nz, back),
            [field(rows + 2 * depth)] * 2 + [field(rows + 2)] * 2,
            [],
            conc_own, main_a, main_b, x_low, x_high, corner_a, corner_b,
            cost=2,
        )
        tiles = [(inside, lanes, cols), (inside, nz, cols)]
        results = call(
            functools.partial(next_interior, rows, cols, nz, final),
            (tiles if final else [field(inside)] * 2) + [field(rows - 2)],
            [field(rows), field(inside)] + ([field(inside)] * 2 if final else []),
            *fields, rate_in, inner, outer, inner_grad,
            cost=3,
        )
        pot = results[2]
        if final:
            adj, grad = call(
                functools.partial(next_boundary, rows, cols, nz, final),
                [(flat, cols), (nz * rows, cols)],
                [field(rows + 2 * depth), field(rows + 2), both, both, both],
                *fields, rate, inner, outer, pot, outer_grad, adj_a, adj_b, results[0], results[1],
                cost=3,
            )
        else:
            new_outer, outer_grad, to_a, to_b = call(
                functools.partial(next_boundary, rows, cols, nz, final),
                [both, both, edge, edge],
                [field(rows + 2 * depth), field(rows + 2), both],
                *fields, rate, inner, outer, pot, outer_grad, adj_a, adj_b,
                cost=2,
            )
            inner, inner_grad, outer = results[0], results[1], new_outer
    return adj.reshape(adjoint_end.shape), grad.reshape(rate_field.shape)


def solution(mesh):
    return jax.shard_map(
        shards,
        mesh=mesh,
        in_specs=(P(None, None, None, "gy", "gx"), P(None, None, "gy", "gx"), P(None, "gy", "gx")),
        out_specs=(P(None, None, "gy", "gx"), P(None, "gy", "gx")),
        check_vma=False,
    )
```

```python
import functools

import jax
import jax.numpy as jnp
from jax import lax
from jax.experimental import pallas as pl
from jax.experimental.pallas import tpu as pltpu
from jax.sharding import PartitionSpec as P

mix_energy = 2.5
grad_energy = 1.0
time_step = 0.1
diff_step = 0.03
bath_potential = 0.5

pad = 16
chunk = 72
depth = 2
vmem_limit = 20 * 1024 * 1024
f32 = jnp.float32


def slots(steps):
    widths = [2 * steps] + [2 * steps - 2 * back for back in range(steps)] + [2 * steps - 1]
    starts = [sum(widths[:i]) for i in range(len(widths))]
    total = -(-sum(widths) // 8) * 8
    return list(zip(starts, widths)), total


def chunks(low, high):
    return [(at, min(chunk, high - at)) for at in range(low, high, chunk)]


def reach(cols):
    return pad - 8, pad + cols + 8


def up(value):
    return pltpu.roll(value, value.shape[1] - 1, 1)


def down(value):
    return pltpu.roll(value, 1, 1)


def face_mask(size, lanes, nz):
    lane = lax.broadcasted_iota(jnp.int32, (size, lanes), 1)
    return jnp.where(lane % nz == nz - 1, 0.0, 1.0).astype(f32)


def row_of(ref, y):
    return lambda dy, cut: ref[y + dy, cut, :]


def laplace(field, at, size, mask):
    span = slice(at, at + size)
    here = field(0, span)
    step_z = (up(here) - here) * mask
    sides = field(0, slice(at + 1, at + size + 1)) + field(0, slice(at - 1, at + size - 1))
    return here, (
        (sides + (field(-1, span) + field(1, span))) - 4.0 * here + (step_z - down(step_z))
    )


def chem_row(conc, chem, curve, at, size, mask):
    c, lap = laplace(conc, at, size, mask)
    inv = 1.0 / (c * (1.0 - c))
    span = slice(at, at + size)
    chem(span, jnp.log(c * c * inv) + mix_energy * (1.0 - 2.0 * c) - grad_energy * lap)
    curve(span, inv - 2.0 * mix_energy)


def face_sums(adj, mob, chem, at, size, mask, across=(1, -1)):
    span = slice(at, at + size)
    a = adj(0, span)
    m = None if mob is None else mob(0, span)
    mu = None if chem is None else chem(0, span)
    flow = pair = None
    for dy, cut in (
        (0, slice(at + 1, at + size + 1)),
        (0, slice(at - 1, at + size - 1)),
    ) + tuple((dy, span) for dy in across):
        diff = adj(dy, cut) - a
        if mob is not None:
            term = (mob(dy, cut) + m) * diff
            flow = term if flow is None else flow + term
        if chem is not None:
            term = (chem(dy, cut) - mu) * diff
            pair = term if pair is None else pair + term
    diff = (up(a) - a) * mask
    if mob is not None:
        term = (up(m) + m) * diff
        flow = flow + (term - down(term))
    if chem is not None:
        term = (up(mu) - mu) * diff
        pair = pair + (term + down(term))
    return a, mu, flow, pair


def source(flow, rate, a):
    return (0.5 * diff_step) * flow - time_step * rate * a


def partial(a, c, pair, curve, g):
    return a + (1.0 - 2.0 * c) * ((-0.5 * diff_step) * pair) + curve * g


def gain(a, mu, before):
    value = time_step * a * (bath_potential - mu)
    return value if before is None else before + value


def set_row(ref, y):
    def put(span, value):
        ref[y, span, :] = value

    return put


def interior(rows, cols, nz, conc, mob, chem, curve, adj, rate, pot, part, grad, before, store):
    low, high = reach(cols)
    lanes = adj[0].shape[-1]

    def at_row(field, y):
        return row_of(field[0], field[1] + y)

    def body(y, _):
        for at, size in chunks(low, high):
            mask = face_mask(size, lanes, nz)
            span = slice(at, at + size)
            a, mu, flow, pair = face_sums(
                at_row(adj, y), at_row(mob, y), at_row(chem, y), at, size, mask
            )
            g = source(flow, at_row(rate, y)(0, span), a)
            pot[y - 1, span, :] = g
            part[y - depth, span, :] = partial(
                a, at_row(conc, y)(0, span), pair, at_row(curve, y)(0, span), g
            )
            old = None if before is None else before[y - depth, span, :]
            grad[y - depth, span, :] = gain(a, mu, old)
        return 0

    def edge(i, _):
        y = 1 + i * (rows - 3)
        for at, size in chunks(low, high):
            mask = face_mask(size, lanes, nz)
            a, _mu, flow, _pair = face_sums(at_row(adj, y), at_row(mob, y), None, at, size, mask)
            span = slice(at, at + size)
            pot[y - 1, span, :] = source(flow, at_row(rate, y)(0, span), a)
        return 0

    def close(y, _):
        for at, size in chunks(low, high):
            mask = face_mask(size, lanes, nz)
            span = slice(at, at + size)
            _g, lap = laplace(row_of(pot, y - 1), at, size, mask)
            store(y - depth, span, part[y - depth, span, :] - grad_energy * lap)
        return 0

    lax.fori_loop(depth, rows - depth, body, 0)
    lax.fori_loop(0, 2, edge, 0)
    lax.fori_loop(depth, rows - depth, close, 0)


def boundary(rows, cols, nz, conc, mob, chem, curve, adj, rate, pot, part, grad, before, store,
             fresh):
    low, high = reach(cols)
    lanes = adj[0].shape[-1]
    last = rows - 1

    def at_row(field, y):
        return row_of(field[0], field[1] + y)

    def mirror(s, y):
        return y + s * (last - 2 * y)

    if fresh:

        def mu_side(i, _):
            s, k = i // 2, i % 2
            y = mirror(s, k - 1)
            for at, size in chunks(low, high):
                chem_row(at_row(conc, y), set_row(chem[0], chem[1] + y),
                         set_row(curve[0], curve[1] + y), at, size, face_mask(size, lanes, nz))
            return 0

        lax.fori_loop(0, 4, mu_side, 0)

    def side(s, _):
        y = mirror(s, -1)
        for at, size in chunks(low, high):
            mask = face_mask(size, lanes, nz)
            span = slice(at, at + size)
            a, _mu, flow, _pair = face_sums(at_row(adj, y), at_row(mob, y), None, at, size, mask)
            pot[1 + y, span, :] = source(flow, rate[3 * s, span, :], a)
        y0 = mirror(s, 0)
        for at, size in chunks(low, high):
            mask = face_mask(size, lanes, nz)
            span = slice(at, at + size)
            a, mu, flow, pair = face_sums(
                at_row(adj, y0), at_row(mob, y0), at_row(chem, y0), at, size, mask
            )
            g = source(flow, rate[1 + s, span, :], a)
            pot[1 + y0, span, :] = g
            part[s, 0, span, :] = partial(
                a, at_row(conc, y0)(0, span), pair, at_row(curve, y0)(0, span), g
            )
            old = None if before is None else before[s, 0, span, :]
            grad[s, 0, span, :] = gain(a, mu, old)
        y1 = mirror(s, 1)
        for at, size in chunks(low, high):
            mask = face_mask(size, lanes, nz)
            span = slice(at, at + size)
            a, mu, _flow, pair = face_sums(at_row(adj, y1), None, at_row(chem, y1), at, size, mask)
            part[s, 1, span, :] = partial(
                a, at_row(conc, y1)(0, span), pair, at_row(curve, y1)(0, span), pot[1 + y1, span, :]
            )
            old = None if before is None else before[s, 1, span, :]
            grad[s, 1, span, :] = gain(a, mu, old)
        return 0

    lax.fori_loop(0, 2, side, 0)

    def close(i, _):
        s, k = i // 2, i % 2
        y = mirror(s, k)
        for at, size in chunks(low, high):
            mask = face_mask(size, lanes, nz)
            span = slice(at, at + size)
            _g, lap = laplace(row_of(pot, 1 + y), at, size, mask)
            store(s, k, span, part[s, k, span, :] - grad_energy * lap)
        return 0

    lax.fori_loop(0, 4, close, 0)


def is_even(axis):
    return lax.rem(lax.axis_index(axis), 2) == 0


def bases(rows):
    even = is_even("gy")
    top = rows - depth
    return jnp.where(even, top, 0), jnp.where(even, 0, top)


def landings(rows):
    even = is_even("gy")
    top = rows + depth
    return jnp.where(even, top, 0), jnp.where(even, 0, top)


def sides_of(rows):
    return [(0, 0, 0), (0, 1, 1), (1, 0, rows - 1), (1, 1, rows - 2)]


def edge_kernel(steps, rows, cols, nz, conc_hbm, adj_hbm, rate_hbm, conc_in, adj_in, rate_in,
                main_a, main_b, sems):
    lanes = main_a.shape[1]
    half = cols // 2
    lower = lax.broadcasted_iota(jnp.int32, (half, lanes), 1) < nz
    copies = [
        pltpu.make_async_copy(adj_hbm, adj_in, sems.at[0]),
        pltpu.make_async_copy(rate_hbm, rate_in, sems.at[1]),
    ] + [
        pltpu.make_async_copy(conc_hbm.at[steps - 1 - back], conc_in.at[back], sems.at[2 + back])
        for back in range(steps)
    ]
    for copy in copies:
        copy.start()
    copies[0].wait()
    for side, base in zip((main_a, main_b), bases(rows)):
        for at in range(depth):
            side[pl.ds(at * cols, cols), :] = adj_in[pl.ds(base + at, lanes, stride=rows), :].T
    copies[1].wait()
    for side, base in zip((main_a, main_b), bases(rows)):
        edge = jnp.where(base == 0, 0, rows - 1)
        rate = turned_rate(rate_in, edge, rows, nz, lanes)
        side[pl.ds((1 + steps) * depth * cols, half), :] = jnp.where(
            lower, rate[:half], rate[half:]
        )
    for back in range(steps):
        copies[2 + back].wait()
        for side, base in zip((main_a, main_b), bases(rows)):
            for at in range(depth):
                side[pl.ds(((1 + back) * depth + at) * cols, cols), :] = conc_in[
                    back, pl.ds(base + at, lanes, stride=rows), :
                ].T


def turned_rate(rate, y, rows, nz, lanes):
    value = rate[pl.ds(y, nz, stride=rows), :]
    return jnp.concatenate([value] * (lanes // nz), axis=0).T


def turn_kernel(steps, rows, cols, nz, conc_in, adj_in, rate_in, conc_out, adj_out, rate_out,
                x_a, x_b):
    places, total = slots(steps)
    lanes = adj_out.shape[2]
    even_x = is_even("gx")

    def to_x(y, value, place):
        start, width = place
        last, first = value[cols - width :, :], value[:width, :]
        x_a[y, start : start + width, :] = jnp.where(even_x, last, first)
        x_b[y, start : start + width, :] = jnp.where(even_x, first, last)

    used = sum(places[-1])
    for y in range(rows):
        adj = adj_in[pl.ds(y, lanes, stride=rows), :].T
        adj_out[y] = adj
        to_x(y, adj, places[0])
        rate = turned_rate(rate_in, y, rows, nz, lanes)
        rate_out[y] = rate
        to_x(y, rate, places[steps + 1])
        if used < total:
            x_a[y, used:, :] = jnp.zeros((total - used, lanes), f32)
            x_b[y, used:, :] = jnp.zeros((total - used, lanes), f32)
        for back in range(steps):
            conc = conc_in[back, pl.ds(y, lanes, stride=rows), :].T
            conc_out[back, y] = conc
            to_x(y, conc, places[1 + back])


def put_own(out, row, value, y, place, cols, x_low, x_high):
    start, width = place
    right = pad + cols
    out[row, pad:right, :] = value
    out[row, pad - width : pad, :] = x_low[y, start : start + width, :]
    out[row, right : right + width, :] = x_high[y, start : start + width, :]


def put_halo(out, row, value, from_row, place, cols, corner):
    start, width = place
    right = pad + cols
    out[row, pad:right, :] = value
    out[row, pad - width : pad, :] = corner[0, from_row, start : start + width, :]
    out[row, right : right + width, :] = corner[1, from_row, start : start + width, :]


def corner_kernel(rows, got_a, got_b, x_low, x_high, corner_a, corner_b):
    even_x = is_even("gx")
    x_low[...] = jnp.where(even_x, got_b[...], got_a[...])
    x_high[...] = jnp.where(even_x, got_a[...], got_b[...])
    for out, base in zip((corner_a, corner_b), bases(rows)):
        for at in range(depth):
            out[0, at] = x_low[base + at]
            out[1, at] = x_high[base + at]


def first_interior(steps, rows, cols, nz, conc_own, adj_own, rate_own, x_low, x_high,
                   conc, adj, rate, chem, curve, pot, out, grad, ahead, mob, part):
    places, _ = slots(steps)
    low, high = reach(cols)
    lanes = adj.shape[2]
    for y in range(rows):
        put_own(conc, y, conc_own[0, y], y, places[1], cols, x_low, x_high)
        put_own(adj, y, adj_own[y], y, places[0], cols, x_low, x_high)
        put_own(rate, y, rate_own[y], y, places[steps + 1], cols, x_low, x_high)
    put_ahead(ahead, conc_own, 1, x_low, x_high, places, rows, cols)

    def mob_row(y, _):
        for at, size in chunks(low - 8, high + 8):
            c = conc[y, at : at + size, :]
            mob[y, at : at + size, :] = c * (1.0 - c)
        return 0

    def mu_row(y, _):
        for at, size in chunks(low, high):
            chem_row(row_of(conc, y), set_row(chem, y - 1), set_row(curve, y - 1), at, size,
                     face_mask(size, lanes, nz))
        return 0

    lax.fori_loop(0, rows, mob_row, 0)
    lax.fori_loop(1, rows - 1, mu_row, 0)

    def store(k, span, value):
        out[k, span, :] = value

    interior(rows, cols, nz, (conc, 0), (mob, 0), (chem, -1), (curve, -1), (adj, 0), (rate, 0),
             pot, part, grad, None, store)


def copy_rows(pairs):
    for out, to, ref, at in pairs:
        out[to] = ref[at]


def send_rows(out, ahead, rate, to_a, to_b, open_g, cols, nz):
    low, high = reach(cols)
    rows, lanes = rate.shape[0], rate.shape[2]
    for s in range(2):
        for at, size in chunks(low, high):
            mask = face_mask(size, lanes, nz)
            a, _mu, flow, _pair = face_sums(
                lambda dy, cut: out[s, dy, cut, :], lambda dy, cut: ahead[s, dy, cut, :], None,
                at, size, mask, (1,)
            )
            open_g[s, at - low : at - low + size, :] = source(
                flow, rate[s * (rows - 1), at : at + size, :], a
            )
    even = is_even("gy")
    for to, side in ((to_a, jnp.where(even, 1, 0)), (to_b, jnp.where(even, 0, 1))):
        to[0] = out[side, 0, low:high, :]
        to[1] = open_g[side]


def put_ahead(ahead, conc_own, back, x_low, x_high, places, rows, cols):
    for s, k, y in sides_of(rows):
        put_own(ahead.at[s], k, conc_own[back, y], y, places[1 + back], cols, x_low, x_high)
        c = ahead[s, k]
        ahead[s, k] = c * (1.0 - c)


def first_boundary(steps, rows, cols, nz, conc_in, adj_in, rate_in, chem_in, curve_in, pot_in,
                   from_a, from_b, corner_a, corner_b, ahead,
                   out, grad, to_a, to_b, rate, conc, adj, mob, chem, curve, pot, part, open_g):
    places, _ = slots(steps)
    low, high = reach(cols)
    half = cols // 2
    lanes = conc.shape[2]
    lower = lax.broadcasted_iota(jnp.int32, (half, lanes), 1) < nz

    def unpack(side):
        packed = side[pl.ds((1 + steps) * depth * cols, half), :]
        turned = pltpu.roll(packed, lanes // 2, 1)
        return jnp.concatenate(
            [jnp.where(lower, packed, turned), jnp.where(lower, turned, packed)], axis=0
        )

    near = [0, 1, 2, rows - 3, rows - 2, rows - 1]
    for y in near:
        conc[depth + y] = conc_in[y]
        adj[depth + y] = adj_in[y]
    for y in (1, 2, rows - 3, rows - 2):
        chem[1 + y] = chem_in[y - 1]
        pot[1 + y] = pot_in[y - 1]
    for y in (1, rows - 2):
        curve[1 + y] = curve_in[y - 1]
    rate[1] = rate_in[0]
    rate[2] = rate_in[rows - 1]
    for halo, corner, base in zip((from_a, from_b), (corner_a, corner_b), landings(rows)):
        for at in range(depth):
            for ref, place, first in ((adj, places[0], 0), (conc, places[1], depth)):
                span = pl.ds((first + at) * cols, cols)
                put_halo(ref, base + at, halo[span, :], at, place, cols, corner)
        below = base == 0
        put_halo(rate, jnp.where(below, 0, 3), unpack(halo), jnp.where(below, depth - 1, 0),
                 places[steps + 1], cols, corner)
    for row in [0, 1, 2, 3, rows, rows + 1, rows + 2, rows + 3]:
        for at, size in chunks(low - 8, high + 8):
            c = conc[row, at : at + size, :]
            mob[row, at : at + size, :] = c * (1.0 - c)

    def store(s, k, span, value):
        out[s, k, span, :] = value

    boundary(rows, cols, nz, (conc, depth), (mob, depth), (chem, 1), (curve, 1), (adj, depth),
             rate, pot, part, grad, None, store, True)
    send_rows(out, ahead, rate_in, to_a, to_b, open_g, cols, nz)


def prepare_kernel(steps, rows, cols, nz, back, conc_own, from_a, from_b, x_low, x_high,
                   corner_a, corner_b, conc, mob, chem, curve, *ahead):
    places, _ = slots(steps)
    low, high = reach(cols)
    lanes = conc.shape[2]
    place = places[1 + back]
    for y in range(rows):
        put_own(conc, depth + y, conc_own[back, y], y, place, cols, x_low, x_high)
    for halo, corner, base in zip((from_a, from_b), (corner_a, corner_b), landings(rows)):
        for at in range(depth):
            span = pl.ds(((1 + back) * depth + at) * cols, cols)
            put_halo(conc, base + at, halo[span, :], at, place, cols, corner)

    if ahead:
        put_ahead(ahead[0], conc_own, back + 1, x_low, x_high, places, rows, cols)

    def mob_row(row, _):
        for at, size in chunks(low - 8, high + 8):
            c = conc[row, at : at + size, :]
            mob[row, at : at + size, :] = c * (1.0 - c)
        return 0

    def mu_row(row, _):
        for at, size in chunks(low, high):
            chem_row(row_of(conc, row + 1), set_row(chem, row), set_row(curve, row), at, size,
                     face_mask(size, lanes, nz))
        return 0

    lax.fori_loop(0, rows + 2 * depth, mob_row, 0)
    lax.fori_loop(0, rows + 2, mu_row, 0)


def next_interior(rows, cols, nz, final, conc, mob, chem, curve, rate, inner, outer, *rest):
    if final:
        before, out, tiles, grad_out, adj, pot, part, grad = rest
    elif len(rest) == 8:
        inner_grad, outer_grad, out, grad, adj, pot, part, before = rest
        for k in range(rows - 2 * depth):
            before[depth + k] = inner_grad[k]
        for s, k, y in sides_of(rows):
            before[y] = outer_grad[s, k]
    else:
        before, out, grad, adj, pot, part = rest
    low, high = reach(cols)
    lanes = adj.shape[2]
    skip = (inner.shape[0] - (rows - 2 * depth)) // 2
    for k in range(rows - 2 * depth):
        adj[1 + depth + k] = inner[skip + k]
    for s, k, y in sides_of(rows):
        adj[1 + y] = outer[s, k]
    adj[0] = outer[0, 0]
    adj[1 + rows] = outer[1, 0]
    pot[0] = jnp.zeros(pot.shape[1:], f32)
    pot[1 + rows] = jnp.zeros(pot.shape[1:], f32)

    def body(y, _):
        for at, size in chunks(low, high):
            mask = face_mask(size, lanes, nz)
            span = slice(at, at + size)
            a, mu, flow, pair = face_sums(
                row_of(adj, y + 1), row_of(mob, y + depth), row_of(chem, y + 1), at, size, mask
            )
            g = source(flow, rate[y, span, :], a)
            pot[y + 1, span, :] = g
            part[y, span, :] = partial(
                a, conc[y + depth, span, :], pair, curve[y + 1, span, :], g
            )
            grad[y, span, :] = gain(a, mu, before[y, span, :])
        return 0

    def close(y, _):
        for at, size in chunks(low, high):
            mask = face_mask(size, lanes, nz)
            span = slice(at, at + size)
            _g, lap = laplace(row_of(pot, y + 1), at, size, mask)
            out[y, span, :] = part[y, span, :] - grad_energy * lap
        return 0

    lax.fori_loop(0, rows, body, 0)
    lax.fori_loop(0, rows, close, 0)
    if final:
        for y in range(rows):
            grad_out[pl.ds(y, nz, stride=rows), :] = fold(grad[y, pad : pad + cols, :].T, nz)
        for y in range(depth, rows - depth):
            tiles[pl.ds(y, lanes, stride=rows), :] = out[y, pad : pad + cols, :].T


def fold(value, nz):
    total = value[:nz]
    for frame in range(1, value.shape[0] // nz):
        total = total + value[frame * nz : (frame + 1) * nz]
    return total


def next_boundary(rows, cols, nz, final, conc, mob, chem, curve, inside, outer, from_a, from_b,
                  *rest):
    if final:
        tiles, out, halo, delta, result = rest
    else:
        ahead, rate, result, to_a, to_b, halo, delta, open_g = rest
    low, high = reach(cols)
    lanes = conc.shape[2]
    even = is_even("gy")
    for got, side in ((from_a, jnp.where(even, 1, 0)), (from_b, jnp.where(even, 0, 1))):
        for k in range(2):
            halo[side, k, low:high, :] = got[k]
    for s in range(2):
        y, beyond = s * (rows - 1), s * (rows + 1) - 1
        for at, size in chunks(low, high):
            span = slice(at, at + size)
            diff = halo[s, 0, span, :] - outer[s, 0, span, :]
            both = mob[depth + beyond, span, :] + mob[depth + y, span, :]
            delta[s, span, :] = (0.5 * diff_step) * both * diff
        for at, size in chunks(low, high):
            mask = face_mask(size, lanes, nz)
            span = slice(at, at + size)
            more = delta[s, span, :]
            diff = halo[s, 0, span, :] - outer[s, 0, span, :]
            pair = (chem[1 + beyond, span, :] - chem[1 + y, span, :]) * diff
            step_z = (up(more) - more) * mask
            lap = (
                (delta[s, at + 1 : at + size + 1, :] + delta[s, at - 1 : at + size - 1, :])
                + (halo[s, 1, span, :] - more)
                - 4.0 * more
                + (step_z - down(step_z))
            )
            c = conc[depth + y, span, :]
            result[s, 0, span, :] = (
                inside[y, span, :]
                + ((1.0 - 2.0 * c) * ((-0.5 * diff_step) * pair) + curve[1 + y, span, :] * more)
                - grad_energy * lap
            )
            result[s, 1, span, :] = inside[1 + s * (rows - 3), span, :] - grad_energy * more
    if final:
        out[...] = tiles[...]
        for s, k, y in sides_of(rows):
            out[pl.ds(y, lanes, stride=rows), :] = result[s, k, pad : pad + cols, :].T
    else:
        send_rows(result, ahead, rate, to_a, to_b, open_g, cols, nz)


def call(kernel, outs, scratch, *operands, cost=0, far=False):
    if far:
        operands = [pltpu.with_memory_space_constraint(value, pltpu.HBM) for value in operands]
    space = pl.ANY if far else pltpu.VMEM
    return pl.pallas_call(
        kernel,
        out_shape=[jax.ShapeDtypeStruct(shape, f32) for shape in outs],
        in_specs=[pl.BlockSpec(memory_space=space)] * len(operands),
        out_specs=[pl.BlockSpec(memory_space=pltpu.VMEM)] * len(outs),
        scratch_shapes=[pltpu.VMEM(s, f32) if isinstance(s, tuple) else s for s in scratch],
        compiler_params=pltpu.CompilerParams(vmem_limit_bytes=vmem_limit),
        cost_estimate=pl.CostEstimate(
            flops=cost * 1_000_000, bytes_accessed=cost * 2_000_000, transcendentals=0
        ),
    )(*operands)


def swap(value_a, value_b, axis):
    count = lax.axis_size(axis)
    pairs_a = [(i, i + 1 - 2 * (i % 2)) for i in range(count)]
    pairs_b = [(i, (i - 1 + 2 * (i % 2)) % count) for i in range(count)]
    return lax.ppermute(value_a, axis, pairs_a), lax.ppermute(value_b, axis, pairs_b)


def shards(saved_conc, adjoint_end, rate_field):
    steps, frames, nz, rows, cols = saved_conc.shape
    lanes = frames * nz
    _, total = slots(steps)
    width = cols + 2 * pad
    flat = lanes * rows
    inside = rows - 2 * depth

    def field(count):
        return (count, width, lanes)

    both = (2, depth, width, lanes)
    edge = (2, cols + 16, lanes)
    open_g = (2, cols + 16, lanes)
    raw = [(steps, flat, cols), (flat, cols), (nz * rows, cols)]
    conc_raw, adj_raw, rate_raw, main_a, main_b = call(
        functools.partial(edge_kernel, steps, rows, cols, nz),
        raw + [((1 + steps) * depth * cols + cols // 2, lanes)] * 2,
        [pltpu.SemaphoreType.DMA((2 + steps,))],
        saved_conc.reshape(raw[0]), adjoint_end.reshape(raw[1]), rate_field.reshape(raw[2]),
        cost=2,
        far=True,
    )
    main_a, main_b = swap(main_a, main_b, "gy")
    conc_own, adj_own, rate_own, x_a, x_b = call(
        functools.partial(turn_kernel, steps, rows, cols, nz),
        [(steps, rows, cols, lanes), (rows, cols, lanes), (rows, cols, lanes)]
        + [(rows, total, lanes)] * 2,
        [],
        conc_raw, adj_raw, rate_raw,
        cost=1,
    )
    x_a, x_b = swap(x_a, x_b, "gx")
    x_low, x_high, corner_a, corner_b = call(
        functools.partial(corner_kernel, rows),
        [(rows, total, lanes)] * 2 + [(2, depth, total, lanes)] * 2,
        [],
        x_a, x_b,
    )
    corner_a, corner_b = swap(corner_a, corner_b, "gy")

    conc, adj, rate, chem, curve, pot, inner, inner_grad, ahead = call(
        functools.partial(first_interior, steps, rows, cols, nz),
        [field(rows)] * 3 + [field(rows - 2)] * 3 + [field(inside)] * 2 + [both],
        [field(rows), field(inside)],
        conc_own, adj_own, rate_own, x_low, x_high,
        cost=3,
    )
    outer, outer_grad, to_a, to_b = call(
        functools.partial(first_boundary, steps, rows, cols, nz),
        [both, both, edge, edge],
        [field(4)] + [field(rows + 2 * depth)] * 3 + [field(rows + 2)] * 3 + [both, open_g],
        conc, adj, rate, chem, curve, pot, main_a, main_b, corner_a, corner_b, ahead,
        cost=2,
    )
    before = (inner_grad, outer_grad)
    for back in range(1, steps):
        adj_a, adj_b = swap(to_a, to_b, "gy")
        final = back == steps - 1
        fields = call(
            functools.partial(prepare_kernel, steps, rows, cols, nz, back),
            [field(rows + 2 * depth)] * 2 + [field(rows + 2)] * 2 + ([] if final else [both]),
            [],
            conc_own, main_a, main_b, x_low, x_high, corner_a, corner_b,
            cost=2,
        )
        fields, ahead = fields[:4], fields[4:]
        work = [field(rows + 2)] * 2 + [field(rows)]
        if final:
            rows_in, tiles, grad = call(
                functools.partial(next_interior, rows, cols, nz, final),
                [field(rows), (flat, cols), (nz * rows, cols)],
                work + [field(rows)],
                *fields, rate, inner, outer, *before,
                cost=3,
            )
            (adj,) = call(
                functools.partial(next_boundary, rows, cols, nz, final),
                [(flat, cols)],
                [both, field(2), both],
                *fields, rows_in, outer, adj_a, adj_b, tiles,
                cost=1,
            )
        else:
            rows_in, grad = call(
                functools.partial(next_interior, rows, cols, nz, final),
                [field(rows)] * 2,
                work + ([field(rows)] if len(before) == 2 else []),
                *fields, rate, inner, outer, *before,
                cost=3,
            )
            outer, to_a, to_b = call(
                functools.partial(next_boundary, rows, cols, nz, final),
                [both, edge, edge],
                [both, field(2), open_g],
                *fields, rows_in, outer, adj_a, adj_b, *ahead, rate,
                cost=1,
            )
            inner, before = rows_in, (grad,)
    return adj.reshape(adjoint_end.shape), grad.reshape(rate_field.shape)


def solution(mesh):
    return jax.shard_map(
        shards,
        mesh=mesh,
        in_specs=(P(None, None, None, "gy", "gx"), P(None, None, "gy", "gx"), P(None, "gy", "gx")),
        out_specs=(P(None, None, "gy", "gx"), P(None, "gy", "gx")),
        check_vma=False,
    )
```

```python
import functools

import jax
import jax.numpy as jnp
from jax import lax
from jax.experimental import pallas as pl
from jax.experimental.pallas import tpu as pltpu
from jax.sharding import PartitionSpec as P

mix_energy = 2.5
grad_energy = 1.0
time_step = 0.1
diff_step = 0.03
bath_potential = 0.5

pad = 16
chunk = 72
depth = 2
vmem_limit = 20 * 1024 * 1024
f32 = jnp.float32


def slots(steps):
    widths = [2 * steps] + [2 * steps - 2 * back for back in range(steps)] + [2 * steps - 1]
    starts = [sum(widths[:i]) for i in range(len(widths))]
    total = -(-sum(widths) // 8) * 8
    return list(zip(starts, widths)), total


def chunks(low, high):
    return [(at, min(chunk, high - at)) for at in range(low, high, chunk)]


def reach(cols):
    return pad - 8, pad + cols + 8


def sent(cols):
    return pad - 4, pad + cols + 4


def up(value):
    return pltpu.roll(value, value.shape[1] - 1, 1)


def down(value):
    return pltpu.roll(value, 1, 1)


def face_mask(lanes, nz):
    lane = lax.broadcasted_iota(jnp.int32, (1, lanes), 1)
    return jnp.where(lane % nz == nz - 1, 0.0, 1.0).astype(f32)


def row_of(ref, y):
    return lambda dy, cut: ref[y + dy, cut, :]


def laplace(field, at, size, mask):
    span = slice(at, at + size)
    here = field(0, span)
    step_z = (up(here) - here) * mask
    sides = field(0, slice(at + 1, at + size + 1)) + field(0, slice(at - 1, at + size - 1))
    return here, (
        (sides + (field(-1, span) + field(1, span))) - 4.0 * here + (step_z - down(step_z))
    )


def mobility(c):
    return (0.5 * diff_step) * c * (1.0 - c)


def chem_row(conc, chem, curve, swing, at, size, mask):
    c, lap = laplace(conc, at, size, mask)
    inv = 1.0 / (c * (1.0 - c))
    span = slice(at, at + size)
    chem(
        span,
        time_step * (jnp.log(c * c * inv) - grad_energy * lap)
        + (time_step * (mix_energy - bath_potential) - (2.0 * time_step * mix_energy) * c),
    )
    curve(span, inv - 2.0 * mix_energy)
    swing(span, c * (diff_step / time_step) - 0.5 * diff_step / time_step)


def face_sums(adj, mob, chem, at, size, mask, across=(1, -1)):
    span = slice(at, at + size)
    a = adj(0, span)
    m = None if mob is None else mob(0, span)
    mu = None if chem is None else chem(0, span)
    flow = pair = None
    for dy, cut in (
        (0, slice(at + 1, at + size + 1)),
        (0, slice(at - 1, at + size - 1)),
    ) + tuple((dy, span) for dy in across):
        diff = adj(dy, cut) - a
        if mob is not None:
            term = (mob(dy, cut) + m) * diff
            flow = term if flow is None else flow + term
        if chem is not None:
            term = (chem(dy, cut) - mu) * diff
            pair = term if pair is None else pair + term
    diff = (up(a) - a) * mask
    if mob is not None:
        term = (up(m) + m) * diff
        flow = flow + (term - down(term))
    if chem is not None:
        term = (up(mu) - mu) * diff
        pair = pair + (term + down(term))
    return a, mu, flow, pair


def partial(a, swing, pair, curve, g):
    return a + swing * pair + curve * g


def gain(a, chem, before):
    value = a * chem
    return -value if before is None else before - value


def set_row(ref, y):
    def put(span, value):
        ref[y, span, :] = value

    return put


def interior(rows, cols, nz, swing, mob, chem, curve, adj, rate, pot, part, grad, store):
    low, high = reach(cols)
    lanes = adj[0].shape[-1]
    mask = face_mask(lanes, nz)

    def at_row(field, y):
        return row_of(field[0], field[1] + y)

    def body(y, _):
        for at, size in chunks(low, high):
            span = slice(at, at + size)
            a, mu, flow, pair = face_sums(
                at_row(adj, y), at_row(mob, y), at_row(chem, y), at, size, mask
            )
            g = flow - at_row(rate, y)(0, span) * a
            pot[y - 1, span, :] = g
            part[y - depth, span, :] = partial(
                a, at_row(swing, y)(0, span), pair, at_row(curve, y)(0, span), g
            )
            grad[y - depth, span, :] = gain(a, mu, None)
        return 0

    def edge(i, _):
        y = 1 + i * (rows - 3)
        for at, size in chunks(low, high):
            a, _mu, flow, _pair = face_sums(at_row(adj, y), at_row(mob, y), None, at, size, mask)
            span = slice(at, at + size)
            pot[y - 1, span, :] = flow - at_row(rate, y)(0, span) * a
        return 0

    def close(y, _):
        for at, size in chunks(low, high):
            span = slice(at, at + size)
            _g, lap = laplace(row_of(pot, y - 1), at, size, mask)
            store(y - depth, span, part[y - depth, span, :] - grad_energy * lap)
        return 0

    lax.fori_loop(depth, rows - depth, body, 0)
    lax.fori_loop(0, 2, edge, 0)
    lax.fori_loop(depth, rows - depth, close, 0)


def boundary(rows, cols, nz, conc, mob, chem, curve, swing, adj, rate, pot, part, grad, store):
    low, high = reach(cols)
    lanes = adj[0].shape[-1]
    mask = face_mask(lanes, nz)
    last = rows - 1

    def at_row(field, y):
        return row_of(field[0], field[1] + y)

    def mirror(s, y):
        return y + s * (last - 2 * y)

    def mu_side(i, _):
        s, k = i // 2, i % 2
        y = mirror(s, k - 1)
        for at, size in chunks(low, high):
            chem_row(at_row(conc, y), set_row(chem[0], chem[1] + y),
                     set_row(curve[0], curve[1] + y), set_row(swing[0], swing[1] + y), at, size,
                     mask)
        return 0

    lax.fori_loop(0, 4, mu_side, 0)

    def side(s, _):
        y = mirror(s, -1)
        for at, size in chunks(low, high):
            span = slice(at, at + size)
            a, _mu, flow, _pair = face_sums(at_row(adj, y), at_row(mob, y), None, at, size, mask)
            pot[1 + y, span, :] = flow - rate[3 * s, span, :] * a
        y0 = mirror(s, 0)
        for at, size in chunks(low, high):
            span = slice(at, at + size)
            a, mu, flow, pair = face_sums(
                at_row(adj, y0), at_row(mob, y0), at_row(chem, y0), at, size, mask
            )
            g = flow - rate[1 + s, span, :] * a
            pot[1 + y0, span, :] = g
            part[s, 0, span, :] = partial(
                a, at_row(swing, y0)(0, span), pair, at_row(curve, y0)(0, span), g
            )
            grad[s, 0, span, :] = gain(a, mu, None)
        y1 = mirror(s, 1)
        for at, size in chunks(low, high):
            span = slice(at, at + size)
            a, mu, _flow, pair = face_sums(at_row(adj, y1), None, at_row(chem, y1), at, size, mask)
            part[s, 1, span, :] = partial(
                a, at_row(swing, y1)(0, span), pair, at_row(curve, y1)(0, span), pot[1 + y1, span, :]
            )
            grad[s, 1, span, :] = gain(a, mu, None)
        return 0

    lax.fori_loop(0, 2, side, 0)

    def close(i, _):
        s, k = i // 2, i % 2
        y = mirror(s, k)
        for at, size in chunks(low, high):
            span = slice(at, at + size)
            _g, lap = laplace(row_of(pot, 1 + y), at, size, mask)
            store(s, k, span, part[s, k, span, :] - grad_energy * lap)
        return 0

    lax.fori_loop(0, 4, close, 0)


def is_odd(axis):
    return lax.rem(lax.axis_index(axis), 2) == 1


def bases(rows):
    odd = is_odd("gy")
    top = rows - depth
    return jnp.where(odd, top, 0), jnp.where(odd, 0, top)


def landings(rows):
    odd = is_odd("gy")
    top = rows + depth
    return jnp.where(odd, top, 0), jnp.where(odd, 0, top)


def sides_of(rows):
    return [(0, 0, 0), (0, 1, 1), (1, 0, rows - 1), (1, 1, rows - 2)]


def edge_kernel(steps, rows, cols, nz, conc_hbm, adj_hbm, rate_hbm, conc_in, adj_in, rate_in,
                main_a, main_b, sems):
    lanes = main_a.shape[1]
    half = cols // 2
    lower = lax.broadcasted_iota(jnp.int32, (half, lanes), 1) < nz
    copies = [
        pltpu.make_async_copy(adj_hbm, adj_in, sems.at[0]),
        pltpu.make_async_copy(rate_hbm, rate_in, sems.at[1]),
    ] + [
        pltpu.make_async_copy(conc_hbm.at[steps - 1 - back], conc_in.at[back], sems.at[2 + back])
        for back in range(steps)
    ]
    for copy in copies:
        copy.start()
    copies[0].wait()
    for side, base in zip((main_a, main_b), bases(rows)):
        for at in range(depth):
            side[pl.ds(at * cols, cols), :] = adj_in[pl.ds(base + at, lanes, stride=rows), :].T
    copies[1].wait()
    for side, base in zip((main_a, main_b), bases(rows)):
        edge = jnp.where(base == 0, 0, rows - 1)
        rate = turned_rate(rate_in, edge, rows, nz, lanes)
        side[pl.ds((1 + steps) * depth * cols, half), :] = jnp.where(
            lower, rate[:half], rate[half:]
        )
    for back in range(steps):
        copies[2 + back].wait()
        for side, base in zip((main_a, main_b), bases(rows)):
            for at in range(depth):
                side[pl.ds(((1 + back) * depth + at) * cols, cols), :] = conc_in[
                    back, pl.ds(base + at, lanes, stride=rows), :
                ].T


def turned_rate(rate, y, rows, nz, lanes):
    value = time_step * rate[pl.ds(y, nz, stride=rows), :]
    return jnp.concatenate([value] * (lanes // nz), axis=0).T


def turn_kernel(steps, rows, cols, nz, conc_in, adj_in, rate_in, conc_out, adj_out, rate_out,
                x_a, x_b):
    places, total = slots(steps)
    lanes = adj_out.shape[2]
    odd_x = is_odd("gx")

    def to_x(y, value, place):
        start, width = place
        last, first = value[cols - width :, :], value[:width, :]
        x_a[y, start : start + width, :] = jnp.where(odd_x, last, first)
        x_b[y, start : start + width, :] = jnp.where(odd_x, first, last)

    used = sum(places[-1])
    for y in range(rows):
        adj = adj_in[pl.ds(y, lanes, stride=rows), :].T
        adj_out[y] = adj
        to_x(y, adj, places[0])
        rate = turned_rate(rate_in, y, rows, nz, lanes)
        rate_out[y] = rate
        to_x(y, rate, places[steps + 1])
        if used < total:
            x_a[y, used:, :] = jnp.zeros((total - used, lanes), f32)
            x_b[y, used:, :] = jnp.zeros((total - used, lanes), f32)
        for back in range(steps):
            conc = conc_in[back, pl.ds(y, lanes, stride=rows), :].T
            conc_out[back, y] = conc
            to_x(y, conc, places[1 + back])


def put_own(out, row, value, y, place, cols, x_low, x_high):
    start, width = place
    right = pad + cols
    out[row, pad:right, :] = value
    out[row, pad - width : pad, :] = x_low[y, start : start + width, :]
    out[row, right : right + width, :] = x_high[y, start : start + width, :]


def put_halo(out, row, value, from_row, place, cols, corner):
    start, width = place
    right = pad + cols
    out[row, pad:right, :] = value
    out[row, pad - width : pad, :] = corner[0, from_row, start : start + width, :]
    out[row, right : right + width, :] = corner[1, from_row, start : start + width, :]


def corner_kernel(rows, got_a, got_b, x_low, x_high, corner_a, corner_b):
    odd_x = is_odd("gx")
    x_low[...] = jnp.where(odd_x, got_b[...], got_a[...])
    x_high[...] = jnp.where(odd_x, got_a[...], got_b[...])
    for out, base in zip((corner_a, corner_b), bases(rows)):
        for at in range(depth):
            out[0, at] = x_low[base + at]
            out[1, at] = x_high[base + at]


def first_interior(steps, rows, cols, nz, conc_own, adj_own, rate_own, x_low, x_high,
                   conc, adj, rate, chem, curve, swing, pot, out, grad, ahead, mob, part):
    places, _ = slots(steps)
    low, high = reach(cols)
    lanes = adj.shape[2]
    mask = face_mask(lanes, nz)
    for y in range(rows):
        put_own(conc, y, conc_own[0, y], y, places[1], cols, x_low, x_high)
        put_own(adj, y, adj_own[y], y, places[0], cols, x_low, x_high)
        put_own(rate, y, rate_own[y], y, places[steps + 1], cols, x_low, x_high)
    put_ahead(ahead, conc_own, 1, x_low, x_high, places, rows, cols)

    def mob_row(y, _):
        for at, size in chunks(low - 8, high + 8):
            c = conc[y, at : at + size, :]
            mob[y, at : at + size, :] = mobility(c)
        return 0

    def mu_row(y, _):
        for at, size in chunks(low, high):
            chem_row(row_of(conc, y), set_row(chem, y - 1), set_row(curve, y - 1),
                     set_row(swing, y - 1), at, size, mask)
        return 0

    lax.fori_loop(0, rows, mob_row, 0)
    lax.fori_loop(1, rows - 1, mu_row, 0)

    def store(k, span, value):
        out[k, span, :] = value

    interior(rows, cols, nz, (swing, -1), (mob, 0), (chem, -1), (curve, -1), (adj, 0), (rate, 0),
             pot, part, grad, store)


def copy_rows(pairs):
    for out, to, ref, at in pairs:
        out[to] = ref[at]


def send_rows(out, ahead, rate, to_a, to_b, open_g, cols, nz):
    low, high = reach(cols)
    first, last = sent(cols)
    rows, lanes = rate.shape[0], rate.shape[2]
    mask = face_mask(lanes, nz)
    for s in range(2):
        for at, size in chunks(low, high):
            a, _mu, flow, _pair = face_sums(
                lambda dy, cut: out[s, dy, cut, :], lambda dy, cut: ahead[s, dy, cut, :], None,
                at, size, mask, (1,)
            )
            open_g[s, at - low : at - low + size, :] = (
                flow - rate[s * (rows - 1), at : at + size, :] * a
            )
    odd = is_odd("gy")
    for to, side in ((to_a, jnp.where(odd, 1, 0)), (to_b, jnp.where(odd, 0, 1))):
        to[0] = out[side, 0, first:last, :]
        to[1] = open_g[side, first - low : last - low, :]


def put_ahead(ahead, conc_own, back, x_low, x_high, places, rows, cols):
    for s, k, y in sides_of(rows):
        put_own(ahead.at[s], k, conc_own[back, y], y, places[1 + back], cols, x_low, x_high)
        ahead[s, k] = mobility(ahead[s, k])


def first_boundary(steps, rows, cols, nz, conc_in, adj_in, rate_in, chem_in, curve_in, swing_in,
                   pot_in,
                   from_a, from_b, corner_a, corner_b, ahead,
                   out, grad, to_a, to_b, rate, conc, adj, mob, chem, curve, swing, pot,
                   part, open_g):
    places, _ = slots(steps)
    low, high = reach(cols)
    half = cols // 2
    lanes = conc.shape[2]
    lower = lax.broadcasted_iota(jnp.int32, (half, lanes), 1) < nz

    def unpack(side):
        packed = side[pl.ds((1 + steps) * depth * cols, half), :]
        turned = pltpu.roll(packed, lanes // 2, 1)
        return jnp.concatenate(
            [jnp.where(lower, packed, turned), jnp.where(lower, turned, packed)], axis=0
        )

    near = [0, 1, 2, rows - 3, rows - 2, rows - 1]
    for y in near:
        conc[depth + y] = conc_in[y]
        adj[depth + y] = adj_in[y]
    for y in (1, 2, rows - 3, rows - 2):
        chem[1 + y] = chem_in[y - 1]
        pot[1 + y] = pot_in[y - 1]
    for y in (1, rows - 2):
        curve[1 + y] = curve_in[y - 1]
        swing[1 + y] = swing_in[y - 1]
    rate[1] = rate_in[0]
    rate[2] = rate_in[rows - 1]
    for halo, corner, base in zip((from_a, from_b), (corner_a, corner_b), landings(rows)):
        for at in range(depth):
            for ref, place, first in ((adj, places[0], 0), (conc, places[1], depth)):
                span = pl.ds((first + at) * cols, cols)
                put_halo(ref, base + at, halo[span, :], at, place, cols, corner)
        below = base == 0
        put_halo(rate, jnp.where(below, 0, 3), unpack(halo), jnp.where(below, depth - 1, 0),
                 places[steps + 1], cols, corner)
    for row in [0, 1, 2, 3, rows, rows + 1, rows + 2, rows + 3]:
        for at, size in chunks(low - 8, high + 8):
            c = conc[row, at : at + size, :]
            mob[row, at : at + size, :] = mobility(c)

    def store(s, k, span, value):
        out[s, k, span, :] = value

    boundary(rows, cols, nz, (conc, depth), (mob, depth), (chem, 1), (curve, 1), (swing, 1),
             (adj, depth), rate, pot, part, grad, store)
    send_rows(out, ahead, rate_in, to_a, to_b, open_g, cols, nz)


def prepare_kernel(steps, rows, cols, nz, back, conc_own, from_a, from_b, x_low, x_high,
                   corner_a, corner_b, mob, chem, curve, swing, *rest):
    *ahead, conc = rest
    places, _ = slots(steps)
    low, high = reach(cols)
    lanes = conc.shape[2]
    mask = face_mask(lanes, nz)
    place = places[1 + back]
    for y in range(rows):
        put_own(conc, depth + y, conc_own[back, y], y, place, cols, x_low, x_high)
    for halo, corner, base in zip((from_a, from_b), (corner_a, corner_b), landings(rows)):
        for at in range(depth):
            span = pl.ds(((1 + back) * depth + at) * cols, cols)
            put_halo(conc, base + at, halo[span, :], at, place, cols, corner)

    if ahead:
        put_ahead(ahead[0], conc_own, back + 1, x_low, x_high, places, rows, cols)

    def mob_row(row, _):
        for at, size in chunks(low - 8, high + 8):
            c = conc[row, at : at + size, :]
            mob[row, at : at + size, :] = mobility(c)
        return 0

    def mu_row(row, _):
        for at, size in chunks(low, high):
            chem_row(row_of(conc, row + 1), set_row(chem, row), set_row(curve, row),
                     set_row(swing, row), at, size, mask)
        return 0

    lax.fori_loop(0, rows + 2 * depth, mob_row, 0)
    lax.fori_loop(0, rows + 2, mu_row, 0)


def next_interior(rows, cols, nz, final, mob, chem, curve, swing, rate, inner, outer, *rest):
    if final:
        before, out, tiles, grad_out, adj, pot, part, grad = rest
    elif len(rest) == 8:
        inner_grad, outer_grad, out, grad, adj, pot, part, before = rest
        for k in range(rows - 2 * depth):
            before[depth + k] = inner_grad[k]
        for s, k, y in sides_of(rows):
            before[y] = outer_grad[s, k]
    else:
        before, out, grad, adj, pot, part = rest
    low, high = reach(cols)
    lanes = adj.shape[2]
    mask = face_mask(lanes, nz)
    skip = (inner.shape[0] - (rows - 2 * depth)) // 2
    for k in range(rows - 2 * depth):
        adj[1 + depth + k] = inner[skip + k]
    for s, k, y in sides_of(rows):
        adj[1 + y] = outer[s, k]
    adj[0] = outer[0, 0]
    adj[1 + rows] = outer[1, 0]
    pot[0] = jnp.zeros(pot.shape[1:], f32)
    pot[1 + rows] = jnp.zeros(pot.shape[1:], f32)

    def body(y, _):
        for at, size in chunks(low, high):
            span = slice(at, at + size)
            a, mu, flow, pair = face_sums(
                row_of(adj, y + 1), row_of(mob, y + depth), row_of(chem, y + 1), at, size, mask
            )
            g = flow - rate[y, span, :] * a
            pot[y + 1, span, :] = g
            part[y, span, :] = partial(
                a, swing[y + 1, span, :], pair, curve[y + 1, span, :], g
            )
            grad[y, span, :] = gain(a, mu, before[y, span, :])
        return 0

    def close(y, _):
        for at, size in chunks(low, high):
            span = slice(at, at + size)
            _g, lap = laplace(row_of(pot, y + 1), at, size, mask)
            out[y, span, :] = part[y, span, :] - grad_energy * lap
        return 0

    lax.fori_loop(0, rows, body, 0)
    lax.fori_loop(0, rows, close, 0)
    if final:
        for y in range(rows):
            grad_out[pl.ds(y, nz, stride=rows), :] = fold(grad[y, pad : pad + cols, :].T, nz)
        for y in range(depth, rows - depth):
            tiles[pl.ds(y, lanes, stride=rows), :] = out[y, pad : pad + cols, :].T


def fold(value, nz):
    total = value[:nz]
    for frame in range(1, value.shape[0] // nz):
        total = total + value[frame * nz : (frame + 1) * nz]
    return total


def next_boundary(rows, cols, nz, final, mob, chem, curve, swing, inside, outer, from_a, from_b,
                  *rest):
    if final:
        tiles, out, halo, delta, result = rest
    else:
        ahead, rate, result, to_a, to_b, halo, delta, open_g = rest
    low, high = reach(cols)
    first, last = sent(cols)
    lanes = mob.shape[2]
    mask = face_mask(lanes, nz)
    odd = is_odd("gy")
    for got, side in ((from_a, jnp.where(odd, 1, 0)), (from_b, jnp.where(odd, 0, 1))):
        for k in range(2):
            halo[side, k, first:last, :] = got[k]
    for s in range(2):
        y, beyond = s * (rows - 1), s * (rows + 1) - 1
        for at, size in chunks(low, high):
            span = slice(at, at + size)
            diff = halo[s, 0, span, :] - outer[s, 0, span, :]
            both = mob[depth + beyond, span, :] + mob[depth + y, span, :]
            delta[s, span, :] = both * diff
        for at, size in chunks(low, high):
            span = slice(at, at + size)
            more = delta[s, span, :]
            diff = halo[s, 0, span, :] - outer[s, 0, span, :]
            pair = (chem[1 + beyond, span, :] - chem[1 + y, span, :]) * diff
            step_z = (up(more) - more) * mask
            lap = (
                (delta[s, at + 1 : at + size + 1, :] + delta[s, at - 1 : at + size - 1, :])
                + (halo[s, 1, span, :] - more)
                - 4.0 * more
                + (step_z - down(step_z))
            )
            result[s, 0, span, :] = (
                inside[y, span, :]
                + (swing[1 + y, span, :] * pair + curve[1 + y, span, :] * more)
                - grad_energy * lap
            )
            result[s, 1, span, :] = inside[1 + s * (rows - 3), span, :] - grad_energy * more
    if final:
        out[...] = tiles[...]
        for s, k, y in sides_of(rows):
            out[pl.ds(y, lanes, stride=rows), :] = result[s, k, pad : pad + cols, :].T
    else:
        send_rows(result, ahead, rate, to_a, to_b, open_g, cols, nz)


def call(kernel, outs, scratch, *operands, cost=0, far=False):
    if far:
        operands = [pltpu.with_memory_space_constraint(value, pltpu.HBM) for value in operands]
    space = pl.ANY if far else pltpu.VMEM
    return pl.pallas_call(
        kernel,
        out_shape=[jax.ShapeDtypeStruct(shape, f32) for shape in outs],
        in_specs=[pl.BlockSpec(memory_space=space)] * len(operands),
        out_specs=[pl.BlockSpec(memory_space=pltpu.VMEM)] * len(outs),
        scratch_shapes=[pltpu.VMEM(s, f32) if isinstance(s, tuple) else s for s in scratch],
        compiler_params=pltpu.CompilerParams(vmem_limit_bytes=vmem_limit),
        cost_estimate=pl.CostEstimate(
            flops=cost * 1_000_000, bytes_accessed=cost * 2_000_000, transcendentals=0
        ),
    )(*operands)


def swap(value_a, value_b, axis):
    count = lax.axis_size(axis)
    pairs_a = [(i, (i - 1 + 2 * (i % 2)) % count) for i in range(count)]
    pairs_b = [(i, i + 1 - 2 * (i % 2)) for i in range(count)]
    return lax.ppermute(value_a, axis, pairs_a), lax.ppermute(value_b, axis, pairs_b)


def shards(saved_conc, adjoint_end, rate_field):
    steps, frames, nz, rows, cols = saved_conc.shape
    lanes = frames * nz
    _, total = slots(steps)
    width = cols + 2 * pad
    flat = lanes * rows
    inside = rows - 2 * depth

    def field(count):
        return (count, width, lanes)

    both = (2, depth, width, lanes)
    edge = (2, cols + 8, lanes)
    open_g = (2, cols + 16, lanes)
    raw = [(steps, flat, cols), (flat, cols), (nz * rows, cols)]
    conc_raw, adj_raw, rate_raw, main_a, main_b = call(
        functools.partial(edge_kernel, steps, rows, cols, nz),
        raw + [((1 + steps) * depth * cols + cols // 2, lanes)] * 2,
        [pltpu.SemaphoreType.DMA((2 + steps,))],
        saved_conc.reshape(raw[0]), adjoint_end.reshape(raw[1]), rate_field.reshape(raw[2]),
        cost=2,
        far=True,
    )
    main_a, main_b = swap(main_a, main_b, "gy")
    conc_own, adj_own, rate_own, x_a, x_b = call(
        functools.partial(turn_kernel, steps, rows, cols, nz),
        [(steps, rows, cols, lanes), (rows, cols, lanes), (rows, cols, lanes)]
        + [(rows, total, lanes)] * 2,
        [],
        conc_raw, adj_raw, rate_raw,
        cost=1,
    )
    x_a, x_b = swap(x_a, x_b, "gx")
    x_low, x_high, corner_a, corner_b = call(
        functools.partial(corner_kernel, rows),
        [(rows, total, lanes)] * 2 + [(2, depth, total, lanes)] * 2,
        [],
        x_a, x_b,
    )
    corner_a, corner_b = swap(corner_a, corner_b, "gy")

    conc, adj, rate, chem, curve, swing, pot, inner, inner_grad, ahead = call(
        functools.partial(first_interior, steps, rows, cols, nz),
        [field(rows)] * 3 + [field(rows - 2)] * 4 + [field(inside)] * 2 + [both],
        [field(rows), field(inside)],
        conc_own, adj_own, rate_own, x_low, x_high,
        cost=3,
    )
    outer, outer_grad, to_a, to_b = call(
        functools.partial(first_boundary, steps, rows, cols, nz),
        [both, both, edge, edge],
        [field(4)] + [field(rows + 2 * depth)] * 3 + [field(rows + 2)] * 4 + [both, open_g],
        conc, adj, rate, chem, curve, swing, pot, main_a, main_b, corner_a, corner_b, ahead,
        cost=2,
    )
    before = (inner_grad, outer_grad)
    for back in range(1, steps):
        adj_a, adj_b = swap(to_a, to_b, "gy")
        final = back == steps - 1
        fields = call(
            functools.partial(prepare_kernel, steps, rows, cols, nz, back),
            [field(rows + 2 * depth)] + [field(rows + 2)] * 3 + ([] if final else [both]),
            [field(rows + 2 * depth)],
            conc_own, main_a, main_b, x_low, x_high, corner_a, corner_b,
            cost=2,
        )
        fields, ahead = fields[:4], fields[4:]
        work = [field(rows + 2)] * 2 + [field(rows)]
        if final:
            rows_in, tiles, grad = call(
                functools.partial(next_interior, rows, cols, nz, final),
                [field(rows), (flat, cols), (nz * rows, cols)],
                work + [field(rows)],
                *fields, rate, inner, outer, *before,
                cost=3,
            )
            (adj,) = call(
                functools.partial(next_boundary, rows, cols, nz, final),
                [(flat, cols)],
                [both, field(2), both],
                *fields, rows_in, outer, adj_a, adj_b, tiles,
                cost=1,
            )
        else:
            rows_in, grad = call(
                functools.partial(next_interior, rows, cols, nz, final),
                [field(rows)] * 2,
                work + ([field(rows)] if len(before) == 2 else []),
                *fields, rate, inner, outer, *before,
                cost=3,
            )
            outer, to_a, to_b = call(
                functools.partial(next_boundary, rows, cols, nz, final),
                [both, edge, edge],
                [both, field(2), open_g],
                *fields, rows_in, outer, adj_a, adj_b, *ahead, rate,
                cost=1,
            )
            inner, before = rows_in, (grad,)
    return adj.reshape(adjoint_end.shape), grad.reshape(rate_field.shape)


def solution(mesh):
    return jax.shard_map(
        shards,
        mesh=mesh,
        in_specs=(P(None, None, None, "gy", "gx"), P(None, None, "gy", "gx"), P(None, "gy", "gx")),
        out_specs=(P(None, None, "gy", "gx"), P(None, "gy", "gx")),
        check_vma=False,
    )
```

```python
import functools

import jax
import jax.numpy as jnp
from jax import lax
from jax.experimental import pallas as pl
from jax.experimental.pallas import tpu as pltpu
from jax.sharding import PartitionSpec as P

mix_energy = 2.5
grad_energy = 1.0
time_step = 0.1
diff_step = 0.03
bath_potential = 0.5

pad = 16
chunk = 72
piece = 24
depth = 2
early = 2
vmem_limit = 20 * 1024 * 1024
f32 = jnp.float32


def slots(steps):
    widths = [2 * steps] + [2 * steps - 2 * back for back in range(steps)] + [2 * steps - 1]
    starts = [sum(widths[:i]) for i in range(len(widths))]
    total = -(-sum(widths) // 8) * 8
    return list(zip(starts, widths)), total


def chunks(low, high, most=chunk):
    return [(at, min(most, high - at)) for at in range(low, high, most)]


def reach(cols):
    return pad - 8, pad + cols + 8


def sent(cols):
    return pad - 4, pad + cols + 4


def up(value):
    return pltpu.roll(value, value.shape[1] - 1, 1)


def down(value):
    return pltpu.roll(value, 1, 1)


def face_mask(lanes, nz):
    lane = lax.broadcasted_iota(jnp.int32, (1, lanes), 1)
    return jnp.where(lane % nz == nz - 1, 0.0, 1.0).astype(f32)


def row_of(ref, y):
    return lambda dy, cut: ref[y + dy, cut, :]


def laplace(field, at, size, mask):
    span = slice(at, at + size)
    here = field(0, span)
    step_z = (up(here) - here) * mask
    sides = field(0, slice(at + 1, at + size + 1)) + field(0, slice(at - 1, at + size - 1))
    return here, (
        (sides + (field(-1, span) + field(1, span))) - 4.0 * here + (step_z - down(step_z))
    )


def mobility(c):
    return (0.5 * diff_step) * c * (1.0 - c)


def chem_row(conc, chem, curve, swing, at, size, mask):
    c, lap = laplace(conc, at, size, mask)
    inv = 1.0 / (c * (1.0 - c))
    span = slice(at, at + size)
    chem(
        span,
        time_step * (jnp.log(c * c * inv) - grad_energy * lap)
        + (time_step * (mix_energy - bath_potential) - (2.0 * time_step * mix_energy) * c),
    )
    curve(span, inv - 2.0 * mix_energy)
    swing(span, c * (diff_step / time_step) - 0.5 * diff_step / time_step)


def face_sums(adj, mob, chem, at, size, mask, across=(1, -1)):
    span = slice(at, at + size)
    a = adj(0, span)
    m = None if mob is None else mob(0, span)
    mu = None if chem is None else chem(0, span)
    flow = pair = None
    for dy, cut in (
        (0, slice(at + 1, at + size + 1)),
        (0, slice(at - 1, at + size - 1)),
    ) + tuple((dy, span) for dy in across):
        diff = adj(dy, cut) - a
        if mob is not None:
            term = (mob(dy, cut) + m) * diff
            flow = term if flow is None else flow + term
        if chem is not None:
            term = (chem(dy, cut) - mu) * diff
            pair = term if pair is None else pair + term
    diff = (up(a) - a) * mask
    if mob is not None:
        term = (up(m) + m) * diff
        flow = flow + (term - down(term))
    if chem is not None:
        term = (up(mu) - mu) * diff
        pair = pair + (term + down(term))
    return a, mu, flow, pair


def partial(a, swing, pair, curve, g):
    return a + swing * pair + curve * g


def gain(a, chem, before):
    value = a * chem
    return -value if before is None else before - value


def set_row(ref, y):
    def put(span, value):
        ref[y, span, :] = value

    return put


class Rows:
    def __init__(self, row, at, size):
        self.row, self.at, self.size = row, at, size
        self.wide = {}

    def around(self, y):
        if y not in self.wide:
            self.wide[y] = self.row(y, slice(self.at - 8, self.at + self.size + 8))
        return self.wide[y]

    def here(self, y):
        return self.around(y)[8 : 8 + self.size]

    def sides(self, y):
        wide = self.around(y)
        count = self.size + 16
        return (
            pltpu.roll(wide, count - 1, 0)[8 : 8 + self.size],
            pltpu.roll(wide, 1, 0)[8 : 8 + self.size],
        )


def sweep(g_rows, term_rows, own_rows, adj, mob, chem, mask, cols, emit):
    for at, size in chunks(*reach(cols), piece):
        adj_rows, mob_rows, chem_rows = (Rows(f, at, size) for f in (adj, mob, chem))
        for y in g_rows:
            with_terms = y in term_rows
            a, m = adj_rows.here(y), mob_rows.here(y)
            mu = chem_rows.here(y) if with_terms else None
            across = [other for other in (y + 1, y - 1) if other in own_rows]
            diffs = [other - a for other in adj_rows.sides(y)]
            diffs += [adj_rows.here(other) - a for other in across]
            mobs = list(mob_rows.sides(y)) + [mob_rows.here(other) for other in across]
            flow = sum_of([(other + m) * diff for other, diff in zip(mobs, diffs)])
            diff = (up(a) - a) * mask
            term = (up(m) + m) * diff
            flow = flow + (term - down(term))
            pair = None
            if with_terms:
                chems = list(chem_rows.sides(y)) + [chem_rows.here(other) for other in across]
                pair = sum_of([(other - mu) * diff for other, diff in zip(chems, diffs)])
                term = (up(mu) - mu) * diff
                pair = pair + (term + down(term))
            emit(y, slice(at, at + size), a, mu, flow, pair)


def sum_of(values):
    total = values[0]
    for value in values[1:]:
        total = total + value
    return total


def close_rows(out_rows, pot_rows, pot, mask, cols, emit):
    for at, size in chunks(*reach(cols), piece):
        held = Rows(pot, at, size)
        for y in out_rows:
            g = held.here(y)
            step_z = (up(g) - g) * mask
            values = list(held.sides(y)) + [held.here(k) for k in (y - 1, y + 1) if k in pot_rows]
            emit(y, slice(at, at + size), sum_of(values) - 4.0 * g + (step_z - down(step_z)))


def interior(rows, cols, nz, swing, mob, chem, curve, adj, rate, pot, part, grad, store):
    lanes = adj[0].shape[-1]
    mask = face_mask(lanes, nz)
    inside = range(depth, rows - depth)

    def reader(field):
        return lambda y, span: field[0][field[1] + y, span, :]

    def emit(y, span, a, mu, flow, pair):
        g = flow - reader(rate)(y, span) * a
        pot[y - 1, span, :] = g
        if pair is not None:
            part[y - depth, span, :] = partial(
                a, reader(swing)(y, span), pair, reader(curve)(y, span), g
            )
            grad[y - depth, span, :] = gain(a, mu, None)

    def close(y, span, lap):
        store(y - depth, span, part[y - depth, span, :] - grad_energy * lap)

    sweep(range(1, rows - 1), inside, range(rows), reader(adj), reader(mob), reader(chem), mask,
          cols, emit)
    close_rows(inside, range(1, rows - 1), lambda y, span: pot[y - 1, span, :], mask, cols, close)


def boundary(rows, cols, nz, conc, mob, chem, curve, swing, adj, rate, pot, part, grad, store):
    low, high = reach(cols)
    lanes = adj[0].shape[-1]
    mask = face_mask(lanes, nz)
    last = rows - 1

    def at_row(field, y):
        return row_of(field[0], field[1] + y)

    def mirror(s, y):
        return y + s * (last - 2 * y)

    def mu_side(i, _):
        s, k = i // 2, i % 2
        y = mirror(s, k - 1)
        for at, size in chunks(low, high):
            chem_row(at_row(conc, y), set_row(chem[0], chem[1] + y),
                     set_row(curve[0], curve[1] + y), set_row(swing[0], swing[1] + y), at, size,
                     mask)
        return 0

    lax.fori_loop(0, 4, mu_side, 0)

    def side(s, _):
        y = mirror(s, -1)
        for at, size in chunks(low, high):
            span = slice(at, at + size)
            a, _mu, flow, _pair = face_sums(at_row(adj, y), at_row(mob, y), None, at, size, mask)
            pot[1 + y, span, :] = flow - rate[3 * s, span, :] * a
        y0 = mirror(s, 0)
        for at, size in chunks(low, high):
            span = slice(at, at + size)
            a, mu, flow, pair = face_sums(
                at_row(adj, y0), at_row(mob, y0), at_row(chem, y0), at, size, mask
            )
            g = flow - rate[1 + s, span, :] * a
            pot[1 + y0, span, :] = g
            part[s, 0, span, :] = partial(
                a, at_row(swing, y0)(0, span), pair, at_row(curve, y0)(0, span), g
            )
            grad[s, 0, span, :] = gain(a, mu, None)
        y1 = mirror(s, 1)
        for at, size in chunks(low, high):
            span = slice(at, at + size)
            a, mu, _flow, pair = face_sums(at_row(adj, y1), None, at_row(chem, y1), at, size, mask)
            part[s, 1, span, :] = partial(
                a, at_row(swing, y1)(0, span), pair, at_row(curve, y1)(0, span), pot[1 + y1, span, :]
            )
            grad[s, 1, span, :] = gain(a, mu, None)
        return 0

    lax.fori_loop(0, 2, side, 0)

    def close(i, _):
        s, k = i // 2, i % 2
        y = mirror(s, k)
        for at, size in chunks(low, high):
            span = slice(at, at + size)
            _g, lap = laplace(row_of(pot, 1 + y), at, size, mask)
            store(s, k, span, part[s, k, span, :] - grad_energy * lap)
        return 0

    lax.fori_loop(0, 4, close, 0)


def is_odd(axis):
    return lax.rem(lax.axis_index(axis), 2) == 1


def bases(rows):
    odd = is_odd("gy")
    top = rows - depth
    return jnp.where(odd, top, 0), jnp.where(odd, 0, top)


def landings(rows):
    odd = is_odd("gy")
    top = rows + depth
    return jnp.where(odd, top, 0), jnp.where(odd, 0, top)


def sides_of(rows):
    return [(0, 0, 0), (0, 1, 1), (1, 0, rows - 1), (1, 1, rows - 2)]


def edge_kernel(steps, rows, cols, nz, conc_hbm, adj_hbm, rate_hbm, conc_in, adj_in, rate_in,
                main_a, main_b, sems):
    lanes = main_a.shape[1]
    half = cols // 2
    lower = lax.broadcasted_iota(jnp.int32, (half, lanes), 1) < nz
    copies = [
        pltpu.make_async_copy(adj_hbm, adj_in, sems.at[0]),
        pltpu.make_async_copy(rate_hbm, rate_in, sems.at[1]),
    ] + [
        pltpu.make_async_copy(conc_hbm.at[steps - 1 - back], conc_in.at[back], sems.at[2 + back])
        for back in range(steps)
    ]
    for copy in copies:
        copy.start()
    copies[0].wait()
    for side, base in zip((main_a, main_b), bases(rows)):
        for at in range(depth):
            side[pl.ds(at * cols, cols), :] = adj_in[pl.ds(base + at, lanes, stride=rows), :].T
    copies[1].wait()
    for side, base in zip((main_a, main_b), bases(rows)):
        edge = jnp.where(base == 0, 0, rows - 1)
        rate = turned_rate(rate_in, edge, rows, nz, lanes)
        side[pl.ds((1 + early) * depth * cols, half), :] = jnp.where(
            lower, rate[:half], rate[half:]
        )
    for back in range(steps):
        copies[2 + back].wait()
        if back >= early:
            continue
        for side, base in zip((main_a, main_b), bases(rows)):
            for at in range(depth):
                side[pl.ds(((1 + back) * depth + at) * cols, cols), :] = conc_in[
                    back, pl.ds(base + at, lanes, stride=rows), :
                ].T


def turned_rate(rate, y, rows, nz, lanes):
    value = time_step * rate[pl.ds(y, nz, stride=rows), :]
    return jnp.concatenate([value] * (lanes // nz), axis=0).T


def turn_kernel(steps, rows, cols, nz, conc_in, adj_in, rate_in, conc_out, adj_out, rate_out,
                x_a, x_b):
    places, total = slots(steps)
    lanes = adj_out.shape[2]
    odd_x = is_odd("gx")

    def to_x(y, value, place):
        start, width = place
        last, first = value[cols - width :, :], value[:width, :]
        x_a[y, start : start + width, :] = jnp.where(odd_x, last, first)
        x_b[y, start : start + width, :] = jnp.where(odd_x, first, last)

    used = sum(places[-1])
    for y in range(rows):
        adj = adj_in[pl.ds(y, lanes, stride=rows), :].T
        adj_out[y] = adj
        to_x(y, adj, places[0])
        rate = turned_rate(rate_in, y, rows, nz, lanes)
        rate_out[y] = rate
        to_x(y, rate, places[steps + 1])
        if used < total:
            x_a[y, used:, :] = jnp.zeros((total - used, lanes), f32)
            x_b[y, used:, :] = jnp.zeros((total - used, lanes), f32)
        for back in range(steps):
            conc = conc_in[back, pl.ds(y, lanes, stride=rows), :].T
            conc_out[back, y] = conc
            to_x(y, conc, places[1 + back])


def put_own(out, row, value, y, place, cols, x_low, x_high):
    start, width = place
    right = pad + cols
    out[row, pad:right, :] = value
    out[row, pad - width : pad, :] = x_low[y, start : start + width, :]
    out[row, right : right + width, :] = x_high[y, start : start + width, :]


def put_halo(out, row, value, from_row, place, cols, corner):
    start, width = place
    right = pad + cols
    out[row, pad:right, :] = value
    out[row, pad - width : pad, :] = corner[0, from_row, start : start + width, :]
    out[row, right : right + width, :] = corner[1, from_row, start : start + width, :]


def corner_kernel(rows, got_a, got_b, x_low, x_high, corner_a, corner_b):
    odd_x = is_odd("gx")
    x_low[...] = jnp.where(odd_x, got_b[...], got_a[...])
    x_high[...] = jnp.where(odd_x, got_a[...], got_b[...])
    for out, base in zip((corner_a, corner_b), bases(rows)):
        for at in range(depth):
            out[0, at] = x_low[base + at]
            out[1, at] = x_high[base + at]


def first_interior(steps, rows, cols, nz, conc_own, adj_own, rate_own, x_low, x_high,
                   conc, adj, rate, chem, curve, swing, pot, out, grad, ahead, mob, part):
    places, _ = slots(steps)
    low, high = reach(cols)
    lanes = adj.shape[2]
    mask = face_mask(lanes, nz)
    for y in range(rows):
        put_own(conc, y, conc_own[0, y], y, places[1], cols, x_low, x_high)
        put_own(adj, y, adj_own[y], y, places[0], cols, x_low, x_high)
        put_own(rate, y, rate_own[y], y, places[steps + 1], cols, x_low, x_high)
    put_ahead(ahead, conc_own, 1, x_low, x_high, places, rows, cols)

    def mob_row(y, _):
        for at, size in chunks(low - 8, high + 8):
            c = conc[y, at : at + size, :]
            mob[y, at : at + size, :] = mobility(c)
        return 0

    def mu_row(y, _):
        for at, size in chunks(low, high):
            chem_row(row_of(conc, y), set_row(chem, y - 1), set_row(curve, y - 1),
                     set_row(swing, y - 1), at, size, mask)
        return 0

    lax.fori_loop(0, rows, mob_row, 0)
    lax.fori_loop(1, rows - 1, mu_row, 0)

    def store(k, span, value):
        out[k, span, :] = value

    interior(rows, cols, nz, (swing, -1), (mob, 0), (chem, -1), (curve, -1), (adj, 0), (rate, 0),
             pot, part, grad, store)


def copy_rows(pairs):
    for out, to, ref, at in pairs:
        out[to] = ref[at]


def send_rows(out, ahead, rate, to_a, to_b, open_g, cols, nz):
    low, high = reach(cols)
    first, last = sent(cols)
    rows, lanes = rate.shape[0], rate.shape[2]
    mask = face_mask(lanes, nz)
    for s in range(2):
        for at, size in chunks(low, high):
            a, _mu, flow, _pair = face_sums(
                lambda dy, cut: out[s, dy, cut, :], lambda dy, cut: ahead[s, dy, cut, :], None,
                at, size, mask, (1,)
            )
            open_g[s, at - low : at - low + size, :] = (
                flow - rate[s * (rows - 1), at : at + size, :] * a
            )
    odd = is_odd("gy")
    for to, side in ((to_a, jnp.where(odd, 1, 0)), (to_b, jnp.where(odd, 0, 1))):
        to[0] = out[side, 0, first:last, :]
        to[1] = open_g[side, first - low : last - low, :]


def put_ahead(ahead, conc_own, back, x_low, x_high, places, rows, cols):
    for s, k, y in sides_of(rows):
        put_own(ahead.at[s], k, conc_own[back, y], y, places[1 + back], cols, x_low, x_high)
        ahead[s, k] = mobility(ahead[s, k])


def first_boundary(steps, rows, cols, nz, conc_in, adj_in, rate_in, chem_in, curve_in, swing_in,
                   pot_in,
                   from_a, from_b, corner_a, corner_b, ahead,
                   out, grad, to_a, to_b, rate, conc, adj, mob, chem, curve, swing, pot,
                   part, open_g):
    places, _ = slots(steps)
    low, high = reach(cols)
    half = cols // 2
    lanes = conc.shape[2]
    lower = lax.broadcasted_iota(jnp.int32, (half, lanes), 1) < nz

    def unpack(side):
        packed = side[pl.ds((1 + early) * depth * cols, half), :]
        turned = pltpu.roll(packed, lanes // 2, 1)
        return jnp.concatenate(
            [jnp.where(lower, packed, turned), jnp.where(lower, turned, packed)], axis=0
        )

    near = [0, 1, 2, rows - 3, rows - 2, rows - 1]
    for y in near:
        conc[depth + y] = conc_in[y]
        adj[depth + y] = adj_in[y]
    for y in (1, 2, rows - 3, rows - 2):
        chem[1 + y] = chem_in[y - 1]
        pot[1 + y] = pot_in[y - 1]
    for y in (1, rows - 2):
        curve[1 + y] = curve_in[y - 1]
        swing[1 + y] = swing_in[y - 1]
    rate[1] = rate_in[0]
    rate[2] = rate_in[rows - 1]
    for halo, corner, base in zip((from_a, from_b), (corner_a, corner_b), landings(rows)):
        for at in range(depth):
            for ref, place, first in ((adj, places[0], 0), (conc, places[1], depth)):
                span = pl.ds((first + at) * cols, cols)
                put_halo(ref, base + at, halo[span, :], at, place, cols, corner)
        below = base == 0
        put_halo(rate, jnp.where(below, 0, 3), unpack(halo), jnp.where(below, depth - 1, 0),
                 places[steps + 1], cols, corner)
    for row in [0, 1, 2, 3, rows, rows + 1, rows + 2, rows + 3]:
        for at, size in chunks(low - 8, high + 8):
            c = conc[row, at : at + size, :]
            mob[row, at : at + size, :] = mobility(c)

    def store(s, k, span, value):
        out[s, k, span, :] = value

    boundary(rows, cols, nz, (conc, depth), (mob, depth), (chem, 1), (curve, 1), (swing, 1),
             (adj, depth), rate, pot, part, grad, store)
    send_rows(out, ahead, rate_in, to_a, to_b, open_g, cols, nz)


def prepare_kernel(steps, rows, cols, nz, back, conc_own, from_a, from_b, x_low, x_high,
                   corner_a, corner_b, mob, chem, curve, swing, *rest):
    *more, conc = rest
    places, _ = slots(steps)
    low, high = reach(cols)
    lanes = conc.shape[2]
    mask = face_mask(lanes, nz)
    place = places[1 + back]
    for y in range(rows):
        put_own(conc, depth + y, conc_own[back, y], y, place, cols, x_low, x_high)
    for halo, corner, base in zip((from_a, from_b), (corner_a, corner_b), landings(rows)):
        for at in range(depth):
            first = (1 + back) * depth if back < early else (back - early) * depth
            span = pl.ds((first + at) * cols, cols)
            put_halo(conc, base + at, halo[span, :], at, place, cols, corner)

    if more:
        ahead, late_a, late_b = more
        put_ahead(ahead, conc_own, back + 1, x_low, x_high, places, rows, cols)
        for side, base in zip((late_a, late_b), bases(rows)):
            for after in range(early, steps):
                for at in range(depth):
                    span = pl.ds(((after - early) * depth + at) * cols, cols)
                    side[span, :] = conc_own[after, base + at]
            used = (steps - early) * depth * cols
            side[used:, :] = jnp.zeros((side.shape[0] - used, lanes), f32)

    def mob_row(row, _):
        for at, size in chunks(low - 8, high + 8):
            c = conc[row, at : at + size, :]
            mob[row, at : at + size, :] = mobility(c)
        return 0

    def mu_row(row, _):
        for at, size in chunks(low, high):
            chem_row(row_of(conc, row + 1), set_row(chem, row), set_row(curve, row),
                     set_row(swing, row), at, size, mask)
        return 0

    lax.fori_loop(0, rows + 2 * depth, mob_row, 0)
    lax.fori_loop(0, rows + 2, mu_row, 0)


def next_interior(rows, cols, nz, final, mob, chem, curve, swing, rate, inner, outer, *rest):
    if final:
        *before, out, tiles, grad_out, pot, part, grad = rest
    else:
        *before, out, grad, pot, part = rest
    mask = face_mask(mob.shape[2], nz)
    skip = (inner.shape[0] - (rows - 2 * depth)) // 2
    edges = {y: (s, k) for s, k, y in sides_of(rows)}

    def pick(middle, middle_skip, ends, y, span):
        if y in edges:
            return ends[(*edges[y], span)]
        return middle[y - depth + middle_skip, span]

    def earlier(y, span):
        if len(before) == 1:
            return before[0][y, span, :]
        return pick(before[0], 0, before[1], y, span)

    def emit(y, span, a, mu, flow, pair):
        g = flow - rate[y, span, :] * a
        pot[y, span, :] = g
        part[y, span, :] = partial(a, swing[y + 1, span, :], pair, curve[y + 1, span, :], g)
        grad[y, span, :] = gain(a, mu, earlier(y, span))

    def close(y, span, lap):
        out[y, span, :] = part[y, span, :] - grad_energy * lap

    every = range(rows)
    sweep(every, every, every, lambda y, span: pick(inner, skip, outer, y, span),
          lambda y, span: mob[depth + y, span, :], lambda y, span: chem[1 + y, span, :], mask,
          cols, emit)
    close_rows(every, every, lambda y, span: pot[y, span, :], mask, cols, close)
    if final:
        for y in range(rows):
            grad_out[pl.ds(y, nz, stride=rows), :] = fold(grad[y, pad : pad + cols, :].T, nz)
        for y in range(depth, rows - depth):
            tiles[pl.ds(y, lanes_of(out), stride=rows), :] = out[y, pad : pad + cols, :].T


def lanes_of(ref):
    return ref.shape[-1]


def fold(value, nz):
    total = value[:nz]
    for frame in range(1, value.shape[0] // nz):
        total = total + value[frame * nz : (frame + 1) * nz]
    return total


def next_boundary(rows, cols, nz, final, mob, chem, curve, swing, inside, outer, from_a, from_b,
                  *rest):
    if final:
        tiles, out, halo, delta, result = rest
    else:
        ahead, rate, result, to_a, to_b, halo, delta, open_g = rest
    low, high = reach(cols)
    first, last = sent(cols)
    lanes = mob.shape[2]
    mask = face_mask(lanes, nz)
    odd = is_odd("gy")
    for got, side in ((from_a, jnp.where(odd, 1, 0)), (from_b, jnp.where(odd, 0, 1))):
        for k in range(2):
            halo[side, k, first:last, :] = got[k]
    for s in range(2):
        y, beyond = s * (rows - 1), s * (rows + 1) - 1
        for at, size in chunks(low, high):
            span = slice(at, at + size)
            diff = halo[s, 0, span, :] - outer[s, 0, span, :]
            both = mob[depth + beyond, span, :] + mob[depth + y, span, :]
            delta[s, span, :] = both * diff
        for at, size in chunks(low, high):
            span = slice(at, at + size)
            more = delta[s, span, :]
            diff = halo[s, 0, span, :] - outer[s, 0, span, :]
            pair = (chem[1 + beyond, span, :] - chem[1 + y, span, :]) * diff
            step_z = (up(more) - more) * mask
            lap = (
                (delta[s, at + 1 : at + size + 1, :] + delta[s, at - 1 : at + size - 1, :])
                + (halo[s, 1, span, :] - more)
                - 4.0 * more
                + (step_z - down(step_z))
            )
            result[s, 0, span, :] = (
                inside[y, span, :]
                + (swing[1 + y, span, :] * pair + curve[1 + y, span, :] * more)
                - grad_energy * lap
            )
            result[s, 1, span, :] = inside[1 + s * (rows - 3), span, :] - grad_energy * more
    if final:
        out[...] = tiles[...]
        for s, k, y in sides_of(rows):
            out[pl.ds(y, lanes, stride=rows), :] = result[s, k, pad : pad + cols, :].T
    else:
        send_rows(result, ahead, rate, to_a, to_b, open_g, cols, nz)


def call(kernel, outs, scratch, *operands, cost=0, far=False):
    if far:
        operands = [pltpu.with_memory_space_constraint(value, pltpu.HBM) for value in operands]
    space = pl.ANY if far else pltpu.VMEM
    return pl.pallas_call(
        kernel,
        out_shape=[jax.ShapeDtypeStruct(shape, f32) for shape in outs],
        in_specs=[pl.BlockSpec(memory_space=space)] * len(operands),
        out_specs=[pl.BlockSpec(memory_space=pltpu.VMEM)] * len(outs),
        scratch_shapes=[pltpu.VMEM(s, f32) if isinstance(s, tuple) else s for s in scratch],
        compiler_params=pltpu.CompilerParams(vmem_limit_bytes=vmem_limit),
        cost_estimate=pl.CostEstimate(
            flops=cost * 1_000_000, bytes_accessed=cost * 2_000_000, transcendentals=0
        ),
    )(*operands)


def swap(value_a, value_b, axis):
    count = lax.axis_size(axis)
    pairs_a = [(i, (i - 1 + 2 * (i % 2)) % count) for i in range(count)]
    pairs_b = [(i, i + 1 - 2 * (i % 2)) for i in range(count)]
    return lax.ppermute(value_a, axis, pairs_a), lax.ppermute(value_b, axis, pairs_b)


def shards(saved_conc, adjoint_end, rate_field):
    steps, frames, nz, rows, cols = saved_conc.shape
    lanes = frames * nz
    _, total = slots(steps)
    width = cols + 2 * pad
    flat = lanes * rows
    inside = rows - 2 * depth

    def field(count):
        return (count, width, lanes)

    both = (2, depth, width, lanes)
    edge = (2, cols + 8, lanes)
    open_g = (2, cols + 16, lanes)
    raw = [(steps, flat, cols), (flat, cols), (nz * rows, cols)]
    conc_raw, adj_raw, rate_raw, main_a, main_b = call(
        functools.partial(edge_kernel, steps, rows, cols, nz),
        raw + [((1 + early) * depth * cols + cols // 2, lanes)] * 2,
        [pltpu.SemaphoreType.DMA((2 + steps,))],
        saved_conc.reshape(raw[0]), adjoint_end.reshape(raw[1]), rate_field.reshape(raw[2]),
        cost=2,
        far=True,
    )
    main_a, main_b = swap(main_a, main_b, "gy")
    conc_own, adj_own, rate_own, x_a, x_b = call(
        functools.partial(turn_kernel, steps, rows, cols, nz),
        [(steps, rows, cols, lanes), (rows, cols, lanes), (rows, cols, lanes)]
        + [(rows, total, lanes)] * 2,
        [],
        conc_raw, adj_raw, rate_raw,
        cost=1,
    )
    x_a, x_b = swap(x_a, x_b, "gx")
    x_low, x_high, corner_a, corner_b = call(
        functools.partial(corner_kernel, rows),
        [(rows, total, lanes)] * 2 + [(2, depth, total, lanes)] * 2,
        [],
        x_a, x_b,
    )
    corner_a, corner_b = swap(corner_a, corner_b, "gy")

    conc, adj, rate, chem, curve, swing, pot, inner, inner_grad, ahead = call(
        functools.partial(first_interior, steps, rows, cols, nz),
        [field(rows)] * 3 + [field(rows - 2)] * 4 + [field(inside)] * 2 + [both],
        [field(rows), field(inside)],
        conc_own, adj_own, rate_own, x_low, x_high,
        cost=3,
    )
    outer, outer_grad, to_a, to_b = call(
        functools.partial(first_boundary, steps, rows, cols, nz),
        [both, both, edge, edge],
        [field(4)] + [field(rows + 2 * depth)] * 3 + [field(rows + 2)] * 4 + [both, open_g],
        conc, adj, rate, chem, curve, swing, pot, main_a, main_b, corner_a, corner_b, ahead,
        cost=2,
    )
    before = (inner_grad, outer_grad)
    got = main_a, main_b
    late = (max((steps - early) * depth * cols, 2 * (cols + 8) + 8), lanes)
    for back in range(1, steps):
        adj_a, adj_b = swap(to_a, to_b, "gy")
        final = back == steps - 1
        fields = call(
            functools.partial(prepare_kernel, steps, rows, cols, nz, back),
            [field(rows + 2 * depth)] + [field(rows + 2)] * 3
            + ([] if final else [both, late, late]),
            [field(rows + 2 * depth)],
            conc_own, *got, x_low, x_high, corner_a, corner_b,
            cost=2,
        )
        fields, ahead, more = fields[:4], fields[4:5], fields[5:]
        if not final:
            got = swap(*more, "gy")
        work = [field(rows)] * 2
        if final:
            rows_in, tiles, grad = call(
                functools.partial(next_interior, rows, cols, nz, final),
                [field(rows), (flat, cols), (nz * rows, cols)],
                work + [field(rows)],
                *fields, rate, inner, outer, *before,
                cost=3,
            )
            (adj,) = call(
                functools.partial(next_boundary, rows, cols, nz, final),
                [(flat, cols)],
                [both, field(2), both],
                *fields, rows_in, outer, adj_a, adj_b, tiles,
                cost=1,
            )
        else:
            rows_in, grad = call(
                functools.partial(next_interior, rows, cols, nz, final),
                [field(rows)] * 2,
                work,
                *fields, rate, inner, outer, *before,
                cost=3,
            )
            outer, to_a, to_b = call(
                functools.partial(next_boundary, rows, cols, nz, final),
                [both, edge, edge],
                [both, field(2), open_g],
                *fields, rows_in, outer, adj_a, adj_b, *ahead, rate,
                cost=1,
            )
            inner, before = rows_in, (grad,)
    return adj.reshape(adjoint_end.shape), grad.reshape(rate_field.shape)


def solution(mesh):
    return jax.shard_map(
        shards,
        mesh=mesh,
        in_specs=(P(None, None, None, "gy", "gx"), P(None, None, "gy", "gx"), P(None, "gy", "gx")),
        out_specs=(P(None, None, "gy", "gx"), P(None, "gy", "gx")),
        check_vma=False,
    )
```

```python
import functools

import jax
import jax.numpy as jnp
from jax import lax
from jax.experimental import pallas as pl
from jax.experimental.pallas import tpu as pltpu
from jax.sharding import PartitionSpec as P

mix_energy = 2.5
grad_energy = 1.0
time_step = 0.1
diff_step = 0.03
bath_potential = 0.5

pad = 16
chunk = 72
depth = 2
early = 2
vmem_limit = 20 * 1024 * 1024
f32 = jnp.float32


def slots(steps):
    widths = [2 * steps] + [2 * steps - 2 * back for back in range(steps)] + [2 * steps - 1]
    starts = [sum(widths[:i]) for i in range(len(widths))]
    total = -(-sum(widths) // 8) * 8
    return list(zip(starts, widths)), total


def chunks(low, high):
    return [(at, min(chunk, high - at)) for at in range(low, high, chunk)]


def reach(cols):
    return pad - 8, pad + cols + 8


def sent(cols):
    return pad - 4, pad + cols + 4


def up(value):
    return pltpu.roll(value, value.shape[1] - 1, 1)


def down(value):
    return pltpu.roll(value, 1, 1)


def face_mask(lanes, nz):
    lane = lax.broadcasted_iota(jnp.int32, (1, lanes), 1)
    return jnp.where(lane % nz == nz - 1, 0.0, 1.0).astype(f32)


def row_of(ref, y):
    return lambda dy, cut: ref[y + dy, cut, :]


def laplace(field, at, size, mask):
    span = slice(at, at + size)
    here = field(0, span)
    step_z = (up(here) - here) * mask
    sides = field(0, slice(at + 1, at + size + 1)) + field(0, slice(at - 1, at + size - 1))
    return here, (
        (sides + (field(-1, span) + field(1, span))) - 4.0 * here + (step_z - down(step_z))
    )


def mobility(c):
    return (0.5 * diff_step) * c * (1.0 - c)


def chem_row(conc, chem, curve, swing, at, size, mask):
    c, lap = laplace(conc, at, size, mask)
    inv = 1.0 / (c * (1.0 - c))
    span = slice(at, at + size)
    chem(
        span,
        time_step * (jnp.log(c * c * inv) - grad_energy * lap)
        + (time_step * (mix_energy - bath_potential) - (2.0 * time_step * mix_energy) * c),
    )
    curve(span, inv - 2.0 * mix_energy)
    swing(span, c * (diff_step / time_step) - 0.5 * diff_step / time_step)


def face_sums(adj, mob, chem, at, size, mask, across=(1, -1)):
    span = slice(at, at + size)
    a = adj(0, span)
    m = None if mob is None else mob(0, span)
    mu = None if chem is None else chem(0, span)
    flow = pair = None
    for dy, cut in (
        (0, slice(at + 1, at + size + 1)),
        (0, slice(at - 1, at + size - 1)),
    ) + tuple((dy, span) for dy in across):
        diff = adj(dy, cut) - a
        if mob is not None:
            term = (mob(dy, cut) + m) * diff
            flow = term if flow is None else flow + term
        if chem is not None:
            term = (chem(dy, cut) - mu) * diff
            pair = term if pair is None else pair + term
    diff = (up(a) - a) * mask
    if mob is not None:
        term = (up(m) + m) * diff
        flow = flow + (term - down(term))
    if chem is not None:
        term = (up(mu) - mu) * diff
        pair = pair + (term + down(term))
    return a, mu, flow, pair


def partial(a, swing, pair, curve, g):
    return a + swing * pair + curve * g


def gain(a, chem, before):
    value = a * chem
    return -value if before is None else before - value


def set_row(ref, y):
    def put(span, value):
        ref[y, span, :] = value

    return put


def interior(rows, cols, nz, swing, mob, chem, curve, adj, rate, pot, part, grad, store):
    low, high = reach(cols)
    lanes = adj[0].shape[-1]
    mask = face_mask(lanes, nz)

    def at_row(field, y):
        return row_of(field[0], field[1] + y)

    def body(y, _):
        for at, size in chunks(low, high):
            span = slice(at, at + size)
            a, mu, flow, pair = face_sums(
                at_row(adj, y), at_row(mob, y), at_row(chem, y), at, size, mask
            )
            g = flow - at_row(rate, y)(0, span) * a
            pot[y - 1, span, :] = g
            part[y - depth, span, :] = partial(
                a, at_row(swing, y)(0, span), pair, at_row(curve, y)(0, span), g
            )
            grad[y - depth, span, :] = gain(a, mu, None)
        return 0

    def edge(i, _):
        y = 1 + i * (rows - 3)
        for at, size in chunks(low, high):
            a, _mu, flow, _pair = face_sums(at_row(adj, y), at_row(mob, y), None, at, size, mask)
            span = slice(at, at + size)
            pot[y - 1, span, :] = flow - at_row(rate, y)(0, span) * a
        return 0

    def close(y, _):
        for at, size in chunks(low, high):
            span = slice(at, at + size)
            _g, lap = laplace(row_of(pot, y - 1), at, size, mask)
            store(y - depth, span, part[y - depth, span, :] - grad_energy * lap)
        return 0

    lax.fori_loop(depth, rows - depth, body, 0)
    lax.fori_loop(0, 2, edge, 0)
    lax.fori_loop(depth, rows - depth, close, 0)


def boundary(rows, cols, nz, conc, mob, chem, curve, swing, adj, rate, pot, part, grad, store):
    low, high = reach(cols)
    lanes = adj[0].shape[-1]
    mask = face_mask(lanes, nz)
    last = rows - 1

    def at_row(field, y):
        return row_of(field[0], field[1] + y)

    def mirror(s, y):
        return y + s * (last - 2 * y)

    def mu_side(i, _):
        s, k = i // 2, i % 2
        y = mirror(s, k - 1)
        for at, size in chunks(low, high):
            chem_row(at_row(conc, y), set_row(chem[0], chem[1] + y),
                     set_row(curve[0], curve[1] + y), set_row(swing[0], swing[1] + y), at, size,
                     mask)
        return 0

    lax.fori_loop(0, 4, mu_side, 0)

    def side(s, _):
        y = mirror(s, -1)
        for at, size in chunks(low, high):
            span = slice(at, at + size)
            a, _mu, flow, _pair = face_sums(at_row(adj, y), at_row(mob, y), None, at, size, mask)
            pot[1 + y, span, :] = flow - rate[3 * s, span, :] * a
        y0 = mirror(s, 0)
        for at, size in chunks(low, high):
            span = slice(at, at + size)
            a, mu, flow, pair = face_sums(
                at_row(adj, y0), at_row(mob, y0), at_row(chem, y0), at, size, mask
            )
            g = flow - rate[1 + s, span, :] * a
            pot[1 + y0, span, :] = g
            part[s, 0, span, :] = partial(
                a, at_row(swing, y0)(0, span), pair, at_row(curve, y0)(0, span), g
            )
            grad[s, 0, span, :] = gain(a, mu, None)
        y1 = mirror(s, 1)
        for at, size in chunks(low, high):
            span = slice(at, at + size)
            a, mu, _flow, pair = face_sums(at_row(adj, y1), None, at_row(chem, y1), at, size, mask)
            part[s, 1, span, :] = partial(
                a, at_row(swing, y1)(0, span), pair, at_row(curve, y1)(0, span), pot[1 + y1, span, :]
            )
            grad[s, 1, span, :] = gain(a, mu, None)
        return 0

    lax.fori_loop(0, 2, side, 0)

    def close(i, _):
        s, k = i // 2, i % 2
        y = mirror(s, k)
        for at, size in chunks(low, high):
            span = slice(at, at + size)
            _g, lap = laplace(row_of(pot, 1 + y), at, size, mask)
            store(s, k, span, part[s, k, span, :] - grad_energy * lap)
        return 0

    lax.fori_loop(0, 4, close, 0)


def is_odd(axis):
    return lax.rem(lax.axis_index(axis), 2) == 1


def bases(rows):
    odd = is_odd("gy")
    top = rows - depth
    return jnp.where(odd, top, 0), jnp.where(odd, 0, top)


def landings(rows):
    odd = is_odd("gy")
    top = rows + depth
    return jnp.where(odd, top, 0), jnp.where(odd, 0, top)


def sides_of(rows):
    return [(0, 0, 0), (0, 1, 1), (1, 0, rows - 1), (1, 1, rows - 2)]


def edge_kernel(steps, rows, cols, nz, conc_hbm, adj_hbm, rate_hbm, conc_in, adj_in, rate_in,
                main_a, main_b, sems):
    lanes = main_a.shape[1]
    half = cols // 2
    lower = lax.broadcasted_iota(jnp.int32, (half, lanes), 1) < nz
    copies = [
        pltpu.make_async_copy(adj_hbm, adj_in, sems.at[0]),
        pltpu.make_async_copy(rate_hbm, rate_in, sems.at[1]),
    ] + [
        pltpu.make_async_copy(conc_hbm.at[steps - 1 - back], conc_in.at[back], sems.at[2 + back])
        for back in range(steps)
    ]
    for copy in copies:
        copy.start()
    copies[0].wait()
    for side, base in zip((main_a, main_b), bases(rows)):
        for at in range(depth):
            side[pl.ds(at * cols, cols), :] = adj_in[pl.ds(base + at, lanes, stride=rows), :].T
    copies[1].wait()
    for side, base in zip((main_a, main_b), bases(rows)):
        edge = jnp.where(base == 0, 0, rows - 1)
        rate = turned_rate(rate_in, edge, rows, nz, lanes)
        side[pl.ds((1 + early) * depth * cols, half), :] = jnp.where(
            lower, rate[:half], rate[half:]
        )
    for back in range(steps):
        copies[2 + back].wait()
        if back >= early:
            continue
        for side, base in zip((main_a, main_b), bases(rows)):
            for at in range(depth):
                side[pl.ds(((1 + back) * depth + at) * cols, cols), :] = conc_in[
                    back, pl.ds(base + at, lanes, stride=rows), :
                ].T


def turned_rate(rate, y, rows, nz, lanes):
    value = time_step * rate[pl.ds(y, nz, stride=rows), :]
    return jnp.concatenate([value] * (lanes // nz), axis=0).T


def turn_kernel(steps, rows, cols, nz, conc_in, adj_in, rate_in, conc_out, adj_out, rate_out,
                x_a, x_b):
    places, total = slots(steps)
    lanes = adj_out.shape[2]
    odd_x = is_odd("gx")

    def to_x(y, value, place):
        start, width = place
        last, first = value[cols - width :, :], value[:width, :]
        x_a[y, start : start + width, :] = jnp.where(odd_x, last, first)
        x_b[y, start : start + width, :] = jnp.where(odd_x, first, last)

    used = sum(places[-1])
    for y in range(rows):
        adj = adj_in[pl.ds(y, lanes, stride=rows), :].T
        adj_out[y] = adj
        to_x(y, adj, places[0])
        rate = turned_rate(rate_in, y, rows, nz, lanes)
        rate_out[y] = rate
        to_x(y, rate, places[steps + 1])
        if used < total:
            x_a[y, used:, :] = jnp.zeros((total - used, lanes), f32)
            x_b[y, used:, :] = jnp.zeros((total - used, lanes), f32)
        for back in range(steps):
            conc = conc_in[back, pl.ds(y, lanes, stride=rows), :].T
            conc_out[back, y] = conc
            to_x(y, conc, places[1 + back])


def put_own(out, row, value, y, place, cols, x_low, x_high):
    start, width = place
    right = pad + cols
    out[row, pad:right, :] = value
    out[row, pad - width : pad, :] = x_low[y, start : start + width, :]
    out[row, right : right + width, :] = x_high[y, start : start + width, :]


def put_halo(out, row, value, from_row, place, cols, corner):
    start, width = place
    right = pad + cols
    out[row, pad:right, :] = value
    out[row, pad - width : pad, :] = corner[0, from_row, start : start + width, :]
    out[row, right : right + width, :] = corner[1, from_row, start : start + width, :]


def corner_kernel(rows, got_a, got_b, x_low, x_high, corner_a, corner_b):
    odd_x = is_odd("gx")
    x_low[...] = jnp.where(odd_x, got_b[...], got_a[...])
    x_high[...] = jnp.where(odd_x, got_a[...], got_b[...])
    for out, base in zip((corner_a, corner_b), bases(rows)):
        for at in range(depth):
            out[0, at] = x_low[base + at]
            out[1, at] = x_high[base + at]


def first_interior(steps, rows, cols, nz, conc_own, adj_own, rate_own, x_low, x_high,
                   conc, adj, rate, chem, curve, swing, pot, out, grad, ahead, mob, part):
    places, _ = slots(steps)
    low, high = reach(cols)
    lanes = adj.shape[2]
    mask = face_mask(lanes, nz)
    for y in range(rows):
        put_own(conc, y, conc_own[0, y], y, places[1], cols, x_low, x_high)
        put_own(adj, y, adj_own[y], y, places[0], cols, x_low, x_high)
        put_own(rate, y, rate_own[y], y, places[steps + 1], cols, x_low, x_high)
    put_ahead(ahead, conc_own, 1, x_low, x_high, places, rows, cols)

    def mob_row(y, _):
        for at, size in chunks(low - 8, high + 8):
            c = conc[y, at : at + size, :]
            mob[y, at : at + size, :] = mobility(c)
        return 0

    def mu_row(y, _):
        for at, size in chunks(low, high):
            chem_row(row_of(conc, y), set_row(chem, y - 1), set_row(curve, y - 1),
                     set_row(swing, y - 1), at, size, mask)
        return 0

    lax.fori_loop(0, rows, mob_row, 0)
    lax.fori_loop(1, rows - 1, mu_row, 0)

    def store(k, span, value):
        out[k, span, :] = value

    interior(rows, cols, nz, (swing, -1), (mob, 0), (chem, -1), (curve, -1), (adj, 0), (rate, 0),
             pot, part, grad, store)


def copy_rows(pairs):
    for out, to, ref, at in pairs:
        out[to] = ref[at]


def send_rows(out, ahead, rate, to_a, to_b, open_g, cols, nz):
    low, high = reach(cols)
    first, last = sent(cols)
    rows, lanes = rate.shape[0], rate.shape[2]
    mask = face_mask(lanes, nz)
    for s in range(2):
        for at, size in chunks(low, high):
            a, _mu, flow, _pair = face_sums(
                lambda dy, cut: out[s, dy, cut, :], lambda dy, cut: ahead[s, dy, cut, :], None,
                at, size, mask, (1,)
            )
            open_g[s, at - low : at - low + size, :] = (
                flow - rate[s * (rows - 1), at : at + size, :] * a
            )
    odd = is_odd("gy")
    for to, side in ((to_a, jnp.where(odd, 1, 0)), (to_b, jnp.where(odd, 0, 1))):
        to[0] = out[side, 0, first:last, :]
        to[1] = open_g[side, first - low : last - low, :]


def put_ahead(ahead, conc_own, back, x_low, x_high, places, rows, cols):
    for s, k, y in sides_of(rows):
        put_own(ahead.at[s], k, conc_own[back, y], y, places[1 + back], cols, x_low, x_high)
        ahead[s, k] = mobility(ahead[s, k])


def first_boundary(steps, rows, cols, nz, conc_in, adj_in, rate_in, chem_in, curve_in, swing_in,
                   pot_in,
                   from_a, from_b, corner_a, corner_b, ahead,
                   out, grad, to_a, to_b, rate, conc, adj, mob, chem, curve, swing, pot,
                   part, open_g):
    places, _ = slots(steps)
    low, high = reach(cols)
    half = cols // 2
    lanes = conc.shape[2]
    lower = lax.broadcasted_iota(jnp.int32, (half, lanes), 1) < nz

    def unpack(side):
        packed = side[pl.ds((1 + early) * depth * cols, half), :]
        turned = pltpu.roll(packed, lanes // 2, 1)
        return jnp.concatenate(
            [jnp.where(lower, packed, turned), jnp.where(lower, turned, packed)], axis=0
        )

    near = [0, 1, 2, rows - 3, rows - 2, rows - 1]
    for y in near:
        conc[depth + y] = conc_in[y]
        adj[depth + y] = adj_in[y]
    for y in (1, 2, rows - 3, rows - 2):
        chem[1 + y] = chem_in[y - 1]
        pot[1 + y] = pot_in[y - 1]
    for y in (1, rows - 2):
        curve[1 + y] = curve_in[y - 1]
        swing[1 + y] = swing_in[y - 1]
    rate[1] = rate_in[0]
    rate[2] = rate_in[rows - 1]
    for halo, corner, base in zip((from_a, from_b), (corner_a, corner_b), landings(rows)):
        for at in range(depth):
            for ref, place, first in ((adj, places[0], 0), (conc, places[1], depth)):
                span = pl.ds((first + at) * cols, cols)
                put_halo(ref, base + at, halo[span, :], at, place, cols, corner)
        below = base == 0
        put_halo(rate, jnp.where(below, 0, 3), unpack(halo), jnp.where(below, depth - 1, 0),
                 places[steps + 1], cols, corner)
    for row in [0, 1, 2, 3, rows, rows + 1, rows + 2, rows + 3]:
        for at, size in chunks(low - 8, high + 8):
            c = conc[row, at : at + size, :]
            mob[row, at : at + size, :] = mobility(c)

    def store(s, k, span, value):
        out[s, k, span, :] = value

    boundary(rows, cols, nz, (conc, depth), (mob, depth), (chem, 1), (curve, 1), (swing, 1),
             (adj, depth), rate, pot, part, grad, store)
    send_rows(out, ahead, rate_in, to_a, to_b, open_g, cols, nz)


def prepare_kernel(steps, rows, cols, nz, back, conc_own, from_a, from_b, x_low, x_high,
                   corner_a, corner_b, mob, chem, curve, swing, *rest):
    *more, conc = rest
    places, _ = slots(steps)
    low, high = reach(cols)
    lanes = conc.shape[2]
    mask = face_mask(lanes, nz)
    place = places[1 + back]
    for y in range(rows):
        put_own(conc, depth + y, conc_own[back, y], y, place, cols, x_low, x_high)
    for halo, corner, base in zip((from_a, from_b), (corner_a, corner_b), landings(rows)):
        for at in range(depth):
            first = (1 + back) * depth if back < early else (back - early) * depth
            span = pl.ds((first + at) * cols, cols)
            put_halo(conc, base + at, halo[span, :], at, place, cols, corner)

    if more:
        ahead, late_a, late_b = more
        put_ahead(ahead, conc_own, back + 1, x_low, x_high, places, rows, cols)
        for side, base in zip((late_a, late_b), bases(rows)):
            for after in range(early, steps):
                for at in range(depth):
                    span = pl.ds(((after - early) * depth + at) * cols, cols)
                    side[span, :] = conc_own[after, base + at]
            used = (steps - early) * depth * cols
            side[used:, :] = jnp.zeros((side.shape[0] - used, lanes), f32)

    def mob_row(row, _):
        for at, size in chunks(low - 8, high + 8):
            c = conc[row, at : at + size, :]
            mob[row, at : at + size, :] = mobility(c)
        return 0

    def mu_row(row, _):
        for at, size in chunks(low, high):
            chem_row(row_of(conc, row + 1), set_row(chem, row), set_row(curve, row),
                     set_row(swing, row), at, size, mask)
        return 0

    lax.fori_loop(0, rows + 2 * depth, mob_row, 0)
    lax.fori_loop(0, rows + 2, mu_row, 0)


def next_interior(rows, cols, nz, final, mob, chem, curve, swing, rate, inner, outer, *rest):
    if final:
        before, out, tiles, grad_out, adj, pot, part, grad = rest
    elif len(rest) == 8:
        inner_grad, outer_grad, out, grad, adj, pot, part, before = rest
        for k in range(rows - 2 * depth):
            before[depth + k] = inner_grad[k]
        for s, k, y in sides_of(rows):
            before[y] = outer_grad[s, k]
    else:
        before, out, grad, adj, pot, part = rest
    low, high = reach(cols)
    lanes = adj.shape[2]
    mask = face_mask(lanes, nz)
    skip = (inner.shape[0] - (rows - 2 * depth)) // 2
    for k in range(rows - 2 * depth):
        adj[1 + depth + k] = inner[skip + k]
    for s, k, y in sides_of(rows):
        adj[1 + y] = outer[s, k]
    adj[0] = outer[0, 0]
    adj[1 + rows] = outer[1, 0]
    pot[0] = jnp.zeros(pot.shape[1:], f32)
    pot[1 + rows] = jnp.zeros(pot.shape[1:], f32)

    def body(y, _):
        for at, size in chunks(low, high):
            span = slice(at, at + size)
            a, mu, flow, pair = face_sums(
                row_of(adj, y + 1), row_of(mob, y + depth), row_of(chem, y + 1), at, size, mask
            )
            g = flow - rate[y, span, :] * a
            pot[y + 1, span, :] = g
            part[y, span, :] = partial(
                a, swing[y + 1, span, :], pair, curve[y + 1, span, :], g
            )
            grad[y, span, :] = gain(a, mu, before[y, span, :])
        return 0

    def close(y, _):
        for at, size in chunks(low, high):
            span = slice(at, at + size)
            _g, lap = laplace(row_of(pot, y + 1), at, size, mask)
            out[y, span, :] = part[y, span, :] - grad_energy * lap
        return 0

    lax.fori_loop(0, rows, body, 0)
    lax.fori_loop(0, rows, close, 0)
    if final:
        for y in range(rows):
            grad_out[pl.ds(y, nz, stride=rows), :] = fold(grad[y, pad : pad + cols, :].T, nz)
        for y in range(depth, rows - depth):
            tiles[pl.ds(y, lanes, stride=rows), :] = out[y, pad : pad + cols, :].T


def fold(value, nz):
    total = value[:nz]
    for frame in range(1, value.shape[0] // nz):
        total = total + value[frame * nz : (frame + 1) * nz]
    return total


def next_boundary(rows, cols, nz, final, mob, chem, curve, swing, inside, outer, from_a, from_b,
                  *rest):
    if final:
        tiles, out, halo, delta, result = rest
    else:
        ahead, rate, result, to_a, to_b, halo, delta, open_g = rest
    low, high = reach(cols)
    first, last = sent(cols)
    lanes = mob.shape[2]
    mask = face_mask(lanes, nz)
    odd = is_odd("gy")
    for got, side in ((from_a, jnp.where(odd, 1, 0)), (from_b, jnp.where(odd, 0, 1))):
        for k in range(2):
            halo[side, k, first:last, :] = got[k]
    for s in range(2):
        y, beyond = s * (rows - 1), s * (rows + 1) - 1
        for at, size in chunks(low, high):
            span = slice(at, at + size)
            diff = halo[s, 0, span, :] - outer[s, 0, span, :]
            both = mob[depth + beyond, span, :] + mob[depth + y, span, :]
            delta[s, span, :] = both * diff
        for at, size in chunks(low, high):
            span = slice(at, at + size)
            more = delta[s, span, :]
            diff = halo[s, 0, span, :] - outer[s, 0, span, :]
            pair = (chem[1 + beyond, span, :] - chem[1 + y, span, :]) * diff
            step_z = (up(more) - more) * mask
            lap = (
                (delta[s, at + 1 : at + size + 1, :] + delta[s, at - 1 : at + size - 1, :])
                + (halo[s, 1, span, :] - more)
                - 4.0 * more
                + (step_z - down(step_z))
            )
            result[s, 0, span, :] = (
                inside[y, span, :]
                + (swing[1 + y, span, :] * pair + curve[1 + y, span, :] * more)
                - grad_energy * lap
            )
            result[s, 1, span, :] = inside[1 + s * (rows - 3), span, :] - grad_energy * more
    if final:
        out[...] = tiles[...]
        for s, k, y in sides_of(rows):
            out[pl.ds(y, lanes, stride=rows), :] = result[s, k, pad : pad + cols, :].T
    else:
        send_rows(result, ahead, rate, to_a, to_b, open_g, cols, nz)


def call(kernel, outs, scratch, *operands, cost=0, far=False):
    if far:
        operands = [pltpu.with_memory_space_constraint(value, pltpu.HBM) for value in operands]
    space = pl.ANY if far else pltpu.VMEM
    return pl.pallas_call(
        kernel,
        out_shape=[jax.ShapeDtypeStruct(shape, f32) for shape in outs],
        in_specs=[pl.BlockSpec(memory_space=space)] * len(operands),
        out_specs=[pl.BlockSpec(memory_space=pltpu.VMEM)] * len(outs),
        scratch_shapes=[pltpu.VMEM(s, f32) if isinstance(s, tuple) else s for s in scratch],
        compiler_params=pltpu.CompilerParams(vmem_limit_bytes=vmem_limit),
        cost_estimate=pl.CostEstimate(
            flops=cost * 1_000_000, bytes_accessed=cost * 2_000_000, transcendentals=0
        ),
    )(*operands)


def swap(value_a, value_b, axis):
    count = lax.axis_size(axis)
    pairs_a = [(i, (i - 1 + 2 * (i % 2)) % count) for i in range(count)]
    pairs_b = [(i, i + 1 - 2 * (i % 2)) for i in range(count)]
    return lax.ppermute(value_a, axis, pairs_a), lax.ppermute(value_b, axis, pairs_b)


def shards(saved_conc, adjoint_end, rate_field):
    steps, frames, nz, rows, cols = saved_conc.shape
    lanes = frames * nz
    _, total = slots(steps)
    width = cols + 2 * pad
    flat = lanes * rows
    inside = rows - 2 * depth

    def field(count):
        return (count, width, lanes)

    both = (2, depth, width, lanes)
    edge = (2, cols + 8, lanes)
    open_g = (2, cols + 16, lanes)
    raw = [(steps, flat, cols), (flat, cols), (nz * rows, cols)]
    conc_raw, adj_raw, rate_raw, main_a, main_b = call(
        functools.partial(edge_kernel, steps, rows, cols, nz),
        raw + [((1 + early) * depth * cols + cols // 2, lanes)] * 2,
        [pltpu.SemaphoreType.DMA((2 + steps,))],
        saved_conc.reshape(raw[0]), adjoint_end.reshape(raw[1]), rate_field.reshape(raw[2]),
        cost=2,
        far=True,
    )
    main_a, main_b = swap(main_a, main_b, "gy")
    conc_own, adj_own, rate_own, x_a, x_b = call(
        functools.partial(turn_kernel, steps, rows, cols, nz),
        [(steps, rows, cols, lanes), (rows, cols, lanes), (rows, cols, lanes)]
        + [(rows, total, lanes)] * 2,
        [],
        conc_raw, adj_raw, rate_raw,
        cost=1,
    )
    x_a, x_b = swap(x_a, x_b, "gx")
    x_low, x_high, corner_a, corner_b = call(
        functools.partial(corner_kernel, rows),
        [(rows, total, lanes)] * 2 + [(2, depth, total, lanes)] * 2,
        [],
        x_a, x_b,
    )
    corner_a, corner_b = swap(corner_a, corner_b, "gy")

    conc, adj, rate, chem, curve, swing, pot, inner, inner_grad, ahead = call(
        functools.partial(first_interior, steps, rows, cols, nz),
        [field(rows)] * 3 + [field(rows - 2)] * 4 + [field(inside)] * 2 + [both],
        [field(rows), field(inside)],
        conc_own, adj_own, rate_own, x_low, x_high,
        cost=3,
    )
    outer, outer_grad, to_a, to_b = call(
        functools.partial(first_boundary, steps, rows, cols, nz),
        [both, both, edge, edge],
        [field(4)] + [field(rows + 2 * depth)] * 3 + [field(rows + 2)] * 4 + [both, open_g],
        conc, adj, rate, chem, curve, swing, pot, main_a, main_b, corner_a, corner_b, ahead,
        cost=2,
    )
    before = (inner_grad, outer_grad)
    got = main_a, main_b
    late = (max((steps - early) * depth * cols, 2 * (cols + 8) + 8), lanes)
    for back in range(1, steps):
        adj_a, adj_b = swap(to_a, to_b, "gy")
        final = back == steps - 1
        fields = call(
            functools.partial(prepare_kernel, steps, rows, cols, nz, back),
            [field(rows + 2 * depth)] + [field(rows + 2)] * 3
            + ([] if final else [both, late, late]),
            [field(rows + 2 * depth)],
            conc_own, *got, x_low, x_high, corner_a, corner_b,
            cost=2,
        )
        fields, ahead, more = fields[:4], fields[4:5], fields[5:]
        if not final:
            got = swap(*more, "gy")
        work = [field(rows + 2)] * 2 + [field(rows)]
        if final:
            rows_in, tiles, grad = call(
                functools.partial(next_interior, rows, cols, nz, final),
                [field(rows), (flat, cols), (nz * rows, cols)],
                work + [field(rows)],
                *fields, rate, inner, outer, *before,
                cost=3,
            )
            (adj,) = call(
                functools.partial(next_boundary, rows, cols, nz, final),
                [(flat, cols)],
                [both, field(2), both],
                *fields, rows_in, outer, adj_a, adj_b, tiles,
                cost=1,
            )
        else:
            rows_in, grad = call(
                functools.partial(next_interior, rows, cols, nz, final),
                [field(rows)] * 2,
                work + ([field(rows)] if len(before) == 2 else []),
                *fields, rate, inner, outer, *before,
                cost=3,
            )
            outer, to_a, to_b = call(
                functools.partial(next_boundary, rows, cols, nz, final),
                [both, edge, edge],
                [both, field(2), open_g],
                *fields, rows_in, outer, adj_a, adj_b, *ahead, rate,
                cost=1,
            )
            inner, before = rows_in, (grad,)
    return adj.reshape(adjoint_end.shape), grad.reshape(rate_field.shape)


def solution(mesh):
    return jax.shard_map(
        shards,
        mesh=mesh,
        in_specs=(P(None, None, None, "gy", "gx"), P(None, None, "gy", "gx"), P(None, "gy", "gx")),
        out_specs=(P(None, None, "gy", "gx"), P(None, "gy", "gx")),
        check_vma=False,
    )
```

```python
import functools

import jax
import jax.numpy as jnp
from jax import lax
from jax.experimental import pallas as pl
from jax.experimental.pallas import tpu as pltpu
from jax.sharding import PartitionSpec as P

mix_energy = 2.5
grad_energy = 1.0
time_step = 0.1
diff_step = 0.03
bath_potential = 0.5

pad = 16
chunk = 72
depth = 2
first_pair = {"gx": 0, "gy": 1}
vmem_limit = 20 * 1024 * 1024
f32 = jnp.float32


def slots(steps):
    widths = [2 * steps] + [2 * steps - 2 * back for back in range(steps)] + [2 * steps - 1]
    starts = [sum(widths[:i]) for i in range(len(widths))]
    total = -(-sum(widths) // 8) * 8
    return list(zip(starts, widths)), total


def chunks(low, high):
    return [(at, min(chunk, high - at)) for at in range(low, high, chunk)]


def reach(cols):
    return pad - 8, pad + cols + 8


def sent(cols):
    return pad - 4, pad + cols + 4


def up(value):
    return pltpu.roll(value, value.shape[1] - 1, 1)


def down(value):
    return pltpu.roll(value, 1, 1)


def face_mask(lanes, nz):
    lane = lax.broadcasted_iota(jnp.int32, (1, lanes), 1)
    return jnp.where(lane % nz == nz - 1, 0.0, 1.0).astype(f32)


def row_of(ref, y):
    return lambda dy, cut: ref[y + dy, cut, :]


def laplace(field, at, size, mask):
    span = slice(at, at + size)
    here = field(0, span)
    step_z = (up(here) - here) * mask
    sides = field(0, slice(at + 1, at + size + 1)) + field(0, slice(at - 1, at + size - 1))
    return here, (
        (sides + (field(-1, span) + field(1, span))) - 4.0 * here + (step_z - down(step_z))
    )


def mobility(c):
    return (0.5 * diff_step) * c * (1.0 - c)


def chem_row(conc, chem, curve, swing, at, size, mask):
    c, lap = laplace(conc, at, size, mask)
    inv = 1.0 / (c * (1.0 - c))
    span = slice(at, at + size)
    chem(
        span,
        time_step * (jnp.log(c * c * inv) - grad_energy * lap)
        + (time_step * (mix_energy - bath_potential) - (2.0 * time_step * mix_energy) * c),
    )
    curve(span, inv - 2.0 * mix_energy)
    swing(span, c * (diff_step / time_step) - 0.5 * diff_step / time_step)


def face_sums(adj, mob, chem, at, size, mask, across=(1, -1)):
    span = slice(at, at + size)
    a = adj(0, span)
    m = None if mob is None else mob(0, span)
    mu = None if chem is None else chem(0, span)
    flow = pair = None
    for dy, cut in (
        (0, slice(at + 1, at + size + 1)),
        (0, slice(at - 1, at + size - 1)),
    ) + tuple((dy, span) for dy in across):
        diff = adj(dy, cut) - a
        if mob is not None:
            term = (mob(dy, cut) + m) * diff
            flow = term if flow is None else flow + term
        if chem is not None:
            term = (chem(dy, cut) - mu) * diff
            pair = term if pair is None else pair + term
    diff = (up(a) - a) * mask
    if mob is not None:
        term = (up(m) + m) * diff
        flow = flow + (term - down(term))
    if chem is not None:
        term = (up(mu) - mu) * diff
        pair = pair + (term + down(term))
    return a, mu, flow, pair


def partial(a, swing, pair, curve, g):
    return a + swing * pair + curve * g


def gain(a, chem, before):
    value = a * chem
    return -value if before is None else before - value


def set_row(ref, y):
    def put(span, value):
        ref[y, span, :] = value

    return put


def interior(rows, cols, nz, swing, mob, chem, curve, adj, rate, pot, part, grad, store):
    low, high = reach(cols)
    lanes = adj[0].shape[-1]
    mask = face_mask(lanes, nz)

    def at_row(field, y):
        return row_of(field[0], field[1] + y)

    def body(y, _):
        for at, size in chunks(low, high):
            span = slice(at, at + size)
            a, mu, flow, pair = face_sums(
                at_row(adj, y), at_row(mob, y), at_row(chem, y), at, size, mask
            )
            g = flow - at_row(rate, y)(0, span) * a
            pot[y - 1, span, :] = g
            part[y - depth, span, :] = partial(
                a, at_row(swing, y)(0, span), pair, at_row(curve, y)(0, span), g
            )
            grad[y - depth, span, :] = gain(a, mu, None)
        return 0

    def edge(i, _):
        y = 1 + i * (rows - 3)
        for at, size in chunks(low, high):
            a, _mu, flow, _pair = face_sums(at_row(adj, y), at_row(mob, y), None, at, size, mask)
            span = slice(at, at + size)
            pot[y - 1, span, :] = flow - at_row(rate, y)(0, span) * a
        return 0

    def close(y, _):
        for at, size in chunks(low, high):
            span = slice(at, at + size)
            _g, lap = laplace(row_of(pot, y - 1), at, size, mask)
            store(y - depth, span, part[y - depth, span, :] - grad_energy * lap)
        return 0

    lax.fori_loop(depth, rows - depth, body, 0)
    lax.fori_loop(0, 2, edge, 0)
    lax.fori_loop(depth, rows - depth, close, 0)


def boundary(rows, cols, nz, conc, mob, chem, curve, swing, adj, rate, pot, part, grad, store):
    low, high = reach(cols)
    lanes = adj[0].shape[-1]
    mask = face_mask(lanes, nz)
    last = rows - 1

    def at_row(field, y):
        return row_of(field[0], field[1] + y)

    def mirror(s, y):
        return y + s * (last - 2 * y)

    def mu_side(i, _):
        s, k = i // 2, i % 2
        y = mirror(s, k - 1)
        for at, size in chunks(low, high):
            chem_row(at_row(conc, y), set_row(chem[0], chem[1] + y),
                     set_row(curve[0], curve[1] + y), set_row(swing[0], swing[1] + y), at, size,
                     mask)
        return 0

    lax.fori_loop(0, 4, mu_side, 0)

    def side(s, _):
        y = mirror(s, -1)
        for at, size in chunks(low, high):
            span = slice(at, at + size)
            a, _mu, flow, _pair = face_sums(at_row(adj, y), at_row(mob, y), None, at, size, mask)
            pot[1 + y, span, :] = flow - rate[3 * s, span, :] * a
        y0 = mirror(s, 0)
        for at, size in chunks(low, high):
            span = slice(at, at + size)
            a, mu, flow, pair = face_sums(
                at_row(adj, y0), at_row(mob, y0), at_row(chem, y0), at, size, mask
            )
            g = flow - rate[1 + s, span, :] * a
            pot[1 + y0, span, :] = g
            part[s, 0, span, :] = partial(
                a, at_row(swing, y0)(0, span), pair, at_row(curve, y0)(0, span), g
            )
            grad[s, 0, span, :] = gain(a, mu, None)
        y1 = mirror(s, 1)
        for at, size in chunks(low, high):
            span = slice(at, at + size)
            a, mu, _flow, pair = face_sums(at_row(adj, y1), None, at_row(chem, y1), at, size, mask)
            part[s, 1, span, :] = partial(
                a, at_row(swing, y1)(0, span), pair, at_row(curve, y1)(0, span), pot[1 + y1, span, :]
            )
            grad[s, 1, span, :] = gain(a, mu, None)
        return 0

    lax.fori_loop(0, 2, side, 0)

    def close(i, _):
        s, k = i // 2, i % 2
        y = mirror(s, k)
        for at, size in chunks(low, high):
            span = slice(at, at + size)
            _g, lap = laplace(row_of(pot, 1 + y), at, size, mask)
            store(s, k, span, part[s, k, span, :] - grad_energy * lap)
        return 0

    lax.fori_loop(0, 4, close, 0)


def a_is_next(axis):
    return lax.rem(lax.axis_index(axis), 2) == first_pair[axis]


def bases(rows):
    to_next = a_is_next("gy")
    top = rows - depth
    return jnp.where(to_next, top, 0), jnp.where(to_next, 0, top)


def landings(rows):
    to_next = a_is_next("gy")
    top = rows + depth
    return jnp.where(to_next, top, 0), jnp.where(to_next, 0, top)


def sides_of(rows):
    return [(0, 0, 0), (0, 1, 1), (1, 0, rows - 1), (1, 1, rows - 2)]


def edge_kernel(steps, rows, cols, nz, conc_hbm, adj_hbm, rate_hbm, conc_in, adj_in, rate_in,
                main_a, main_b, sems):
    lanes = main_a.shape[1]
    half = cols // 2
    lower = lax.broadcasted_iota(jnp.int32, (half, lanes), 1) < nz
    copies = [
        pltpu.make_async_copy(adj_hbm, adj_in, sems.at[0]),
        pltpu.make_async_copy(rate_hbm, rate_in, sems.at[1]),
    ] + [
        pltpu.make_async_copy(conc_hbm.at[steps - 1 - back], conc_in.at[back], sems.at[2 + back])
        for back in range(steps)
    ]
    for copy in copies:
        copy.start()
    copies[0].wait()
    for side, base in zip((main_a, main_b), bases(rows)):
        for at in range(depth):
            side[pl.ds(at * cols, cols), :] = adj_in[pl.ds(base + at, lanes, stride=rows), :].T
    copies[1].wait()
    for side, base in zip((main_a, main_b), bases(rows)):
        edge = jnp.where(base == 0, 0, rows - 1)
        rate = turned_rate(rate_in, edge, rows, nz, lanes)
        side[pl.ds((1 + steps) * depth * cols, half), :] = jnp.where(
            lower, rate[:half], rate[half:]
        )
    for back in range(steps):
        copies[2 + back].wait()
        for side, base in zip((main_a, main_b), bases(rows)):
            for at in range(depth):
                side[pl.ds(((1 + back) * depth + at) * cols, cols), :] = conc_in[
                    back, pl.ds(base + at, lanes, stride=rows), :
                ].T


def turned_rate(rate, y, rows, nz, lanes):
    value = time_step * rate[pl.ds(y, nz, stride=rows), :]
    return jnp.concatenate([value] * (lanes // nz), axis=0).T


def turn_kernel(steps, rows, cols, nz, conc_in, adj_in, rate_in, conc_out, adj_out, rate_out,
                x_a, x_b):
    places, total = slots(steps)
    lanes = adj_out.shape[2]
    next_x = a_is_next("gx")

    def to_x(y, value, place):
        start, width = place
        last, first = value[cols - width :, :], value[:width, :]
        x_a[y, start : start + width, :] = jnp.where(next_x, last, first)
        x_b[y, start : start + width, :] = jnp.where(next_x, first, last)

    used = sum(places[-1])
    for y in range(rows):
        adj = adj_in[pl.ds(y, lanes, stride=rows), :].T
        adj_out[y] = adj
        to_x(y, adj, places[0])
        rate = turned_rate(rate_in, y, rows, nz, lanes)
        rate_out[y] = rate
        to_x(y, rate, places[steps + 1])
        if used < total:
            x_a[y, used:, :] = jnp.zeros((total - used, lanes), f32)
            x_b[y, used:, :] = jnp.zeros((total - used, lanes), f32)
        for back in range(steps):
            conc = conc_in[back, pl.ds(y, lanes, stride=rows), :].T
            conc_out[back, y] = conc
            to_x(y, conc, places[1 + back])


def put_own(out, row, value, y, place, cols, x_low, x_high):
    start, width = place
    right = pad + cols
    out[row, pad:right, :] = value
    out[row, pad - width : pad, :] = x_low[y, start : start + width, :]
    out[row, right : right + width, :] = x_high[y, start : start + width, :]


def put_halo(out, row, value, from_row, place, cols, corner):
    start, width = place
    right = pad + cols
    out[row, pad:right, :] = value
    out[row, pad - width : pad, :] = corner[0, from_row, start : start + width, :]
    out[row, right : right + width, :] = corner[1, from_row, start : start + width, :]


def corner_kernel(rows, got_a, got_b, x_low, x_high, corner_a, corner_b):
    next_x = a_is_next("gx")
    x_low[...] = jnp.where(next_x, got_b[...], got_a[...])
    x_high[...] = jnp.where(next_x, got_a[...], got_b[...])
    for out, base in zip((corner_a, corner_b), bases(rows)):
        for at in range(depth):
            out[0, at] = x_low[base + at]
            out[1, at] = x_high[base + at]


def first_interior(steps, rows, cols, nz, conc_own, adj_own, rate_own, x_low, x_high,
                   conc, adj, rate, chem, curve, swing, pot, out, grad, ahead, mob, part):
    places, _ = slots(steps)
    low, high = reach(cols)
    lanes = adj.shape[2]
    mask = face_mask(lanes, nz)
    for y in range(rows):
        put_own(conc, y, conc_own[0, y], y, places[1], cols, x_low, x_high)
        put_own(adj, y, adj_own[y], y, places[0], cols, x_low, x_high)
        put_own(rate, y, rate_own[y], y, places[steps + 1], cols, x_low, x_high)
    put_ahead(ahead, conc_own, 1, x_low, x_high, places, rows, cols)

    def mob_row(y, _):
        for at, size in chunks(low - 8, high + 8):
            c = conc[y, at : at + size, :]
            mob[y, at : at + size, :] = mobility(c)
        return 0

    def mu_row(y, _):
        for at, size in chunks(low, high):
            chem_row(row_of(conc, y), set_row(chem, y - 1), set_row(curve, y - 1),
                     set_row(swing, y - 1), at, size, mask)
        return 0

    lax.fori_loop(0, rows, mob_row, 0)
    lax.fori_loop(1, rows - 1, mu_row, 0)

    def store(k, span, value):
        out[k, span, :] = value

    interior(rows, cols, nz, (swing, -1), (mob, 0), (chem, -1), (curve, -1), (adj, 0), (rate, 0),
             pot, part, grad, store)


def copy_rows(pairs):
    for out, to, ref, at in pairs:
        out[to] = ref[at]


def send_rows(out, ahead, rate, to_a, to_b, open_g, cols, nz):
    low, high = reach(cols)
    first, last = sent(cols)
    rows, lanes = rate.shape[0], rate.shape[2]
    mask = face_mask(lanes, nz)
    for s in range(2):
        for at, size in chunks(low, high):
            a, _mu, flow, _pair = face_sums(
                lambda dy, cut: out[s, dy, cut, :], lambda dy, cut: ahead[s, dy, cut, :], None,
                at, size, mask, (1,)
            )
            open_g[s, at - low : at - low + size, :] = (
                flow - rate[s * (rows - 1), at : at + size, :] * a
            )
    to_next = a_is_next("gy")
    for to, side in ((to_a, jnp.where(to_next, 1, 0)), (to_b, jnp.where(to_next, 0, 1))):
        to[0] = out[side, 0, first:last, :]
        to[1] = open_g[side, first - low : last - low, :]


def put_ahead(ahead, conc_own, back, x_low, x_high, places, rows, cols):
    for s, k, y in sides_of(rows):
        put_own(ahead.at[s], k, conc_own[back, y], y, places[1 + back], cols, x_low, x_high)
        ahead[s, k] = mobility(ahead[s, k])


def first_boundary(steps, rows, cols, nz, conc_in, adj_in, rate_in, chem_in, curve_in, swing_in,
                   pot_in,
                   from_a, from_b, corner_a, corner_b, ahead,
                   out, grad, to_a, to_b, rate, conc, adj, mob, chem, curve, swing, pot,
                   part, open_g):
    places, _ = slots(steps)
    low, high = reach(cols)
    half = cols // 2
    lanes = conc.shape[2]
    lower = lax.broadcasted_iota(jnp.int32, (half, lanes), 1) < nz

    def unpack(side):
        packed = side[pl.ds((1 + steps) * depth * cols, half), :]
        turned = pltpu.roll(packed, lanes // 2, 1)
        return jnp.concatenate(
            [jnp.where(lower, packed, turned), jnp.where(lower, turned, packed)], axis=0
        )

    near = [0, 1, 2, rows - 3, rows - 2, rows - 1]
    for y in near:
        conc[depth + y] = conc_in[y]
        adj[depth + y] = adj_in[y]
    for y in (1, 2, rows - 3, rows - 2):
        chem[1 + y] = chem_in[y - 1]
        pot[1 + y] = pot_in[y - 1]
    for y in (1, rows - 2):
        curve[1 + y] = curve_in[y - 1]
        swing[1 + y] = swing_in[y - 1]
    rate[1] = rate_in[0]
    rate[2] = rate_in[rows - 1]
    for halo, corner, base in zip((from_a, from_b), (corner_a, corner_b), landings(rows)):
        for at in range(depth):
            for ref, place, first in ((adj, places[0], 0), (conc, places[1], depth)):
                span = pl.ds((first + at) * cols, cols)
                put_halo(ref, base + at, halo[span, :], at, place, cols, corner)
        below = base == 0
        put_halo(rate, jnp.where(below, 0, 3), unpack(halo), jnp.where(below, depth - 1, 0),
                 places[steps + 1], cols, corner)
    for row in [0, 1, 2, 3, rows, rows + 1, rows + 2, rows + 3]:
        for at, size in chunks(low - 8, high + 8):
            c = conc[row, at : at + size, :]
            mob[row, at : at + size, :] = mobility(c)

    def store(s, k, span, value):
        out[s, k, span, :] = value

    boundary(rows, cols, nz, (conc, depth), (mob, depth), (chem, 1), (curve, 1), (swing, 1),
             (adj, depth), rate, pot, part, grad, store)
    send_rows(out, ahead, rate_in, to_a, to_b, open_g, cols, nz)


def prepare_kernel(steps, rows, cols, nz, back, conc_own, from_a, from_b, x_low, x_high,
                   corner_a, corner_b, mob, chem, curve, swing, *rest):
    *ahead, conc = rest
    places, _ = slots(steps)
    low, high = reach(cols)
    lanes = conc.shape[2]
    mask = face_mask(lanes, nz)
    place = places[1 + back]
    for y in range(rows):
        put_own(conc, depth + y, conc_own[back, y], y, place, cols, x_low, x_high)
    for halo, corner, base in zip((from_a, from_b), (corner_a, corner_b), landings(rows)):
        for at in range(depth):
            span = pl.ds(((1 + back) * depth + at) * cols, cols)
            put_halo(conc, base + at, halo[span, :], at, place, cols, corner)

    if ahead:
        put_ahead(ahead[0], conc_own, back + 1, x_low, x_high, places, rows, cols)

    def mob_row(row, _):
        for at, size in chunks(low - 8, high + 8):
            c = conc[row, at : at + size, :]
            mob[row, at : at + size, :] = mobility(c)
        return 0

    def mu_row(row, _):
        for at, size in chunks(low, high):
            chem_row(row_of(conc, row + 1), set_row(chem, row), set_row(curve, row),
                     set_row(swing, row), at, size, mask)
        return 0

    lax.fori_loop(0, rows + 2 * depth, mob_row, 0)
    lax.fori_loop(0, rows + 2, mu_row, 0)


def next_interior(rows, cols, nz, final, mob, chem, curve, swing, rate, inner, outer, *rest):
    if final:
        before, out, tiles, grad_out, adj, pot, part, grad = rest
    elif len(rest) == 8:
        inner_grad, outer_grad, out, grad, adj, pot, part, before = rest
        for k in range(rows - 2 * depth):
            before[depth + k] = inner_grad[k]
        for s, k, y in sides_of(rows):
            before[y] = outer_grad[s, k]
    else:
        before, out, grad, adj, pot, part = rest
    low, high = reach(cols)
    lanes = adj.shape[2]
    mask = face_mask(lanes, nz)
    skip = (inner.shape[0] - (rows - 2 * depth)) // 2
    for k in range(rows - 2 * depth):
        adj[1 + depth + k] = inner[skip + k]
    for s, k, y in sides_of(rows):
        adj[1 + y] = outer[s, k]
    adj[0] = outer[0, 0]
    adj[1 + rows] = outer[1, 0]
    pot[0] = jnp.zeros(pot.shape[1:], f32)
    pot[1 + rows] = jnp.zeros(pot.shape[1:], f32)

    def body(y, _):
        for at, size in chunks(low, high):
            span = slice(at, at + size)
            a, mu, flow, pair = face_sums(
                row_of(adj, y + 1), row_of(mob, y + depth), row_of(chem, y + 1), at, size, mask
            )
            g = flow - rate[y, span, :] * a
            pot[y + 1, span, :] = g
            part[y, span, :] = partial(
                a, swing[y + 1, span, :], pair, curve[y + 1, span, :], g
            )
            grad[y, span, :] = gain(a, mu, before[y, span, :])
        return 0

    def close(y, _):
        for at, size in chunks(low, high):
            span = slice(at, at + size)
            _g, lap = laplace(row_of(pot, y + 1), at, size, mask)
            out[y, span, :] = part[y, span, :] - grad_energy * lap
        return 0

    lax.fori_loop(0, rows, body, 0)
    lax.fori_loop(0, rows, close, 0)
    if final:
        for y in range(rows):
            grad_out[pl.ds(y, nz, stride=rows), :] = fold(grad[y, pad : pad + cols, :].T, nz)
        for y in range(depth, rows - depth):
            tiles[pl.ds(y, lanes, stride=rows), :] = out[y, pad : pad + cols, :].T


def fold(value, nz):
    total = value[:nz]
    for frame in range(1, value.shape[0] // nz):
        total = total + value[frame * nz : (frame + 1) * nz]
    return total


def next_boundary(rows, cols, nz, final, mob, chem, curve, swing, inside, outer, from_a, from_b,
                  *rest):
    if final:
        tiles, out, halo, delta, result = rest
    else:
        ahead, rate, result, to_a, to_b, halo, delta, open_g = rest
    low, high = reach(cols)
    first, last = sent(cols)
    lanes = mob.shape[2]
    mask = face_mask(lanes, nz)
    to_next = a_is_next("gy")
    for got, side in ((from_a, jnp.where(to_next, 1, 0)), (from_b, jnp.where(to_next, 0, 1))):
        for k in range(2):
            halo[side, k, first:last, :] = got[k]
    for s in range(2):
        y, beyond = s * (rows - 1), s * (rows + 1) - 1
        for at, size in chunks(low, high):
            span = slice(at, at + size)
            diff = halo[s, 0, span, :] - outer[s, 0, span, :]
            both = mob[depth + beyond, span, :] + mob[depth + y, span, :]
            delta[s, span, :] = both * diff
        for at, size in chunks(low, high):
            span = slice(at, at + size)
            more = delta[s, span, :]
            diff = halo[s, 0, span, :] - outer[s, 0, span, :]
            pair = (chem[1 + beyond, span, :] - chem[1 + y, span, :]) * diff
            step_z = (up(more) - more) * mask
            lap = (
                (delta[s, at + 1 : at + size + 1, :] + delta[s, at - 1 : at + size - 1, :])
                + (halo[s, 1, span, :] - more)
                - 4.0 * more
                + (step_z - down(step_z))
            )
            result[s, 0, span, :] = (
                inside[y, span, :]
                + (swing[1 + y, span, :] * pair + curve[1 + y, span, :] * more)
                - grad_energy * lap
            )
            result[s, 1, span, :] = inside[1 + s * (rows - 3), span, :] - grad_energy * more
    if final:
        out[...] = tiles[...]
        for s, k, y in sides_of(rows):
            out[pl.ds(y, lanes, stride=rows), :] = result[s, k, pad : pad + cols, :].T
    else:
        send_rows(result, ahead, rate, to_a, to_b, open_g, cols, nz)


def call(kernel, outs, scratch, *operands, cost=0, far=False):
    if far:
        operands = [pltpu.with_memory_space_constraint(value, pltpu.HBM) for value in operands]
    space = pl.ANY if far else pltpu.VMEM
    return pl.pallas_call(
        kernel,
        out_shape=[jax.ShapeDtypeStruct(shape, f32) for shape in outs],
        in_specs=[pl.BlockSpec(memory_space=space)] * len(operands),
        out_specs=[pl.BlockSpec(memory_space=pltpu.VMEM)] * len(outs),
        scratch_shapes=[pltpu.VMEM(s, f32) if isinstance(s, tuple) else s for s in scratch],
        compiler_params=pltpu.CompilerParams(vmem_limit_bytes=vmem_limit),
        cost_estimate=pl.CostEstimate(
            flops=cost * 1_000_000, bytes_accessed=cost * 2_000_000, transcendentals=0
        ),
    )(*operands)


def swap(value_a, value_b, axis):
    count, start = lax.axis_size(axis), first_pair[axis]
    pairs_a = [(i, (i + 1 - 2 * ((i + start) % 2)) % count) for i in range(count)]
    pairs_b = [(i, (i - 1 + 2 * ((i + start) % 2)) % count) for i in range(count)]
    return lax.ppermute(value_a, axis, pairs_a), lax.ppermute(value_b, axis, pairs_b)


def shards(saved_conc, adjoint_end, rate_field):
    steps, frames, nz, rows, cols = saved_conc.shape
    lanes = frames * nz
    _, total = slots(steps)
    width = cols + 2 * pad
    flat = lanes * rows
    inside = rows - 2 * depth

    def field(count):
        return (count, width, lanes)

    both = (2, depth, width, lanes)
    edge = (2, cols + 8, lanes)
    open_g = (2, cols + 16, lanes)
    raw = [(steps, flat, cols), (flat, cols), (nz * rows, cols)]
    conc_raw, adj_raw, rate_raw, main_a, main_b = call(
        functools.partial(edge_kernel, steps, rows, cols, nz),
        raw + [((1 + steps) * depth * cols + cols // 2, lanes)] * 2,
        [pltpu.SemaphoreType.DMA((2 + steps,))],
        saved_conc.reshape(raw[0]), adjoint_end.reshape(raw[1]), rate_field.reshape(raw[2]),
        cost=2,
        far=True,
    )
    main_a, main_b = swap(main_a, main_b, "gy")
    conc_own, adj_own, rate_own, x_a, x_b = call(
        functools.partial(turn_kernel, steps, rows, cols, nz),
        [(steps, rows, cols, lanes), (rows, cols, lanes), (rows, cols, lanes)]
        + [(rows, total, lanes)] * 2,
        [],
        conc_raw, adj_raw, rate_raw,
        cost=1,
    )
    x_a, x_b = swap(x_a, x_b, "gx")
    x_low, x_high, corner_a, corner_b = call(
        functools.partial(corner_kernel, rows),
        [(rows, total, lanes)] * 2 + [(2, depth, total, lanes)] * 2,
        [],
        x_a, x_b,
    )
    corner_a, corner_b = swap(corner_a, corner_b, "gy")

    conc, adj, rate, chem, curve, swing, pot, inner, inner_grad, ahead = call(
        functools.partial(first_interior, steps, rows, cols, nz),
        [field(rows)] * 3 + [field(rows - 2)] * 4 + [field(inside)] * 2 + [both],
        [field(rows), field(inside)],
        conc_own, adj_own, rate_own, x_low, x_high,
        cost=3,
    )
    outer, outer_grad, to_a, to_b = call(
        functools.partial(first_boundary, steps, rows, cols, nz),
        [both, both, edge, edge],
        [field(4)] + [field(rows + 2 * depth)] * 3 + [field(rows + 2)] * 4 + [both, open_g],
        conc, adj, rate, chem, curve, swing, pot, main_a, main_b, corner_a, corner_b, ahead,
        cost=2,
    )
    before = (inner_grad, outer_grad)
    for back in range(1, steps):
        adj_a, adj_b = swap(to_a, to_b, "gy")
        final = back == steps - 1
        fields = call(
            functools.partial(prepare_kernel, steps, rows, cols, nz, back),
            [field(rows + 2 * depth)] + [field(rows + 2)] * 3 + ([] if final else [both]),
            [field(rows + 2 * depth)],
            conc_own, main_a, main_b, x_low, x_high, corner_a, corner_b,
            cost=2,
        )
        fields, ahead = fields[:4], fields[4:]
        work = [field(rows + 2)] * 2 + [field(rows)]
        if final:
            rows_in, tiles, grad = call(
                functools.partial(next_interior, rows, cols, nz, final),
                [field(rows), (flat, cols), (nz * rows, cols)],
                work + [field(rows)],
                *fields, rate, inner, outer, *before,
                cost=3,
            )
            (adj,) = call(
                functools.partial(next_boundary, rows, cols, nz, final),
                [(flat, cols)],
                [both, field(2), both],
                *fields, rows_in, outer, adj_a, adj_b, tiles,
                cost=1,
            )
        else:
            rows_in, grad = call(
                functools.partial(next_interior, rows, cols, nz, final),
                [field(rows)] * 2,
                work + ([field(rows)] if len(before) == 2 else []),
                *fields, rate, inner, outer, *before,
                cost=3,
            )
            outer, to_a, to_b = call(
                functools.partial(next_boundary, rows, cols, nz, final),
                [both, edge, edge],
                [both, field(2), open_g],
                *fields, rows_in, outer, adj_a, adj_b, *ahead, rate,
                cost=1,
            )
            inner, before = rows_in, (grad,)
    return adj.reshape(adjoint_end.shape), grad.reshape(rate_field.shape)


def solution(mesh):
    return jax.shard_map(
        shards,
        mesh=mesh,
        in_specs=(P(None, None, None, "gy", "gx"), P(None, None, "gy", "gx"), P(None, "gy", "gx")),
        out_specs=(P(None, None, "gy", "gx"), P(None, "gy", "gx")),
        check_vma=False,
    )
```

```python
import functools

import jax
import jax.numpy as jnp
from jax import lax
from jax.experimental import pallas as pl
from jax.experimental.pallas import tpu as pltpu
from jax.sharding import PartitionSpec as P

mix_energy = 2.5
grad_energy = 1.0
time_step = 0.1
diff_step = 0.03
bath_potential = 0.5

pad = 16
chunk = 72
depth = 2
x_first, main_first, round_first = 0, 0, 1
vmem_limit = 20 * 1024 * 1024
f32 = jnp.float32


def slots(steps):
    widths = [2 * steps] + [2 * steps - 2 * back for back in range(steps)] + [2 * steps - 1]
    starts = [sum(widths[:i]) for i in range(len(widths))]
    total = -(-sum(widths) // 8) * 8
    return list(zip(starts, widths)), total


def chunks(low, high):
    return [(at, min(chunk, high - at)) for at in range(low, high, chunk)]


def reach(cols):
    return pad - 8, pad + cols + 8


def sent(cols):
    return pad - 4, pad + cols + 4


def up(value):
    return pltpu.roll(value, value.shape[1] - 1, 1)


def down(value):
    return pltpu.roll(value, 1, 1)


def face_mask(lanes, nz):
    lane = lax.broadcasted_iota(jnp.int32, (1, lanes), 1)
    return jnp.where(lane % nz == nz - 1, 0.0, 1.0).astype(f32)


def row_of(ref, y):
    return lambda dy, cut: ref[y + dy, cut, :]


def laplace(field, at, size, mask):
    span = slice(at, at + size)
    here = field(0, span)
    step_z = (up(here) - here) * mask
    sides = field(0, slice(at + 1, at + size + 1)) + field(0, slice(at - 1, at + size - 1))
    return here, (
        (sides + (field(-1, span) + field(1, span))) - 4.0 * here + (step_z - down(step_z))
    )


def mobility(c):
    return (0.5 * diff_step) * c * (1.0 - c)


def chem_row(conc, chem, curve, swing, at, size, mask):
    c, lap = laplace(conc, at, size, mask)
    inv = 1.0 / (c * (1.0 - c))
    span = slice(at, at + size)
    chem(
        span,
        time_step * (jnp.log(c * c * inv) - grad_energy * lap)
        + (time_step * (mix_energy - bath_potential) - (2.0 * time_step * mix_energy) * c),
    )
    curve(span, inv - 2.0 * mix_energy)
    swing(span, c * (diff_step / time_step) - 0.5 * diff_step / time_step)


def face_sums(adj, mob, chem, at, size, mask, across=(1, -1)):
    span = slice(at, at + size)
    a = adj(0, span)
    m = None if mob is None else mob(0, span)
    mu = None if chem is None else chem(0, span)
    flow = pair = None
    for dy, cut in (
        (0, slice(at + 1, at + size + 1)),
        (0, slice(at - 1, at + size - 1)),
    ) + tuple((dy, span) for dy in across):
        diff = adj(dy, cut) - a
        if mob is not None:
            term = (mob(dy, cut) + m) * diff
            flow = term if flow is None else flow + term
        if chem is not None:
            term = (chem(dy, cut) - mu) * diff
            pair = term if pair is None else pair + term
    diff = (up(a) - a) * mask
    if mob is not None:
        term = (up(m) + m) * diff
        flow = flow + (term - down(term))
    if chem is not None:
        term = (up(mu) - mu) * diff
        pair = pair + (term + down(term))
    return a, mu, flow, pair


def partial(a, swing, pair, curve, g):
    return a + swing * pair + curve * g


def gain(a, chem, before):
    value = a * chem
    return -value if before is None else before - value


def set_row(ref, y):
    def put(span, value):
        ref[y, span, :] = value

    return put


def interior(rows, cols, nz, swing, mob, chem, curve, adj, rate, pot, part, grad, store):
    low, high = reach(cols)
    lanes = adj[0].shape[-1]
    mask = face_mask(lanes, nz)

    def at_row(field, y):
        return row_of(field[0], field[1] + y)

    def body(y, _):
        for at, size in chunks(low, high):
            span = slice(at, at + size)
            a, mu, flow, pair = face_sums(
                at_row(adj, y), at_row(mob, y), at_row(chem, y), at, size, mask
            )
            g = flow - at_row(rate, y)(0, span) * a
            pot[y - 1, span, :] = g
            part[y - depth, span, :] = partial(
                a, at_row(swing, y)(0, span), pair, at_row(curve, y)(0, span), g
            )
            grad[y - depth, span, :] = gain(a, mu, None)
        return 0

    def edge(i, _):
        y = 1 + i * (rows - 3)
        for at, size in chunks(low, high):
            a, _mu, flow, _pair = face_sums(at_row(adj, y), at_row(mob, y), None, at, size, mask)
            span = slice(at, at + size)
            pot[y - 1, span, :] = flow - at_row(rate, y)(0, span) * a
        return 0

    def close(y, _):
        for at, size in chunks(low, high):
            span = slice(at, at + size)
            _g, lap = laplace(row_of(pot, y - 1), at, size, mask)
            store(y - depth, span, part[y - depth, span, :] - grad_energy * lap)
        return 0

    lax.fori_loop(depth, rows - depth, body, 0)
    lax.fori_loop(0, 2, edge, 0)
    lax.fori_loop(depth, rows - depth, close, 0)


def boundary(rows, cols, nz, conc, mob, chem, curve, swing, adj, rate, pot, part, grad, store):
    low, high = reach(cols)
    lanes = adj[0].shape[-1]
    mask = face_mask(lanes, nz)
    last = rows - 1

    def at_row(field, y):
        return row_of(field[0], field[1] + y)

    def mirror(s, y):
        return y + s * (last - 2 * y)

    def mu_side(i, _):
        s, k = i // 2, i % 2
        y = mirror(s, k - 1)
        for at, size in chunks(low, high):
            chem_row(at_row(conc, y), set_row(chem[0], chem[1] + y),
                     set_row(curve[0], curve[1] + y), set_row(swing[0], swing[1] + y), at, size,
                     mask)
        return 0

    lax.fori_loop(0, 4, mu_side, 0)

    def side(s, _):
        y = mirror(s, -1)
        for at, size in chunks(low, high):
            span = slice(at, at + size)
            a, _mu, flow, _pair = face_sums(at_row(adj, y), at_row(mob, y), None, at, size, mask)
            pot[1 + y, span, :] = flow - rate[3 * s, span, :] * a
        y0 = mirror(s, 0)
        for at, size in chunks(low, high):
            span = slice(at, at + size)
            a, mu, flow, pair = face_sums(
                at_row(adj, y0), at_row(mob, y0), at_row(chem, y0), at, size, mask
            )
            g = flow - rate[1 + s, span, :] * a
            pot[1 + y0, span, :] = g
            part[s, 0, span, :] = partial(
                a, at_row(swing, y0)(0, span), pair, at_row(curve, y0)(0, span), g
            )
            grad[s, 0, span, :] = gain(a, mu, None)
        y1 = mirror(s, 1)
        for at, size in chunks(low, high):
            span = slice(at, at + size)
            a, mu, _flow, pair = face_sums(at_row(adj, y1), None, at_row(chem, y1), at, size, mask)
            part[s, 1, span, :] = partial(
                a, at_row(swing, y1)(0, span), pair, at_row(curve, y1)(0, span), pot[1 + y1, span, :]
            )
            grad[s, 1, span, :] = gain(a, mu, None)
        return 0

    lax.fori_loop(0, 2, side, 0)

    def close(i, _):
        s, k = i // 2, i % 2
        y = mirror(s, k)
        for at, size in chunks(low, high):
            span = slice(at, at + size)
            _g, lap = laplace(row_of(pot, 1 + y), at, size, mask)
            store(s, k, span, part[s, k, span, :] - grad_energy * lap)
        return 0

    lax.fori_loop(0, 4, close, 0)


def a_is_next(axis, first):
    return lax.rem(lax.axis_index(axis), 2) == first


def bases(rows, first):
    to_next = a_is_next("gy", first)
    top = rows - depth
    return jnp.where(to_next, top, 0), jnp.where(to_next, 0, top)


def landings(rows, first):
    to_next = a_is_next("gy", first)
    top = rows + depth
    return jnp.where(to_next, top, 0), jnp.where(to_next, 0, top)


def sides_of(rows):
    return [(0, 0, 0), (0, 1, 1), (1, 0, rows - 1), (1, 1, rows - 2)]


def edge_kernel(steps, rows, cols, nz, conc_hbm, adj_hbm, rate_hbm, conc_in, adj_in, rate_in,
                main_a, main_b, sems):
    lanes = main_a.shape[1]
    half = cols // 2
    lower = lax.broadcasted_iota(jnp.int32, (half, lanes), 1) < nz
    copies = [
        pltpu.make_async_copy(adj_hbm, adj_in, sems.at[0]),
        pltpu.make_async_copy(rate_hbm, rate_in, sems.at[1]),
    ] + [
        pltpu.make_async_copy(conc_hbm.at[steps - 1 - back], conc_in.at[back], sems.at[2 + back])
        for back in range(steps)
    ]
    for copy in copies:
        copy.start()
    copies[0].wait()
    for side, base in zip((main_a, main_b), bases(rows, main_first)):
        for at in range(depth):
            side[pl.ds(at * cols, cols), :] = adj_in[pl.ds(base + at, lanes, stride=rows), :].T
    copies[1].wait()
    for side, base in zip((main_a, main_b), bases(rows, main_first)):
        edge = jnp.where(base == 0, 0, rows - 1)
        rate = turned_rate(rate_in, edge, rows, nz, lanes)
        side[pl.ds((1 + steps) * depth * cols, half), :] = jnp.where(
            lower, rate[:half], rate[half:]
        )
    for back in range(steps):
        copies[2 + back].wait()
        for side, base in zip((main_a, main_b), bases(rows, main_first)):
            for at in range(depth):
                side[pl.ds(((1 + back) * depth + at) * cols, cols), :] = conc_in[
                    back, pl.ds(base + at, lanes, stride=rows), :
                ].T


def turned_rate(rate, y, rows, nz, lanes):
    value = time_step * rate[pl.ds(y, nz, stride=rows), :]
    return jnp.concatenate([value] * (lanes // nz), axis=0).T


def turn_kernel(steps, rows, cols, nz, conc_in, adj_in, rate_in, conc_out, adj_out, rate_out,
                x_a, x_b):
    places, total = slots(steps)
    lanes = adj_out.shape[2]
    next_x = a_is_next("gx", x_first)

    def to_x(y, value, place):
        start, width = place
        last, first = value[cols - width :, :], value[:width, :]
        x_a[y, start : start + width, :] = jnp.where(next_x, last, first)
        x_b[y, start : start + width, :] = jnp.where(next_x, first, last)

    used = sum(places[-1])
    for y in range(rows):
        adj = adj_in[pl.ds(y, lanes, stride=rows), :].T
        adj_out[y] = adj
        to_x(y, adj, places[0])
        rate = turned_rate(rate_in, y, rows, nz, lanes)
        rate_out[y] = rate
        to_x(y, rate, places[steps + 1])
        if used < total:
            x_a[y, used:, :] = jnp.zeros((total - used, lanes), f32)
            x_b[y, used:, :] = jnp.zeros((total - used, lanes), f32)
        for back in range(steps):
            conc = conc_in[back, pl.ds(y, lanes, stride=rows), :].T
            conc_out[back, y] = conc
            to_x(y, conc, places[1 + back])


def put_own(out, row, value, y, place, cols, x_low, x_high):
    start, width = place
    right = pad + cols
    out[row, pad:right, :] = value
    out[row, pad - width : pad, :] = x_low[y, start : start + width, :]
    out[row, right : right + width, :] = x_high[y, start : start + width, :]


def put_halo(out, row, value, from_row, place, cols, corner):
    start, width = place
    right = pad + cols
    out[row, pad:right, :] = value
    out[row, pad - width : pad, :] = corner[0, from_row, start : start + width, :]
    out[row, right : right + width, :] = corner[1, from_row, start : start + width, :]


def corner_kernel(rows, got_a, got_b, x_low, x_high, corner_a, corner_b):
    next_x = a_is_next("gx", x_first)
    x_low[...] = jnp.where(next_x, got_b[...], got_a[...])
    x_high[...] = jnp.where(next_x, got_a[...], got_b[...])
    for out, base in zip((corner_a, corner_b), bases(rows, round_first)):
        for at in range(depth):
            out[0, at] = x_low[base + at]
            out[1, at] = x_high[base + at]


def first_interior(steps, rows, cols, nz, conc_own, adj_own, rate_own, x_low, x_high,
                   conc, adj, rate, chem, curve, swing, pot, out, grad, ahead, mob, part):
    places, _ = slots(steps)
    low, high = reach(cols)
    lanes = adj.shape[2]
    mask = face_mask(lanes, nz)
    for y in range(rows):
        put_own(conc, y, conc_own[0, y], y, places[1], cols, x_low, x_high)
        put_own(adj, y, adj_own[y], y, places[0], cols, x_low, x_high)
        put_own(rate, y, rate_own[y], y, places[steps + 1], cols, x_low, x_high)
    put_ahead(ahead, conc_own, 1, x_low, x_high, places, rows, cols)

    def mob_row(y, _):
        for at, size in chunks(low - 8, high + 8):
            c = conc[y, at : at + size, :]
            mob[y, at : at + size, :] = mobility(c)
        return 0

    def mu_row(y, _):
        for at, size in chunks(low, high):
            chem_row(row_of(conc, y), set_row(chem, y - 1), set_row(curve, y - 1),
                     set_row(swing, y - 1), at, size, mask)
        return 0

    lax.fori_loop(0, rows, mob_row, 0)
    lax.fori_loop(1, rows - 1, mu_row, 0)

    def store(k, span, value):
        out[k, span, :] = value

    interior(rows, cols, nz, (swing, -1), (mob, 0), (chem, -1), (curve, -1), (adj, 0), (rate, 0),
             pot, part, grad, store)


def copy_rows(pairs):
    for out, to, ref, at in pairs:
        out[to] = ref[at]


def send_rows(out, ahead, rate, to_a, to_b, open_g, cols, nz):
    low, high = reach(cols)
    first, last = sent(cols)
    rows, lanes = rate.shape[0], rate.shape[2]
    mask = face_mask(lanes, nz)
    for s in range(2):
        for at, size in chunks(low, high):
            a, _mu, flow, _pair = face_sums(
                lambda dy, cut: out[s, dy, cut, :], lambda dy, cut: ahead[s, dy, cut, :], None,
                at, size, mask, (1,)
            )
            open_g[s, at - low : at - low + size, :] = (
                flow - rate[s * (rows - 1), at : at + size, :] * a
            )
    to_next = a_is_next("gy", round_first)
    for to, side in ((to_a, jnp.where(to_next, 1, 0)), (to_b, jnp.where(to_next, 0, 1))):
        to[0] = out[side, 0, first:last, :]
        to[1] = open_g[side, first - low : last - low, :]


def put_ahead(ahead, conc_own, back, x_low, x_high, places, rows, cols):
    for s, k, y in sides_of(rows):
        put_own(ahead.at[s], k, conc_own[back, y], y, places[1 + back], cols, x_low, x_high)
        ahead[s, k] = mobility(ahead[s, k])


def first_boundary(steps, rows, cols, nz, conc_in, adj_in, rate_in, chem_in, curve_in, swing_in,
                   pot_in,
                   from_a, from_b, corner_b, corner_a, ahead,
                   out, grad, to_a, to_b, rate, conc, adj, mob, chem, curve, swing, pot,
                   part, open_g):
    places, _ = slots(steps)
    low, high = reach(cols)
    half = cols // 2
    lanes = conc.shape[2]
    lower = lax.broadcasted_iota(jnp.int32, (half, lanes), 1) < nz

    def unpack(side):
        packed = side[pl.ds((1 + steps) * depth * cols, half), :]
        turned = pltpu.roll(packed, lanes // 2, 1)
        return jnp.concatenate(
            [jnp.where(lower, packed, turned), jnp.where(lower, turned, packed)], axis=0
        )

    near = [0, 1, 2, rows - 3, rows - 2, rows - 1]
    for y in near:
        conc[depth + y] = conc_in[y]
        adj[depth + y] = adj_in[y]
    for y in (1, 2, rows - 3, rows - 2):
        chem[1 + y] = chem_in[y - 1]
        pot[1 + y] = pot_in[y - 1]
    for y in (1, rows - 2):
        curve[1 + y] = curve_in[y - 1]
        swing[1 + y] = swing_in[y - 1]
    rate[1] = rate_in[0]
    rate[2] = rate_in[rows - 1]
    for halo, corner, base in zip((from_a, from_b), (corner_a, corner_b), landings(rows, main_first)):
        for at in range(depth):
            for ref, place, first in ((adj, places[0], 0), (conc, places[1], depth)):
                span = pl.ds((first + at) * cols, cols)
                put_halo(ref, base + at, halo[span, :], at, place, cols, corner)
        below = base == 0
        put_halo(rate, jnp.where(below, 0, 3), unpack(halo), jnp.where(below, depth - 1, 0),
                 places[steps + 1], cols, corner)
    for row in [0, 1, 2, 3, rows, rows + 1, rows + 2, rows + 3]:
        for at, size in chunks(low - 8, high + 8):
            c = conc[row, at : at + size, :]
            mob[row, at : at + size, :] = mobility(c)

    def store(s, k, span, value):
        out[s, k, span, :] = value

    boundary(rows, cols, nz, (conc, depth), (mob, depth), (chem, 1), (curve, 1), (swing, 1),
             (adj, depth), rate, pot, part, grad, store)
    send_rows(out, ahead, rate_in, to_a, to_b, open_g, cols, nz)


def prepare_kernel(steps, rows, cols, nz, back, conc_own, from_a, from_b, x_low, x_high,
                   corner_b, corner_a, mob, chem, curve, swing, *rest):
    *ahead, conc = rest
    places, _ = slots(steps)
    low, high = reach(cols)
    lanes = conc.shape[2]
    mask = face_mask(lanes, nz)
    place = places[1 + back]
    for y in range(rows):
        put_own(conc, depth + y, conc_own[back, y], y, place, cols, x_low, x_high)
    for halo, corner, base in zip((from_a, from_b), (corner_a, corner_b), landings(rows, main_first)):
        for at in range(depth):
            span = pl.ds(((1 + back) * depth + at) * cols, cols)
            put_halo(conc, base + at, halo[span, :], at, place, cols, corner)

    if ahead:
        put_ahead(ahead[0], conc_own, back + 1, x_low, x_high, places, rows, cols)

    def mob_row(row, _):
        for at, size in chunks(low - 8, high + 8):
            c = conc[row, at : at + size, :]
            mob[row, at : at + size, :] = mobility(c)
        return 0

    def mu_row(row, _):
        for at, size in chunks(low, high):
            chem_row(row_of(conc, row + 1), set_row(chem, row), set_row(curve, row),
                     set_row(swing, row), at, size, mask)
        return 0

    lax.fori_loop(0, rows + 2 * depth, mob_row, 0)
    lax.fori_loop(0, rows + 2, mu_row, 0)


def next_interior(rows, cols, nz, final, mob, chem, curve, swing, rate, inner, outer, *rest):
    if final:
        before, out, tiles, grad_out, adj, pot, part, grad = rest
    elif len(rest) == 8:
        inner_grad, outer_grad, out, grad, adj, pot, part, before = rest
        for k in range(rows - 2 * depth):
            before[depth + k] = inner_grad[k]
        for s, k, y in sides_of(rows):
            before[y] = outer_grad[s, k]
    else:
        before, out, grad, adj, pot, part = rest
    low, high = reach(cols)
    lanes = adj.shape[2]
    mask = face_mask(lanes, nz)
    skip = (inner.shape[0] - (rows - 2 * depth)) // 2
    for k in range(rows - 2 * depth):
        adj[1 + depth + k] = inner[skip + k]
    for s, k, y in sides_of(rows):
        adj[1 + y] = outer[s, k]
    adj[0] = outer[0, 0]
    adj[1 + rows] = outer[1, 0]
    pot[0] = jnp.zeros(pot.shape[1:], f32)
    pot[1 + rows] = jnp.zeros(pot.shape[1:], f32)

    def body(y, _):
        for at, size in chunks(low, high):
            span = slice(at, at + size)
            a, mu, flow, pair = face_sums(
                row_of(adj, y + 1), row_of(mob, y + depth), row_of(chem, y + 1), at, size, mask
            )
            g = flow - rate[y, span, :] * a
            pot[y + 1, span, :] = g
            part[y, span, :] = partial(
                a, swing[y + 1, span, :], pair, curve[y + 1, span, :], g
            )
            grad[y, span, :] = gain(a, mu, before[y, span, :])
        return 0

    def close(y, _):
        for at, size in chunks(low, high):
            span = slice(at, at + size)
            _g, lap = laplace(row_of(pot, y + 1), at, size, mask)
            out[y, span, :] = part[y, span, :] - grad_energy * lap
        return 0

    lax.fori_loop(0, rows, body, 0)
    lax.fori_loop(0, rows, close, 0)
    if final:
        for y in range(rows):
            grad_out[pl.ds(y, nz, stride=rows), :] = fold(grad[y, pad : pad + cols, :].T, nz)
        for y in range(depth, rows - depth):
            tiles[pl.ds(y, lanes, stride=rows), :] = out[y, pad : pad + cols, :].T


def fold(value, nz):
    total = value[:nz]
    for frame in range(1, value.shape[0] // nz):
        total = total + value[frame * nz : (frame + 1) * nz]
    return total


def next_boundary(rows, cols, nz, final, mob, chem, curve, swing, inside, outer, from_a, from_b,
                  *rest):
    if final:
        tiles, out, halo, delta, result = rest
    else:
        ahead, rate, result, to_a, to_b, halo, delta, open_g = rest
    low, high = reach(cols)
    first, last = sent(cols)
    lanes = mob.shape[2]
    mask = face_mask(lanes, nz)
    to_next = a_is_next("gy", round_first)
    for got, side in ((from_a, jnp.where(to_next, 1, 0)), (from_b, jnp.where(to_next, 0, 1))):
        for k in range(2):
            halo[side, k, first:last, :] = got[k]
    for s in range(2):
        y, beyond = s * (rows - 1), s * (rows + 1) - 1
        for at, size in chunks(low, high):
            span = slice(at, at + size)
            diff = halo[s, 0, span, :] - outer[s, 0, span, :]
            both = mob[depth + beyond, span, :] + mob[depth + y, span, :]
            delta[s, span, :] = both * diff
        for at, size in chunks(low, high):
            span = slice(at, at + size)
            more = delta[s, span, :]
            diff = halo[s, 0, span, :] - outer[s, 0, span, :]
            pair = (chem[1 + beyond, span, :] - chem[1 + y, span, :]) * diff
            step_z = (up(more) - more) * mask
            lap = (
                (delta[s, at + 1 : at + size + 1, :] + delta[s, at - 1 : at + size - 1, :])
                + (halo[s, 1, span, :] - more)
                - 4.0 * more
                + (step_z - down(step_z))
            )
            result[s, 0, span, :] = (
                inside[y, span, :]
                + (swing[1 + y, span, :] * pair + curve[1 + y, span, :] * more)
                - grad_energy * lap
            )
            result[s, 1, span, :] = inside[1 + s * (rows - 3), span, :] - grad_energy * more
    if final:
        out[...] = tiles[...]
        for s, k, y in sides_of(rows):
            out[pl.ds(y, lanes, stride=rows), :] = result[s, k, pad : pad + cols, :].T
    else:
        send_rows(result, ahead, rate, to_a, to_b, open_g, cols, nz)


def call(kernel, outs, scratch, *operands, cost=0, far=False):
    if far:
        operands = [pltpu.with_memory_space_constraint(value, pltpu.HBM) for value in operands]
    space = pl.ANY if far else pltpu.VMEM
    return pl.pallas_call(
        kernel,
        out_shape=[jax.ShapeDtypeStruct(shape, f32) for shape in outs],
        in_specs=[pl.BlockSpec(memory_space=space)] * len(operands),
        out_specs=[pl.BlockSpec(memory_space=pltpu.VMEM)] * len(outs),
        scratch_shapes=[pltpu.VMEM(s, f32) if isinstance(s, tuple) else s for s in scratch],
        compiler_params=pltpu.CompilerParams(vmem_limit_bytes=vmem_limit),
        cost_estimate=pl.CostEstimate(
            flops=cost * 1_000_000, bytes_accessed=cost * 2_000_000, transcendentals=0
        ),
    )(*operands)


def swap(value_a, value_b, axis, first):
    count = lax.axis_size(axis)
    pairs_a = [(i, (i + 1 - 2 * ((i + first) % 2)) % count) for i in range(count)]
    pairs_b = [(i, (i - 1 + 2 * ((i + first) % 2)) % count) for i in range(count)]
    return lax.ppermute(value_a, axis, pairs_a), lax.ppermute(value_b, axis, pairs_b)


def shards(saved_conc, adjoint_end, rate_field):
    steps, frames, nz, rows, cols = saved_conc.shape
    lanes = frames * nz
    _, total = slots(steps)
    width = cols + 2 * pad
    flat = lanes * rows
    inside = rows - 2 * depth

    def field(count):
        return (count, width, lanes)

    both = (2, depth, width, lanes)
    edge = (2, cols + 8, lanes)
    open_g = (2, cols + 16, lanes)
    raw = [(steps, flat, cols), (flat, cols), (nz * rows, cols)]
    conc_raw, adj_raw, rate_raw, main_a, main_b = call(
        functools.partial(edge_kernel, steps, rows, cols, nz),
        raw + [((1 + steps) * depth * cols + cols // 2, lanes)] * 2,
        [pltpu.SemaphoreType.DMA((2 + steps,))],
        saved_conc.reshape(raw[0]), adjoint_end.reshape(raw[1]), rate_field.reshape(raw[2]),
        cost=2,
        far=True,
    )
    main_a, main_b = swap(main_a, main_b, "gy", main_first)
    conc_own, adj_own, rate_own, x_a, x_b = call(
        functools.partial(turn_kernel, steps, rows, cols, nz),
        [(steps, rows, cols, lanes), (rows, cols, lanes), (rows, cols, lanes)]
        + [(rows, total, lanes)] * 2,
        [],
        conc_raw, adj_raw, rate_raw,
        cost=1,
    )
    x_a, x_b = swap(x_a, x_b, "gx", x_first)
    x_low, x_high, corner_a, corner_b = call(
        functools.partial(corner_kernel, rows),
        [(rows, total, lanes)] * 2 + [(2, depth, total, lanes)] * 2,
        [],
        x_a, x_b,
    )
    corners = swap(corner_a, corner_b, "gy", round_first)
    corner_a, corner_b = corners if main_first == round_first else corners[::-1]

    conc, adj, rate, chem, curve, swing, pot, inner, inner_grad, ahead = call(
        functools.partial(first_interior, steps, rows, cols, nz),
        [field(rows)] * 3 + [field(rows - 2)] * 4 + [field(inside)] * 2 + [both],
        [field(rows), field(inside)],
        conc_own, adj_own, rate_own, x_low, x_high,
        cost=3,
    )
    outer, outer_grad, to_a, to_b = call(
        functools.partial(first_boundary, steps, rows, cols, nz),
        [both, both, edge, edge],
        [field(4)] + [field(rows + 2 * depth)] * 3 + [field(rows + 2)] * 4 + [both, open_g],
        conc, adj, rate, chem, curve, swing, pot, main_a, main_b, corner_b, corner_a, ahead,
        cost=2,
    )
    before = (inner_grad, outer_grad)
    for back in range(1, steps):
        adj_a, adj_b = swap(to_a, to_b, "gy", round_first)
        final = back == steps - 1
        fields = call(
            functools.partial(prepare_kernel, steps, rows, cols, nz, back),
            [field(rows + 2 * depth)] + [field(rows + 2)] * 3 + ([] if final else [both]),
            [field(rows + 2 * depth)],
            conc_own, main_a, main_b, x_low, x_high, corner_b, corner_a,
            cost=2,
        )
        fields, ahead = fields[:4], fields[4:]
        work = [field(rows + 2)] * 2 + [field(rows)]
        if final:
            rows_in, tiles, grad = call(
                functools.partial(next_interior, rows, cols, nz, final),
                [field(rows), (flat, cols), (nz * rows, cols)],
                work + [field(rows)],
                *fields, rate, inner, outer, *before,
                cost=3,
            )
            (adj,) = call(
                functools.partial(next_boundary, rows, cols, nz, final),
                [(flat, cols)],
                [both, field(2), both],
                *fields, rows_in, outer, adj_a, adj_b, tiles,
                cost=1,
            )
        else:
            rows_in, grad = call(
                functools.partial(next_interior, rows, cols, nz, final),
                [field(rows)] * 2,
                work + ([field(rows)] if len(before) == 2 else []),
                *fields, rate, inner, outer, *before,
                cost=3,
            )
            outer, to_a, to_b = call(
                functools.partial(next_boundary, rows, cols, nz, final),
                [both, edge, edge],
                [both, field(2), open_g],
                *fields, rows_in, outer, adj_a, adj_b, *ahead, rate,
                cost=1,
            )
            inner, before = rows_in, (grad,)
    return adj.reshape(adjoint_end.shape), grad.reshape(rate_field.shape)


def solution(mesh):
    return jax.shard_map(
        shards,
        mesh=mesh,
        in_specs=(P(None, None, None, "gy", "gx"), P(None, None, "gy", "gx"), P(None, "gy", "gx")),
        out_specs=(P(None, None, "gy", "gx"), P(None, "gy", "gx")),
        check_vma=False,
    )
```

```python
import functools

import jax
import jax.numpy as jnp
from jax import lax
from jax.experimental import pallas as pl
from jax.experimental.pallas import tpu as pltpu
from jax.sharding import PartitionSpec as P

mix_energy = 2.5
grad_energy = 1.0
time_step = 0.1
diff_step = 0.03
bath_potential = 0.5

pad = 16
chunk = 72
depth = 2
x_first, main_first, round_first = 0, 0, 1
vmem_limit = 20 * 1024 * 1024
f32 = jnp.float32


def slots(steps):
    widths = [2 * steps] + [2 * steps - 2 * back for back in range(steps)] + [2 * steps - 1]
    starts = [sum(widths[:i]) for i in range(len(widths))]
    total = -(-sum(widths) // 8) * 8
    return list(zip(starts, widths)), total


def chunks(low, high):
    return [(at, min(chunk, high - at)) for at in range(low, high, chunk)]


def reach(cols):
    return pad - 8, pad + cols + 8


def sent(cols):
    return pad - 4, pad + cols + 4


def up(value):
    return pltpu.roll(value, value.shape[1] - 1, 1)


def down(value):
    return pltpu.roll(value, 1, 1)


def face_mask(lanes, nz):
    lane = lax.broadcasted_iota(jnp.int32, (1, lanes), 1)
    return jnp.where(lane % nz == nz - 1, 0.0, 1.0).astype(f32)


def row_of(ref, y):
    return lambda dy, cut: ref[y + dy, cut, :]


def laplace(field, at, size, mask):
    span = slice(at, at + size)
    here = field(0, span)
    step_z = (up(here) - here) * mask
    sides = field(0, slice(at + 1, at + size + 1)) + field(0, slice(at - 1, at + size - 1))
    return here, (
        (sides + (field(-1, span) + field(1, span))) - 4.0 * here + (step_z - down(step_z))
    )


def mobility(c):
    return (0.5 * diff_step) * c * (1.0 - c)


def chem_row(conc, chem, curve, swing, at, size, mask):
    c, lap = laplace(conc, at, size, mask)
    inv = 1.0 / (c * (1.0 - c))
    span = slice(at, at + size)
    chem(
        span,
        time_step * (jnp.log(c * c * inv) - grad_energy * lap)
        + (time_step * (mix_energy - bath_potential) - (2.0 * time_step * mix_energy) * c),
    )
    curve(span, inv - 2.0 * mix_energy)
    swing(span, c * (diff_step / time_step) - 0.5 * diff_step / time_step)


def face_sums(adj, mob, chem, at, size, mask, across=(1, -1)):
    span = slice(at, at + size)
    a = adj(0, span)
    m = None if mob is None else mob(0, span)
    mu = None if chem is None else chem(0, span)
    flow = pair = None
    for dy, cut in (
        (0, slice(at + 1, at + size + 1)),
        (0, slice(at - 1, at + size - 1)),
    ) + tuple((dy, span) for dy in across):
        diff = adj(dy, cut) - a
        if mob is not None:
            term = (mob(dy, cut) + m) * diff
            flow = term if flow is None else flow + term
        if chem is not None:
            term = (chem(dy, cut) - mu) * diff
            pair = term if pair is None else pair + term
    diff = (up(a) - a) * mask
    if mob is not None:
        term = (up(m) + m) * diff
        flow = flow + (term - down(term))
    if chem is not None:
        term = (up(mu) - mu) * diff
        pair = pair + (term + down(term))
    return a, mu, flow, pair


def partial(a, swing, pair, curve, g):
    return a + swing * pair + curve * g


def gain(a, chem, before):
    value = a * chem
    return -value if before is None else before - value


def set_row(ref, y):
    def put(span, value):
        ref[y, span, :] = value

    return put


def all_rows(rows, cols, nz, adj, mob, mob_skip, chem, curve, swing, rate, before, pot, part, out,
             grad):
    low, high = reach(cols)
    mask = face_mask(adj.shape[2], nz)

    def body(y, _):
        for at, size in chunks(low, high):
            span = slice(at, at + size)
            a, mu, flow, pair = face_sums(
                row_of(adj, y + 1), row_of(mob, y + mob_skip), row_of(chem, y + 1), at, size, mask
            )
            g = flow - rate[y, span, :] * a
            pot[y + 1, span, :] = g
            part[y, span, :] = partial(
                a, swing[y + 1, span, :], pair, curve[y + 1, span, :], g
            )
            grad[y, span, :] = gain(a, mu, None if before is None else before[y, span, :])
        return 0

    def close(y, _):
        for at, size in chunks(low, high):
            span = slice(at, at + size)
            _g, lap = laplace(row_of(pot, y + 1), at, size, mask)
            out[y, span, :] = part[y, span, :] - grad_energy * lap
        return 0

    for row in (0, rows + 1):
        pot[row] = jnp.zeros(pot.shape[1:], f32)
    lax.fori_loop(0, rows, body, 0)
    lax.fori_loop(0, rows, close, 0)


def a_is_next(axis, first):
    return lax.rem(lax.axis_index(axis), 2) == first


def bases(rows, first):
    to_next = a_is_next("gy", first)
    top = rows - depth
    return jnp.where(to_next, top, 0), jnp.where(to_next, 0, top)


def landings(rows, first):
    to_next = a_is_next("gy", first)
    top = rows + depth
    return jnp.where(to_next, top, 0), jnp.where(to_next, 0, top)


def sides_of(rows):
    return [(0, 0, 0), (0, 1, 1), (1, 0, rows - 1), (1, 1, rows - 2)]


def edge_kernel(steps, rows, cols, nz, conc_hbm, adj_hbm, rate_hbm, conc_in, adj_in, rate_in,
                main_a, main_b, sems):
    lanes = main_a.shape[1]
    half = cols // 2
    lower = lax.broadcasted_iota(jnp.int32, (half, lanes), 1) < nz
    copies = [
        pltpu.make_async_copy(adj_hbm, adj_in, sems.at[0]),
        pltpu.make_async_copy(rate_hbm, rate_in, sems.at[1]),
    ] + [
        pltpu.make_async_copy(conc_hbm.at[steps - 1 - back], conc_in.at[back], sems.at[2 + back])
        for back in range(steps)
    ]
    for copy in copies:
        copy.start()
    copies[0].wait()
    for side, base in zip((main_a, main_b), bases(rows, main_first)):
        for at in range(depth):
            side[pl.ds(at * cols, cols), :] = adj_in[pl.ds(base + at, lanes, stride=rows), :].T
    copies[1].wait()
    for side, base in zip((main_a, main_b), bases(rows, main_first)):
        edge = jnp.where(base == 0, 0, rows - 1)
        rate = turned_rate(rate_in, edge, rows, nz, lanes)
        side[pl.ds((1 + steps) * depth * cols, half), :] = jnp.where(
            lower, rate[:half], rate[half:]
        )
    for back in range(steps):
        copies[2 + back].wait()
        for side, base in zip((main_a, main_b), bases(rows, main_first)):
            for at in range(depth):
                side[pl.ds(((1 + back) * depth + at) * cols, cols), :] = conc_in[
                    back, pl.ds(base + at, lanes, stride=rows), :
                ].T


def turned_rate(rate, y, rows, nz, lanes):
    value = time_step * rate[pl.ds(y, nz, stride=rows), :]
    return jnp.concatenate([value] * (lanes // nz), axis=0).T


def turn_kernel(steps, rows, cols, nz, conc_in, adj_in, rate_in, conc_out, adj_out, rate_out,
                x_a, x_b):
    places, total = slots(steps)
    lanes = adj_out.shape[2]
    next_x = a_is_next("gx", x_first)

    def to_x(y, value, place):
        start, width = place
        last, first = value[cols - width :, :], value[:width, :]
        x_a[y, start : start + width, :] = jnp.where(next_x, last, first)
        x_b[y, start : start + width, :] = jnp.where(next_x, first, last)

    used = sum(places[-1])
    for y in range(rows):
        adj = adj_in[pl.ds(y, lanes, stride=rows), :].T
        adj_out[y] = adj
        to_x(y, adj, places[0])
        rate = turned_rate(rate_in, y, rows, nz, lanes)
        rate_out[y] = rate
        to_x(y, rate, places[steps + 1])
        if used < total:
            x_a[y, used:, :] = jnp.zeros((total - used, lanes), f32)
            x_b[y, used:, :] = jnp.zeros((total - used, lanes), f32)
        for back in range(steps):
            conc = conc_in[back, pl.ds(y, lanes, stride=rows), :].T
            conc_out[back, y] = conc
            to_x(y, conc, places[1 + back])


def put_own(out, row, value, y, place, cols, x_low, x_high):
    start, width = place
    right = pad + cols
    out[row, pad:right, :] = value
    out[row, pad - width : pad, :] = x_low[y, start : start + width, :]
    out[row, right : right + width, :] = x_high[y, start : start + width, :]


def put_halo(out, index, value, from_row, place, cols, corner):
    start, width = place
    right = pad + cols
    out[(*index, slice(pad, right))] = value
    out[(*index, slice(pad - width, pad))] = corner[0, from_row, start : start + width, :]
    out[(*index, slice(right, right + width))] = corner[1, from_row, start : start + width, :]


def corner_kernel(rows, got_a, got_b, x_low, x_high, corner_a, corner_b):
    next_x = a_is_next("gx", x_first)
    x_low[...] = jnp.where(next_x, got_b[...], got_a[...])
    x_high[...] = jnp.where(next_x, got_a[...], got_b[...])
    for out, base in zip((corner_a, corner_b), bases(rows, round_first)):
        for at in range(depth):
            out[0, at] = x_low[base + at]
            out[1, at] = x_high[base + at]


def first_interior(steps, rows, cols, nz, conc_own, adj_own, rate_own, x_low, x_high,
                   conc, adj, rate, chem, curve, swing, out, grad, ahead, mob, pot, part):
    places, _ = slots(steps)
    low, high = reach(cols)
    lanes = adj.shape[2]
    mask = face_mask(lanes, nz)
    for y in range(rows):
        put_own(conc, 1 + y, conc_own[0, y], y, places[1], cols, x_low, x_high)
        put_own(adj, 1 + y, adj_own[y], y, places[0], cols, x_low, x_high)
        put_own(rate, y, rate_own[y], y, places[steps + 1], cols, x_low, x_high)
    for row, beside in ((0, 1), (rows + 1, rows)):
        adj[row] = adj[beside]
        for ref in (conc, chem, mob):
            ref[row] = jnp.zeros(ref.shape[1:], f32)
    put_ahead(ahead, conc_own, 1, x_low, x_high, places, rows, cols)

    def mob_row(row, _):
        for at, size in chunks(low - 8, high + 8):
            mob[row, at : at + size, :] = mobility(conc[row, at : at + size, :])
        return 0

    def mu_row(row, _):
        for at, size in chunks(low, high):
            chem_row(row_of(conc, row), set_row(chem, row), set_row(curve, row),
                     set_row(swing, row), at, size, mask)
        return 0

    lax.fori_loop(1, rows + 1, mob_row, 0)
    lax.fori_loop(1, rows + 1, mu_row, 0)
    all_rows(rows, cols, nz, adj, mob, 1, chem, curve, swing, rate, None, pot, part, out, grad)


def send_rows(out, ahead, rate, to_a, to_b, open_g, cols, nz):
    low, high = reach(cols)
    first, last = sent(cols)
    rows, lanes = rate.shape[0], rate.shape[2]
    mask = face_mask(lanes, nz)
    for s in range(2):
        for at, size in chunks(low, high):
            a, _mu, flow, _pair = face_sums(
                lambda dy, cut: out[s, dy, cut, :], lambda dy, cut: ahead[s, dy, cut, :], None,
                at, size, mask, (1,)
            )
            open_g[s, at - low : at - low + size, :] = (
                flow - rate[s * (rows - 1), at : at + size, :] * a
            )
    to_next = a_is_next("gy", round_first)
    for to, side in ((to_a, jnp.where(to_next, 1, 0)), (to_b, jnp.where(to_next, 0, 1))):
        to[0] = out[side, 0, first:last, :]
        to[1] = open_g[side, first - low : last - low, :]


def put_ahead(ahead, conc_own, back, x_low, x_high, places, rows, cols):
    for s, k, y in sides_of(rows):
        put_own(ahead.at[s], k, conc_own[back, y], y, places[1 + back], cols, x_low, x_high)
        ahead[s, k] = mobility(ahead[s, k])


def first_boundary(steps, rows, cols, nz, conc, adj, rate, chem, curve, swing, inside, grad,
                   from_a, from_b, corner_b, corner_a, ahead,
                   out, edge_grad, to_a, to_b, far_conc, far_adj, far_rate, far_mob, far_chem,
                   far_pot, delta, open_g):
    places, _ = slots(steps)
    low, high = reach(cols)
    half = cols // 2
    lanes = conc.shape[2]
    mask = face_mask(lanes, nz)
    lower = lax.broadcasted_iota(jnp.int32, (half, lanes), 1) < nz
    to_next = a_is_next("gy", main_first)

    def unpack(side):
        packed = side[pl.ds((1 + steps) * depth * cols, half), :]
        turned = pltpu.roll(packed, lanes // 2, 1)
        return jnp.concatenate(
            [jnp.where(lower, packed, turned), jnp.where(lower, turned, packed)], axis=0
        )

    for halo, corner, side in (
        (from_a, corner_a, jnp.where(to_next, 1, 0)),
        (from_b, corner_b, jnp.where(to_next, 0, 1)),
    ):
        for at in range(depth):
            step = jnp.where(side == 1, at, depth - 1 - at)
            for ref, place, first in ((far_adj, places[0], 0), (far_conc, places[1], depth)):
                span = pl.ds((first + at) * cols, cols)
                put_halo(ref, (side, step), halo[span, :], at, place, cols, corner)
        put_halo(far_rate, (side,), unpack(halo), jnp.where(side == 1, 0, depth - 1),
                 places[steps + 1], cols, corner)

    share = time_step * grad_energy
    for s in range(2):
        y, y1 = s * (rows - 1), 1 + s * (rows - 3)
        for at, size in chunks(low - 8, high + 8):
            span = slice(at, at + size)
            far_mob[s, span, :] = mobility(far_conc[s, 0, span, :])

        def conc_at(dy, cut):
            return conc[1 + y, cut, :] if dy == 1 else far_conc[s, -dy, cut, :]

        def adj_at(dy, cut):
            return adj[1 + y, cut, :] if dy == 1 else far_adj[s, -dy, cut, :]

        def mob_at(dy, cut):
            return far_mob[s, cut, :] if dy == 0 else mobility(conc_at(dy, cut))

        for at, size in chunks(low, high):
            span = slice(at, at + size)
            chem_row(conc_at, set_row(far_chem, s), lambda *_: None, lambda *_: None, at, size,
                     mask)
            a, _mu, flow, _pair = face_sums(adj_at, mob_at, None, at, size, mask)
            far_pot[s, span, :] = flow - far_rate[s, span, :] * a
            diff = a - adj[1 + y, span, :]
            delta[s, span, :] = (far_mob[s, span, :] + mobility(conc[1 + y, span, :])) * diff
        for at, size in chunks(low, high):
            span = slice(at, at + size)
            a, c, _flow, spread = face_sums(
                lambda dy, cut: adj[1 + y, cut, :], None, lambda dy, cut: far_conc[s, 0, cut, :],
                at, size, mask, ()
            )
            less = share * c
            inward = less * (adj[1 + y1, span, :] - a)
            pair = (far_chem[s, span, :] - (chem[1 + y, span, :] - less)) * (
                far_adj[s, 0, span, :] - a
            ) + (inward - share * spread)
            more = delta[s, span, :]
            step_z = (up(more) - more) * mask
            lap = (
                (delta[s, at + 1 : at + size + 1, :] + delta[s, at - 1 : at + size - 1, :])
                + (far_pot[s, span, :] - 4.0 * more)
                + (step_z - down(step_z))
            )
            out[s, 0, span, :] = (
                inside[y, span, :]
                + (swing[1 + y, span, :] * pair + curve[1 + y, span, :] * more)
                - grad_energy * lap
            )
            out[s, 1, span, :] = (
                inside[y1, span, :] + swing[1 + y1, span, :] * inward - grad_energy * more
            )
            edge_grad[s, span, :] = grad[y, span, :] + less * a
    send_rows(out, ahead, rate, to_a, to_b, open_g, cols, nz)


def prepare_kernel(steps, rows, cols, nz, back, conc_own, from_a, from_b, x_low, x_high,
                   corner_b, corner_a, mob, chem, curve, swing, *rest):
    *ahead, conc = rest
    places, _ = slots(steps)
    low, high = reach(cols)
    lanes = conc.shape[2]
    mask = face_mask(lanes, nz)
    place = places[1 + back]
    for y in range(rows):
        put_own(conc, depth + y, conc_own[back, y], y, place, cols, x_low, x_high)
    for halo, corner, base in zip((from_a, from_b), (corner_a, corner_b), landings(rows, main_first)):
        for at in range(depth):
            span = pl.ds(((1 + back) * depth + at) * cols, cols)
            put_halo(conc, (base + at,), halo[span, :], at, place, cols, corner)

    if ahead:
        put_ahead(ahead[0], conc_own, back + 1, x_low, x_high, places, rows, cols)

    def mob_row(row, _):
        for at, size in chunks(low - 8, high + 8):
            c = conc[row, at : at + size, :]
            mob[row, at : at + size, :] = mobility(c)
        return 0

    def mu_row(row, _):
        for at, size in chunks(low, high):
            chem_row(row_of(conc, row + 1), set_row(chem, row), set_row(curve, row),
                     set_row(swing, row), at, size, mask)
        return 0

    lax.fori_loop(0, rows + 2 * depth, mob_row, 0)
    lax.fori_loop(0, rows + 2, mu_row, 0)


def next_interior(rows, cols, nz, final, mob, chem, curve, swing, rate, inner, outer, before, *rest):
    if final:
        out, tiles, grad_out, adj, pot, part, grad = rest
    else:
        edge_before, out, grad, adj, pot, part, sums = rest
        for y in range(rows):
            sums[y] = before[y]
        for s, y in ((0, 0), (1, rows - 1)):
            sums[y] = edge_before[s]
        before = sums
    lanes = adj.shape[2]
    for y in range(depth, rows - depth):
        adj[1 + y] = inner[y]
    for s, k, y in sides_of(rows):
        adj[1 + y] = outer[s, k]
    adj[0] = outer[0, 0]
    adj[1 + rows] = outer[1, 0]
    all_rows(rows, cols, nz, adj, mob, depth, chem, curve, swing, rate, before, pot, part, out,
             grad)
    if final:
        for y in range(rows):
            grad_out[pl.ds(y, nz, stride=rows), :] = fold(grad[y, pad : pad + cols, :].T, nz)
        for y in range(depth, rows - depth):
            tiles[pl.ds(y, lanes, stride=rows), :] = out[y, pad : pad + cols, :].T


def fold(value, nz):
    total = value[:nz]
    for frame in range(1, value.shape[0] // nz):
        total = total + value[frame * nz : (frame + 1) * nz]
    return total


def next_boundary(rows, cols, nz, final, mob, chem, curve, swing, inside, outer, from_a, from_b,
                  *rest):
    if final:
        tiles, out, halo, delta, result = rest
    else:
        ahead, rate, result, to_a, to_b, halo, delta, open_g = rest
    low, high = reach(cols)
    first, last = sent(cols)
    lanes = mob.shape[2]
    mask = face_mask(lanes, nz)
    to_next = a_is_next("gy", round_first)
    for got, side in ((from_a, jnp.where(to_next, 1, 0)), (from_b, jnp.where(to_next, 0, 1))):
        for k in range(2):
            halo[side, k, first:last, :] = got[k]
    for s in range(2):
        y, beyond = s * (rows - 1), s * (rows + 1) - 1
        for at, size in chunks(low, high):
            span = slice(at, at + size)
            diff = halo[s, 0, span, :] - outer[s, 0, span, :]
            both = mob[depth + beyond, span, :] + mob[depth + y, span, :]
            delta[s, span, :] = both * diff
        for at, size in chunks(low, high):
            span = slice(at, at + size)
            more = delta[s, span, :]
            diff = halo[s, 0, span, :] - outer[s, 0, span, :]
            pair = (chem[1 + beyond, span, :] - chem[1 + y, span, :]) * diff
            step_z = (up(more) - more) * mask
            lap = (
                (delta[s, at + 1 : at + size + 1, :] + delta[s, at - 1 : at + size - 1, :])
                + (halo[s, 1, span, :] - more)
                - 4.0 * more
                + (step_z - down(step_z))
            )
            result[s, 0, span, :] = (
                inside[y, span, :]
                + (swing[1 + y, span, :] * pair + curve[1 + y, span, :] * more)
                - grad_energy * lap
            )
            result[s, 1, span, :] = inside[1 + s * (rows - 3), span, :] - grad_energy * more
    if final:
        out[...] = tiles[...]
        for s, k, y in sides_of(rows):
            out[pl.ds(y, lanes, stride=rows), :] = result[s, k, pad : pad + cols, :].T
    else:
        send_rows(result, ahead, rate, to_a, to_b, open_g, cols, nz)


def call(kernel, outs, scratch, *operands, cost=0, far=False):
    if far:
        operands = [pltpu.with_memory_space_constraint(value, pltpu.HBM) for value in operands]
    space = pl.ANY if far else pltpu.VMEM
    return pl.pallas_call(
        kernel,
        out_shape=[jax.ShapeDtypeStruct(shape, f32) for shape in outs],
        in_specs=[pl.BlockSpec(memory_space=space)] * len(operands),
        out_specs=[pl.BlockSpec(memory_space=pltpu.VMEM)] * len(outs),
        scratch_shapes=[pltpu.VMEM(s, f32) if isinstance(s, tuple) else s for s in scratch],
        compiler_params=pltpu.CompilerParams(vmem_limit_bytes=vmem_limit),
        cost_estimate=pl.CostEstimate(
            flops=cost * 1_000_000, bytes_accessed=cost * 2_000_000, transcendentals=0
        ),
    )(*operands)


def swap(value_a, value_b, axis, first):
    count = lax.axis_size(axis)
    pairs_a = [(i, (i + 1 - 2 * ((i + first) % 2)) % count) for i in range(count)]
    pairs_b = [(i, (i - 1 + 2 * ((i + first) % 2)) % count) for i in range(count)]
    return lax.ppermute(value_a, axis, pairs_a), lax.ppermute(value_b, axis, pairs_b)


def shards(saved_conc, adjoint_end, rate_field):
    steps, frames, nz, rows, cols = saved_conc.shape
    lanes = frames * nz
    _, total = slots(steps)
    width = cols + 2 * pad
    flat = lanes * rows

    def field(count):
        return (count, width, lanes)

    both = (2, depth, width, lanes)
    edge = (2, cols + 8, lanes)
    open_g = (2, cols + 16, lanes)
    raw = [(steps, flat, cols), (flat, cols), (nz * rows, cols)]
    conc_raw, adj_raw, rate_raw, main_a, main_b = call(
        functools.partial(edge_kernel, steps, rows, cols, nz),
        raw + [((1 + steps) * depth * cols + cols // 2, lanes)] * 2,
        [pltpu.SemaphoreType.DMA((2 + steps,))],
        saved_conc.reshape(raw[0]), adjoint_end.reshape(raw[1]), rate_field.reshape(raw[2]),
        cost=2,
        far=True,
    )
    main_a, main_b = swap(main_a, main_b, "gy", main_first)
    conc_own, adj_own, rate_own, x_a, x_b = call(
        functools.partial(turn_kernel, steps, rows, cols, nz),
        [(steps, rows, cols, lanes), (rows, cols, lanes), (rows, cols, lanes)]
        + [(rows, total, lanes)] * 2,
        [],
        conc_raw, adj_raw, rate_raw,
        cost=1,
    )
    x_a, x_b = swap(x_a, x_b, "gx", x_first)
    x_low, x_high, corner_a, corner_b = call(
        functools.partial(corner_kernel, rows),
        [(rows, total, lanes)] * 2 + [(2, depth, total, lanes)] * 2,
        [],
        x_a, x_b,
    )
    corners = swap(corner_a, corner_b, "gy", round_first)
    corner_a, corner_b = corners if main_first == round_first else corners[::-1]

    conc, adj, rate, chem, curve, swing, inner, grad, ahead = call(
        functools.partial(first_interior, steps, rows, cols, nz),
        [field(rows + 2)] * 2 + [field(rows)] + [field(rows + 2)] * 3 + [field(rows)] * 2 + [both],
        [field(rows + 2)] * 2 + [field(rows)],
        conc_own, adj_own, rate_own, x_low, x_high,
        cost=3,
    )
    outer, edge_grad, to_a, to_b = call(
        functools.partial(first_boundary, steps, rows, cols, nz),
        [both, field(2), edge, edge],
        [both, both] + [field(2)] * 5 + [open_g],
        conc, adj, rate, chem, curve, swing, inner, grad, main_a, main_b, corner_b, corner_a, ahead,
        cost=2,
    )
    sums = (grad, edge_grad)
    for back in range(1, steps):
        adj_a, adj_b = swap(to_a, to_b, "gy", round_first)
        final = back == steps - 1
        fields = call(
            functools.partial(prepare_kernel, steps, rows, cols, nz, back),
            [field(rows + 2 * depth)] + [field(rows + 2)] * 3 + ([] if final else [both]),
            [field(rows + 2 * depth)],
            conc_own, main_a, main_b, x_low, x_high, corner_b, corner_a,
            cost=2,
        )
        fields, ahead = fields[:4], fields[4:]
        work = [field(rows + 2)] * 2 + [field(rows)] * 2
        if final:
            inner, tiles, grad = call(
                functools.partial(next_interior, rows, cols, nz, final),
                [field(rows), (flat, cols), (nz * rows, cols)],
                work,
                *fields, rate, inner, outer, *sums,
                cost=3,
            )
            (adj,) = call(
                functools.partial(next_boundary, rows, cols, nz, final),
                [(flat, cols)],
                [both, field(2), both],
                *fields, inner, outer, adj_a, adj_b, tiles,
                cost=1,
            )
        else:
            inner, grad = call(
                functools.partial(next_interior, rows, cols, nz, final),
                [field(rows)] * 2,
                work,
                *fields, rate, inner, outer, *sums,
                cost=3,
            )
            outer, to_a, to_b = call(
                functools.partial(next_boundary, rows, cols, nz, final),
                [both, edge, edge],
                [both, field(2), open_g],
                *fields, inner, outer, adj_a, adj_b, *ahead, rate,
                cost=1,
            )
            sums = (grad,)
    return adj.reshape(adjoint_end.shape), grad.reshape(rate_field.shape)


def solution(mesh):
    return jax.shard_map(
        shards,
        mesh=mesh,
        in_specs=(P(None, None, None, "gy", "gx"), P(None, None, "gy", "gx"), P(None, "gy", "gx")),
        out_specs=(P(None, None, "gy", "gx"), P(None, "gy", "gx")),
        check_vma=False,
    )
```

```python
import functools

import jax
import jax.numpy as jnp
from jax import lax
from jax.experimental import pallas as pl
from jax.experimental.pallas import tpu as pltpu
from jax.sharding import PartitionSpec as P

mix_energy = 2.5
grad_energy = 1.0
time_step = 0.1
diff_step = 0.03
bath_potential = 0.5

pad = 16
chunk = 72
depth = 2
x_first, main_first, round_first = 0, 0, 1
vmem_limit = 20 * 1024 * 1024
f32 = jnp.float32


def slots(steps):
    widths = [2 * steps] + [2 * steps - 2 * back for back in range(steps)] + [2 * steps - 1]
    starts = [sum(widths[:i]) for i in range(len(widths))]
    total = -(-sum(widths) // 8) * 8
    return list(zip(starts, widths)), total


def chunks(low, high):
    return [(at, min(chunk, high - at)) for at in range(low, high, chunk)]


def reach(cols):
    return pad - 8, pad + cols + 8


def sent(cols):
    return pad - 4, pad + cols + 4


def up(value):
    return pltpu.roll(value, value.shape[1] - 1, 1)


def down(value):
    return pltpu.roll(value, 1, 1)


def face_mask(lanes, nz):
    lane = lax.broadcasted_iota(jnp.int32, (1, lanes), 1)
    return jnp.where(lane % nz == nz - 1, 0.0, 1.0).astype(f32)


def row_of(ref, y):
    return lambda dy, cut: ref[y + dy, cut, :]


def laplace(field, at, size, mask):
    span = slice(at, at + size)
    here = field(0, span)
    step_z = (up(here) - here) * mask
    sides = field(0, slice(at + 1, at + size + 1)) + field(0, slice(at - 1, at + size - 1))
    return here, (
        (sides + (field(-1, span) + field(1, span))) - 4.0 * here + (step_z - down(step_z))
    )


def mobility(c):
    return (0.5 * diff_step) * c * (1.0 - c)


def chem_row(conc, chem, curve, swing, at, size, mask):
    c, lap = laplace(conc, at, size, mask)
    inv = 1.0 / (c * (1.0 - c))
    span = slice(at, at + size)
    chem(
        span,
        time_step * (jnp.log(c * c * inv) - grad_energy * lap)
        + (time_step * (mix_energy - bath_potential) - (2.0 * time_step * mix_energy) * c),
    )
    curve(span, inv - 2.0 * mix_energy)
    swing(span, c * (diff_step / time_step) - 0.5 * diff_step / time_step)


def face_sums(adj, mob, chem, at, size, mask, across=(1, -1)):
    span = slice(at, at + size)
    a = adj(0, span)
    m = None if mob is None else mob(0, span)
    mu = None if chem is None else chem(0, span)
    flow = pair = None
    for dy, cut in (
        (0, slice(at + 1, at + size + 1)),
        (0, slice(at - 1, at + size - 1)),
    ) + tuple((dy, span) for dy in across):
        diff = adj(dy, cut) - a
        if mob is not None:
            term = (mob(dy, cut) + m) * diff
            flow = term if flow is None else flow + term
        if chem is not None:
            term = (chem(dy, cut) - mu) * diff
            pair = term if pair is None else pair + term
    diff = (up(a) - a) * mask
    if mob is not None:
        term = (up(m) + m) * diff
        flow = flow + (term - down(term))
    if chem is not None:
        term = (up(mu) - mu) * diff
        pair = pair + (term + down(term))
    return a, mu, flow, pair


def partial(a, swing, pair, curve, g):
    return a + swing * pair + curve * g


def gain(a, chem, before):
    value = a * chem
    return -value if before is None else before - value


def set_row(ref, y):
    def put(span, value):
        ref[y, span, :] = value

    return put


def all_rows(rows, cols, nz, adj, mob, mob_skip, chem, curve, swing, rate, before, pot, part, out,
             grad):
    low, high = reach(cols)
    mask = face_mask(adj.shape[2], nz)

    def body(y, _):
        for at, size in chunks(low, high):
            span = slice(at, at + size)
            a, mu, flow, pair = face_sums(
                row_of(adj, y + 1), row_of(mob, y + mob_skip), row_of(chem, y + 1), at, size, mask
            )
            g = flow - rate[y, span, :] * a
            pot[y + 1, span, :] = g
            part[y, span, :] = partial(
                a, swing[y + 1, span, :], pair, curve[y + 1, span, :], g
            )
            grad[y, span, :] = gain(a, mu, None if before is None else before[y, span, :])
        return 0

    def close(y, _):
        for at, size in chunks(low, high):
            span = slice(at, at + size)
            _g, lap = laplace(row_of(pot, y + 1), at, size, mask)
            out[y, span, :] = part[y, span, :] - grad_energy * lap
        return 0

    for row in (0, rows + 1):
        pot[row] = jnp.zeros(pot.shape[1:], f32)
    lax.fori_loop(0, rows, body, 0)
    lax.fori_loop(0, rows, close, 0)


def a_is_next(axis, first):
    return lax.rem(lax.axis_index(axis), 2) == first


def bases(rows, first):
    to_next = a_is_next("gy", first)
    top = rows - depth
    return jnp.where(to_next, top, 0), jnp.where(to_next, 0, top)


def landings(rows, first):
    to_next = a_is_next("gy", first)
    top = rows + depth
    return jnp.where(to_next, top, 0), jnp.where(to_next, 0, top)


def sides_of(rows):
    return [(0, 0, 0), (0, 1, 1), (1, 0, rows - 1), (1, 1, rows - 2)]


def edge_kernel(steps, rows, cols, nz, conc_hbm, adj_hbm, rate_hbm, conc_in, adj_in, rate_in,
                main_a, main_b, sems):
    lanes = main_a.shape[1]
    half = cols // 2
    lower = lax.broadcasted_iota(jnp.int32, (half, lanes), 1) < nz
    copies = [
        pltpu.make_async_copy(adj_hbm, adj_in, sems.at[0]),
        pltpu.make_async_copy(rate_hbm, rate_in, sems.at[1]),
    ] + [
        pltpu.make_async_copy(conc_hbm.at[steps - 1 - back], conc_in.at[back], sems.at[2 + back])
        for back in range(steps)
    ]
    for copy in copies:
        copy.start()
    copies[0].wait()
    for side, base in zip((main_a, main_b), bases(rows, main_first)):
        for at in range(depth):
            side[pl.ds(at * cols, cols), :] = adj_in[pl.ds(base + at, lanes, stride=rows), :].T
    copies[1].wait()
    for side, base in zip((main_a, main_b), bases(rows, main_first)):
        edge = jnp.where(base == 0, 0, rows - 1)
        rate = turned_rate(rate_in, edge, rows, nz, lanes)
        side[pl.ds((1 + steps) * depth * cols, half), :] = jnp.where(
            lower, rate[:half], rate[half:]
        )
    for back in range(steps):
        copies[2 + back].wait()
        for side, base in zip((main_a, main_b), bases(rows, main_first)):
            for at in range(depth):
                side[pl.ds(((1 + back) * depth + at) * cols, cols), :] = conc_in[
                    back, pl.ds(base + at, lanes, stride=rows), :
                ].T


def turned_rate(rate, y, rows, nz, lanes):
    value = time_step * rate[pl.ds(y, nz, stride=rows), :]
    return jnp.concatenate([value] * (lanes // nz), axis=0).T


def turn_kernel(steps, rows, cols, nz, conc_in, adj_in, rate_in, conc_out, adj_out, rate_out,
                x_a, x_b):
    places, total = slots(steps)
    lanes = adj_out.shape[2]
    next_x = a_is_next("gx", x_first)

    def to_x(y, value, place):
        start, width = place
        last, first = value[cols - width :, :], value[:width, :]
        x_a[y, start : start + width, :] = jnp.where(next_x, last, first)
        x_b[y, start : start + width, :] = jnp.where(next_x, first, last)

    used = sum(places[-1])
    for y in range(rows):
        adj = adj_in[pl.ds(y, lanes, stride=rows), :].T
        adj_out[y] = adj
        to_x(y, adj, places[0])
        rate = turned_rate(rate_in, y, rows, nz, lanes)
        rate_out[y] = rate
        to_x(y, rate, places[steps + 1])
        if used < total:
            x_a[y, used:, :] = jnp.zeros((total - used, lanes), f32)
            x_b[y, used:, :] = jnp.zeros((total - used, lanes), f32)
        for back in range(steps):
            conc = conc_in[back, pl.ds(y, lanes, stride=rows), :].T
            conc_out[back, y] = conc
            to_x(y, conc, places[1 + back])


def put_own(out, row, value, y, place, cols, x_low, x_high):
    start, width = place
    right = pad + cols
    out[row, pad:right, :] = value
    out[row, pad - width : pad, :] = x_low[y, start : start + width, :]
    out[row, right : right + width, :] = x_high[y, start : start + width, :]


def put_halo(out, index, value, from_row, place, cols, corner):
    start, width = place
    right = pad + cols
    out[(*index, slice(pad, right))] = value
    out[(*index, slice(pad - width, pad))] = corner[0, from_row, start : start + width, :]
    out[(*index, slice(right, right + width))] = corner[1, from_row, start : start + width, :]


def corner_kernel(rows, got_a, got_b, _core, x_low, x_high, corner_a, corner_b):
    next_x = a_is_next("gx", x_first)
    x_low[...] = jnp.where(next_x, got_b[...], got_a[...])
    x_high[...] = jnp.where(next_x, got_a[...], got_b[...])
    for out, base in zip((corner_a, corner_b), bases(rows, round_first)):
        for at in range(depth):
            out[0, at] = x_low[base + at]
            out[1, at] = x_high[base + at]


def first_interior(steps, rows, cols, nz, conc_own, adj_own, rate_own, x_low, x_high,
                   conc, adj, rate, chem, curve, swing, out, grad, ahead, mob, pot, part):
    places, _ = slots(steps)
    low, high = reach(cols)
    lanes = adj.shape[2]
    mask = face_mask(lanes, nz)
    for y in range(rows):
        put_own(conc, 1 + y, conc_own[0, y], y, places[1], cols, x_low, x_high)
        put_own(adj, 1 + y, adj_own[y], y, places[0], cols, x_low, x_high)
        put_own(rate, y, rate_own[y], y, places[steps + 1], cols, x_low, x_high)
    for row, beside in ((0, 1), (rows + 1, rows)):
        adj[row] = adj[beside]
        for ref in (conc, chem, mob):
            ref[row] = jnp.zeros(ref.shape[1:], f32)
    put_ahead(ahead, conc_own, 1, x_low, x_high, places, rows, cols)

    def mob_row(row, _):
        for at, size in chunks(low - 8, high + 8):
            mob[row, at : at + size, :] = mobility(conc[row, at : at + size, :])
        return 0

    def mu_row(row, _):
        for at, size in chunks(low, high):
            chem_row(row_of(conc, row), set_row(chem, row), set_row(curve, row),
                     set_row(swing, row), at, size, mask)
        return 0

    lax.fori_loop(1, rows + 1, mob_row, 0)
    lax.fori_loop(1, rows + 1, mu_row, 0)
    all_rows(rows, cols, nz, adj, mob, 1, chem, curve, swing, rate, None, pot, part, out, grad)


def send_rows(out, ahead, rate, to_a, to_b, open_g, cols, nz):
    low, high = reach(cols)
    first, last = sent(cols)
    rows, lanes = rate.shape[0], rate.shape[2]
    mask = face_mask(lanes, nz)
    for s in range(2):
        for at, size in chunks(low, high):
            a, _mu, flow, _pair = face_sums(
                lambda dy, cut: out[s, dy, cut, :], lambda dy, cut: ahead[s, dy, cut, :], None,
                at, size, mask, (1,)
            )
            open_g[s, at - low : at - low + size, :] = (
                flow - rate[s * (rows - 1), at : at + size, :] * a
            )
    to_next = a_is_next("gy", round_first)
    for to, side in ((to_a, jnp.where(to_next, 1, 0)), (to_b, jnp.where(to_next, 0, 1))):
        to[0] = out[side, 0, first:last, :]
        to[1] = open_g[side, first - low : last - low, :]


def put_ahead(ahead, conc_own, back, x_low, x_high, places, rows, cols):
    for s, k, y in sides_of(rows):
        put_own(ahead.at[s], k, conc_own[back, y], y, places[1 + back], cols, x_low, x_high)
        ahead[s, k] = mobility(ahead[s, k])


def first_boundary(steps, rows, cols, nz, conc, adj, rate, chem, curve, swing, inside, grad,
                   from_a, from_b, corner_b, corner_a, ahead,
                   out, edge_grad, to_a, to_b, far_conc, far_adj, far_rate, far_mob, far_chem,
                   far_pot, delta, open_g):
    places, _ = slots(steps)
    low, high = reach(cols)
    half = cols // 2
    lanes = conc.shape[2]
    mask = face_mask(lanes, nz)
    lower = lax.broadcasted_iota(jnp.int32, (half, lanes), 1) < nz
    to_next = a_is_next("gy", main_first)

    def unpack(side):
        packed = side[pl.ds((1 + steps) * depth * cols, half), :]
        turned = pltpu.roll(packed, lanes // 2, 1)
        return jnp.concatenate(
            [jnp.where(lower, packed, turned), jnp.where(lower, turned, packed)], axis=0
        )

    for halo, corner, side in (
        (from_a, corner_a, jnp.where(to_next, 1, 0)),
        (from_b, corner_b, jnp.where(to_next, 0, 1)),
    ):
        for at in range(depth):
            step = jnp.where(side == 1, at, depth - 1 - at)
            for ref, place, first in ((far_adj, places[0], 0), (far_conc, places[1], depth)):
                span = pl.ds((first + at) * cols, cols)
                put_halo(ref, (side, step), halo[span, :], at, place, cols, corner)
        put_halo(far_rate, (side,), unpack(halo), jnp.where(side == 1, 0, depth - 1),
                 places[steps + 1], cols, corner)

    share = time_step * grad_energy
    for s in range(2):
        y, y1 = s * (rows - 1), 1 + s * (rows - 3)
        for at, size in chunks(low - 8, high + 8):
            span = slice(at, at + size)
            far_mob[s, span, :] = mobility(far_conc[s, 0, span, :])

        def conc_at(dy, cut):
            return conc[1 + y, cut, :] if dy == 1 else far_conc[s, -dy, cut, :]

        def adj_at(dy, cut):
            return adj[1 + y, cut, :] if dy == 1 else far_adj[s, -dy, cut, :]

        def mob_at(dy, cut):
            return far_mob[s, cut, :] if dy == 0 else mobility(conc_at(dy, cut))

        for at, size in chunks(low, high):
            span = slice(at, at + size)
            chem_row(conc_at, set_row(far_chem, s), lambda *_: None, lambda *_: None, at, size,
                     mask)
            a, _mu, flow, _pair = face_sums(adj_at, mob_at, None, at, size, mask)
            far_pot[s, span, :] = flow - far_rate[s, span, :] * a
            diff = a - adj[1 + y, span, :]
            delta[s, span, :] = (far_mob[s, span, :] + mobility(conc[1 + y, span, :])) * diff
        for at, size in chunks(low, high):
            span = slice(at, at + size)
            a, c, _flow, spread = face_sums(
                lambda dy, cut: adj[1 + y, cut, :], None, lambda dy, cut: far_conc[s, 0, cut, :],
                at, size, mask, ()
            )
            less = share * c
            inward = less * (adj[1 + y1, span, :] - a)
            pair = (far_chem[s, span, :] - (chem[1 + y, span, :] - less)) * (
                far_adj[s, 0, span, :] - a
            ) + (inward - share * spread)
            more = delta[s, span, :]
            step_z = (up(more) - more) * mask
            lap = (
                (delta[s, at + 1 : at + size + 1, :] + delta[s, at - 1 : at + size - 1, :])
                + (far_pot[s, span, :] - 4.0 * more)
                + (step_z - down(step_z))
            )
            out[s, 0, span, :] = (
                inside[y, span, :]
                + (swing[1 + y, span, :] * pair + curve[1 + y, span, :] * more)
                - grad_energy * lap
            )
            out[s, 1, span, :] = (
                inside[y1, span, :] + swing[1 + y1, span, :] * inward - grad_energy * more
            )
            edge_grad[s, span, :] = grad[y, span, :] + less * a
    send_rows(out, ahead, rate, to_a, to_b, open_g, cols, nz)


def core_kernel(steps, rows, cols, nz, conc_own, mob, chem, curve, swing, conc):
    lanes = conc.shape[2]
    mask = face_mask(lanes, nz)
    own = pad, pad + cols
    for row in (0, rows + 1):
        conc[row] = jnp.zeros(conc.shape[1:], f32)
    for i in range(steps - 1):
        for y in range(rows):
            conc[1 + y, pad : pad + cols, :] = conc_own[1 + i, y]

        def row(y, _):
            for at, size in chunks(*own):
                mob[i, y, at : at + size, :] = mobility(conc[1 + y, at : at + size, :])
                chem_row(row_of(conc, 1 + y), set_row(chem.at[i], y), set_row(curve.at[i], y),
                         set_row(swing.at[i], y), at, size, mask)
            return 0

        lax.fori_loop(0, rows, row, 0)


def prepare_kernel(steps, rows, cols, nz, back, conc_own, from_a, from_b, x_low, x_high,
                   corner_b, corner_a, mob_core, chem_core, curve_core, swing_core,
                   mob, chem, curve, swing, *rest):
    *ahead, conc = rest
    places, _ = slots(steps)
    low, high = reach(cols)
    lanes = conc.shape[2]
    mask = face_mask(lanes, nz)
    place = places[1 + back]
    own = slice(pad, pad + cols)
    for y in range(rows):
        put_own(conc, depth + y, conc_own[back, y], y, place, cols, x_low, x_high)
        mob[depth + y, own, :] = mob_core[back - 1, y, own, :]
        chem[1 + y, own, :] = chem_core[back - 1, y, own, :]
        curve[1 + y, own, :] = curve_core[back - 1, y, own, :]
        swing[1 + y, own, :] = swing_core[back - 1, y, own, :]
    for halo, corner, base in zip((from_a, from_b), (corner_a, corner_b), landings(rows, main_first)):
        for at in range(depth):
            span = pl.ds(((1 + back) * depth + at) * cols, cols)
            put_halo(conc, (base + at,), halo[span, :], at, place, cols, corner)

    if ahead:
        put_ahead(ahead[0], conc_own, back + 1, x_low, x_high, places, rows, cols)

    def rim_row(y, _):
        for at in (low - 8, pad + cols):
            span = slice(at, at + 16)
            mob[depth + y, span, :] = mobility(conc[depth + y, span, :])
        for at in (low, pad + cols - 8):
            chem_row(row_of(conc, depth + y), set_row(chem, 1 + y), set_row(curve, 1 + y),
                     set_row(swing, 1 + y), at, 16, mask)
        return 0

    lax.fori_loop(0, rows, rim_row, 0)
    for y, beyond in ((0, -1), (rows - 1, rows)):
        inner = slice(pad + 8, pad + cols - 8)
        chem[1 + y, inner, :] = chem[1 + y, inner, :] - (time_step * grad_energy) * (
            conc[depth + beyond, inner, :]
        )

    def far_row(s, _):
        y = s * (rows + 1) - 1
        for at, size in chunks(low - 8, high + 8):
            mob[depth + y, at : at + size, :] = mobility(conc[depth + y, at : at + size, :])
        for at, size in chunks(low, high):
            chem_row(row_of(conc, depth + y), set_row(chem, 1 + y), lambda *_: None,
                     lambda *_: None, at, size, mask)
        return 0

    lax.fori_loop(0, 2, far_row, 0)


def next_interior(rows, cols, nz, final, mob, chem, curve, swing, rate, inner, outer, before, *rest):
    if final:
        out, tiles, grad_out, adj, pot, part, grad = rest
    else:
        edge_before, out, grad, adj, pot, part, sums = rest
        for y in range(rows):
            sums[y] = before[y]
        for s, y in ((0, 0), (1, rows - 1)):
            sums[y] = edge_before[s]
        before = sums
    lanes = adj.shape[2]
    for y in range(depth, rows - depth):
        adj[1 + y] = inner[y]
    for s, k, y in sides_of(rows):
        adj[1 + y] = outer[s, k]
    adj[0] = outer[0, 0]
    adj[1 + rows] = outer[1, 0]
    all_rows(rows, cols, nz, adj, mob, depth, chem, curve, swing, rate, before, pot, part, out,
             grad)
    if final:
        for y in range(rows):
            grad_out[pl.ds(y, nz, stride=rows), :] = fold(grad[y, pad : pad + cols, :].T, nz)
        for y in range(depth, rows - depth):
            tiles[pl.ds(y, lanes, stride=rows), :] = out[y, pad : pad + cols, :].T


def fold(value, nz):
    total = value[:nz]
    for frame in range(1, value.shape[0] // nz):
        total = total + value[frame * nz : (frame + 1) * nz]
    return total


def next_boundary(rows, cols, nz, final, mob, chem, curve, swing, inside, outer, from_a, from_b,
                  *rest):
    if final:
        tiles, out, halo, delta, result = rest
    else:
        ahead, rate, result, to_a, to_b, halo, delta, open_g = rest
    low, high = reach(cols)
    first, last = sent(cols)
    lanes = mob.shape[2]
    mask = face_mask(lanes, nz)
    to_next = a_is_next("gy", round_first)
    for got, side in ((from_a, jnp.where(to_next, 1, 0)), (from_b, jnp.where(to_next, 0, 1))):
        for k in range(2):
            halo[side, k, first:last, :] = got[k]
    for s in range(2):
        y, beyond = s * (rows - 1), s * (rows + 1) - 1
        for at, size in chunks(low, high):
            span = slice(at, at + size)
            diff = halo[s, 0, span, :] - outer[s, 0, span, :]
            both = mob[depth + beyond, span, :] + mob[depth + y, span, :]
            delta[s, span, :] = both * diff
        for at, size in chunks(low, high):
            span = slice(at, at + size)
            more = delta[s, span, :]
            diff = halo[s, 0, span, :] - outer[s, 0, span, :]
            pair = (chem[1 + beyond, span, :] - chem[1 + y, span, :]) * diff
            step_z = (up(more) - more) * mask
            lap = (
                (delta[s, at + 1 : at + size + 1, :] + delta[s, at - 1 : at + size - 1, :])
                + (halo[s, 1, span, :] - more)
                - 4.0 * more
                + (step_z - down(step_z))
            )
            result[s, 0, span, :] = (
                inside[y, span, :]
                + (swing[1 + y, span, :] * pair + curve[1 + y, span, :] * more)
                - grad_energy * lap
            )
            result[s, 1, span, :] = inside[1 + s * (rows - 3), span, :] - grad_energy * more
    if final:
        out[...] = tiles[...]
        for s, k, y in sides_of(rows):
            out[pl.ds(y, lanes, stride=rows), :] = result[s, k, pad : pad + cols, :].T
    else:
        send_rows(result, ahead, rate, to_a, to_b, open_g, cols, nz)


def call(kernel, outs, scratch, *operands, cost=0, far=False):
    if far:
        operands = [pltpu.with_memory_space_constraint(value, pltpu.HBM) for value in operands]
    space = pl.ANY if far else pltpu.VMEM
    return pl.pallas_call(
        kernel,
        out_shape=[jax.ShapeDtypeStruct(shape, f32) for shape in outs],
        in_specs=[pl.BlockSpec(memory_space=space)] * len(operands),
        out_specs=[pl.BlockSpec(memory_space=pltpu.VMEM)] * len(outs),
        scratch_shapes=[pltpu.VMEM(s, f32) if isinstance(s, tuple) else s for s in scratch],
        compiler_params=pltpu.CompilerParams(vmem_limit_bytes=vmem_limit),
        cost_estimate=pl.CostEstimate(
            flops=cost * 1_000_000, bytes_accessed=cost * 2_000_000, transcendentals=0
        ),
    )(*operands)


def swap(value_a, value_b, axis, first):
    count = lax.axis_size(axis)
    pairs_a = [(i, (i + 1 - 2 * ((i + first) % 2)) % count) for i in range(count)]
    pairs_b = [(i, (i - 1 + 2 * ((i + first) % 2)) % count) for i in range(count)]
    return lax.ppermute(value_a, axis, pairs_a), lax.ppermute(value_b, axis, pairs_b)


def shards(saved_conc, adjoint_end, rate_field):
    steps, frames, nz, rows, cols = saved_conc.shape
    lanes = frames * nz
    _, total = slots(steps)
    width = cols + 2 * pad
    flat = lanes * rows

    def field(count):
        return (count, width, lanes)

    both = (2, depth, width, lanes)
    edge = (2, cols + 8, lanes)
    open_g = (2, cols + 16, lanes)
    raw = [(steps, flat, cols), (flat, cols), (nz * rows, cols)]
    conc_raw, adj_raw, rate_raw, main_a, main_b = call(
        functools.partial(edge_kernel, steps, rows, cols, nz),
        raw + [((1 + steps) * depth * cols + cols // 2, lanes)] * 2,
        [pltpu.SemaphoreType.DMA((2 + steps,))],
        saved_conc.reshape(raw[0]), adjoint_end.reshape(raw[1]), rate_field.reshape(raw[2]),
        cost=2,
        far=True,
    )
    main_a, main_b = swap(main_a, main_b, "gy", main_first)
    conc_own, adj_own, rate_own, x_a, x_b = call(
        functools.partial(turn_kernel, steps, rows, cols, nz),
        [(steps, rows, cols, lanes), (rows, cols, lanes), (rows, cols, lanes)]
        + [(rows, total, lanes)] * 2,
        [],
        conc_raw, adj_raw, rate_raw,
        cost=1,
    )
    x_a, x_b = swap(x_a, x_b, "gx", x_first)
    whole = (steps - 1, rows, width, lanes)
    core = call(
        functools.partial(core_kernel, steps, rows, cols, nz),
        [whole] * 4,
        [field(rows + 2)],
        conc_own,
        cost=2,
    )
    x_low, x_high, corner_a, corner_b = call(
        functools.partial(corner_kernel, rows),
        [(rows, total, lanes)] * 2 + [(2, depth, total, lanes)] * 2,
        [],
        x_a, x_b, core[1],
    )
    corners = swap(corner_a, corner_b, "gy", round_first)
    corner_a, corner_b = corners if main_first == round_first else corners[::-1]

    conc, adj, rate, chem, curve, swing, inner, grad, ahead = call(
        functools.partial(first_interior, steps, rows, cols, nz),
        [field(rows + 2)] * 2 + [field(rows)] + [field(rows + 2)] * 3 + [field(rows)] * 2 + [both],
        [field(rows + 2)] * 2 + [field(rows)],
        conc_own, adj_own, rate_own, x_low, x_high,
        cost=3,
    )
    outer, edge_grad, to_a, to_b = call(
        functools.partial(first_boundary, steps, rows, cols, nz),
        [both, field(2), edge, edge],
        [both, both] + [field(2)] * 5 + [open_g],
        conc, adj, rate, chem, curve, swing, inner, grad, main_a, main_b, corner_b, corner_a, ahead,
        cost=2,
    )
    sums = (grad, edge_grad)
    for back in range(1, steps):
        adj_a, adj_b = swap(to_a, to_b, "gy", round_first)
        final = back == steps - 1
        fields = call(
            functools.partial(prepare_kernel, steps, rows, cols, nz, back),
            [field(rows + 2 * depth)] + [field(rows + 2)] * 3 + ([] if final else [both]),
            [field(rows + 2 * depth)],
            conc_own, main_a, main_b, x_low, x_high, corner_b, corner_a, *core,
            cost=2,
        )
        fields, ahead = fields[:4], fields[4:]
        work = [field(rows + 2)] * 2 + [field(rows)] * 2
        if final:
            inner, tiles, grad = call(
                functools.partial(next_interior, rows, cols, nz, final),
                [field(rows), (flat, cols), (nz * rows, cols)],
                work,
                *fields, rate, inner, outer, *sums,
                cost=3,
            )
            (adj,) = call(
                functools.partial(next_boundary, rows, cols, nz, final),
                [(flat, cols)],
                [both, field(2), both],
                *fields, inner, outer, adj_a, adj_b, tiles,
                cost=1,
            )
        else:
            inner, grad = call(
                functools.partial(next_interior, rows, cols, nz, final),
                [field(rows)] * 2,
                work,
                *fields, rate, inner, outer, *sums,
                cost=3,
            )
            outer, to_a, to_b = call(
                functools.partial(next_boundary, rows, cols, nz, final),
                [both, edge, edge],
                [both, field(2), open_g],
                *fields, inner, outer, adj_a, adj_b, *ahead, rate,
                cost=1,
            )
            sums = (grad,)
    return adj.reshape(adjoint_end.shape), grad.reshape(rate_field.shape)


def solution(mesh):
    return jax.shard_map(
        shards,
        mesh=mesh,
        in_specs=(P(None, None, None, "gy", "gx"), P(None, None, "gy", "gx"), P(None, "gy", "gx")),
        out_specs=(P(None, None, "gy", "gx"), P(None, "gy", "gx")),
        check_vma=False,
    )
```

```python
import functools

import jax
import jax.numpy as jnp
from jax import lax
from jax.experimental import pallas as pl
from jax.experimental.pallas import tpu as pltpu
from jax.sharding import PartitionSpec as P

mix_energy = 2.5
grad_energy = 1.0
time_step = 0.1
diff_step = 0.03
bath_potential = 0.5

pad = 16
chunk = 72
depth = 2
x_first, main_first, round_first = 0, 0, 1
vmem_limit = 20 * 1024 * 1024
f32 = jnp.float32


def slots(steps):
    widths = [2 * steps] + [2 * steps - 2 * back for back in range(steps)] + [2 * steps - 1]
    starts = [sum(widths[:i]) for i in range(len(widths))]
    total = -(-sum(widths) // 8) * 8
    return list(zip(starts, widths)), total


def chunks(low, high):
    return [(at, min(chunk, high - at)) for at in range(low, high, chunk)]


def reach(cols):
    return pad - 8, pad + cols + 8


def sent(cols):
    return pad - 4, pad + cols + 4


def up(value):
    return pltpu.roll(value, value.shape[1] - 1, 1)


def down(value):
    return pltpu.roll(value, 1, 1)


def face_mask(lanes, nz):
    lane = lax.broadcasted_iota(jnp.int32, (1, lanes), 1)
    return jnp.where(lane % nz == nz - 1, 0.0, 1.0).astype(f32)


def row_of(ref, y):
    return lambda dy, cut: ref[y + dy, cut, :]


def laplace(field, at, size, mask):
    span = slice(at, at + size)
    here = field(0, span)
    step_z = (up(here) - here) * mask
    sides = field(0, slice(at + 1, at + size + 1)) + field(0, slice(at - 1, at + size - 1))
    return here, (
        (sides + (field(-1, span) + field(1, span))) - 4.0 * here + (step_z - down(step_z))
    )


def mobility(c):
    return (0.5 * diff_step) * c * (1.0 - c)


def chem_row(conc, chem, curve, swing, at, size, mask):
    c, lap = laplace(conc, at, size, mask)
    inv = 1.0 / (c * (1.0 - c))
    span = slice(at, at + size)
    chem(
        span,
        time_step * (jnp.log(c * c * inv) - grad_energy * lap)
        + (time_step * (mix_energy - bath_potential) - (2.0 * time_step * mix_energy) * c),
    )
    curve(span, inv - 2.0 * mix_energy)
    swing(span, c * (diff_step / time_step) - 0.5 * diff_step / time_step)


def face_sums(adj, mob, chem, at, size, mask, across=(1, -1)):
    span = slice(at, at + size)
    a = adj(0, span)
    m = None if mob is None else mob(0, span)
    mu = None if chem is None else chem(0, span)
    flow = pair = None
    for dy, cut in (
        (0, slice(at + 1, at + size + 1)),
        (0, slice(at - 1, at + size - 1)),
    ) + tuple((dy, span) for dy in across):
        diff = adj(dy, cut) - a
        if mob is not None:
            term = (mob(dy, cut) + m) * diff
            flow = term if flow is None else flow + term
        if chem is not None:
            term = (chem(dy, cut) - mu) * diff
            pair = term if pair is None else pair + term
    diff = (up(a) - a) * mask
    if mob is not None:
        term = (up(m) + m) * diff
        flow = flow + (term - down(term))
    if chem is not None:
        term = (up(mu) - mu) * diff
        pair = pair + (term + down(term))
    return a, mu, flow, pair


def partial(a, swing, pair, curve, g):
    return a + swing * pair + curve * g


def gain(a, chem, before):
    value = a * chem
    return -value if before is None else before - value


def set_row(ref, y):
    def put(span, value):
        ref[y, span, :] = value

    return put


def all_rows(rows, cols, nz, adj, mob, mob_skip, chem, curve, swing, rate, before, pot, part, out,
             grad, between=None):
    low, high = reach(cols)
    mask = face_mask(adj.shape[2], nz)

    def body(y, _):
        for at, size in chunks(low, high):
            span = slice(at, at + size)
            a, mu, flow, pair = face_sums(
                row_of(adj, y + 1), row_of(mob, y + mob_skip), row_of(chem, y + 1), at, size, mask
            )
            g = flow - rate[y, span, :] * a
            pot[y + 1, span, :] = g
            part[y, span, :] = partial(
                a, swing[y + 1, span, :], pair, curve[y + 1, span, :], g
            )
            grad[y, span, :] = gain(a, mu, None if before is None else before[y, span, :])
        return 0

    def close(y, _):
        for at, size in chunks(low, high):
            span = slice(at, at + size)
            _g, lap = laplace(row_of(pot, y + 1), at, size, mask)
            out[y, span, :] = part[y, span, :] - grad_energy * lap
        return 0

    for row in (0, rows + 1):
        pot[row] = jnp.zeros(pot.shape[1:], f32)
    lax.fori_loop(0, rows, body, 0, unroll=2)
    if between is not None:
        between()
    lax.fori_loop(0, rows, close, 0, unroll=4)


def a_is_next(axis, first):
    return lax.rem(lax.axis_index(axis), 2) == first


def bases(rows, first):
    to_next = a_is_next("gy", first)
    top = rows - depth
    return jnp.where(to_next, top, 0), jnp.where(to_next, 0, top)


def landings(rows, first):
    to_next = a_is_next("gy", first)
    top = rows + depth
    return jnp.where(to_next, top, 0), jnp.where(to_next, 0, top)


def sides_of(rows):
    return [(0, 0, 0), (0, 1, 1), (1, 0, rows - 1), (1, 1, rows - 2)]


def edge_kernel(steps, rows, cols, nz, conc_hbm, adj_hbm, rate_hbm, conc_in, adj_in, rate_in,
                main_a, main_b, sems):
    lanes = main_a.shape[1]
    half = cols // 2
    lower = lax.broadcasted_iota(jnp.int32, (half, lanes), 1) < nz
    copies = [
        pltpu.make_async_copy(adj_hbm, adj_in, sems.at[0]),
        pltpu.make_async_copy(rate_hbm, rate_in, sems.at[1]),
    ] + [
        pltpu.make_async_copy(conc_hbm.at[steps - 1 - back], conc_in.at[back], sems.at[2 + back])
        for back in range(steps)
    ]
    for copy in copies:
        copy.start()
    copies[0].wait()
    for side, base in zip((main_a, main_b), bases(rows, main_first)):
        for at in range(depth):
            side[pl.ds(at * cols, cols), :] = adj_in[pl.ds(base + at, lanes, stride=rows), :].T
    copies[1].wait()
    for side, base in zip((main_a, main_b), bases(rows, main_first)):
        edge = jnp.where(base == 0, 0, rows - 1)
        rate = turned_rate(rate_in, edge, rows, nz, lanes)
        side[pl.ds((1 + steps) * depth * cols, half), :] = jnp.where(
            lower, rate[:half], rate[half:]
        )
    for back in range(steps):
        copies[2 + back].wait()
        for side, base in zip((main_a, main_b), bases(rows, main_first)):
            for at in range(depth):
                side[pl.ds(((1 + back) * depth + at) * cols, cols), :] = conc_in[
                    back, pl.ds(base + at, lanes, stride=rows), :
                ].T


def turned_rate(rate, y, rows, nz, lanes):
    value = time_step * rate[pl.ds(y, nz, stride=rows), :]
    return jnp.concatenate([value] * (lanes // nz), axis=0).T


def turn_kernel(steps, rows, cols, nz, conc_in, adj_in, rate_in, conc_out, adj_out, rate_out,
                x_a, x_b):
    places, total = slots(steps)
    lanes = adj_out.shape[2]
    next_x = a_is_next("gx", x_first)

    def to_x(y, value, place):
        start, width = place
        last, first = value[cols - width :, :], value[:width, :]
        x_a[y, start : start + width, :] = jnp.where(next_x, last, first)
        x_b[y, start : start + width, :] = jnp.where(next_x, first, last)

    used = sum(places[-1])
    for y in range(rows):
        adj = adj_in[pl.ds(y, lanes, stride=rows), :].T
        adj_out[y] = adj
        to_x(y, adj, places[0])
        rate = turned_rate(rate_in, y, rows, nz, lanes)
        rate_out[y] = rate
        to_x(y, rate, places[steps + 1])
        if used < total:
            x_a[y, used:, :] = jnp.zeros((total - used, lanes), f32)
            x_b[y, used:, :] = jnp.zeros((total - used, lanes), f32)
        for back in range(steps):
            conc = conc_in[back, pl.ds(y, lanes, stride=rows), :].T
            conc_out[back, y] = conc
            to_x(y, conc, places[1 + back])


def put_own(out, row, value, y, place, cols, x_low, x_high):
    start, width = place
    right = pad + cols
    out[row, pad:right, :] = value
    out[row, pad - width : pad, :] = x_low[y, start : start + width, :]
    out[row, right : right + width, :] = x_high[y, start : start + width, :]


def put_halo(out, index, value, from_row, place, cols, corner):
    start, width = place
    right = pad + cols
    out[(*index, slice(pad, right))] = value
    out[(*index, slice(pad - width, pad))] = corner[0, from_row, start : start + width, :]
    out[(*index, slice(right, right + width))] = corner[1, from_row, start : start + width, :]


def corner_kernel(rows, got_a, got_b, _core, x_low, x_high, corner_a, corner_b):
    next_x = a_is_next("gx", x_first)
    x_low[...] = jnp.where(next_x, got_b[...], got_a[...])
    x_high[...] = jnp.where(next_x, got_a[...], got_b[...])
    for out, base in zip((corner_a, corner_b), bases(rows, round_first)):
        for at in range(depth):
            out[0, at] = x_low[base + at]
            out[1, at] = x_high[base + at]


def first_interior(steps, rows, cols, nz, conc_own, adj_own, rate_own, x_low, x_high,
                   conc, adj, rate, chem, curve, swing, out, grad, ahead, mob, pot, part):
    places, _ = slots(steps)
    low, high = reach(cols)
    lanes = adj.shape[2]
    mask = face_mask(lanes, nz)
    for y in range(rows):
        put_own(conc, 1 + y, conc_own[0, y], y, places[1], cols, x_low, x_high)
        put_own(adj, 1 + y, adj_own[y], y, places[0], cols, x_low, x_high)
        put_own(rate, y, rate_own[y], y, places[steps + 1], cols, x_low, x_high)
    for row, beside in ((0, 1), (rows + 1, rows)):
        adj[row] = adj[beside]
        for ref in (conc, chem, mob):
            ref[row] = jnp.zeros(ref.shape[1:], f32)
    put_ahead(ahead, conc_own, 1, x_low, x_high, places, rows, cols)

    def mob_row(row, _):
        for at, size in chunks(low - 8, high + 8):
            mob[row, at : at + size, :] = mobility(conc[row, at : at + size, :])
        return 0

    def mu_row(row, _):
        for at, size in chunks(low, high):
            chem_row(row_of(conc, row), set_row(chem, row), set_row(curve, row),
                     set_row(swing, row), at, size, mask)
        return 0

    lax.fori_loop(1, rows + 1, mob_row, 0, unroll=4)
    lax.fori_loop(1, rows + 1, mu_row, 0, unroll=2)
    all_rows(rows, cols, nz, adj, mob, 1, chem, curve, swing, rate, None, pot, part, out, grad)


def send_rows(out, ahead, rate, to_a, to_b, open_g, cols, nz):
    low, high = reach(cols)
    first, last = sent(cols)
    rows, lanes = rate.shape[0], rate.shape[2]
    mask = face_mask(lanes, nz)
    for s in range(2):
        for at, size in chunks(low, high):
            a, _mu, flow, _pair = face_sums(
                lambda dy, cut: out[s, dy, cut, :], lambda dy, cut: ahead[s, dy, cut, :], None,
                at, size, mask, (1,)
            )
            open_g[s, at - low : at - low + size, :] = (
                flow - rate[s * (rows - 1), at : at + size, :] * a
            )
    to_next = a_is_next("gy", round_first)
    for to, side in ((to_a, jnp.where(to_next, 1, 0)), (to_b, jnp.where(to_next, 0, 1))):
        to[0] = out[side, 0, first:last, :]
        to[1] = open_g[side, first - low : last - low, :]


def put_ahead(ahead, conc_own, back, x_low, x_high, places, rows, cols):
    for s, k, y in sides_of(rows):
        put_own(ahead.at[s], k, conc_own[back, y], y, places[1 + back], cols, x_low, x_high)
        ahead[s, k] = mobility(ahead[s, k])


def first_boundary(steps, rows, cols, nz, conc, adj, rate, chem, curve, swing, inside, grad,
                   from_a, from_b, corner_b, corner_a, ahead,
                   out, edge_grad, to_a, to_b, far_conc, far_adj, far_rate, far_mob, far_chem,
                   far_pot, delta, open_g):
    places, _ = slots(steps)
    low, high = reach(cols)
    half = cols // 2
    lanes = conc.shape[2]
    mask = face_mask(lanes, nz)
    lower = lax.broadcasted_iota(jnp.int32, (half, lanes), 1) < nz
    to_next = a_is_next("gy", main_first)

    def unpack(side):
        packed = side[pl.ds((1 + steps) * depth * cols, half), :]
        turned = pltpu.roll(packed, lanes // 2, 1)
        return jnp.concatenate(
            [jnp.where(lower, packed, turned), jnp.where(lower, turned, packed)], axis=0
        )

    for halo, corner, side in (
        (from_a, corner_a, jnp.where(to_next, 1, 0)),
        (from_b, corner_b, jnp.where(to_next, 0, 1)),
    ):
        for at in range(depth):
            step = jnp.where(side == 1, at, depth - 1 - at)
            for ref, place, first in ((far_adj, places[0], 0), (far_conc, places[1], depth)):
                span = pl.ds((first + at) * cols, cols)
                put_halo(ref, (side, step), halo[span, :], at, place, cols, corner)
        put_halo(far_rate, (side,), unpack(halo), jnp.where(side == 1, 0, depth - 1),
                 places[steps + 1], cols, corner)

    share = time_step * grad_energy
    for s in range(2):
        y, y1 = s * (rows - 1), 1 + s * (rows - 3)
        for at, size in chunks(low - 8, high + 8):
            span = slice(at, at + size)
            far_mob[s, span, :] = mobility(far_conc[s, 0, span, :])

        def conc_at(dy, cut):
            return conc[1 + y, cut, :] if dy == 1 else far_conc[s, -dy, cut, :]

        def adj_at(dy, cut):
            return adj[1 + y, cut, :] if dy == 1 else far_adj[s, -dy, cut, :]

        def mob_at(dy, cut):
            return far_mob[s, cut, :] if dy == 0 else mobility(conc_at(dy, cut))

        for at, size in chunks(low, high):
            span = slice(at, at + size)
            chem_row(conc_at, set_row(far_chem, s), lambda *_: None, lambda *_: None, at, size,
                     mask)
            a, _mu, flow, _pair = face_sums(adj_at, mob_at, None, at, size, mask)
            far_pot[s, span, :] = flow - far_rate[s, span, :] * a
            diff = a - adj[1 + y, span, :]
            delta[s, span, :] = (far_mob[s, span, :] + mobility(conc[1 + y, span, :])) * diff
        for at, size in chunks(low, high):
            span = slice(at, at + size)
            a, c, _flow, spread = face_sums(
                lambda dy, cut: adj[1 + y, cut, :], None, lambda dy, cut: far_conc[s, 0, cut, :],
                at, size, mask, ()
            )
            less = share * c
            inward = less * (adj[1 + y1, span, :] - a)
            pair = (far_chem[s, span, :] - (chem[1 + y, span, :] - less)) * (
                far_adj[s, 0, span, :] - a
            ) + (inward - share * spread)
            more = delta[s, span, :]
            step_z = (up(more) - more) * mask
            lap = (
                (delta[s, at + 1 : at + size + 1, :] + delta[s, at - 1 : at + size - 1, :])
                + (far_pot[s, span, :] - 4.0 * more)
                + (step_z - down(step_z))
            )
            out[s, 0, span, :] = (
                inside[y, span, :]
                + (swing[1 + y, span, :] * pair + curve[1 + y, span, :] * more)
                - grad_energy * lap
            )
            out[s, 1, span, :] = (
                inside[y1, span, :] + swing[1 + y1, span, :] * inward - grad_energy * more
            )
            edge_grad[s, span, :] = grad[y, span, :] + less * a
    send_rows(out, ahead, rate, to_a, to_b, open_g, cols, nz)


def core_kernel(steps, rows, cols, nz, conc_own, mob, chem, curve, swing, conc):
    lanes = conc.shape[2]
    mask = face_mask(lanes, nz)
    own = pad, pad + cols
    for row in (0, rows + 1):
        conc[row] = jnp.zeros(conc.shape[1:], f32)
    for i in range(steps - 1):
        for y in range(rows):
            conc[1 + y, pad : pad + cols, :] = conc_own[1 + i, y]

        def row(y, _):
            for at, size in chunks(*own):
                mob[i, y, at : at + size, :] = mobility(conc[1 + y, at : at + size, :])
                chem_row(row_of(conc, 1 + y), set_row(chem.at[i], y), set_row(curve.at[i], y),
                         set_row(swing.at[i], y), at, size, mask)
            return 0

        lax.fori_loop(0, rows, row, 0, unroll=2)


def prepare_kernel(steps, rows, cols, nz, back, conc_own, from_a, from_b, x_low, x_high,
                   corner_b, corner_a, mob_core, chem_core, curve_core, swing_core,
                   mob, chem, curve, swing, *rest):
    *ahead, conc = rest
    places, _ = slots(steps)
    low, high = reach(cols)
    lanes = conc.shape[2]
    mask = face_mask(lanes, nz)
    place = places[1 + back]
    own = slice(pad, pad + cols)
    for y in range(rows):
        put_own(conc, depth + y, conc_own[back, y], y, place, cols, x_low, x_high)
        mob[depth + y, own, :] = mob_core[back - 1, y, own, :]
        chem[1 + y, own, :] = chem_core[back - 1, y, own, :]
        curve[1 + y, own, :] = curve_core[back - 1, y, own, :]
        swing[1 + y, own, :] = swing_core[back - 1, y, own, :]
    for halo, corner, base in zip((from_a, from_b), (corner_a, corner_b), landings(rows, main_first)):
        for at in range(depth):
            span = pl.ds(((1 + back) * depth + at) * cols, cols)
            put_halo(conc, (base + at,), halo[span, :], at, place, cols, corner)

    if ahead:
        put_ahead(ahead[0], conc_own, back + 1, x_low, x_high, places, rows, cols)

    for y in range(rows):
        for at in (low - 8, pad + cols):
            span = slice(at, at + 16)
            mob[depth + y, span, :] = mobility(conc[depth + y, span, :])
        for at in (low, pad + cols - 8):
            chem_row(row_of(conc, depth + y), set_row(chem, 1 + y), set_row(curve, 1 + y),
                     set_row(swing, 1 + y), at, 16, mask)
    for y, beyond in ((0, -1), (rows - 1, rows)):
        inner = slice(pad + 8, pad + cols - 8)
        chem[1 + y, inner, :] = chem[1 + y, inner, :] - (time_step * grad_energy) * (
            conc[depth + beyond, inner, :]
        )

    for y in (-1, rows):
        for at, size in chunks(low - 8, high + 8):
            mob[depth + y, at : at + size, :] = mobility(conc[depth + y, at : at + size, :])
        for at, size in chunks(low, high):
            chem_row(row_of(conc, depth + y), set_row(chem, 1 + y), lambda *_: None,
                     lambda *_: None, at, size, mask)


def next_interior(rows, cols, nz, final, mob, chem, curve, swing, rate, inner, outer, before, *rest):
    if final:
        out, tiles, grad_out, adj, pot, part, grad, turned, sem = rest
        send = pltpu.make_async_copy(turned, grad_out, sem)
    else:
        edge_before, out, grad, adj, pot, part, sums = rest
        for y in range(rows):
            sums[y] = before[y]
        for s, y in ((0, 0), (1, rows - 1)):
            sums[y] = edge_before[s]
        before = sums
    lanes = adj.shape[2]
    for y in range(depth, rows - depth):
        adj[1 + y] = inner[y]
    for s, k, y in sides_of(rows):
        adj[1 + y] = outer[s, k]
    adj[0] = outer[0, 0]
    adj[1 + rows] = outer[1, 0]

    def send_grad():
        for y in range(rows):
            turned[pl.ds(y, nz, stride=rows), :] = fold(grad[y, pad : pad + cols, :].T, nz)
        send.start()

    all_rows(rows, cols, nz, adj, mob, depth, chem, curve, swing, rate, before, pot, part, out,
             grad, send_grad if final else None)
    if final:
        for y in range(depth, rows - depth):
            tiles[pl.ds(y, lanes, stride=rows), :] = out[y, pad : pad + cols, :].T
        send.wait()


def fold(value, nz):
    total = value[:nz]
    for frame in range(1, value.shape[0] // nz):
        total = total + value[frame * nz : (frame + 1) * nz]
    return total


def next_boundary(rows, cols, nz, final, mob, chem, curve, swing, inside, outer, from_a, from_b,
                  *rest):
    if final:
        tiles, out, halo, delta, result = rest
    else:
        ahead, rate, result, to_a, to_b, halo, delta, open_g = rest
    low, high = reach(cols)
    first, last = sent(cols)
    lanes = mob.shape[2]
    mask = face_mask(lanes, nz)
    to_next = a_is_next("gy", round_first)
    for got, side in ((from_a, jnp.where(to_next, 1, 0)), (from_b, jnp.where(to_next, 0, 1))):
        for k in range(2):
            halo[side, k, first:last, :] = got[k]
    for s in range(2):
        y, beyond = s * (rows - 1), s * (rows + 1) - 1
        for at, size in chunks(low, high):
            span = slice(at, at + size)
            diff = halo[s, 0, span, :] - outer[s, 0, span, :]
            both = mob[depth + beyond, span, :] + mob[depth + y, span, :]
            delta[s, span, :] = both * diff
        for at, size in chunks(low, high):
            span = slice(at, at + size)
            more = delta[s, span, :]
            diff = halo[s, 0, span, :] - outer[s, 0, span, :]
            pair = (chem[1 + beyond, span, :] - chem[1 + y, span, :]) * diff
            step_z = (up(more) - more) * mask
            lap = (
                (delta[s, at + 1 : at + size + 1, :] + delta[s, at - 1 : at + size - 1, :])
                + (halo[s, 1, span, :] - more)
                - 4.0 * more
                + (step_z - down(step_z))
            )
            result[s, 0, span, :] = (
                inside[y, span, :]
                + (swing[1 + y, span, :] * pair + curve[1 + y, span, :] * more)
                - grad_energy * lap
            )
            result[s, 1, span, :] = inside[1 + s * (rows - 3), span, :] - grad_energy * more
    if final:
        out[...] = tiles[...]
        for s, k, y in sides_of(rows):
            out[pl.ds(y, lanes, stride=rows), :] = result[s, k, pad : pad + cols, :].T
    else:
        send_rows(result, ahead, rate, to_a, to_b, open_g, cols, nz)


def call(kernel, outs, scratch, *operands, cost=0, far=False, far_outs=()):
    if far:
        operands = [pltpu.with_memory_space_constraint(value, pltpu.HBM) for value in operands]
    space = pl.ANY if far else pltpu.VMEM
    return pl.pallas_call(
        kernel,
        out_shape=[jax.ShapeDtypeStruct(shape, f32) for shape in outs],
        in_specs=[pl.BlockSpec(memory_space=space)] * len(operands),
        out_specs=[
            pl.BlockSpec(memory_space=pltpu.HBM if i in far_outs else pltpu.VMEM)
            for i in range(len(outs))
        ],
        scratch_shapes=[pltpu.VMEM(s, f32) if isinstance(s, tuple) else s for s in scratch],
        compiler_params=pltpu.CompilerParams(vmem_limit_bytes=vmem_limit),
        cost_estimate=pl.CostEstimate(
            flops=cost * 1_000_000, bytes_accessed=cost * 2_000_000, transcendentals=0
        ),
    )(*operands)


def swap(value_a, value_b, axis, first):
    count = lax.axis_size(axis)
    pairs_a = [(i, (i + 1 - 2 * ((i + first) % 2)) % count) for i in range(count)]
    pairs_b = [(i, (i - 1 + 2 * ((i + first) % 2)) % count) for i in range(count)]
    return lax.ppermute(value_a, axis, pairs_a), lax.ppermute(value_b, axis, pairs_b)


def shards(saved_conc, adjoint_end, rate_field):
    steps, frames, nz, rows, cols = saved_conc.shape
    lanes = frames * nz
    _, total = slots(steps)
    width = cols + 2 * pad
    flat = lanes * rows

    def field(count):
        return (count, width, lanes)

    both = (2, depth, width, lanes)
    edge = (2, cols + 8, lanes)
    open_g = (2, cols + 16, lanes)
    raw = [(steps, flat, cols), (flat, cols), (nz * rows, cols)]
    conc_raw, adj_raw, rate_raw, main_a, main_b = call(
        functools.partial(edge_kernel, steps, rows, cols, nz),
        raw + [((1 + steps) * depth * cols + cols // 2, lanes)] * 2,
        [pltpu.SemaphoreType.DMA((2 + steps,))],
        saved_conc.reshape(raw[0]), adjoint_end.reshape(raw[1]), rate_field.reshape(raw[2]),
        cost=2,
        far=True,
    )
    main_a, main_b = swap(main_a, main_b, "gy", main_first)
    conc_own, adj_own, rate_own, x_a, x_b = call(
        functools.partial(turn_kernel, steps, rows, cols, nz),
        [(steps, rows, cols, lanes), (rows, cols, lanes), (rows, cols, lanes)]
        + [(rows, total, lanes)] * 2,
        [],
        conc_raw, adj_raw, rate_raw,
        cost=1,
    )
    x_a, x_b = swap(x_a, x_b, "gx", x_first)
    whole = (steps - 1, rows, width, lanes)
    core = call(
        functools.partial(core_kernel, steps, rows, cols, nz),
        [whole] * 4,
        [field(rows + 2)],
        conc_own,
        cost=2,
    )
    x_low, x_high, corner_a, corner_b = call(
        functools.partial(corner_kernel, rows),
        [(rows, total, lanes)] * 2 + [(2, depth, total, lanes)] * 2,
        [],
        x_a, x_b, core[1],
    )
    corners = swap(corner_a, corner_b, "gy", round_first)
    corner_a, corner_b = corners if main_first == round_first else corners[::-1]

    conc, adj, rate, chem, curve, swing, inner, grad, ahead = call(
        functools.partial(first_interior, steps, rows, cols, nz),
        [field(rows + 2)] * 2 + [field(rows)] + [field(rows + 2)] * 3 + [field(rows)] * 2 + [both],
        [field(rows + 2)] * 2 + [field(rows)],
        conc_own, adj_own, rate_own, x_low, x_high,
        cost=3,
    )
    outer, edge_grad, to_a, to_b = call(
        functools.partial(first_boundary, steps, rows, cols, nz),
        [both, field(2), edge, edge],
        [both, both] + [field(2)] * 5 + [open_g],
        conc, adj, rate, chem, curve, swing, inner, grad, main_a, main_b, corner_b, corner_a, ahead,
        cost=2,
    )
    sums = (grad, edge_grad)
    for back in range(1, steps):
        adj_a, adj_b = swap(to_a, to_b, "gy", round_first)
        final = back == steps - 1
        fields = call(
            functools.partial(prepare_kernel, steps, rows, cols, nz, back),
            [field(rows + 2 * depth)] + [field(rows + 2)] * 3 + ([] if final else [both]),
            [field(rows + 2 * depth)],
            conc_own, main_a, main_b, x_low, x_high, corner_b, corner_a, *core,
            cost=2,
        )
        fields, ahead = fields[:4], fields[4:]
        work = [field(rows + 2)] * 2 + [field(rows)] * 2
        if final:
            inner, tiles, grad = call(
                functools.partial(next_interior, rows, cols, nz, final),
                [field(rows), (flat, cols), (nz * rows, cols)],
                work + [(nz * rows, cols), pltpu.SemaphoreType.DMA],
                *fields, rate, inner, outer, *sums,
                cost=3,
                far_outs=(2,),
            )
            (adj,) = call(
                functools.partial(next_boundary, rows, cols, nz, final),
                [(flat, cols)],
                [both, field(2), both],
                *fields, inner, outer, adj_a, adj_b, tiles,
                cost=1,
            )
        else:
            inner, grad = call(
                functools.partial(next_interior, rows, cols, nz, final),
                [field(rows)] * 2,
                work,
                *fields, rate, inner, outer, *sums,
                cost=3,
            )
            outer, to_a, to_b = call(
                functools.partial(next_boundary, rows, cols, nz, final),
                [both, edge, edge],
                [both, field(2), open_g],
                *fields, inner, outer, adj_a, adj_b, *ahead, rate,
                cost=1,
            )
            sums = (grad,)
    return adj.reshape(adjoint_end.shape), grad.reshape(rate_field.shape)


def solution(mesh):
    return jax.shard_map(
        shards,
        mesh=mesh,
        in_specs=(P(None, None, None, "gy", "gx"), P(None, None, "gy", "gx"), P(None, "gy", "gx")),
        out_specs=(P(None, None, "gy", "gx"), P(None, "gy", "gx")),
        check_vma=False,
    )
```

```python
import functools

import jax
import jax.numpy as jnp
from jax import lax
from jax.experimental import pallas as pl
from jax.experimental.pallas import tpu as pltpu
from jax.sharding import PartitionSpec as P

mix_energy = 2.5
grad_energy = 1.0
time_step = 0.1
diff_step = 0.03
bath_potential = 0.5

pad = 16
chunk = 72
depth = 2
early = 2
x_first, main_first, round_first = 0, 0, 1
vmem_limit = 20 * 1024 * 1024
f32 = jnp.float32


def slots(steps):
    widths = [2 * steps] + [2 * steps - 2 * back for back in range(steps)] + [2 * steps - 1]
    starts = [sum(widths[:i]) for i in range(len(widths))]
    total = -(-sum(widths) // 8) * 8
    return list(zip(starts, widths)), total


def chunks(low, high):
    return [(at, min(chunk, high - at)) for at in range(low, high, chunk)]


def reach(cols):
    return pad - 8, pad + cols + 8


def sent(cols):
    return pad - 4, pad + cols + 4


def up(value):
    return pltpu.roll(value, value.shape[1] - 1, 1)


def down(value):
    return pltpu.roll(value, 1, 1)


def face_mask(lanes, nz):
    lane = lax.broadcasted_iota(jnp.int32, (1, lanes), 1)
    return jnp.where(lane % nz == nz - 1, 0.0, 1.0).astype(f32)


def row_of(ref, y):
    return lambda dy, cut: ref[y + dy, cut, :]


def laplace(field, at, size, mask):
    span = slice(at, at + size)
    here = field(0, span)
    step_z = (up(here) - here) * mask
    sides = field(0, slice(at + 1, at + size + 1)) + field(0, slice(at - 1, at + size - 1))
    return here, (
        (sides + (field(-1, span) + field(1, span))) - 4.0 * here + (step_z - down(step_z))
    )


def mobility(c):
    return (0.5 * diff_step) * c * (1.0 - c)


def chem_row(conc, chem, curve, swing, at, size, mask):
    c, lap = laplace(conc, at, size, mask)
    inv = 1.0 / (c * (1.0 - c))
    span = slice(at, at + size)
    chem(
        span,
        time_step * (jnp.log(c * c * inv) - grad_energy * lap)
        + (time_step * (mix_energy - bath_potential) - (2.0 * time_step * mix_energy) * c),
    )
    curve(span, inv - 2.0 * mix_energy)
    swing(span, c * (diff_step / time_step) - 0.5 * diff_step / time_step)


def face_sums(adj, mob, chem, at, size, mask, across=(1, -1)):
    span = slice(at, at + size)
    a = adj(0, span)
    m = None if mob is None else mob(0, span)
    mu = None if chem is None else chem(0, span)
    flow = pair = None
    for dy, cut in (
        (0, slice(at + 1, at + size + 1)),
        (0, slice(at - 1, at + size - 1)),
    ) + tuple((dy, span) for dy in across):
        diff = adj(dy, cut) - a
        if mob is not None:
            term = (mob(dy, cut) + m) * diff
            flow = term if flow is None else flow + term
        if chem is not None:
            term = (chem(dy, cut) - mu) * diff
            pair = term if pair is None else pair + term
    diff = (up(a) - a) * mask
    if mob is not None:
        term = (up(m) + m) * diff
        flow = flow + (term - down(term))
    if chem is not None:
        term = (up(mu) - mu) * diff
        pair = pair + (term + down(term))
    return a, mu, flow, pair


def partial(a, swing, pair, curve, g):
    return a + swing * pair + curve * g


def gain(a, chem, before):
    value = a * chem
    return -value if before is None else before - value


def set_row(ref, y):
    def put(span, value):
        ref[y, span, :] = value

    return put


def all_rows(rows, cols, nz, adj, mob, mob_skip, chem, curve, swing, rate, before, pot, part, out,
             grad, between=None):
    low, high = reach(cols)
    mask = face_mask(adj.shape[2], nz)

    def body(y, _):
        for at, size in chunks(low, high):
            span = slice(at, at + size)
            a, mu, flow, pair = face_sums(
                row_of(adj, y + 1), row_of(mob, y + mob_skip), row_of(chem, y + 1), at, size, mask
            )
            g = flow - rate[y, span, :] * a
            pot[y + 1, span, :] = g
            part[y, span, :] = partial(
                a, swing[y + 1, span, :], pair, curve[y + 1, span, :], g
            )
            grad[y, span, :] = gain(a, mu, None if before is None else before[y, span, :])
        return 0

    def close(y, _):
        for at, size in chunks(low, high):
            span = slice(at, at + size)
            _g, lap = laplace(row_of(pot, y + 1), at, size, mask)
            out[y, span, :] = part[y, span, :] - grad_energy * lap
        return 0

    for row in (0, rows + 1):
        pot[row] = jnp.zeros(pot.shape[1:], f32)
    lax.fori_loop(0, rows, body, 0, unroll=2)
    if between is not None:
        between()
    lax.fori_loop(0, rows, close, 0, unroll=4)


def a_is_next(axis, first):
    return lax.rem(lax.axis_index(axis), 2) == first


def bases(rows, first):
    to_next = a_is_next("gy", first)
    top = rows - depth
    return jnp.where(to_next, top, 0), jnp.where(to_next, 0, top)


def landings(rows, first):
    to_next = a_is_next("gy", first)
    top = rows + depth
    return jnp.where(to_next, top, 0), jnp.where(to_next, 0, top)


def sides_of(rows):
    return [(0, 0, 0), (0, 1, 1), (1, 0, rows - 1), (1, 1, rows - 2)]


def edge_kernel(steps, rows, cols, nz, conc_hbm, adj_hbm, rate_hbm, conc_in, adj_in, rate_in,
                main_a, main_b, sems):
    lanes = main_a.shape[1]
    half = cols // 2
    lower = lax.broadcasted_iota(jnp.int32, (half, lanes), 1) < nz
    fetches = [(adj_hbm, adj_in), (rate_hbm, rate_in)] + [
        (conc_hbm.at[steps - 1 - back], conc_in.at[back]) for back in range(steps)
    ]
    copies = []
    for i, (there, here) in enumerate(fetches):
        part = here.shape[0] // 2
        copies.append(
            [
                pltpu.make_async_copy(
                    there.at[pl.ds(k * part, part)], here.at[pl.ds(k * part, part)], sems.at[i, k]
                )
                for k in range(2)
            ]
        )
    for pair in copies:
        for copy in pair:
            copy.start()

    def arrived(i):
        for copy in copies[i]:
            copy.wait()

    arrived(0)
    for side, base in zip((main_a, main_b), bases(rows, main_first)):
        for at in range(depth):
            side[pl.ds(at * cols, cols), :] = adj_in[pl.ds(base + at, lanes, stride=rows), :].T
    arrived(1)
    for side, base in zip((main_a, main_b), bases(rows, main_first)):
        edge = jnp.where(base == 0, 0, rows - 1)
        rate = turned_rate(rate_in, edge, rows, nz, lanes)
        side[pl.ds((1 + early) * depth * cols, half), :] = jnp.where(
            lower, rate[:half], rate[half:]
        )
    for back in range(steps):
        arrived(2 + back)
        if back >= early:
            continue
        for side, base in zip((main_a, main_b), bases(rows, main_first)):
            for at in range(depth):
                side[pl.ds(((1 + back) * depth + at) * cols, cols), :] = conc_in[
                    back, pl.ds(base + at, lanes, stride=rows), :
                ].T


def turned_rate(rate, y, rows, nz, lanes):
    value = time_step * rate[pl.ds(y, nz, stride=rows), :]
    return jnp.concatenate([value] * (lanes // nz), axis=0).T


def turn_kernel(steps, rows, cols, nz, conc_in, adj_in, rate_in, conc_out, adj_out, rate_out,
                x_a, x_b):
    places, total = slots(steps)
    lanes = adj_out.shape[2]
    next_x = a_is_next("gx", x_first)

    def to_x(y, value, place):
        start, width = place
        last, first = value[cols - width :, :], value[:width, :]
        x_a[y, start : start + width, :] = jnp.where(next_x, last, first)
        x_b[y, start : start + width, :] = jnp.where(next_x, first, last)

    used = sum(places[-1])
    for y in range(rows):
        adj = adj_in[pl.ds(y, lanes, stride=rows), :].T
        adj_out[y] = adj
        to_x(y, adj, places[0])
        rate = turned_rate(rate_in, y, rows, nz, lanes)
        rate_out[y] = rate
        to_x(y, rate, places[steps + 1])
        if used < total:
            x_a[y, used:, :] = jnp.zeros((total - used, lanes), f32)
            x_b[y, used:, :] = jnp.zeros((total - used, lanes), f32)
        for back in range(steps):
            conc = conc_in[back, pl.ds(y, lanes, stride=rows), :].T
            conc_out[back, y] = conc
            to_x(y, conc, places[1 + back])


def put_own(out, row, value, y, place, cols, x_low, x_high):
    start, width = place
    right = pad + cols
    out[row, pad:right, :] = value
    out[row, pad - width : pad, :] = x_low[y, start : start + width, :]
    out[row, right : right + width, :] = x_high[y, start : start + width, :]


def put_halo(out, index, value, from_row, place, cols, corner):
    start, width = place
    right = pad + cols
    out[(*index, slice(pad, right))] = value
    out[(*index, slice(pad - width, pad))] = corner[0, from_row, start : start + width, :]
    out[(*index, slice(right, right + width))] = corner[1, from_row, start : start + width, :]


def corner_kernel(rows, got_a, got_b, _core, x_low, x_high, corner_a, corner_b):
    next_x = a_is_next("gx", x_first)
    x_low[...] = jnp.where(next_x, got_b[...], got_a[...])
    x_high[...] = jnp.where(next_x, got_a[...], got_b[...])
    for out, base in zip((corner_a, corner_b), bases(rows, round_first)):
        for at in range(depth):
            out[0, at] = x_low[base + at]
            out[1, at] = x_high[base + at]


def first_interior(steps, rows, cols, nz, conc_own, adj_own, rate_own, x_low, x_high,
                   conc, adj, rate, chem, curve, swing, out, grad, ahead, mob, pot, part):
    places, _ = slots(steps)
    low, high = reach(cols)
    lanes = adj.shape[2]
    mask = face_mask(lanes, nz)
    for y in range(rows):
        put_own(conc, 1 + y, conc_own[0, y], y, places[1], cols, x_low, x_high)
        put_own(adj, 1 + y, adj_own[y], y, places[0], cols, x_low, x_high)
        put_own(rate, y, rate_own[y], y, places[steps + 1], cols, x_low, x_high)
    for row, beside in ((0, 1), (rows + 1, rows)):
        adj[row] = adj[beside]
        for ref in (conc, chem, mob):
            ref[row] = jnp.zeros(ref.shape[1:], f32)
    put_ahead(ahead, conc_own, 1, x_low, x_high, places, rows, cols)

    def mob_row(row, _):
        for at, size in chunks(low - 8, high + 8):
            mob[row, at : at + size, :] = mobility(conc[row, at : at + size, :])
        return 0

    def mu_row(row, _):
        for at, size in chunks(low, high):
            chem_row(row_of(conc, row), set_row(chem, row), set_row(curve, row),
                     set_row(swing, row), at, size, mask)
        return 0

    lax.fori_loop(1, rows + 1, mob_row, 0, unroll=4)
    lax.fori_loop(1, rows + 1, mu_row, 0, unroll=2)
    all_rows(rows, cols, nz, adj, mob, 1, chem, curve, swing, rate, None, pot, part, out, grad)


def send_rows(out, ahead, rate, to_a, to_b, open_g, cols, nz):
    low, high = reach(cols)
    first, last = sent(cols)
    rows, lanes = rate.shape[0], rate.shape[2]
    mask = face_mask(lanes, nz)
    for s in range(2):
        for at, size in chunks(low, high):
            a, _mu, flow, _pair = face_sums(
                lambda dy, cut: out[s, dy, cut, :], lambda dy, cut: ahead[s, dy, cut, :], None,
                at, size, mask, (1,)
            )
            open_g[s, at - low : at - low + size, :] = (
                flow - rate[s * (rows - 1), at : at + size, :] * a
            )
    to_next = a_is_next("gy", round_first)
    for to, side in ((to_a, jnp.where(to_next, 1, 0)), (to_b, jnp.where(to_next, 0, 1))):
        to[0] = out[side, 0, first:last, :]
        to[1] = open_g[side, first - low : last - low, :]


def put_ahead(ahead, conc_own, back, x_low, x_high, places, rows, cols):
    for s, k, y in sides_of(rows):
        put_own(ahead.at[s], k, conc_own[back, y], y, places[1 + back], cols, x_low, x_high)
        ahead[s, k] = mobility(ahead[s, k])


def first_boundary(steps, rows, cols, nz, conc, adj, rate, chem, curve, swing, inside, grad,
                   from_a, from_b, corner_b, corner_a, ahead,
                   out, edge_grad, to_a, to_b, far_conc, far_adj, far_rate, far_mob, far_chem,
                   far_pot, delta, open_g):
    places, _ = slots(steps)
    low, high = reach(cols)
    half = cols // 2
    lanes = conc.shape[2]
    mask = face_mask(lanes, nz)
    lower = lax.broadcasted_iota(jnp.int32, (half, lanes), 1) < nz
    to_next = a_is_next("gy", main_first)

    def unpack(side):
        packed = side[pl.ds((1 + early) * depth * cols, half), :]
        turned = pltpu.roll(packed, lanes // 2, 1)
        return jnp.concatenate(
            [jnp.where(lower, packed, turned), jnp.where(lower, turned, packed)], axis=0
        )

    for halo, corner, side in (
        (from_a, corner_a, jnp.where(to_next, 1, 0)),
        (from_b, corner_b, jnp.where(to_next, 0, 1)),
    ):
        for at in range(depth):
            step = jnp.where(side == 1, at, depth - 1 - at)
            for ref, place, first in ((far_adj, places[0], 0), (far_conc, places[1], depth)):
                span = pl.ds((first + at) * cols, cols)
                put_halo(ref, (side, step), halo[span, :], at, place, cols, corner)
        put_halo(far_rate, (side,), unpack(halo), jnp.where(side == 1, 0, depth - 1),
                 places[steps + 1], cols, corner)

    share = time_step * grad_energy
    for s in range(2):
        y, y1 = s * (rows - 1), 1 + s * (rows - 3)
        for at, size in chunks(low - 8, high + 8):
            span = slice(at, at + size)
            far_mob[s, span, :] = mobility(far_conc[s, 0, span, :])

        def conc_at(dy, cut):
            return conc[1 + y, cut, :] if dy == 1 else far_conc[s, -dy, cut, :]

        def adj_at(dy, cut):
            return adj[1 + y, cut, :] if dy == 1 else far_adj[s, -dy, cut, :]

        def mob_at(dy, cut):
            return far_mob[s, cut, :] if dy == 0 else mobility(conc_at(dy, cut))

        for at, size in chunks(low, high):
            span = slice(at, at + size)
            chem_row(conc_at, set_row(far_chem, s), lambda *_: None, lambda *_: None, at, size,
                     mask)
            a, _mu, flow, _pair = face_sums(adj_at, mob_at, None, at, size, mask)
            far_pot[s, span, :] = flow - far_rate[s, span, :] * a
            diff = a - adj[1 + y, span, :]
            delta[s, span, :] = (far_mob[s, span, :] + mobility(conc[1 + y, span, :])) * diff
        for at, size in chunks(low, high):
            span = slice(at, at + size)
            a, c, _flow, spread = face_sums(
                lambda dy, cut: adj[1 + y, cut, :], None, lambda dy, cut: far_conc[s, 0, cut, :],
                at, size, mask, ()
            )
            less = share * c
            inward = less * (adj[1 + y1, span, :] - a)
            pair = (far_chem[s, span, :] - (chem[1 + y, span, :] - less)) * (
                far_adj[s, 0, span, :] - a
            ) + (inward - share * spread)
            more = delta[s, span, :]
            step_z = (up(more) - more) * mask
            lap = (
                (delta[s, at + 1 : at + size + 1, :] + delta[s, at - 1 : at + size - 1, :])
                + (far_pot[s, span, :] - 4.0 * more)
                + (step_z - down(step_z))
            )
            out[s, 0, span, :] = (
                inside[y, span, :]
                + (swing[1 + y, span, :] * pair + curve[1 + y, span, :] * more)
                - grad_energy * lap
            )
            out[s, 1, span, :] = (
                inside[y1, span, :] + swing[1 + y1, span, :] * inward - grad_energy * more
            )
            edge_grad[s, span, :] = grad[y, span, :] + less * a
    send_rows(out, ahead, rate, to_a, to_b, open_g, cols, nz)


def core_kernel(steps, rows, cols, nz, conc_own, mob, chem, curve, swing, conc):
    lanes = conc.shape[2]
    mask = face_mask(lanes, nz)
    own = pad, pad + cols
    for row in (0, rows + 1):
        conc[row] = jnp.zeros(conc.shape[1:], f32)
    for i in range(steps - 1):
        for y in range(rows):
            conc[1 + y, pad : pad + cols, :] = conc_own[1 + i, y]

        def row(y, _):
            for at, size in chunks(*own):
                mob[i, y, at : at + size, :] = mobility(conc[1 + y, at : at + size, :])
                chem_row(row_of(conc, 1 + y), set_row(chem.at[i], y), set_row(curve.at[i], y),
                         set_row(swing.at[i], y), at, size, mask)
            return 0

        lax.fori_loop(0, rows, row, 0, unroll=2)


def prepare_kernel(steps, rows, cols, nz, back, conc_own, from_a, from_b, x_low, x_high,
                   corner_b, corner_a, mob_core, chem_core, curve_core, swing_core,
                   mob, chem, curve, swing, *rest):
    *more, conc = rest
    places, _ = slots(steps)
    low, high = reach(cols)
    lanes = conc.shape[2]
    mask = face_mask(lanes, nz)
    place = places[1 + back]
    own = slice(pad, pad + cols)
    for y in range(rows):
        put_own(conc, depth + y, conc_own[back, y], y, place, cols, x_low, x_high)
        mob[depth + y, own, :] = mob_core[back - 1, y, own, :]
        chem[1 + y, own, :] = chem_core[back - 1, y, own, :]
        curve[1 + y, own, :] = curve_core[back - 1, y, own, :]
        swing[1 + y, own, :] = swing_core[back - 1, y, own, :]
    for halo, corner, base in zip((from_a, from_b), (corner_a, corner_b), landings(rows, main_first)):
        for at in range(depth):
            first = (1 + back) * depth if back < early else (back - early) * depth
            span = pl.ds((first + at) * cols, cols)
            put_halo(conc, (base + at,), halo[span, :], at, place, cols, corner)

    if more:
        ahead, late_a, late_b = more
        put_ahead(ahead, conc_own, back + 1, x_low, x_high, places, rows, cols)
        for side, base in zip((late_a, late_b), bases(rows, main_first)):
            for after in range(early, steps):
                for at in range(depth):
                    span = pl.ds(((after - early) * depth + at) * cols, cols)
                    side[span, :] = conc_own[after, base + at]
            used = (steps - early) * depth * cols
            side[used:, :] = jnp.zeros((side.shape[0] - used, lanes), f32)

    for y in range(rows):
        for at in (low - 8, pad + cols):
            span = slice(at, at + 16)
            mob[depth + y, span, :] = mobility(conc[depth + y, span, :])
        for at in (low, pad + cols - 8):
            chem_row(row_of(conc, depth + y), set_row(chem, 1 + y), set_row(curve, 1 + y),
                     set_row(swing, 1 + y), at, 16, mask)
    for y, beyond in ((0, -1), (rows - 1, rows)):
        inner = slice(pad + 8, pad + cols - 8)
        chem[1 + y, inner, :] = chem[1 + y, inner, :] - (time_step * grad_energy) * (
            conc[depth + beyond, inner, :]
        )

    for y in (-1, rows):
        for at, size in chunks(low - 8, high + 8):
            mob[depth + y, at : at + size, :] = mobility(conc[depth + y, at : at + size, :])
        for at, size in chunks(low, high):
            chem_row(row_of(conc, depth + y), set_row(chem, 1 + y), lambda *_: None,
                     lambda *_: None, at, size, mask)


def next_interior(rows, cols, nz, final, mob, chem, curve, swing, rate, inner, outer, before, *rest):
    if final:
        out, tiles, grad_out, adj, pot, part, grad, turned, sem = rest
        send = pltpu.make_async_copy(turned, grad_out, sem)
    else:
        edge_before, out, grad, adj, pot, part, sums = rest
        for y in range(rows):
            sums[y] = before[y]
        for s, y in ((0, 0), (1, rows - 1)):
            sums[y] = edge_before[s]
        before = sums
    lanes = adj.shape[2]
    for y in range(depth, rows - depth):
        adj[1 + y] = inner[y]
    for s, k, y in sides_of(rows):
        adj[1 + y] = outer[s, k]
    adj[0] = outer[0, 0]
    adj[1 + rows] = outer[1, 0]

    def send_grad():
        for y in range(rows):
            turned[pl.ds(y, nz, stride=rows), :] = fold(grad[y, pad : pad + cols, :].T, nz)
        send.start()

    all_rows(rows, cols, nz, adj, mob, depth, chem, curve, swing, rate, before, pot, part, out,
             grad, send_grad if final else None)
    if final:
        for y in range(depth, rows - depth):
            tiles[pl.ds(y, lanes, stride=rows), :] = out[y, pad : pad + cols, :].T
        send.wait()


def fold(value, nz):
    total = value[:nz]
    for frame in range(1, value.shape[0] // nz):
        total = total + value[frame * nz : (frame + 1) * nz]
    return total


def next_boundary(rows, cols, nz, final, mob, chem, curve, swing, inside, outer, from_a, from_b,
                  *rest):
    if final:
        tiles, out, halo, delta, result = rest
    else:
        ahead, rate, result, to_a, to_b, halo, delta, open_g = rest
    low, high = reach(cols)
    first, last = sent(cols)
    lanes = mob.shape[2]
    mask = face_mask(lanes, nz)
    to_next = a_is_next("gy", round_first)
    for got, side in ((from_a, jnp.where(to_next, 1, 0)), (from_b, jnp.where(to_next, 0, 1))):
        for k in range(2):
            halo[side, k, first:last, :] = got[k]
    for s in range(2):
        y, beyond = s * (rows - 1), s * (rows + 1) - 1
        for at, size in chunks(low, high):
            span = slice(at, at + size)
            diff = halo[s, 0, span, :] - outer[s, 0, span, :]
            both = mob[depth + beyond, span, :] + mob[depth + y, span, :]
            delta[s, span, :] = both * diff
        for at, size in chunks(low, high):
            span = slice(at, at + size)
            more = delta[s, span, :]
            diff = halo[s, 0, span, :] - outer[s, 0, span, :]
            pair = (chem[1 + beyond, span, :] - chem[1 + y, span, :]) * diff
            step_z = (up(more) - more) * mask
            lap = (
                (delta[s, at + 1 : at + size + 1, :] + delta[s, at - 1 : at + size - 1, :])
                + (halo[s, 1, span, :] - more)
                - 4.0 * more
                + (step_z - down(step_z))
            )
            result[s, 0, span, :] = (
                inside[y, span, :]
                + (swing[1 + y, span, :] * pair + curve[1 + y, span, :] * more)
                - grad_energy * lap
            )
            result[s, 1, span, :] = inside[1 + s * (rows - 3), span, :] - grad_energy * more
    if final:
        out[...] = tiles[...]
        for s, k, y in sides_of(rows):
            out[pl.ds(y, lanes, stride=rows), :] = result[s, k, pad : pad + cols, :].T
    else:
        send_rows(result, ahead, rate, to_a, to_b, open_g, cols, nz)


def call(kernel, outs, scratch, *operands, cost=0, far=False, far_outs=()):
    if far:
        operands = [pltpu.with_memory_space_constraint(value, pltpu.HBM) for value in operands]
    space = pl.ANY if far else pltpu.VMEM
    return pl.pallas_call(
        kernel,
        out_shape=[jax.ShapeDtypeStruct(shape, f32) for shape in outs],
        in_specs=[pl.BlockSpec(memory_space=space)] * len(operands),
        out_specs=[
            pl.BlockSpec(memory_space=pltpu.HBM if i in far_outs else pltpu.VMEM)
            for i in range(len(outs))
        ],
        scratch_shapes=[pltpu.VMEM(s, f32) if isinstance(s, tuple) else s for s in scratch],
        compiler_params=pltpu.CompilerParams(vmem_limit_bytes=vmem_limit),
        cost_estimate=pl.CostEstimate(
            flops=cost * 1_000_000, bytes_accessed=cost * 2_000_000, transcendentals=0
        ),
    )(*operands)


def swap(value_a, value_b, axis, first):
    count = lax.axis_size(axis)
    pairs_a = [(i, (i + 1 - 2 * ((i + first) % 2)) % count) for i in range(count)]
    pairs_b = [(i, (i - 1 + 2 * ((i + first) % 2)) % count) for i in range(count)]
    return lax.ppermute(value_a, axis, pairs_a), lax.ppermute(value_b, axis, pairs_b)


def shards(saved_conc, adjoint_end, rate_field):
    steps, frames, nz, rows, cols = saved_conc.shape
    lanes = frames * nz
    _, total = slots(steps)
    width = cols + 2 * pad
    flat = lanes * rows

    def field(count):
        return (count, width, lanes)

    both = (2, depth, width, lanes)
    edge = (2, cols + 8, lanes)
    open_g = (2, cols + 16, lanes)
    raw = [(steps, flat, cols), (flat, cols), (nz * rows, cols)]
    conc_raw, adj_raw, rate_raw, main_a, main_b = call(
        functools.partial(edge_kernel, steps, rows, cols, nz),
        raw + [((1 + early) * depth * cols + cols // 2, lanes)] * 2,
        [pltpu.SemaphoreType.DMA((2 + steps, 2))],
        saved_conc.reshape(raw[0]), adjoint_end.reshape(raw[1]), rate_field.reshape(raw[2]),
        cost=2,
        far=True,
    )
    main_a, main_b = swap(main_a, main_b, "gy", main_first)
    conc_own, adj_own, rate_own, x_a, x_b = call(
        functools.partial(turn_kernel, steps, rows, cols, nz),
        [(steps, rows, cols, lanes), (rows, cols, lanes), (rows, cols, lanes)]
        + [(rows, total, lanes)] * 2,
        [],
        conc_raw, adj_raw, rate_raw,
        cost=1,
    )
    x_a, x_b = swap(x_a, x_b, "gx", x_first)
    whole = (steps - 1, rows, width, lanes)
    core = call(
        functools.partial(core_kernel, steps, rows, cols, nz),
        [whole] * 4,
        [field(rows + 2)],
        conc_own,
        cost=2,
    )
    x_low, x_high, corner_a, corner_b = call(
        functools.partial(corner_kernel, rows),
        [(rows, total, lanes)] * 2 + [(2, depth, total, lanes)] * 2,
        [],
        x_a, x_b, core[1],
    )
    corners = swap(corner_a, corner_b, "gy", round_first)
    corner_a, corner_b = corners if main_first == round_first else corners[::-1]

    conc, adj, rate, chem, curve, swing, inner, grad, ahead = call(
        functools.partial(first_interior, steps, rows, cols, nz),
        [field(rows + 2)] * 2 + [field(rows)] + [field(rows + 2)] * 3 + [field(rows)] * 2 + [both],
        [field(rows + 2)] * 2 + [field(rows)],
        conc_own, adj_own, rate_own, x_low, x_high,
        cost=3,
    )
    outer, edge_grad, to_a, to_b = call(
        functools.partial(first_boundary, steps, rows, cols, nz),
        [both, field(2), edge, edge],
        [both, both] + [field(2)] * 5 + [open_g],
        conc, adj, rate, chem, curve, swing, inner, grad, main_a, main_b, corner_b, corner_a, ahead,
        cost=2,
    )
    sums = (grad, edge_grad)
    got = main_a, main_b
    late = (max((steps - early) * depth * cols, 2 * (cols + 8) + 8), lanes)
    for back in range(1, steps):
        adj_a, adj_b = swap(to_a, to_b, "gy", round_first)
        final = back == steps - 1
        fields = call(
            functools.partial(prepare_kernel, steps, rows, cols, nz, back),
            [field(rows + 2 * depth)] + [field(rows + 2)] * 3
            + ([] if final else [both, late, late]),
            [field(rows + 2 * depth)],
            conc_own, *got, x_low, x_high, corner_b, corner_a, *core,
            cost=2,
        )
        fields, ahead, more = fields[:4], fields[4:5], fields[5:]
        if not final:
            got = swap(*more, "gy", main_first)
        work = [field(rows + 2)] * 2 + [field(rows)] * 2
        if final:
            inner, tiles, grad = call(
                functools.partial(next_interior, rows, cols, nz, final),
                [field(rows), (flat, cols), (nz * rows, cols)],
                work + [(nz * rows, cols), pltpu.SemaphoreType.DMA],
                *fields, rate, inner, outer, *sums,
                cost=3,
                far_outs=(2,),
            )
            (adj,) = call(
                functools.partial(next_boundary, rows, cols, nz, final),
                [(flat, cols)],
                [both, field(2), both],
                *fields, inner, outer, adj_a, adj_b, tiles,
                cost=1,
            )
        else:
            inner, grad = call(
                functools.partial(next_interior, rows, cols, nz, final),
                [field(rows)] * 2,
                work,
                *fields, rate, inner, outer, *sums,
                cost=3,
            )
            outer, to_a, to_b = call(
                functools.partial(next_boundary, rows, cols, nz, final),
                [both, edge, edge],
                [both, field(2), open_g],
                *fields, inner, outer, adj_a, adj_b, *ahead, rate,
                cost=1,
            )
            sums = (grad,)
    return adj.reshape(adjoint_end.shape), grad.reshape(rate_field.shape)


def solution(mesh):
    return jax.shard_map(
        shards,
        mesh=mesh,
        in_specs=(P(None, None, None, "gy", "gx"), P(None, None, "gy", "gx"), P(None, "gy", "gx")),
        out_specs=(P(None, None, "gy", "gx"), P(None, "gy", "gx")),
        check_vma=False,
    )
```

```python
import functools

import jax
import jax.numpy as jnp
from jax import lax
from jax.experimental import pallas as pl
from jax.experimental.pallas import tpu as pltpu
from jax.sharding import PartitionSpec as P

mix_energy = 2.5
grad_energy = 1.0
time_step = 0.1
diff_step = 0.03
bath_potential = 0.5

pad = 16
chunk = 72
depth = 2
early = 2
x_first, main_first, round_first = 0, 0, 1
vmem_limit = 20 * 1024 * 1024
f32 = jnp.float32


def slots(steps):
    widths = [2 * steps] + [2 * steps - 2 * back for back in range(steps)] + [2 * steps - 1]
    starts = [sum(widths[:i]) for i in range(len(widths))]
    total = -(-sum(widths) // 8) * 8
    return list(zip(starts, widths)), total


def chunks(low, high):
    return [(at, min(chunk, high - at)) for at in range(low, high, chunk)]


def reach(cols):
    return pad - 8, pad + cols + 8


def sent(cols):
    return pad - 4, pad + cols + 4


def up(value):
    return pltpu.roll(value, value.shape[1] - 1, 1)


def down(value):
    return pltpu.roll(value, 1, 1)


def face_mask(lanes, nz):
    lane = lax.broadcasted_iota(jnp.int32, (1, lanes), 1)
    return jnp.where(lane % nz == nz - 1, 0.0, 1.0).astype(f32)


def row_of(ref, y):
    return lambda dy, cut: ref[y + dy, cut, :]


def laplace(field, at, size, mask):
    span = slice(at, at + size)
    here = field(0, span)
    step_z = (up(here) - here) * mask
    sides = field(0, slice(at + 1, at + size + 1)) + field(0, slice(at - 1, at + size - 1))
    return here, (
        (sides + (field(-1, span) + field(1, span))) - 4.0 * here + (step_z - down(step_z))
    )


def mobility(c):
    return (0.5 * diff_step) * c * (1.0 - c)


def chem_row(conc, chem, curve, swing, at, size, mask):
    c, lap = laplace(conc, at, size, mask)
    inv = 1.0 / (c * (1.0 - c))
    span = slice(at, at + size)
    chem(
        span,
        time_step * (jnp.log(c * c * inv) - grad_energy * lap)
        + (time_step * (mix_energy - bath_potential) - (2.0 * time_step * mix_energy) * c),
    )
    curve(span, inv - 2.0 * mix_energy)
    swing(span, c * (diff_step / time_step) - 0.5 * diff_step / time_step)


def face_sums(adj, mob, chem, at, size, mask, across=(1, -1)):
    span = slice(at, at + size)
    a = adj(0, span)
    m = None if mob is None else mob(0, span)
    mu = None if chem is None else chem(0, span)
    flow = pair = None
    for dy, cut in (
        (0, slice(at + 1, at + size + 1)),
        (0, slice(at - 1, at + size - 1)),
    ) + tuple((dy, span) for dy in across):
        diff = adj(dy, cut) - a
        if mob is not None:
            term = (mob(dy, cut) + m) * diff
            flow = term if flow is None else flow + term
        if chem is not None:
            term = (chem(dy, cut) - mu) * diff
            pair = term if pair is None else pair + term
    diff = (up(a) - a) * mask
    if mob is not None:
        term = (up(m) + m) * diff
        flow = flow + (term - down(term))
    if chem is not None:
        term = (up(mu) - mu) * diff
        pair = pair + (term + down(term))
    return a, mu, flow, pair


def partial(a, swing, pair, curve, g):
    return a + swing * pair + curve * g


def gain(a, chem, before):
    value = a * chem
    return -value if before is None else before - value


def set_row(ref, y):
    def put(span, value):
        ref[y, span, :] = value

    return put


def all_rows(rows, cols, nz, adj, mob, mob_skip, chem, curve, swing, rate, before, pot, part, out,
             grad, between=None):
    low, high = reach(cols)
    mask = face_mask(adj.shape[2], nz)

    def body(y, _):
        for at, size in chunks(low, high):
            span = slice(at, at + size)
            a, mu, flow, pair = face_sums(
                row_of(adj, y + 1), row_of(mob, y + mob_skip), row_of(chem, y + 1), at, size, mask
            )
            g = flow - rate[y, span, :] * a
            pot[y + 1, span, :] = g
            part[y, span, :] = partial(
                a, swing[y + 1, span, :], pair, curve[y + 1, span, :], g
            )
            grad[y, span, :] = gain(a, mu, None if before is None else before[y, span, :])
        return 0

    def close(y, _):
        for at, size in chunks(low, high):
            span = slice(at, at + size)
            _g, lap = laplace(row_of(pot, y + 1), at, size, mask)
            out[y, span, :] = part[y, span, :] - grad_energy * lap
        return 0

    for row in (0, rows + 1):
        pot[row] = jnp.zeros(pot.shape[1:], f32)
    lax.fori_loop(0, rows, body, 0, unroll=4)
    if between is not None:
        between()
    lax.fori_loop(0, rows, close, 0, unroll=8)


def a_is_next(axis, first):
    return lax.rem(lax.axis_index(axis), 2) == first


def bases(rows, first):
    to_next = a_is_next("gy", first)
    top = rows - depth
    return jnp.where(to_next, top, 0), jnp.where(to_next, 0, top)


def landings(rows, first):
    to_next = a_is_next("gy", first)
    top = rows + depth
    return jnp.where(to_next, top, 0), jnp.where(to_next, 0, top)


def sides_of(rows):
    return [(0, 0, 0), (0, 1, 1), (1, 0, rows - 1), (1, 1, rows - 2)]


def edge_kernel(steps, rows, cols, nz, conc_hbm, adj_hbm, rate_hbm, conc_in, adj_in, rate_in,
                main_a, main_b, sems):
    lanes = main_a.shape[1]
    half = cols // 2
    lower = lax.broadcasted_iota(jnp.int32, (half, lanes), 1) < nz
    fetches = [(adj_hbm, adj_in), (rate_hbm, rate_in)] + [
        (conc_hbm.at[steps - 1 - back], conc_in.at[back]) for back in range(steps)
    ]
    copies = []
    for i, (there, here) in enumerate(fetches):
        part = here.shape[0] // 2
        copies.append(
            [
                pltpu.make_async_copy(
                    there.at[pl.ds(k * part, part)], here.at[pl.ds(k * part, part)], sems.at[i, k]
                )
                for k in range(2)
            ]
        )
    for pair in copies:
        for copy in pair:
            copy.start()

    def arrived(i):
        for copy in copies[i]:
            copy.wait()

    arrived(0)
    for side, base in zip((main_a, main_b), bases(rows, main_first)):
        for at in range(depth):
            side[pl.ds(at * cols, cols), :] = adj_in[pl.ds(base + at, lanes, stride=rows), :].T
    arrived(1)
    for side, base in zip((main_a, main_b), bases(rows, main_first)):
        edge = jnp.where(base == 0, 0, rows - 1)
        rate = turned_rate(rate_in, edge, rows, nz, lanes)
        side[pl.ds((1 + early) * depth * cols, half), :] = jnp.where(
            lower, rate[:half], rate[half:]
        )
    for back in range(steps):
        arrived(2 + back)
        if back >= early:
            continue
        for side, base in zip((main_a, main_b), bases(rows, main_first)):
            for at in range(depth):
                side[pl.ds(((1 + back) * depth + at) * cols, cols), :] = conc_in[
                    back, pl.ds(base + at, lanes, stride=rows), :
                ].T


def turned_rate(rate, y, rows, nz, lanes):
    value = time_step * rate[pl.ds(y, nz, stride=rows), :]
    return jnp.concatenate([value] * (lanes // nz), axis=0).T


def turn_kernel(steps, rows, cols, nz, conc_in, adj_in, rate_in, conc_out, adj_out, rate_out,
                x_a, x_b):
    places, total = slots(steps)
    lanes = adj_out.shape[2]
    next_x = a_is_next("gx", x_first)

    def to_x(y, value, place):
        start, width = place
        last, first = value[cols - width :, :], value[:width, :]
        x_a[y, start : start + width, :] = jnp.where(next_x, last, first)
        x_b[y, start : start + width, :] = jnp.where(next_x, first, last)

    used = sum(places[-1])
    for y in range(rows):
        adj = adj_in[pl.ds(y, lanes, stride=rows), :].T
        adj_out[y] = adj
        to_x(y, adj, places[0])
        rate = turned_rate(rate_in, y, rows, nz, lanes)
        rate_out[y] = rate
        to_x(y, rate, places[steps + 1])
        if used < total:
            x_a[y, used:, :] = jnp.zeros((total - used, lanes), f32)
            x_b[y, used:, :] = jnp.zeros((total - used, lanes), f32)
        for back in range(steps):
            conc = conc_in[back, pl.ds(y, lanes, stride=rows), :].T
            conc_out[back, y] = conc
            to_x(y, conc, places[1 + back])


def put_own(out, row, value, y, place, cols, x_low, x_high):
    start, width = place
    right = pad + cols
    out[row, pad:right, :] = value
    out[row, pad - width : pad, :] = x_low[y, start : start + width, :]
    out[row, right : right + width, :] = x_high[y, start : start + width, :]


def put_halo(out, index, value, from_row, place, cols, corner):
    start, width = place
    right = pad + cols
    out[(*index, slice(pad, right))] = value
    out[(*index, slice(pad - width, pad))] = corner[0, from_row, start : start + width, :]
    out[(*index, slice(right, right + width))] = corner[1, from_row, start : start + width, :]


def corner_kernel(rows, got_a, got_b, _core, x_low, x_high, corner_a, corner_b):
    next_x = a_is_next("gx", x_first)
    x_low[...] = jnp.where(next_x, got_b[...], got_a[...])
    x_high[...] = jnp.where(next_x, got_a[...], got_b[...])
    for out, base in zip((corner_a, corner_b), bases(rows, round_first)):
        for at in range(depth):
            out[0, at] = x_low[base + at]
            out[1, at] = x_high[base + at]


def first_interior(steps, rows, cols, nz, conc_own, adj_own, rate_own, x_low, x_high,
                   conc, adj, rate, chem, curve, swing, out, grad, ahead, mob, pot, part):
    places, _ = slots(steps)
    low, high = reach(cols)
    lanes = adj.shape[2]
    mask = face_mask(lanes, nz)
    for y in range(rows):
        put_own(conc, 1 + y, conc_own[0, y], y, places[1], cols, x_low, x_high)
        put_own(adj, 1 + y, adj_own[y], y, places[0], cols, x_low, x_high)
        put_own(rate, y, rate_own[y], y, places[steps + 1], cols, x_low, x_high)
    for row, beside in ((0, 1), (rows + 1, rows)):
        adj[row] = adj[beside]
        for ref in (conc, chem, mob):
            ref[row] = jnp.zeros(ref.shape[1:], f32)
    put_ahead(ahead, conc_own, 1, x_low, x_high, places, rows, cols)

    def mob_row(row, _):
        for at, size in chunks(low - 8, high + 8):
            mob[row, at : at + size, :] = mobility(conc[row, at : at + size, :])
        return 0

    def mu_row(row, _):
        for at, size in chunks(low, high):
            chem_row(row_of(conc, row), set_row(chem, row), set_row(curve, row),
                     set_row(swing, row), at, size, mask)
        return 0

    lax.fori_loop(1, rows + 1, mob_row, 0, unroll=8)
    lax.fori_loop(1, rows + 1, mu_row, 0, unroll=4)
    all_rows(rows, cols, nz, adj, mob, 1, chem, curve, swing, rate, None, pot, part, out, grad)


def send_rows(out, ahead, rate, to_a, to_b, open_g, cols, nz):
    low, high = reach(cols)
    first, last = sent(cols)
    rows, lanes = rate.shape[0], rate.shape[2]
    mask = face_mask(lanes, nz)
    for s in range(2):
        for at, size in chunks(low, high):
            a, _mu, flow, _pair = face_sums(
                lambda dy, cut: out[s, dy, cut, :], lambda dy, cut: ahead[s, dy, cut, :], None,
                at, size, mask, (1,)
            )
            open_g[s, at - low : at - low + size, :] = (
                flow - rate[s * (rows - 1), at : at + size, :] * a
            )
    to_next = a_is_next("gy", round_first)
    for to, side in ((to_a, jnp.where(to_next, 1, 0)), (to_b, jnp.where(to_next, 0, 1))):
        to[0] = out[side, 0, first:last, :]
        to[1] = open_g[side, first - low : last - low, :]


def put_ahead(ahead, conc_own, back, x_low, x_high, places, rows, cols):
    for s, k, y in sides_of(rows):
        put_own(ahead.at[s], k, conc_own[back, y], y, places[1 + back], cols, x_low, x_high)
        ahead[s, k] = mobility(ahead[s, k])


def first_boundary(steps, rows, cols, nz, conc, adj, rate, chem, curve, swing, inside, grad,
                   from_a, from_b, corner_b, corner_a, ahead,
                   out, edge_grad, to_a, to_b, far_conc, far_adj, far_rate, far_mob, far_chem,
                   far_pot, delta, open_g):
    places, _ = slots(steps)
    low, high = reach(cols)
    half = cols // 2
    lanes = conc.shape[2]
    mask = face_mask(lanes, nz)
    lower = lax.broadcasted_iota(jnp.int32, (half, lanes), 1) < nz
    to_next = a_is_next("gy", main_first)

    def unpack(side):
        packed = side[pl.ds((1 + early) * depth * cols, half), :]
        turned = pltpu.roll(packed, lanes // 2, 1)
        return jnp.concatenate(
            [jnp.where(lower, packed, turned), jnp.where(lower, turned, packed)], axis=0
        )

    for halo, corner, side in (
        (from_a, corner_a, jnp.where(to_next, 1, 0)),
        (from_b, corner_b, jnp.where(to_next, 0, 1)),
    ):
        for at in range(depth):
            step = jnp.where(side == 1, at, depth - 1 - at)
            for ref, place, first in ((far_adj, places[0], 0), (far_conc, places[1], depth)):
                span = pl.ds((first + at) * cols, cols)
                put_halo(ref, (side, step), halo[span, :], at, place, cols, corner)
        put_halo(far_rate, (side,), unpack(halo), jnp.where(side == 1, 0, depth - 1),
                 places[steps + 1], cols, corner)

    share = time_step * grad_energy
    for s in range(2):
        y, y1 = s * (rows - 1), 1 + s * (rows - 3)
        for at, size in chunks(low - 8, high + 8):
            span = slice(at, at + size)
            far_mob[s, span, :] = mobility(far_conc[s, 0, span, :])

        def conc_at(dy, cut):
            return conc[1 + y, cut, :] if dy == 1 else far_conc[s, -dy, cut, :]

        def adj_at(dy, cut):
            return adj[1 + y, cut, :] if dy == 1 else far_adj[s, -dy, cut, :]

        def mob_at(dy, cut):
            return far_mob[s, cut, :] if dy == 0 else mobility(conc_at(dy, cut))

        for at, size in chunks(low, high):
            span = slice(at, at + size)
            chem_row(conc_at, set_row(far_chem, s), lambda *_: None, lambda *_: None, at, size,
                     mask)
            a, _mu, flow, _pair = face_sums(adj_at, mob_at, None, at, size, mask)
            far_pot[s, span, :] = flow - far_rate[s, span, :] * a
            diff = a - adj[1 + y, span, :]
            delta[s, span, :] = (far_mob[s, span, :] + mobility(conc[1 + y, span, :])) * diff
        for at, size in chunks(low, high):
            span = slice(at, at + size)
            a, c, _flow, spread = face_sums(
                lambda dy, cut: adj[1 + y, cut, :], None, lambda dy, cut: far_conc[s, 0, cut, :],
                at, size, mask, ()
            )
            less = share * c
            inward = less * (adj[1 + y1, span, :] - a)
            pair = (far_chem[s, span, :] - (chem[1 + y, span, :] - less)) * (
                far_adj[s, 0, span, :] - a
            ) + (inward - share * spread)
            more = delta[s, span, :]
            step_z = (up(more) - more) * mask
            lap = (
                (delta[s, at + 1 : at + size + 1, :] + delta[s, at - 1 : at + size - 1, :])
                + (far_pot[s, span, :] - 4.0 * more)
                + (step_z - down(step_z))
            )
            out[s, 0, span, :] = (
                inside[y, span, :]
                + (swing[1 + y, span, :] * pair + curve[1 + y, span, :] * more)
                - grad_energy * lap
            )
            out[s, 1, span, :] = (
                inside[y1, span, :] + swing[1 + y1, span, :] * inward - grad_energy * more
            )
            edge_grad[s, span, :] = grad[y, span, :] + less * a
    send_rows(out, ahead, rate, to_a, to_b, open_g, cols, nz)


def core_kernel(steps, rows, cols, nz, conc_own, mob, chem, curve, swing, conc):
    lanes = conc.shape[2]
    mask = face_mask(lanes, nz)
    own = pad, pad + cols
    for row in (0, rows + 1):
        conc[row] = jnp.zeros(conc.shape[1:], f32)
    for i in range(steps - 1):
        for y in range(rows):
            conc[1 + y, pad : pad + cols, :] = conc_own[1 + i, y]

        def row(y, _):
            for at, size in chunks(*own):
                mob[i, y, at : at + size, :] = mobility(conc[1 + y, at : at + size, :])
                chem_row(row_of(conc, 1 + y), set_row(chem.at[i], y), set_row(curve.at[i], y),
                         set_row(swing.at[i], y), at, size, mask)
            return 0

        lax.fori_loop(0, rows, row, 0, unroll=4)


def prepare_kernel(steps, rows, cols, nz, back, conc_own, from_a, from_b, x_low, x_high,
                   corner_b, corner_a, mob_core, chem_core, curve_core, swing_core,
                   mob, chem, curve, swing, *rest):
    *more, conc = rest
    places, _ = slots(steps)
    low, high = reach(cols)
    lanes = conc.shape[2]
    mask = face_mask(lanes, nz)
    place = places[1 + back]
    own = slice(pad, pad + cols)
    for y in range(rows):
        put_own(conc, depth + y, conc_own[back, y], y, place, cols, x_low, x_high)
        mob[depth + y, own, :] = mob_core[back - 1, y, own, :]
        chem[1 + y, own, :] = chem_core[back - 1, y, own, :]
        curve[1 + y, own, :] = curve_core[back - 1, y, own, :]
        swing[1 + y, own, :] = swing_core[back - 1, y, own, :]
    for halo, corner, base in zip((from_a, from_b), (corner_a, corner_b), landings(rows, main_first)):
        for at in range(depth):
            first = (1 + back) * depth if back < early else (back - early) * depth
            span = pl.ds((first + at) * cols, cols)
            put_halo(conc, (base + at,), halo[span, :], at, place, cols, corner)

    if more:
        ahead, late_a, late_b = more
        put_ahead(ahead, conc_own, back + 1, x_low, x_high, places, rows, cols)
        for side, base in zip((late_a, late_b), bases(rows, main_first)):
            for after in range(early, steps):
                for at in range(depth):
                    span = pl.ds(((after - early) * depth + at) * cols, cols)
                    side[span, :] = conc_own[after, base + at]
            used = (steps - early) * depth * cols
            side[used:, :] = jnp.zeros((side.shape[0] - used, lanes), f32)

    for y in range(rows):
        for at in (low - 8, pad + cols):
            span = slice(at, at + 16)
            mob[depth + y, span, :] = mobility(conc[depth + y, span, :])
        for at in (low, pad + cols - 8):
            chem_row(row_of(conc, depth + y), set_row(chem, 1 + y), set_row(curve, 1 + y),
                     set_row(swing, 1 + y), at, 16, mask)
    for y, beyond in ((0, -1), (rows - 1, rows)):
        inner = slice(pad + 8, pad + cols - 8)
        chem[1 + y, inner, :] = chem[1 + y, inner, :] - (time_step * grad_energy) * (
            conc[depth + beyond, inner, :]
        )

    for y in (-1, rows):
        for at, size in chunks(low - 8, high + 8):
            mob[depth + y, at : at + size, :] = mobility(conc[depth + y, at : at + size, :])
        for at, size in chunks(low, high):
            chem_row(row_of(conc, depth + y), set_row(chem, 1 + y), lambda *_: None,
                     lambda *_: None, at, size, mask)


def next_interior(rows, cols, nz, final, mob, chem, curve, swing, rate, inner, outer, before, *rest):
    if final:
        out, tiles, grad_out, adj, pot, part, grad, turned, sem = rest
        send = pltpu.make_async_copy(turned, grad_out, sem)
    else:
        edge_before, out, grad, adj, pot, part, sums = rest
        for y in range(rows):
            sums[y] = before[y]
        for s, y in ((0, 0), (1, rows - 1)):
            sums[y] = edge_before[s]
        before = sums
    lanes = adj.shape[2]
    for y in range(depth, rows - depth):
        adj[1 + y] = inner[y]
    for s, k, y in sides_of(rows):
        adj[1 + y] = outer[s, k]
    adj[0] = outer[0, 0]
    adj[1 + rows] = outer[1, 0]

    def send_grad():
        for y in range(rows):
            turned[pl.ds(y, nz, stride=rows), :] = fold(grad[y, pad : pad + cols, :].T, nz)
        send.start()

    all_rows(rows, cols, nz, adj, mob, depth, chem, curve, swing, rate, before, pot, part, out,
             grad, send_grad if final else None)
    if final:
        for y in range(depth, rows - depth):
            tiles[pl.ds(y, lanes, stride=rows), :] = out[y, pad : pad + cols, :].T
        send.wait()


def fold(value, nz):
    total = value[:nz]
    for frame in range(1, value.shape[0] // nz):
        total = total + value[frame * nz : (frame + 1) * nz]
    return total


def next_boundary(rows, cols, nz, final, mob, chem, curve, swing, inside, outer, from_a, from_b,
                  *rest):
    if final:
        tiles, out, halo, delta, result = rest
    else:
        ahead, rate, result, to_a, to_b, halo, delta, open_g = rest
    low, high = reach(cols)
    first, last = sent(cols)
    lanes = mob.shape[2]
    mask = face_mask(lanes, nz)
    to_next = a_is_next("gy", round_first)
    for got, side in ((from_a, jnp.where(to_next, 1, 0)), (from_b, jnp.where(to_next, 0, 1))):
        for k in range(2):
            halo[side, k, first:last, :] = got[k]
    for s in range(2):
        y, beyond = s * (rows - 1), s * (rows + 1) - 1
        for at, size in chunks(low, high):
            span = slice(at, at + size)
            diff = halo[s, 0, span, :] - outer[s, 0, span, :]
            both = mob[depth + beyond, span, :] + mob[depth + y, span, :]
            delta[s, span, :] = both * diff
        for at, size in chunks(low, high):
            span = slice(at, at + size)
            more = delta[s, span, :]
            diff = halo[s, 0, span, :] - outer[s, 0, span, :]
            pair = (chem[1 + beyond, span, :] - chem[1 + y, span, :]) * diff
            step_z = (up(more) - more) * mask
            lap = (
                (delta[s, at + 1 : at + size + 1, :] + delta[s, at - 1 : at + size - 1, :])
                + (halo[s, 1, span, :] - more)
                - 4.0 * more
                + (step_z - down(step_z))
            )
            result[s, 0, span, :] = (
                inside[y, span, :]
                + (swing[1 + y, span, :] * pair + curve[1 + y, span, :] * more)
                - grad_energy * lap
            )
            result[s, 1, span, :] = inside[1 + s * (rows - 3), span, :] - grad_energy * more
    if final:
        out[...] = tiles[...]
        for s, k, y in sides_of(rows):
            out[pl.ds(y, lanes, stride=rows), :] = result[s, k, pad : pad + cols, :].T
    else:
        send_rows(result, ahead, rate, to_a, to_b, open_g, cols, nz)


def call(kernel, outs, scratch, *operands, cost=0, far=False, far_outs=()):
    if far:
        operands = [pltpu.with_memory_space_constraint(value, pltpu.HBM) for value in operands]
    space = pl.ANY if far else pltpu.VMEM
    return pl.pallas_call(
        kernel,
        out_shape=[jax.ShapeDtypeStruct(shape, f32) for shape in outs],
        in_specs=[pl.BlockSpec(memory_space=space)] * len(operands),
        out_specs=[
            pl.BlockSpec(memory_space=pltpu.HBM if i in far_outs else pltpu.VMEM)
            for i in range(len(outs))
        ],
        scratch_shapes=[pltpu.VMEM(s, f32) if isinstance(s, tuple) else s for s in scratch],
        compiler_params=pltpu.CompilerParams(vmem_limit_bytes=vmem_limit),
        cost_estimate=pl.CostEstimate(
            flops=cost * 1_000_000, bytes_accessed=cost * 2_000_000, transcendentals=0
        ),
    )(*operands)


def swap(value_a, value_b, axis, first):
    count = lax.axis_size(axis)
    pairs_a = [(i, (i + 1 - 2 * ((i + first) % 2)) % count) for i in range(count)]
    pairs_b = [(i, (i - 1 + 2 * ((i + first) % 2)) % count) for i in range(count)]
    return lax.ppermute(value_a, axis, pairs_a), lax.ppermute(value_b, axis, pairs_b)


def shards(saved_conc, adjoint_end, rate_field):
    steps, frames, nz, rows, cols = saved_conc.shape
    lanes = frames * nz
    _, total = slots(steps)
    width = cols + 2 * pad
    flat = lanes * rows

    def field(count):
        return (count, width, lanes)

    both = (2, depth, width, lanes)
    edge = (2, cols + 8, lanes)
    open_g = (2, cols + 16, lanes)
    raw = [(steps, flat, cols), (flat, cols), (nz * rows, cols)]
    conc_raw, adj_raw, rate_raw, main_a, main_b = call(
        functools.partial(edge_kernel, steps, rows, cols, nz),
        raw + [((1 + early) * depth * cols + cols // 2, lanes)] * 2,
        [pltpu.SemaphoreType.DMA((2 + steps, 2))],
        saved_conc.reshape(raw[0]), adjoint_end.reshape(raw[1]), rate_field.reshape(raw[2]),
        cost=2,
        far=True,
    )
    main_a, main_b = swap(main_a, main_b, "gy", main_first)
    conc_own, adj_own, rate_own, x_a, x_b = call(
        functools.partial(turn_kernel, steps, rows, cols, nz),
        [(steps, rows, cols, lanes), (rows, cols, lanes), (rows, cols, lanes)]
        + [(rows, total, lanes)] * 2,
        [],
        conc_raw, adj_raw, rate_raw,
        cost=1,
    )
    x_a, x_b = swap(x_a, x_b, "gx", x_first)
    whole = (steps - 1, rows, width, lanes)
    core = call(
        functools.partial(core_kernel, steps, rows, cols, nz),
        [whole] * 4,
        [field(rows + 2)],
        conc_own,
        cost=2,
    )
    x_low, x_high, corner_a, corner_b = call(
        functools.partial(corner_kernel, rows),
        [(rows, total, lanes)] * 2 + [(2, depth, total, lanes)] * 2,
        [],
        x_a, x_b, core[1],
    )
    corners = swap(corner_a, corner_b, "gy", round_first)
    corner_a, corner_b = corners if main_first == round_first else corners[::-1]

    conc, adj, rate, chem, curve, swing, inner, grad, ahead = call(
        functools.partial(first_interior, steps, rows, cols, nz),
        [field(rows + 2)] * 2 + [field(rows)] + [field(rows + 2)] * 3 + [field(rows)] * 2 + [both],
        [field(rows + 2)] * 2 + [field(rows)],
        conc_own, adj_own, rate_own, x_low, x_high,
        cost=3,
    )
    outer, edge_grad, to_a, to_b = call(
        functools.partial(first_boundary, steps, rows, cols, nz),
        [both, field(2), edge, edge],
        [both, both] + [field(2)] * 5 + [open_g],
        conc, adj, rate, chem, curve, swing, inner, grad, main_a, main_b, corner_b, corner_a, ahead,
        cost=2,
    )
    sums = (grad, edge_grad)
    got = main_a, main_b
    late = (max((steps - early) * depth * cols, 2 * (cols + 8) + 8), lanes)
    for back in range(1, steps):
        adj_a, adj_b = swap(to_a, to_b, "gy", round_first)
        final = back == steps - 1
        fields = call(
            functools.partial(prepare_kernel, steps, rows, cols, nz, back),
            [field(rows + 2 * depth)] + [field(rows + 2)] * 3
            + ([] if final else [both, late, late]),
            [field(rows + 2 * depth)],
            conc_own, *got, x_low, x_high, corner_b, corner_a, *core,
            cost=2,
        )
        fields, ahead, more = fields[:4], fields[4:5], fields[5:]
        if not final:
            got = swap(*more, "gy", main_first)
        work = [field(rows + 2)] * 2 + [field(rows)] * 2
        if final:
            inner, tiles, grad = call(
                functools.partial(next_interior, rows, cols, nz, final),
                [field(rows), (flat, cols), (nz * rows, cols)],
                work + [(nz * rows, cols), pltpu.SemaphoreType.DMA],
                *fields, rate, inner, outer, *sums,
                cost=3,
                far_outs=(2,),
            )
            (adj,) = call(
                functools.partial(next_boundary, rows, cols, nz, final),
                [(flat, cols)],
                [both, field(2), both],
                *fields, inner, outer, adj_a, adj_b, tiles,
                cost=1,
            )
        else:
            inner, grad = call(
                functools.partial(next_interior, rows, cols, nz, final),
                [field(rows)] * 2,
                work,
                *fields, rate, inner, outer, *sums,
                cost=3,
            )
            outer, to_a, to_b = call(
                functools.partial(next_boundary, rows, cols, nz, final),
                [both, edge, edge],
                [both, field(2), open_g],
                *fields, inner, outer, adj_a, adj_b, *ahead, rate,
                cost=1,
            )
            sums = (grad,)
    return adj.reshape(adjoint_end.shape), grad.reshape(rate_field.shape)


def solution(mesh):
    return jax.shard_map(
        shards,
        mesh=mesh,
        in_specs=(P(None, None, None, "gy", "gx"), P(None, None, "gy", "gx"), P(None, "gy", "gx")),
        out_specs=(P(None, None, "gy", "gx"), P(None, "gy", "gx")),
        check_vma=False,
    )
```

```python
import functools

import jax
import jax.numpy as jnp
from jax import lax
from jax.experimental import pallas as pl
from jax.experimental.pallas import tpu as pltpu
from jax.sharding import PartitionSpec as P

mix_energy = 2.5
grad_energy = 1.0
time_step = 0.1
diff_step = 0.03
bath_potential = 0.5

pad = 16
chunk = 72
depth = 2
early = 2
x_first, main_first, round_first = 0, 0, 1
vmem_limit = 20 * 1024 * 1024
f32 = jnp.float32


def slots(steps):
    widths = [2 * steps] + [2 * steps - 2 * back for back in range(steps)] + [2 * steps - 1]
    starts = [sum(widths[:i]) for i in range(len(widths))]
    total = -(-sum(widths) // 8) * 8
    return list(zip(starts, widths)), total


def chunks(low, high):
    return [(at, min(chunk, high - at)) for at in range(low, high, chunk)]


def reach(cols):
    return pad - 8, pad + cols + 8


def sent(cols):
    return pad - 4, pad + cols + 4


def up(value):
    return pltpu.roll(value, value.shape[1] - 1, 1)


def down(value):
    return pltpu.roll(value, 1, 1)


def face_mask(lanes, nz):
    lane = lax.broadcasted_iota(jnp.int32, (1, lanes), 1)
    return jnp.where(lane % nz == nz - 1, 0.0, 1.0).astype(f32)


def row_of(ref, y):
    return lambda dy, cut: ref[y + dy, cut, :]


def laplace(field, at, size, mask):
    span = slice(at, at + size)
    here = field(0, span)
    step_z = (up(here) - here) * mask
    sides = field(0, slice(at + 1, at + size + 1)) + field(0, slice(at - 1, at + size - 1))
    return here, (
        (sides + (field(-1, span) + field(1, span))) - 4.0 * here + (step_z - down(step_z))
    )


def mobility(c):
    return (0.5 * diff_step) * c * (1.0 - c)


def chem_row(conc, chem, curve, swing, at, size, mask):
    c, lap = laplace(conc, at, size, mask)
    inv = 1.0 / (c * (1.0 - c))
    span = slice(at, at + size)
    chem(
        span,
        time_step * (jnp.log(c * c * inv) - grad_energy * lap)
        + (time_step * (mix_energy - bath_potential) - (2.0 * time_step * mix_energy) * c),
    )
    curve(span, inv - 2.0 * mix_energy)
    swing(span, c * (diff_step / time_step) - 0.5 * diff_step / time_step)


def face_sums(adj, mob, chem, at, size, mask, across=(1, -1)):
    span = slice(at, at + size)
    a = adj(0, span)
    m = None if mob is None else mob(0, span)
    mu = None if chem is None else chem(0, span)
    flow = pair = None
    for dy, cut in (
        (0, slice(at + 1, at + size + 1)),
        (0, slice(at - 1, at + size - 1)),
    ) + tuple((dy, span) for dy in across):
        diff = adj(dy, cut) - a
        if mob is not None:
            term = (mob(dy, cut) + m) * diff
            flow = term if flow is None else flow + term
        if chem is not None:
            term = (chem(dy, cut) - mu) * diff
            pair = term if pair is None else pair + term
    diff = (up(a) - a) * mask
    if mob is not None:
        term = (up(m) + m) * diff
        flow = flow + (term - down(term))
    if chem is not None:
        term = (up(mu) - mu) * diff
        pair = pair + (term + down(term))
    return a, mu, flow, pair


def partial(a, swing, pair, curve, g):
    return a + swing * pair + curve * g


def gain(a, chem, before):
    value = a * chem
    return -value if before is None else before - value


def set_row(ref, y):
    def put(span, value):
        ref[y, span, :] = value

    return put


def all_rows(rows, cols, nz, adj, mob, mob_skip, chem, curve, swing, rate, before, pot, part, out,
             grad, between=None):
    low, high = reach(cols)
    mask = face_mask(adj.shape[2], nz)

    def body(y, _):
        for at, size in chunks(low, high):
            span = slice(at, at + size)
            a, mu, flow, pair = face_sums(
                row_of(adj, y + 1), row_of(mob, y + mob_skip), row_of(chem, y + 1), at, size, mask
            )
            g = flow - rate[y, span, :] * a
            pot[y + 1, span, :] = g
            part[y, span, :] = partial(
                a, swing[y + 1, span, :], pair, curve[y + 1, span, :], g
            )
            grad[y, span, :] = gain(a, mu, None if before is None else before[y, span, :])
        return 0

    def close(y, _):
        for at, size in chunks(low, high):
            span = slice(at, at + size)
            _g, lap = laplace(row_of(pot, y + 1), at, size, mask)
            out[y, span, :] = part[y, span, :] - grad_energy * lap
        return 0

    for row in (0, rows + 1):
        pot[row] = jnp.zeros(pot.shape[1:], f32)
    lax.fori_loop(0, rows, body, 0, unroll=2)
    if between is not None:
        between()
    lax.fori_loop(0, rows, close, 0, unroll=4)


def a_is_next(axis, first):
    return lax.rem(lax.axis_index(axis), 2) == first


def bases(rows, first):
    to_next = a_is_next("gy", first)
    top = rows - depth
    return jnp.where(to_next, top, 0), jnp.where(to_next, 0, top)


def landings(rows, first):
    to_next = a_is_next("gy", first)
    top = rows + depth
    return jnp.where(to_next, top, 0), jnp.where(to_next, 0, top)


def sides_of(rows):
    return [(0, 0, 0), (0, 1, 1), (1, 0, rows - 1), (1, 1, rows - 2)]


def edge_kernel(steps, rows, cols, nz, conc_hbm, adj_hbm, rate_hbm, conc_in, adj_in, rate_in,
                main_a, main_b, sems):
    lanes = main_a.shape[1]
    half = cols // 2
    lower = lax.broadcasted_iota(jnp.int32, (half, lanes), 1) < nz
    fetches = [(adj_hbm, adj_in), (rate_hbm, rate_in)] + [
        (conc_hbm.at[steps - 1 - back], conc_in.at[back]) for back in range(steps)
    ]
    copies = []
    for i, (there, here) in enumerate(fetches):
        part = here.shape[0] // 2
        copies.append(
            [
                pltpu.make_async_copy(
                    there.at[pl.ds(k * part, part)], here.at[pl.ds(k * part, part)], sems.at[i, k]
                )
                for k in range(2)
            ]
        )
    for pair in copies:
        for copy in pair:
            copy.start()

    def arrived(i):
        for copy in copies[i]:
            copy.wait()

    arrived(0)
    for side, base in zip((main_a, main_b), bases(rows, main_first)):
        for at in range(depth):
            side[pl.ds(at * cols, cols), :] = adj_in[pl.ds(base + at, lanes, stride=rows), :].T
    arrived(1)
    for side, base in zip((main_a, main_b), bases(rows, main_first)):
        edge = jnp.where(base == 0, 0, rows - 1)
        rate = turned_rate(rate_in, edge, rows, nz, lanes)
        side[pl.ds((1 + early) * depth * cols, half), :] = jnp.where(
            lower, rate[:half], rate[half:]
        )
    for back in range(steps):
        arrived(2 + back)
        if back >= early:
            continue
        for side, base in zip((main_a, main_b), bases(rows, main_first)):
            for at in range(depth):
                side[pl.ds(((1 + back) * depth + at) * cols, cols), :] = conc_in[
                    back, pl.ds(base + at, lanes, stride=rows), :
                ].T


def turned_rate(rate, y, rows, nz, lanes):
    value = time_step * rate[pl.ds(y, nz, stride=rows), :]
    return jnp.concatenate([value] * (lanes // nz), axis=0).T


def turn_kernel(steps, rows, cols, nz, conc_in, adj_in, rate_in, conc_out, adj_out, rate_out,
                x_a, x_b):
    places, total = slots(steps)
    lanes = adj_out.shape[2]
    next_x = a_is_next("gx", x_first)

    def to_x(y, value, place):
        start, width = place
        last, first = value[cols - width :, :], value[:width, :]
        x_a[y, start : start + width, :] = jnp.where(next_x, last, first)
        x_b[y, start : start + width, :] = jnp.where(next_x, first, last)

    used = sum(places[-1])
    for y in range(rows):
        adj = adj_in[pl.ds(y, lanes, stride=rows), :].T
        adj_out[y] = adj
        to_x(y, adj, places[0])
        rate = turned_rate(rate_in, y, rows, nz, lanes)
        rate_out[y] = rate
        to_x(y, rate, places[steps + 1])
        if used < total:
            x_a[y, used:, :] = jnp.zeros((total - used, lanes), f32)
            x_b[y, used:, :] = jnp.zeros((total - used, lanes), f32)
        for back in range(steps):
            conc = conc_in[back, pl.ds(y, lanes, stride=rows), :].T
            conc_out[back, y] = conc
            to_x(y, conc, places[1 + back])


def put_own(out, row, value, y, place, cols, x_low, x_high):
    start, width = place
    right = pad + cols
    out[row, pad:right, :] = value
    out[row, pad - width : pad, :] = x_low[y, start : start + width, :]
    out[row, right : right + width, :] = x_high[y, start : start + width, :]


def put_halo(out, index, value, from_row, place, cols, corner):
    start, width = place
    right = pad + cols
    out[(*index, slice(pad, right))] = value
    out[(*index, slice(pad - width, pad))] = corner[0, from_row, start : start + width, :]
    out[(*index, slice(right, right + width))] = corner[1, from_row, start : start + width, :]


def corner_kernel(rows, got_a, got_b, _core, x_low, x_high, corner_a, corner_b):
    next_x = a_is_next("gx", x_first)
    x_low[...] = jnp.where(next_x, got_b[...], got_a[...])
    x_high[...] = jnp.where(next_x, got_a[...], got_b[...])
    for out, base in zip((corner_a, corner_b), bases(rows, round_first)):
        for at in range(depth):
            out[0, at] = x_low[base + at]
            out[1, at] = x_high[base + at]


def first_interior(steps, rows, cols, nz, conc_own, adj_own, rate_own, x_low, x_high,
                   conc, adj, rate, chem, curve, swing, out, grad, ahead, mob, pot, part):
    places, _ = slots(steps)
    low, high = reach(cols)
    lanes = adj.shape[2]
    mask = face_mask(lanes, nz)
    for y in range(rows):
        put_own(conc, 1 + y, conc_own[0, y], y, places[1], cols, x_low, x_high)
        put_own(adj, 1 + y, adj_own[y], y, places[0], cols, x_low, x_high)
        put_own(rate, y, rate_own[y], y, places[steps + 1], cols, x_low, x_high)
    for row, beside in ((0, 1), (rows + 1, rows)):
        adj[row] = adj[beside]
        for ref in (conc, chem, mob):
            ref[row] = jnp.zeros(ref.shape[1:], f32)
    put_ahead(ahead, conc_own, 1, x_low, x_high, places, rows, cols)

    def mob_row(row, _):
        for at, size in chunks(low - 8, high + 8):
            mob[row, at : at + size, :] = mobility(conc[row, at : at + size, :])
        return 0

    def mu_row(row, _):
        for at, size in chunks(low, high):
            chem_row(row_of(conc, row), set_row(chem, row), set_row(curve, row),
                     set_row(swing, row), at, size, mask)
        return 0

    lax.fori_loop(1, rows + 1, mob_row, 0, unroll=4)
    lax.fori_loop(1, rows + 1, mu_row, 0, unroll=2)
    all_rows(rows, cols, nz, adj, mob, 1, chem, curve, swing, rate, None, pot, part, out, grad)


def send_rows(out, ahead, rate, to_a, to_b, open_g, cols, nz):
    low, high = reach(cols)
    first, last = sent(cols)
    rows, lanes = rate.shape[0], rate.shape[2]
    mask = face_mask(lanes, nz)
    for s in range(2):
        for at, size in chunks(low, high):
            a, _mu, flow, _pair = face_sums(
                lambda dy, cut: out[s, dy, cut, :], lambda dy, cut: ahead[s, dy, cut, :], None,
                at, size, mask, (1,)
            )
            open_g[s, at - low : at - low + size, :] = (
                flow - rate[s * (rows - 1), at : at + size, :] * a
            )
    to_next = a_is_next("gy", round_first)
    for to, side in ((to_a, jnp.where(to_next, 1, 0)), (to_b, jnp.where(to_next, 0, 1))):
        to[0] = out[side, 0, first:last, :]
        to[1] = open_g[side, first - low : last - low, :]


def put_ahead(ahead, conc_own, back, x_low, x_high, places, rows, cols):
    for s, k, y in sides_of(rows):
        put_own(ahead.at[s], k, conc_own[back, y], y, places[1 + back], cols, x_low, x_high)
        ahead[s, k] = mobility(ahead[s, k])


def first_boundary(steps, rows, cols, nz, conc, adj, rate, chem, curve, swing, inside, grad,
                   from_a, from_b, corner_b, corner_a, ahead,
                   out, edge_grad, to_a, to_b, far_conc, far_adj, far_rate, far_mob, far_chem,
                   far_pot, delta, open_g):
    places, _ = slots(steps)
    low, high = reach(cols)
    half = cols // 2
    lanes = conc.shape[2]
    mask = face_mask(lanes, nz)
    lower = lax.broadcasted_iota(jnp.int32, (half, lanes), 1) < nz
    to_next = a_is_next("gy", main_first)

    def unpack(side):
        packed = side[pl.ds((1 + early) * depth * cols, half), :]
        turned = pltpu.roll(packed, lanes // 2, 1)
        return jnp.concatenate(
            [jnp.where(lower, packed, turned), jnp.where(lower, turned, packed)], axis=0
        )

    for halo, corner, side in (
        (from_a, corner_a, jnp.where(to_next, 1, 0)),
        (from_b, corner_b, jnp.where(to_next, 0, 1)),
    ):
        for at in range(depth):
            step = jnp.where(side == 1, at, depth - 1 - at)
            for ref, place, first in ((far_adj, places[0], 0), (far_conc, places[1], depth)):
                span = pl.ds((first + at) * cols, cols)
                put_halo(ref, (side, step), halo[span, :], at, place, cols, corner)
        put_halo(far_rate, (side,), unpack(halo), jnp.where(side == 1, 0, depth - 1),
                 places[steps + 1], cols, corner)

    share = time_step * grad_energy
    def side_rows(s, _):
        y, y1 = s * (rows - 1), 1 + s * (rows - 3)
        for at, size in chunks(low - 8, high + 8):
            span = slice(at, at + size)
            far_mob[s, span, :] = mobility(far_conc[s, 0, span, :])

        def conc_at(dy, cut):
            return conc[1 + y, cut, :] if dy == 1 else far_conc[s, -dy, cut, :]

        def adj_at(dy, cut):
            return adj[1 + y, cut, :] if dy == 1 else far_adj[s, -dy, cut, :]

        def mob_at(dy, cut):
            return far_mob[s, cut, :] if dy == 0 else mobility(conc_at(dy, cut))

        for at, size in chunks(low, high):
            span = slice(at, at + size)
            chem_row(conc_at, set_row(far_chem, s), lambda *_: None, lambda *_: None, at, size,
                     mask)
            a, _mu, flow, _pair = face_sums(adj_at, mob_at, None, at, size, mask)
            far_pot[s, span, :] = flow - far_rate[s, span, :] * a
            diff = a - adj[1 + y, span, :]
            delta[s, span, :] = (far_mob[s, span, :] + mobility(conc[1 + y, span, :])) * diff
        for at, size in chunks(low, high):
            span = slice(at, at + size)
            a, c, _flow, spread = face_sums(
                lambda dy, cut: adj[1 + y, cut, :], None, lambda dy, cut: far_conc[s, 0, cut, :],
                at, size, mask, ()
            )
            less = share * c
            inward = less * (adj[1 + y1, span, :] - a)
            pair = (far_chem[s, span, :] - (chem[1 + y, span, :] - less)) * (
                far_adj[s, 0, span, :] - a
            ) + (inward - share * spread)
            more = delta[s, span, :]
            step_z = (up(more) - more) * mask
            lap = (
                (delta[s, at + 1 : at + size + 1, :] + delta[s, at - 1 : at + size - 1, :])
                + (far_pot[s, span, :] - 4.0 * more)
                + (step_z - down(step_z))
            )
            out[s, 0, span, :] = (
                inside[y, span, :]
                + (swing[1 + y, span, :] * pair + curve[1 + y, span, :] * more)
                - grad_energy * lap
            )
            out[s, 1, span, :] = (
                inside[y1, span, :] + swing[1 + y1, span, :] * inward - grad_energy * more
            )
            edge_grad[s, span, :] = grad[y, span, :] + less * a
        return 0

    lax.fori_loop(0, 2, side_rows, 0)
    send_rows(out, ahead, rate, to_a, to_b, open_g, cols, nz)


def core_kernel(steps, rows, cols, nz, conc_own, mob, chem, curve, swing, conc):
    lanes = conc.shape[2]
    mask = face_mask(lanes, nz)
    own = pad, pad + cols
    for row in (0, rows + 1):
        conc[row] = jnp.zeros(conc.shape[1:], f32)
    for i in range(steps - 1):
        for y in range(rows):
            conc[1 + y, pad : pad + cols, :] = conc_own[1 + i, y]

        def row(y, _):
            for at, size in chunks(*own):
                mob[i, y, at : at + size, :] = mobility(conc[1 + y, at : at + size, :])
                chem_row(row_of(conc, 1 + y), set_row(chem.at[i], y), set_row(curve.at[i], y),
                         set_row(swing.at[i], y), at, size, mask)
            return 0

        lax.fori_loop(0, rows, row, 0, unroll=4)


def prepare_kernel(steps, rows, cols, nz, back, conc_own, from_a, from_b, x_low, x_high,
                   corner_b, corner_a, mob_core, chem_core, curve_core, swing_core,
                   mob, chem, curve, swing, *rest):
    *more, conc = rest
    places, _ = slots(steps)
    low, high = reach(cols)
    lanes = conc.shape[2]
    mask = face_mask(lanes, nz)
    place = places[1 + back]
    own = slice(pad, pad + cols)
    for y in range(rows):
        put_own(conc, depth + y, conc_own[back, y], y, place, cols, x_low, x_high)
        mob[depth + y, own, :] = mob_core[back - 1, y, own, :]
        chem[1 + y, own, :] = chem_core[back - 1, y, own, :]
        curve[1 + y, own, :] = curve_core[back - 1, y, own, :]
        swing[1 + y, own, :] = swing_core[back - 1, y, own, :]
    for halo, corner, base in zip((from_a, from_b), (corner_a, corner_b), landings(rows, main_first)):
        for at in range(depth):
            first = (1 + back) * depth if back < early else (back - early) * depth
            span = pl.ds((first + at) * cols, cols)
            put_halo(conc, (base + at,), halo[span, :], at, place, cols, corner)

    if more:
        ahead, late_a, late_b = more
        put_ahead(ahead, conc_own, back + 1, x_low, x_high, places, rows, cols)
        for side, base in zip((late_a, late_b), bases(rows, main_first)):
            for after in range(early, steps):
                for at in range(depth):
                    span = pl.ds(((after - early) * depth + at) * cols, cols)
                    side[span, :] = conc_own[after, base + at]
            used = (steps - early) * depth * cols
            side[used:, :] = jnp.zeros((side.shape[0] - used, lanes), f32)

    for y in range(rows):
        for at in (low - 8, pad + cols):
            span = slice(at, at + 16)
            mob[depth + y, span, :] = mobility(conc[depth + y, span, :])
        for at in (low, pad + cols - 8):
            chem_row(row_of(conc, depth + y), set_row(chem, 1 + y), set_row(curve, 1 + y),
                     set_row(swing, 1 + y), at, 16, mask)
    for y, beyond in ((0, -1), (rows - 1, rows)):
        inner = slice(pad + 8, pad + cols - 8)
        chem[1 + y, inner, :] = chem[1 + y, inner, :] - (time_step * grad_energy) * (
            conc[depth + beyond, inner, :]
        )

    for y in (-1, rows):
        for at, size in chunks(low - 8, high + 8):
            mob[depth + y, at : at + size, :] = mobility(conc[depth + y, at : at + size, :])
        for at, size in chunks(low, high):
            chem_row(row_of(conc, depth + y), set_row(chem, 1 + y), lambda *_: None,
                     lambda *_: None, at, size, mask)


def next_interior(rows, cols, nz, final, mob, chem, curve, swing, rate, inner, outer, before, *rest):
    if final:
        out, tiles, grad_out, adj, pot, part, grad, turned, sem = rest
        send = pltpu.make_async_copy(turned, grad_out, sem)
    else:
        edge_before, out, grad, adj, pot, part, sums = rest
        for y in range(rows):
            sums[y] = before[y]
        for s, y in ((0, 0), (1, rows - 1)):
            sums[y] = edge_before[s]
        before = sums
    lanes = adj.shape[2]
    for y in range(depth, rows - depth):
        adj[1 + y] = inner[y]
    for s, k, y in sides_of(rows):
        adj[1 + y] = outer[s, k]
    adj[0] = outer[0, 0]
    adj[1 + rows] = outer[1, 0]

    def send_grad():
        for y in range(rows):
            turned[pl.ds(y, nz, stride=rows), :] = fold(grad[y, pad : pad + cols, :].T, nz)
        send.start()

    all_rows(rows, cols, nz, adj, mob, depth, chem, curve, swing, rate, before, pot, part, out,
             grad, send_grad if final else None)
    if final:
        for y in range(depth, rows - depth):
            tiles[pl.ds(y, lanes, stride=rows), :] = out[y, pad : pad + cols, :].T
        send.wait()


def fold(value, nz):
    total = value[:nz]
    for frame in range(1, value.shape[0] // nz):
        total = total + value[frame * nz : (frame + 1) * nz]
    return total


def next_boundary(rows, cols, nz, final, mob, chem, curve, swing, inside, outer, from_a, from_b,
                  *rest):
    if final:
        tiles, out, halo, delta, result = rest
    else:
        ahead, rate, result, to_a, to_b, halo, delta, open_g = rest
    low, high = reach(cols)
    first, last = sent(cols)
    lanes = mob.shape[2]
    mask = face_mask(lanes, nz)
    to_next = a_is_next("gy", round_first)
    for got, side in ((from_a, jnp.where(to_next, 1, 0)), (from_b, jnp.where(to_next, 0, 1))):
        for k in range(2):
            halo[side, k, first:last, :] = got[k]
    for s in range(2):
        y, beyond = s * (rows - 1), s * (rows + 1) - 1
        for at, size in chunks(low, high):
            span = slice(at, at + size)
            diff = halo[s, 0, span, :] - outer[s, 0, span, :]
            both = mob[depth + beyond, span, :] + mob[depth + y, span, :]
            delta[s, span, :] = both * diff
        for at, size in chunks(low, high):
            span = slice(at, at + size)
            more = delta[s, span, :]
            diff = halo[s, 0, span, :] - outer[s, 0, span, :]
            pair = (chem[1 + beyond, span, :] - chem[1 + y, span, :]) * diff
            step_z = (up(more) - more) * mask
            lap = (
                (delta[s, at + 1 : at + size + 1, :] + delta[s, at - 1 : at + size - 1, :])
                + (halo[s, 1, span, :] - more)
                - 4.0 * more
                + (step_z - down(step_z))
            )
            result[s, 0, span, :] = (
                inside[y, span, :]
                + (swing[1 + y, span, :] * pair + curve[1 + y, span, :] * more)
                - grad_energy * lap
            )
            result[s, 1, span, :] = inside[1 + s * (rows - 3), span, :] - grad_energy * more
    if final:
        out[...] = tiles[...]
        for s, k, y in sides_of(rows):
            out[pl.ds(y, lanes, stride=rows), :] = result[s, k, pad : pad + cols, :].T
    else:
        send_rows(result, ahead, rate, to_a, to_b, open_g, cols, nz)


def call(kernel, outs, scratch, *operands, cost=0, far=False, far_outs=()):
    if far:
        operands = [pltpu.with_memory_space_constraint(value, pltpu.HBM) for value in operands]
    space = pl.ANY if far else pltpu.VMEM
    return pl.pallas_call(
        kernel,
        out_shape=[jax.ShapeDtypeStruct(shape, f32) for shape in outs],
        in_specs=[pl.BlockSpec(memory_space=space)] * len(operands),
        out_specs=[
            pl.BlockSpec(memory_space=pltpu.HBM if i in far_outs else pltpu.VMEM)
            for i in range(len(outs))
        ],
        scratch_shapes=[pltpu.VMEM(s, f32) if isinstance(s, tuple) else s for s in scratch],
        compiler_params=pltpu.CompilerParams(vmem_limit_bytes=vmem_limit),
        cost_estimate=pl.CostEstimate(
            flops=cost * 1_000_000, bytes_accessed=cost * 2_000_000, transcendentals=0
        ),
    )(*operands)


def swap(value_a, value_b, axis, first):
    count = lax.axis_size(axis)
    pairs_a = [(i, (i + 1 - 2 * ((i + first) % 2)) % count) for i in range(count)]
    pairs_b = [(i, (i - 1 + 2 * ((i + first) % 2)) % count) for i in range(count)]
    return lax.ppermute(value_a, axis, pairs_a), lax.ppermute(value_b, axis, pairs_b)


def shards(saved_conc, adjoint_end, rate_field):
    steps, frames, nz, rows, cols = saved_conc.shape
    lanes = frames * nz
    _, total = slots(steps)
    width = cols + 2 * pad
    flat = lanes * rows

    def field(count):
        return (count, width, lanes)

    both = (2, depth, width, lanes)
    edge = (2, cols + 8, lanes)
    open_g = (2, cols + 16, lanes)
    raw = [(steps, flat, cols), (flat, cols), (nz * rows, cols)]
    conc_raw, adj_raw, rate_raw, main_a, main_b = call(
        functools.partial(edge_kernel, steps, rows, cols, nz),
        raw + [((1 + early) * depth * cols + cols // 2, lanes)] * 2,
        [pltpu.SemaphoreType.DMA((2 + steps, 2))],
        saved_conc.reshape(raw[0]), adjoint_end.reshape(raw[1]), rate_field.reshape(raw[2]),
        cost=2,
        far=True,
    )
    main_a, main_b = swap(main_a, main_b, "gy", main_first)
    conc_own, adj_own, rate_own, x_a, x_b = call(
        functools.partial(turn_kernel, steps, rows, cols, nz),
        [(steps, rows, cols, lanes), (rows, cols, lanes), (rows, cols, lanes)]
        + [(rows, total, lanes)] * 2,
        [],
        conc_raw, adj_raw, rate_raw,
        cost=1,
    )
    x_a, x_b = swap(x_a, x_b, "gx", x_first)
    whole = (steps - 1, rows, width, lanes)
    core = call(
        functools.partial(core_kernel, steps, rows, cols, nz),
        [whole] * 4,
        [field(rows + 2)],
        conc_own,
        cost=2,
    )
    x_low, x_high, corner_a, corner_b = call(
        functools.partial(corner_kernel, rows),
        [(rows, total, lanes)] * 2 + [(2, depth, total, lanes)] * 2,
        [],
        x_a, x_b, core[1],
    )
    corners = swap(corner_a, corner_b, "gy", round_first)
    corner_a, corner_b = corners if main_first == round_first else corners[::-1]

    conc, adj, rate, chem, curve, swing, inner, grad, ahead = call(
        functools.partial(first_interior, steps, rows, cols, nz),
        [field(rows + 2)] * 2 + [field(rows)] + [field(rows + 2)] * 3 + [field(rows)] * 2 + [both],
        [field(rows + 2)] * 2 + [field(rows)],
        conc_own, adj_own, rate_own, x_low, x_high,
        cost=3,
    )
    outer, edge_grad, to_a, to_b = call(
        functools.partial(first_boundary, steps, rows, cols, nz),
        [both, field(2), edge, edge],
        [both, both] + [field(2)] * 5 + [open_g],
        conc, adj, rate, chem, curve, swing, inner, grad, main_a, main_b, corner_b, corner_a, ahead,
        cost=2,
    )
    sums = (grad, edge_grad)
    got = main_a, main_b
    late = (max((steps - early) * depth * cols, 2 * (cols + 8) + 8), lanes)
    for back in range(1, steps):
        adj_a, adj_b = swap(to_a, to_b, "gy", round_first)
        final = back == steps - 1
        fields = call(
            functools.partial(prepare_kernel, steps, rows, cols, nz, back),
            [field(rows + 2 * depth)] + [field(rows + 2)] * 3
            + ([] if final else [both, late, late]),
            [field(rows + 2 * depth)],
            conc_own, *got, x_low, x_high, corner_b, corner_a, *core,
            cost=2,
        )
        fields, ahead, more = fields[:4], fields[4:5], fields[5:]
        if not final:
            got = swap(*more, "gy", main_first)
        work = [field(rows + 2)] * 2 + [field(rows)] * 2
        if final:
            inner, tiles, grad = call(
                functools.partial(next_interior, rows, cols, nz, final),
                [field(rows), (flat, cols), (nz * rows, cols)],
                work + [(nz * rows, cols), pltpu.SemaphoreType.DMA],
                *fields, rate, inner, outer, *sums,
                cost=3,
                far_outs=(2,),
            )
            (adj,) = call(
                functools.partial(next_boundary, rows, cols, nz, final),
                [(flat, cols)],
                [both, field(2), both],
                *fields, inner, outer, adj_a, adj_b, tiles,
                cost=1,
            )
        else:
            inner, grad = call(
                functools.partial(next_interior, rows, cols, nz, final),
                [field(rows)] * 2,
                work,
                *fields, rate, inner, outer, *sums,
                cost=3,
            )
            outer, to_a, to_b = call(
                functools.partial(next_boundary, rows, cols, nz, final),
                [both, edge, edge],
                [both, field(2), open_g],
                *fields, inner, outer, adj_a, adj_b, *ahead, rate,
                cost=1,
            )
            sums = (grad,)
    return adj.reshape(adjoint_end.shape), grad.reshape(rate_field.shape)


def solution(mesh):
    return jax.shard_map(
        shards,
        mesh=mesh,
        in_specs=(P(None, None, None, "gy", "gx"), P(None, None, "gy", "gx"), P(None, "gy", "gx")),
        out_specs=(P(None, None, "gy", "gx"), P(None, "gy", "gx")),
        check_vma=False,
    )
```

```python
import functools

import jax
import jax.numpy as jnp
from jax import lax
from jax.experimental import pallas as pl
from jax.experimental.pallas import tpu as pltpu
from jax.sharding import PartitionSpec as P

mix_energy = 2.5
grad_energy = 1.0
time_step = 0.1
diff_step = 0.03
bath_potential = 0.5

pad = 16
chunk = 72
depth = 2
early = 2
x_first, main_first, round_first = 0, 0, 1
vmem_limit = 20 * 1024 * 1024
f32 = jnp.float32


def slots(steps):
    widths = [2 * steps] + [2 * steps - 2 * back for back in range(steps)] + [2 * steps - 1]
    starts = [sum(widths[:i]) for i in range(len(widths))]
    total = -(-sum(widths) // 8) * 8
    return list(zip(starts, widths)), total


def chunks(low, high):
    return [(at, min(chunk, high - at)) for at in range(low, high, chunk)]


def reach(cols):
    return pad - 8, pad + cols + 8


def sent(cols):
    return pad - 4, pad + cols + 4


def up(value):
    return pltpu.roll(value, value.shape[1] - 1, 1)


def down(value):
    return pltpu.roll(value, 1, 1)


def face_mask(lanes, nz):
    lane = lax.broadcasted_iota(jnp.int32, (1, lanes), 1)
    return jnp.where(lane % nz == nz - 1, 0.0, 1.0).astype(f32)


def row_of(ref, y):
    return lambda dy, cut: ref[y + dy, cut, :]


def laplace(field, at, size, mask):
    span = slice(at, at + size)
    here = field(0, span)
    step_z = (up(here) - here) * mask
    sides = field(0, slice(at + 1, at + size + 1)) + field(0, slice(at - 1, at + size - 1))
    return here, (
        (sides + (field(-1, span) + field(1, span))) - 4.0 * here + (step_z - down(step_z))
    )


def mobility(c):
    return (0.5 * diff_step) * c * (1.0 - c)


def chem_row(conc, chem, curve, swing, at, size, mask):
    c, lap = laplace(conc, at, size, mask)
    inv = 1.0 / (c * (1.0 - c))
    span = slice(at, at + size)
    chem(
        span,
        time_step * (jnp.log(c * c * inv) - grad_energy * lap)
        + (time_step * (mix_energy - bath_potential) - (2.0 * time_step * mix_energy) * c),
    )
    curve(span, inv - 2.0 * mix_energy)
    swing(span, c * (diff_step / time_step) - 0.5 * diff_step / time_step)


def face_sums(adj, mob, chem, at, size, mask, across=(1, -1)):
    span = slice(at, at + size)
    a = adj(0, span)
    m = None if mob is None else mob(0, span)
    mu = None if chem is None else chem(0, span)
    flow = pair = None
    for dy, cut in (
        (0, slice(at + 1, at + size + 1)),
        (0, slice(at - 1, at + size - 1)),
    ) + tuple((dy, span) for dy in across):
        diff = adj(dy, cut) - a
        if mob is not None:
            term = (mob(dy, cut) + m) * diff
            flow = term if flow is None else flow + term
        if chem is not None:
            term = (chem(dy, cut) - mu) * diff
            pair = term if pair is None else pair + term
    diff = (up(a) - a) * mask
    if mob is not None:
        term = (up(m) + m) * diff
        flow = flow + (term - down(term))
    if chem is not None:
        term = (up(mu) - mu) * diff
        pair = pair + (term + down(term))
    return a, mu, flow, pair


def partial(a, swing, pair, curve, g):
    return a + swing * pair + curve * g


def gain(a, chem, before):
    value = a * chem
    return -value if before is None else before - value


def set_row(ref, y):
    def put(span, value):
        ref[y, span, :] = value

    return put


def all_rows(rows, cols, nz, adj, mob, mob_skip, chem, curve, swing, rate, before, pot, part, out,
             grad, between=None):
    low, high = reach(cols)
    mask = face_mask(adj.shape[2], nz)

    def body(y, _):
        for at, size in chunks(low, high):
            span = slice(at, at + size)
            a, mu, flow, pair = face_sums(
                row_of(adj, y + 1), row_of(mob, y + mob_skip), row_of(chem, y + 1), at, size, mask
            )
            g = flow - rate[y, span, :] * a
            pot[y + 1, span, :] = g
            part[y, span, :] = partial(
                a, swing[y + 1, span, :], pair, curve[y + 1, span, :], g
            )
            grad[y, span, :] = gain(a, mu, None if before is None else before[y, span, :])
        return 0

    def close(y, _):
        for at, size in chunks(low, high):
            span = slice(at, at + size)
            _g, lap = laplace(row_of(pot, y + 1), at, size, mask)
            out[y, span, :] = part[y, span, :] - grad_energy * lap
        return 0

    for row in (0, rows + 1):
        pot[row] = jnp.zeros(pot.shape[1:], f32)
    lax.fori_loop(0, rows, body, 0, unroll=2)
    if between is not None:
        between()
    lax.fori_loop(0, rows, close, 0, unroll=4)


def a_is_next(axis, first):
    return lax.rem(lax.axis_index(axis), 2) == first


def bases(rows, first):
    to_next = a_is_next("gy", first)
    top = rows - depth
    return jnp.where(to_next, top, 0), jnp.where(to_next, 0, top)


def landings(rows, first):
    to_next = a_is_next("gy", first)
    top = rows + depth
    return jnp.where(to_next, top, 0), jnp.where(to_next, 0, top)


def sides_of(rows):
    return [(0, 0, 0), (0, 1, 1), (1, 0, rows - 1), (1, 1, rows - 2)]


def edge_kernel(steps, rows, cols, nz, conc_hbm, adj_hbm, rate_hbm, conc_in, adj_in, rate_in,
                main_a, main_b, sems):
    lanes = main_a.shape[1]
    half = cols // 2
    lower = lax.broadcasted_iota(jnp.int32, (half, lanes), 1) < nz
    fetches = [(adj_hbm, adj_in), (rate_hbm, rate_in)] + [
        (conc_hbm.at[steps - 1 - back], conc_in.at[back]) for back in range(steps)
    ]
    copies = []
    for i, (there, here) in enumerate(fetches):
        part = here.shape[0] // 2
        copies.append(
            [
                pltpu.make_async_copy(
                    there.at[pl.ds(k * part, part)], here.at[pl.ds(k * part, part)], sems.at[i, k]
                )
                for k in range(2)
            ]
        )
    for pair in copies:
        for copy in pair:
            copy.start()

    def arrived(i):
        for copy in copies[i]:
            copy.wait()

    arrived(0)
    for side, base in zip((main_a, main_b), bases(rows, main_first)):
        for at in range(depth):
            side[pl.ds(at * cols, cols), :] = adj_in[pl.ds(base + at, lanes, stride=rows), :].T
    arrived(1)
    for side, base in zip((main_a, main_b), bases(rows, main_first)):
        edge = jnp.where(base == 0, 0, rows - 1)
        rate = turned_rate(rate_in, edge, rows, nz, lanes)
        side[pl.ds((1 + early) * depth * cols, half), :] = jnp.where(
            lower, rate[:half], rate[half:]
        )
    for back in range(steps):
        arrived(2 + back)
        if back >= early:
            continue
        for side, base in zip((main_a, main_b), bases(rows, main_first)):
            for at in range(depth):
                side[pl.ds(((1 + back) * depth + at) * cols, cols), :] = conc_in[
                    back, pl.ds(base + at, lanes, stride=rows), :
                ].T


def turned_rate(rate, y, rows, nz, lanes):
    value = time_step * rate[pl.ds(y, nz, stride=rows), :]
    return jnp.concatenate([value] * (lanes // nz), axis=0).T


def turn_kernel(steps, rows, cols, nz, conc_in, adj_in, rate_in, conc_out, adj_out, rate_out,
                x_a, x_b):
    places, total = slots(steps)
    lanes = adj_out.shape[2]
    next_x = a_is_next("gx", x_first)

    def to_x(y, value, place):
        start, width = place
        last, first = value[cols - width :, :], value[:width, :]
        x_a[y, start : start + width, :] = jnp.where(next_x, last, first)
        x_b[y, start : start + width, :] = jnp.where(next_x, first, last)

    used = sum(places[-1])
    def one_row(y, _):
        adj = adj_in[pl.ds(y, lanes, stride=rows), :].T
        adj_out[y] = adj
        to_x(y, adj, places[0])
        rate = turned_rate(rate_in, y, rows, nz, lanes)
        rate_out[y] = rate
        to_x(y, rate, places[steps + 1])
        if used < total:
            x_a[y, used:, :] = jnp.zeros((total - used, lanes), f32)
            x_b[y, used:, :] = jnp.zeros((total - used, lanes), f32)
        for back in range(steps):
            conc = conc_in[back, pl.ds(y, lanes, stride=rows), :].T
            conc_out[back, y] = conc
            to_x(y, conc, places[1 + back])
        return 0

    lax.fori_loop(0, rows, one_row, 0, unroll=2)


def put_own(out, row, value, y, place, cols, x_low, x_high):
    start, width = place
    right = pad + cols
    out[row, pad:right, :] = value
    out[row, pad - width : pad, :] = x_low[y, start : start + width, :]
    out[row, right : right + width, :] = x_high[y, start : start + width, :]


def put_halo(out, index, value, from_row, place, cols, corner):
    start, width = place
    right = pad + cols
    out[(*index, slice(pad, right))] = value
    out[(*index, slice(pad - width, pad))] = corner[0, from_row, start : start + width, :]
    out[(*index, slice(right, right + width))] = corner[1, from_row, start : start + width, :]


def corner_kernel(rows, got_a, got_b, _core, x_low, x_high, corner_a, corner_b):
    next_x = a_is_next("gx", x_first)
    x_low[...] = jnp.where(next_x, got_b[...], got_a[...])
    x_high[...] = jnp.where(next_x, got_a[...], got_b[...])
    for out, base in zip((corner_a, corner_b), bases(rows, round_first)):
        for at in range(depth):
            out[0, at] = x_low[base + at]
            out[1, at] = x_high[base + at]


def first_interior(steps, rows, cols, nz, conc_own, adj_own, rate_own, x_low, x_high,
                   conc, adj, rate, chem, curve, swing, out, grad, ahead, mob, pot, part):
    places, _ = slots(steps)
    low, high = reach(cols)
    lanes = adj.shape[2]
    mask = face_mask(lanes, nz)
    for y in range(rows):
        put_own(conc, 1 + y, conc_own[0, y], y, places[1], cols, x_low, x_high)
        put_own(adj, 1 + y, adj_own[y], y, places[0], cols, x_low, x_high)
        put_own(rate, y, rate_own[y], y, places[steps + 1], cols, x_low, x_high)
    for row, beside in ((0, 1), (rows + 1, rows)):
        adj[row] = adj[beside]
        for ref in (conc, chem, mob):
            ref[row] = jnp.zeros(ref.shape[1:], f32)
    put_ahead(ahead, conc_own, 1, x_low, x_high, places, rows, cols)

    def mob_row(row, _):
        for at, size in chunks(low - 8, high + 8):
            mob[row, at : at + size, :] = mobility(conc[row, at : at + size, :])
        return 0

    def mu_row(row, _):
        for at, size in chunks(low, high):
            chem_row(row_of(conc, row), set_row(chem, row), set_row(curve, row),
                     set_row(swing, row), at, size, mask)
        return 0

    lax.fori_loop(1, rows + 1, mob_row, 0, unroll=4)
    lax.fori_loop(1, rows + 1, mu_row, 0, unroll=2)
    all_rows(rows, cols, nz, adj, mob, 1, chem, curve, swing, rate, None, pot, part, out, grad)


def send_rows(out, ahead, rate, to_a, to_b, open_g, cols, nz):
    low, high = reach(cols)
    first, last = sent(cols)
    rows, lanes = rate.shape[0], rate.shape[2]
    mask = face_mask(lanes, nz)
    def side_rows(s, _):
        for at, size in chunks(low, high):
            a, _mu, flow, _pair = face_sums(
                lambda dy, cut: out[s, dy, cut, :], lambda dy, cut: ahead[s, dy, cut, :], None,
                at, size, mask, (1,)
            )
            open_g[s, at - low : at - low + size, :] = (
                flow - rate[s * (rows - 1), at : at + size, :] * a
            )
        return 0

    lax.fori_loop(0, 2, side_rows, 0)
    to_next = a_is_next("gy", round_first)
    for to, side in ((to_a, jnp.where(to_next, 1, 0)), (to_b, jnp.where(to_next, 0, 1))):
        to[0] = out[side, 0, first:last, :]
        to[1] = open_g[side, first - low : last - low, :]


def put_ahead(ahead, conc_own, back, x_low, x_high, places, rows, cols):
    for s, k, y in sides_of(rows):
        put_own(ahead.at[s], k, conc_own[back, y], y, places[1 + back], cols, x_low, x_high)
        ahead[s, k] = mobility(ahead[s, k])


def first_boundary(steps, rows, cols, nz, conc, adj, rate, chem, curve, swing, inside, grad,
                   from_a, from_b, corner_b, corner_a, ahead,
                   out, edge_grad, to_a, to_b, far_conc, far_adj, far_rate, far_mob, far_chem,
                   far_pot, delta, open_g):
    places, _ = slots(steps)
    low, high = reach(cols)
    half = cols // 2
    lanes = conc.shape[2]
    mask = face_mask(lanes, nz)
    lower = lax.broadcasted_iota(jnp.int32, (half, lanes), 1) < nz
    to_next = a_is_next("gy", main_first)

    def unpack(side):
        packed = side[pl.ds((1 + early) * depth * cols, half), :]
        turned = pltpu.roll(packed, lanes // 2, 1)
        return jnp.concatenate(
            [jnp.where(lower, packed, turned), jnp.where(lower, turned, packed)], axis=0
        )

    for halo, corner, side in (
        (from_a, corner_a, jnp.where(to_next, 1, 0)),
        (from_b, corner_b, jnp.where(to_next, 0, 1)),
    ):
        for at in range(depth):
            step = jnp.where(side == 1, at, depth - 1 - at)
            for ref, place, first in ((far_adj, places[0], 0), (far_conc, places[1], depth)):
                span = pl.ds((first + at) * cols, cols)
                put_halo(ref, (side, step), halo[span, :], at, place, cols, corner)
        put_halo(far_rate, (side,), unpack(halo), jnp.where(side == 1, 0, depth - 1),
                 places[steps + 1], cols, corner)

    share = time_step * grad_energy
    def side_rows(s, _):
        y, y1 = s * (rows - 1), 1 + s * (rows - 3)
        for at, size in chunks(low - 8, high + 8):
            span = slice(at, at + size)
            far_mob[s, span, :] = mobility(far_conc[s, 0, span, :])

        def conc_at(dy, cut):
            return conc[1 + y, cut, :] if dy == 1 else far_conc[s, -dy, cut, :]

        def adj_at(dy, cut):
            return adj[1 + y, cut, :] if dy == 1 else far_adj[s, -dy, cut, :]

        def mob_at(dy, cut):
            return far_mob[s, cut, :] if dy == 0 else mobility(conc_at(dy, cut))

        for at, size in chunks(low, high):
            span = slice(at, at + size)
            chem_row(conc_at, set_row(far_chem, s), lambda *_: None, lambda *_: None, at, size,
                     mask)
            a, _mu, flow, _pair = face_sums(adj_at, mob_at, None, at, size, mask)
            far_pot[s, span, :] = flow - far_rate[s, span, :] * a
            diff = a - adj[1 + y, span, :]
            delta[s, span, :] = (far_mob[s, span, :] + mobility(conc[1 + y, span, :])) * diff
        for at, size in chunks(low, high):
            span = slice(at, at + size)
            a, c, _flow, spread = face_sums(
                lambda dy, cut: adj[1 + y, cut, :], None, lambda dy, cut: far_conc[s, 0, cut, :],
                at, size, mask, ()
            )
            less = share * c
            inward = less * (adj[1 + y1, span, :] - a)
            pair = (far_chem[s, span, :] - (chem[1 + y, span, :] - less)) * (
                far_adj[s, 0, span, :] - a
            ) + (inward - share * spread)
            more = delta[s, span, :]
            step_z = (up(more) - more) * mask
            lap = (
                (delta[s, at + 1 : at + size + 1, :] + delta[s, at - 1 : at + size - 1, :])
                + (far_pot[s, span, :] - 4.0 * more)
                + (step_z - down(step_z))
            )
            out[s, 0, span, :] = (
                inside[y, span, :]
                + (swing[1 + y, span, :] * pair + curve[1 + y, span, :] * more)
                - grad_energy * lap
            )
            out[s, 1, span, :] = (
                inside[y1, span, :] + swing[1 + y1, span, :] * inward - grad_energy * more
            )
            edge_grad[s, span, :] = grad[y, span, :] + less * a
        return 0

    lax.fori_loop(0, 2, side_rows, 0)
    send_rows(out, ahead, rate, to_a, to_b, open_g, cols, nz)


def core_kernel(steps, rows, cols, nz, conc_own, mob, chem, curve, swing, conc):
    lanes = conc.shape[2]
    mask = face_mask(lanes, nz)
    own = pad, pad + cols
    for row in (0, rows + 1):
        conc[row] = jnp.zeros(conc.shape[1:], f32)
    for i in range(steps - 1):
        for y in range(rows):
            conc[1 + y, pad : pad + cols, :] = conc_own[1 + i, y]

        def row(y, _):
            for at, size in chunks(*own):
                mob[i, y, at : at + size, :] = mobility(conc[1 + y, at : at + size, :])
                chem_row(row_of(conc, 1 + y), set_row(chem.at[i], y), set_row(curve.at[i], y),
                         set_row(swing.at[i], y), at, size, mask)
            return 0

        lax.fori_loop(0, rows, row, 0, unroll=4)


def prepare_kernel(steps, rows, cols, nz, back, conc_own, from_a, from_b, x_low, x_high,
                   corner_b, corner_a, mob_core, chem_core, curve_core, swing_core,
                   mob, chem, curve, swing, *rest):
    *more, conc = rest
    places, _ = slots(steps)
    low, high = reach(cols)
    lanes = conc.shape[2]
    mask = face_mask(lanes, nz)
    place = places[1 + back]
    own = slice(pad, pad + cols)
    for y in range(rows):
        put_own(conc, depth + y, conc_own[back, y], y, place, cols, x_low, x_high)
        mob[depth + y, own, :] = mob_core[back - 1, y, own, :]
        chem[1 + y, own, :] = chem_core[back - 1, y, own, :]
        curve[1 + y, own, :] = curve_core[back - 1, y, own, :]
        swing[1 + y, own, :] = swing_core[back - 1, y, own, :]
    for halo, corner, base in zip((from_a, from_b), (corner_a, corner_b), landings(rows, main_first)):
        for at in range(depth):
            first = (1 + back) * depth if back < early else (back - early) * depth
            span = pl.ds((first + at) * cols, cols)
            put_halo(conc, (base + at,), halo[span, :], at, place, cols, corner)

    if more:
        ahead, late_a, late_b = more
        put_ahead(ahead, conc_own, back + 1, x_low, x_high, places, rows, cols)
        for side, base in zip((late_a, late_b), bases(rows, main_first)):
            for after in range(early, steps):
                for at in range(depth):
                    span = pl.ds(((after - early) * depth + at) * cols, cols)
                    side[span, :] = conc_own[after, base + at]
            used = (steps - early) * depth * cols
            side[used:, :] = jnp.zeros((side.shape[0] - used, lanes), f32)

    for y in range(rows):
        for at in (low - 8, pad + cols):
            span = slice(at, at + 16)
            mob[depth + y, span, :] = mobility(conc[depth + y, span, :])
        for at in (low, pad + cols - 8):
            chem_row(row_of(conc, depth + y), set_row(chem, 1 + y), set_row(curve, 1 + y),
                     set_row(swing, 1 + y), at, 16, mask)
    for y, beyond in ((0, -1), (rows - 1, rows)):
        inner = slice(pad + 8, pad + cols - 8)
        chem[1 + y, inner, :] = chem[1 + y, inner, :] - (time_step * grad_energy) * (
            conc[depth + beyond, inner, :]
        )

    for y in (-1, rows):
        for at, size in chunks(low - 8, high + 8):
            mob[depth + y, at : at + size, :] = mobility(conc[depth + y, at : at + size, :])
        for at, size in chunks(low, high):
            chem_row(row_of(conc, depth + y), set_row(chem, 1 + y), lambda *_: None,
                     lambda *_: None, at, size, mask)


def next_interior(rows, cols, nz, final, mob, chem, curve, swing, rate, inner, outer, before, *rest):
    if final:
        out, tiles, grad_out, adj, pot, part, grad, turned, sem = rest
        send = pltpu.make_async_copy(turned, grad_out, sem)
    else:
        edge_before, out, grad, adj, pot, part, sums = rest
        for y in range(rows):
            sums[y] = before[y]
        for s, y in ((0, 0), (1, rows - 1)):
            sums[y] = edge_before[s]
        before = sums
    lanes = adj.shape[2]
    for y in range(depth, rows - depth):
        adj[1 + y] = inner[y]
    for s, k, y in sides_of(rows):
        adj[1 + y] = outer[s, k]
    adj[0] = outer[0, 0]
    adj[1 + rows] = outer[1, 0]

    def send_grad():
        for y in range(rows):
            turned[pl.ds(y, nz, stride=rows), :] = fold(grad[y, pad : pad + cols, :].T, nz)
        send.start()

    all_rows(rows, cols, nz, adj, mob, depth, chem, curve, swing, rate, before, pot, part, out,
             grad, send_grad if final else None)
    if final:
        for y in range(depth, rows - depth):
            tiles[pl.ds(y, lanes, stride=rows), :] = out[y, pad : pad + cols, :].T
        send.wait()


def fold(value, nz):
    total = value[:nz]
    for frame in range(1, value.shape[0] // nz):
        total = total + value[frame * nz : (frame + 1) * nz]
    return total


def next_boundary(rows, cols, nz, final, mob, chem, curve, swing, inside, outer, from_a, from_b,
                  *rest):
    if final:
        tiles, out, halo, delta, result = rest
    else:
        ahead, rate, result, to_a, to_b, halo, delta, open_g = rest
    low, high = reach(cols)
    first, last = sent(cols)
    lanes = mob.shape[2]
    mask = face_mask(lanes, nz)
    to_next = a_is_next("gy", round_first)
    for got, side in ((from_a, jnp.where(to_next, 1, 0)), (from_b, jnp.where(to_next, 0, 1))):
        for k in range(2):
            halo[side, k, first:last, :] = got[k]
    def side_rows(s, _):
        y, beyond = s * (rows - 1), s * (rows + 1) - 1
        for at, size in chunks(low, high):
            span = slice(at, at + size)
            diff = halo[s, 0, span, :] - outer[s, 0, span, :]
            both = mob[depth + beyond, span, :] + mob[depth + y, span, :]
            delta[s, span, :] = both * diff
        for at, size in chunks(low, high):
            span = slice(at, at + size)
            more = delta[s, span, :]
            diff = halo[s, 0, span, :] - outer[s, 0, span, :]
            pair = (chem[1 + beyond, span, :] - chem[1 + y, span, :]) * diff
            step_z = (up(more) - more) * mask
            lap = (
                (delta[s, at + 1 : at + size + 1, :] + delta[s, at - 1 : at + size - 1, :])
                + (halo[s, 1, span, :] - more)
                - 4.0 * more
                + (step_z - down(step_z))
            )
            result[s, 0, span, :] = (
                inside[y, span, :]
                + (swing[1 + y, span, :] * pair + curve[1 + y, span, :] * more)
                - grad_energy * lap
            )
            result[s, 1, span, :] = inside[1 + s * (rows - 3), span, :] - grad_energy * more
        return 0

    lax.fori_loop(0, 2, side_rows, 0)
    if final:
        out[...] = tiles[...]
        for s, k, y in sides_of(rows):
            out[pl.ds(y, lanes, stride=rows), :] = result[s, k, pad : pad + cols, :].T
    else:
        send_rows(result, ahead, rate, to_a, to_b, open_g, cols, nz)


def call(kernel, outs, scratch, *operands, cost=0, far=False, far_outs=()):
    if far:
        operands = [pltpu.with_memory_space_constraint(value, pltpu.HBM) for value in operands]
    space = pl.ANY if far else pltpu.VMEM
    return pl.pallas_call(
        kernel,
        out_shape=[jax.ShapeDtypeStruct(shape, f32) for shape in outs],
        in_specs=[pl.BlockSpec(memory_space=space)] * len(operands),
        out_specs=[
            pl.BlockSpec(memory_space=pltpu.HBM if i in far_outs else pltpu.VMEM)
            for i in range(len(outs))
        ],
        scratch_shapes=[pltpu.VMEM(s, f32) if isinstance(s, tuple) else s for s in scratch],
        compiler_params=pltpu.CompilerParams(vmem_limit_bytes=vmem_limit),
        cost_estimate=pl.CostEstimate(
            flops=cost * 1_000_000, bytes_accessed=cost * 2_000_000, transcendentals=0
        ),
    )(*operands)


def swap(value_a, value_b, axis, first):
    count = lax.axis_size(axis)
    pairs_a = [(i, (i + 1 - 2 * ((i + first) % 2)) % count) for i in range(count)]
    pairs_b = [(i, (i - 1 + 2 * ((i + first) % 2)) % count) for i in range(count)]
    return lax.ppermute(value_a, axis, pairs_a), lax.ppermute(value_b, axis, pairs_b)


def shards(saved_conc, adjoint_end, rate_field):
    steps, frames, nz, rows, cols = saved_conc.shape
    lanes = frames * nz
    _, total = slots(steps)
    width = cols + 2 * pad
    flat = lanes * rows

    def field(count):
        return (count, width, lanes)

    both = (2, depth, width, lanes)
    edge = (2, cols + 8, lanes)
    open_g = (2, cols + 16, lanes)
    raw = [(steps, flat, cols), (flat, cols), (nz * rows, cols)]
    conc_raw, adj_raw, rate_raw, main_a, main_b = call(
        functools.partial(edge_kernel, steps, rows, cols, nz),
        raw + [((1 + early) * depth * cols + cols // 2, lanes)] * 2,
        [pltpu.SemaphoreType.DMA((2 + steps, 2))],
        saved_conc.reshape(raw[0]), adjoint_end.reshape(raw[1]), rate_field.reshape(raw[2]),
        cost=2,
        far=True,
    )
    main_a, main_b = swap(main_a, main_b, "gy", main_first)
    conc_own, adj_own, rate_own, x_a, x_b = call(
        functools.partial(turn_kernel, steps, rows, cols, nz),
        [(steps, rows, cols, lanes), (rows, cols, lanes), (rows, cols, lanes)]
        + [(rows, total, lanes)] * 2,
        [],
        conc_raw, adj_raw, rate_raw,
        cost=1,
    )
    x_a, x_b = swap(x_a, x_b, "gx", x_first)
    whole = (steps - 1, rows, width, lanes)
    core = call(
        functools.partial(core_kernel, steps, rows, cols, nz),
        [whole] * 4,
        [field(rows + 2)],
        conc_own,
        cost=2,
    )
    x_low, x_high, corner_a, corner_b = call(
        functools.partial(corner_kernel, rows),
        [(rows, total, lanes)] * 2 + [(2, depth, total, lanes)] * 2,
        [],
        x_a, x_b, core[1],
    )
    corners = swap(corner_a, corner_b, "gy", round_first)
    corner_a, corner_b = corners if main_first == round_first else corners[::-1]

    conc, adj, rate, chem, curve, swing, inner, grad, ahead = call(
        functools.partial(first_interior, steps, rows, cols, nz),
        [field(rows + 2)] * 2 + [field(rows)] + [field(rows + 2)] * 3 + [field(rows)] * 2 + [both],
        [field(rows + 2)] * 2 + [field(rows)],
        conc_own, adj_own, rate_own, x_low, x_high,
        cost=3,
    )
    outer, edge_grad, to_a, to_b = call(
        functools.partial(first_boundary, steps, rows, cols, nz),
        [both, field(2), edge, edge],
        [both, both] + [field(2)] * 5 + [open_g],
        conc, adj, rate, chem, curve, swing, inner, grad, main_a, main_b, corner_b, corner_a, ahead,
        cost=2,
    )
    sums = (grad, edge_grad)
    got = main_a, main_b
    late = (max((steps - early) * depth * cols, 2 * (cols + 8) + 8), lanes)
    for back in range(1, steps):
        adj_a, adj_b = swap(to_a, to_b, "gy", round_first)
        final = back == steps - 1
        fields = call(
            functools.partial(prepare_kernel, steps, rows, cols, nz, back),
            [field(rows + 2 * depth)] + [field(rows + 2)] * 3
            + ([] if final else [both, late, late]),
            [field(rows + 2 * depth)],
            conc_own, *got, x_low, x_high, corner_b, corner_a, *core,
            cost=2,
        )
        fields, ahead, more = fields[:4], fields[4:5], fields[5:]
        if not final:
            got = swap(*more, "gy", main_first)
        work = [field(rows + 2)] * 2 + [field(rows)] * 2
        if final:
            inner, tiles, grad = call(
                functools.partial(next_interior, rows, cols, nz, final),
                [field(rows), (flat, cols), (nz * rows, cols)],
                work + [(nz * rows, cols), pltpu.SemaphoreType.DMA],
                *fields, rate, inner, outer, *sums,
                cost=3,
                far_outs=(2,),
            )
            (adj,) = call(
                functools.partial(next_boundary, rows, cols, nz, final),
                [(flat, cols)],
                [both, field(2), both],
                *fields, inner, outer, adj_a, adj_b, tiles,
                cost=1,
            )
        else:
            inner, grad = call(
                functools.partial(next_interior, rows, cols, nz, final),
                [field(rows)] * 2,
                work,
                *fields, rate, inner, outer, *sums,
                cost=3,
            )
            outer, to_a, to_b = call(
                functools.partial(next_boundary, rows, cols, nz, final),
                [both, edge, edge],
                [both, field(2), open_g],
                *fields, inner, outer, adj_a, adj_b, *ahead, rate,
                cost=1,
            )
            sums = (grad,)
    return adj.reshape(adjoint_end.shape), grad.reshape(rate_field.shape)


def solution(mesh):
    return jax.shard_map(
        shards,
        mesh=mesh,
        in_specs=(P(None, None, None, "gy", "gx"), P(None, None, "gy", "gx"), P(None, "gy", "gx")),
        out_specs=(P(None, None, "gy", "gx"), P(None, "gy", "gx")),
        check_vma=False,
    )
```

```python
import functools

import jax
import jax.numpy as jnp
from jax import lax
from jax.experimental import pallas as pl
from jax.experimental.pallas import tpu as pltpu
from jax.sharding import PartitionSpec as P

mix_energy = 2.5
grad_energy = 1.0
time_step = 0.1
diff_step = 0.03
bath_potential = 0.5

pad = 16
chunk = 72
depth = 2
early = 2
x_first, main_first, round_first = 0, 0, 1
vmem_limit = 20 * 1024 * 1024
f32 = jnp.float32


def slots(steps):
    widths = [2 * steps] + [2 * steps - 2 * back for back in range(steps)] + [2 * steps - 1]
    starts = [sum(widths[:i]) for i in range(len(widths))]
    total = -(-sum(widths) // 8) * 8
    return list(zip(starts, widths)), total


def chunks(low, high):
    return [(at, min(chunk, high - at)) for at in range(low, high, chunk)]


def reach(cols):
    return pad - 8, pad + cols + 8


def sent(cols):
    return pad - 4, pad + cols + 4


def up(value):
    return pltpu.roll(value, value.shape[1] - 1, 1)


def down(value):
    return pltpu.roll(value, 1, 1)


def face_mask(lanes, nz):
    lane = lax.broadcasted_iota(jnp.int32, (1, lanes), 1)
    return jnp.where(lane % nz == nz - 1, 0.0, 1.0).astype(f32)


def row_of(ref, y):
    return lambda dy, cut: ref[y + dy, cut, :]


def laplace(field, at, size, mask):
    span = slice(at, at + size)
    here = field(0, span)
    step_z = (up(here) - here) * mask
    sides = field(0, slice(at + 1, at + size + 1)) + field(0, slice(at - 1, at + size - 1))
    return here, (
        (sides + (field(-1, span) + field(1, span))) - 4.0 * here + (step_z - down(step_z))
    )


def mobility(c):
    return (0.5 * diff_step) * c * (1.0 - c)


def chem_row(conc, chem, curve, swing, at, size, mask):
    c, lap = laplace(conc, at, size, mask)
    inv = 1.0 / (c * (1.0 - c))
    span = slice(at, at + size)
    chem(
        span,
        time_step * (jnp.log(c * c * inv) - grad_energy * lap)
        + (time_step * (mix_energy - bath_potential) - (2.0 * time_step * mix_energy) * c),
    )
    curve(span, inv - 2.0 * mix_energy)
    swing(span, c * (diff_step / time_step) - 0.5 * diff_step / time_step)


def face_sums(adj, mob, chem, at, size, mask, across=(1, -1)):
    span = slice(at, at + size)
    a = adj(0, span)
    m = None if mob is None else mob(0, span)
    mu = None if chem is None else chem(0, span)
    flow = pair = None
    for dy, cut in (
        (0, slice(at + 1, at + size + 1)),
        (0, slice(at - 1, at + size - 1)),
    ) + tuple((dy, span) for dy in across):
        diff = adj(dy, cut) - a
        if mob is not None:
            term = (mob(dy, cut) + m) * diff
            flow = term if flow is None else flow + term
        if chem is not None:
            term = (chem(dy, cut) - mu) * diff
            pair = term if pair is None else pair + term
    diff = (up(a) - a) * mask
    if mob is not None:
        term = (up(m) + m) * diff
        flow = flow + (term - down(term))
    if chem is not None:
        term = (up(mu) - mu) * diff
        pair = pair + (term + down(term))
    return a, mu, flow, pair


def partial(a, swing, pair, curve, g):
    return a + swing * pair + curve * g


def gain(a, chem, before):
    value = a * chem
    return -value if before is None else before - value


def set_row(ref, y):
    def put(span, value):
        ref[y, span, :] = value

    return put


def all_rows(rows, cols, nz, adj, mob, mob_skip, chem, curve, swing, rate, before, pot, part, out,
             grad, between=None):
    low, high = reach(cols)
    mask = face_mask(adj.shape[2], nz)

    def body(y, _):
        for at, size in chunks(low, high):
            span = slice(at, at + size)
            a, mu, flow, pair = face_sums(
                row_of(adj, y + 1), row_of(mob, y + mob_skip), row_of(chem, y + 1), at, size, mask
            )
            g = flow - rate[y, span, :] * a
            pot[y + 1, span, :] = g
            part[y, span, :] = partial(
                a, swing[y + 1, span, :], pair, curve[y + 1, span, :], g
            )
            grad[y, span, :] = gain(a, mu, None if before is None else before[y, span, :])
        return 0

    def close(y, _):
        for at, size in chunks(low, high):
            span = slice(at, at + size)
            _g, lap = laplace(row_of(pot, y + 1), at, size, mask)
            out[y, span, :] = part[y, span, :] - grad_energy * lap
        return 0

    for row in (0, rows + 1):
        pot[row] = jnp.zeros(pot.shape[1:], f32)
    lax.fori_loop(0, rows, body, 0, unroll=2)
    if between is not None:
        between()
    lax.fori_loop(0, rows, close, 0, unroll=4)


def a_is_next(axis, first):
    return lax.rem(lax.axis_index(axis), 2) == first


def bases(rows, first):
    to_next = a_is_next("gy", first)
    top = rows - depth
    return jnp.where(to_next, top, 0), jnp.where(to_next, 0, top)


def landings(rows, first):
    to_next = a_is_next("gy", first)
    top = rows + depth
    return jnp.where(to_next, top, 0), jnp.where(to_next, 0, top)


def sides_of(rows):
    return [(0, 0, 0), (0, 1, 1), (1, 0, rows - 1), (1, 1, rows - 2)]


def pack_kernel(steps, rows, cols, nz, conc_hbm, adj_hbm, rate_hbm, conc_out, adj_out, rate_out,
                main_a, main_b, x_a, x_b, conc_in, adj_in, rate_in, sems):
    places, total = slots(steps)
    lanes = adj_out.shape[2]
    half = cols // 2
    lower = lax.broadcasted_iota(jnp.int32, (half, lanes), 1) < nz
    next_x = a_is_next("gx", x_first)
    sides = list(zip((main_a, main_b), bases(rows, main_first)))
    fetches = [(adj_hbm, adj_in), (rate_hbm, rate_in)] + [
        (conc_hbm.at[steps - 1 - back], conc_in.at[back]) for back in range(steps)
    ]
    copies = []
    for i, (there, here) in enumerate(fetches):
        part = here.shape[0] // 2
        copies.append(
            [
                pltpu.make_async_copy(
                    there.at[pl.ds(k * part, part)], here.at[pl.ds(k * part, part)], sems.at[i, k]
                )
                for k in range(2)
            ]
        )
    for pair in copies:
        for copy in pair:
            copy.start()

    def arrived(i):
        for copy in copies[i]:
            copy.wait()

    def to_x(y, value, place):
        start, width = place
        last, first = value[cols - width :, :], value[:width, :]
        x_a[y, start : start + width, :] = jnp.where(next_x, last, first)
        x_b[y, start : start + width, :] = jnp.where(next_x, first, last)

    used = sum(places[-1])
    arrived(0)
    for y in range(rows):
        adj = adj_in[pl.ds(y, lanes, stride=rows), :].T
        adj_out[y] = adj
        to_x(y, adj, places[0])
    for side, base in sides:
        for at in range(depth):
            side[pl.ds(at * cols, cols), :] = adj_out[base + at]
    arrived(1)
    for y in range(rows):
        rate = turned_rate(rate_in, y, rows, nz, lanes)
        rate_out[y] = rate
        to_x(y, rate, places[steps + 1])
        if used < total:
            x_a[y, used:, :] = jnp.zeros((total - used, lanes), f32)
            x_b[y, used:, :] = jnp.zeros((total - used, lanes), f32)
    for side, base in sides:
        edge = jnp.where(base == 0, 0, rows - 1)
        side[pl.ds((1 + early) * depth * cols, half), :] = jnp.where(
            lower, rate_out[edge, :half, :], rate_out[edge, half:, :]
        )
    for back in range(steps):
        arrived(2 + back)
        for y in range(rows):
            conc = conc_in[back, pl.ds(y, lanes, stride=rows), :].T
            conc_out[back, y] = conc
            to_x(y, conc, places[1 + back])
        if back < early:
            for side, base in sides:
                for at in range(depth):
                    side[pl.ds(((1 + back) * depth + at) * cols, cols), :] = conc_out[
                        back, base + at
                    ]


def turned_rate(rate, y, rows, nz, lanes):
    value = time_step * rate[pl.ds(y, nz, stride=rows), :]
    return jnp.concatenate([value] * (lanes // nz), axis=0).T


def put_own(out, row, value, y, place, cols, x_low, x_high):
    start, width = place
    right = pad + cols
    out[row, pad:right, :] = value
    out[row, pad - width : pad, :] = x_low[y, start : start + width, :]
    out[row, right : right + width, :] = x_high[y, start : start + width, :]


def put_halo(out, index, value, from_row, place, cols, corner):
    start, width = place
    right = pad + cols
    out[(*index, slice(pad, right))] = value
    out[(*index, slice(pad - width, pad))] = corner[0, from_row, start : start + width, :]
    out[(*index, slice(right, right + width))] = corner[1, from_row, start : start + width, :]


def corner_kernel(rows, got_a, got_b, _core, x_low, x_high, corner_a, corner_b):
    next_x = a_is_next("gx", x_first)
    x_low[...] = jnp.where(next_x, got_b[...], got_a[...])
    x_high[...] = jnp.where(next_x, got_a[...], got_b[...])
    for out, base in zip((corner_a, corner_b), bases(rows, round_first)):
        for at in range(depth):
            out[0, at] = x_low[base + at]
            out[1, at] = x_high[base + at]


def first_interior(steps, rows, cols, nz, conc_own, adj_own, rate_own, x_low, x_high,
                   conc, adj, rate, chem, curve, swing, out, grad, ahead, mob, pot, part):
    places, _ = slots(steps)
    low, high = reach(cols)
    lanes = adj.shape[2]
    mask = face_mask(lanes, nz)
    for y in range(rows):
        put_own(conc, 1 + y, conc_own[0, y], y, places[1], cols, x_low, x_high)
        put_own(adj, 1 + y, adj_own[y], y, places[0], cols, x_low, x_high)
        put_own(rate, y, rate_own[y], y, places[steps + 1], cols, x_low, x_high)
    for row, beside in ((0, 1), (rows + 1, rows)):
        adj[row] = adj[beside]
        for ref in (conc, chem, mob):
            ref[row] = jnp.zeros(ref.shape[1:], f32)
    put_ahead(ahead, conc_own, 1, x_low, x_high, places, rows, cols)

    def mob_row(row, _):
        for at, size in chunks(low - 8, high + 8):
            mob[row, at : at + size, :] = mobility(conc[row, at : at + size, :])
        return 0

    def mu_row(row, _):
        for at, size in chunks(low, high):
            chem_row(row_of(conc, row), set_row(chem, row), set_row(curve, row),
                     set_row(swing, row), at, size, mask)
        return 0

    lax.fori_loop(1, rows + 1, mob_row, 0, unroll=4)
    lax.fori_loop(1, rows + 1, mu_row, 0, unroll=2)
    all_rows(rows, cols, nz, adj, mob, 1, chem, curve, swing, rate, None, pot, part, out, grad)


def send_rows(out, ahead, rate, to_a, to_b, open_g, cols, nz):
    low, high = reach(cols)
    first, last = sent(cols)
    rows, lanes = rate.shape[0], rate.shape[2]
    mask = face_mask(lanes, nz)
    for s in range(2):
        for at, size in chunks(low, high):
            a, _mu, flow, _pair = face_sums(
                lambda dy, cut: out[s, dy, cut, :], lambda dy, cut: ahead[s, dy, cut, :], None,
                at, size, mask, (1,)
            )
            open_g[s, at - low : at - low + size, :] = (
                flow - rate[s * (rows - 1), at : at + size, :] * a
            )
    to_next = a_is_next("gy", round_first)
    for to, side in ((to_a, jnp.where(to_next, 1, 0)), (to_b, jnp.where(to_next, 0, 1))):
        to[0] = out[side, 0, first:last, :]
        to[1] = open_g[side, first - low : last - low, :]


def put_ahead(ahead, conc_own, back, x_low, x_high, places, rows, cols):
    for s, k, y in sides_of(rows):
        put_own(ahead.at[s], k, conc_own[back, y], y, places[1 + back], cols, x_low, x_high)
        ahead[s, k] = mobility(ahead[s, k])


def first_boundary(steps, rows, cols, nz, conc, adj, rate, chem, curve, swing, inside, grad,
                   from_a, from_b, corner_b, corner_a, ahead,
                   out, edge_grad, to_a, to_b, far_conc, far_adj, far_rate, far_mob, far_chem,
                   far_pot, delta, open_g):
    places, _ = slots(steps)
    low, high = reach(cols)
    half = cols // 2
    lanes = conc.shape[2]
    mask = face_mask(lanes, nz)
    lower = lax.broadcasted_iota(jnp.int32, (half, lanes), 1) < nz
    to_next = a_is_next("gy", main_first)

    def unpack(side):
        packed = side[pl.ds((1 + early) * depth * cols, half), :]
        turned = pltpu.roll(packed, lanes // 2, 1)
        return jnp.concatenate(
            [jnp.where(lower, packed, turned), jnp.where(lower, turned, packed)], axis=0
        )

    for halo, corner, side in (
        (from_a, corner_a, jnp.where(to_next, 1, 0)),
        (from_b, corner_b, jnp.where(to_next, 0, 1)),
    ):
        for at in range(depth):
            step = jnp.where(side == 1, at, depth - 1 - at)
            for ref, place, first in ((far_adj, places[0], 0), (far_conc, places[1], depth)):
                span = pl.ds((first + at) * cols, cols)
                put_halo(ref, (side, step), halo[span, :], at, place, cols, corner)
        put_halo(far_rate, (side,), unpack(halo), jnp.where(side == 1, 0, depth - 1),
                 places[steps + 1], cols, corner)

    share = time_step * grad_energy
    def side_rows(s, _):
        y, y1 = s * (rows - 1), 1 + s * (rows - 3)
        for at, size in chunks(low - 8, high + 8):
            span = slice(at, at + size)
            far_mob[s, span, :] = mobility(far_conc[s, 0, span, :])

        def conc_at(dy, cut):
            return conc[1 + y, cut, :] if dy == 1 else far_conc[s, -dy, cut, :]

        def adj_at(dy, cut):
            return adj[1 + y, cut, :] if dy == 1 else far_adj[s, -dy, cut, :]

        def mob_at(dy, cut):
            return far_mob[s, cut, :] if dy == 0 else mobility(conc_at(dy, cut))

        for at, size in chunks(low, high):
            span = slice(at, at + size)
            chem_row(conc_at, set_row(far_chem, s), lambda *_: None, lambda *_: None, at, size,
                     mask)
            a, _mu, flow, _pair = face_sums(adj_at, mob_at, None, at, size, mask)
            far_pot[s, span, :] = flow - far_rate[s, span, :] * a
            diff = a - adj[1 + y, span, :]
            delta[s, span, :] = (far_mob[s, span, :] + mobility(conc[1 + y, span, :])) * diff
        for at, size in chunks(low, high):
            span = slice(at, at + size)
            a, c, _flow, spread = face_sums(
                lambda dy, cut: adj[1 + y, cut, :], None, lambda dy, cut: far_conc[s, 0, cut, :],
                at, size, mask, ()
            )
            less = share * c
            inward = less * (adj[1 + y1, span, :] - a)
            pair = (far_chem[s, span, :] - (chem[1 + y, span, :] - less)) * (
                far_adj[s, 0, span, :] - a
            ) + (inward - share * spread)
            more = delta[s, span, :]
            step_z = (up(more) - more) * mask
            lap = (
                (delta[s, at + 1 : at + size + 1, :] + delta[s, at - 1 : at + size - 1, :])
                + (far_pot[s, span, :] - 4.0 * more)
                + (step_z - down(step_z))
            )
            out[s, 0, span, :] = (
                inside[y, span, :]
                + (swing[1 + y, span, :] * pair + curve[1 + y, span, :] * more)
                - grad_energy * lap
            )
            out[s, 1, span, :] = (
                inside[y1, span, :] + swing[1 + y1, span, :] * inward - grad_energy * more
            )
            edge_grad[s, span, :] = grad[y, span, :] + less * a
        return 0

    lax.fori_loop(0, 2, side_rows, 0)
    send_rows(out, ahead, rate, to_a, to_b, open_g, cols, nz)


def core_kernel(steps, rows, cols, nz, conc_own, mob, chem, curve, swing, conc):
    lanes = conc.shape[2]
    mask = face_mask(lanes, nz)
    own = pad, pad + cols
    for row in (0, rows + 1):
        conc[row] = jnp.zeros(conc.shape[1:], f32)
    for i in range(steps - 1):
        for y in range(rows):
            conc[1 + y, pad : pad + cols, :] = conc_own[1 + i, y]

        def row(y, _):
            for at, size in chunks(*own):
                mob[i, y, at : at + size, :] = mobility(conc[1 + y, at : at + size, :])
                chem_row(row_of(conc, 1 + y), set_row(chem.at[i], y), set_row(curve.at[i], y),
                         set_row(swing.at[i], y), at, size, mask)
            return 0

        lax.fori_loop(0, rows, row, 0, unroll=4)


def prepare_kernel(steps, rows, cols, nz, back, conc_own, from_a, from_b, x_low, x_high,
                   corner_b, corner_a, mob_core, chem_core, curve_core, swing_core,
                   mob, chem, curve, swing, *rest):
    *more, conc = rest
    places, _ = slots(steps)
    low, high = reach(cols)
    lanes = conc.shape[2]
    mask = face_mask(lanes, nz)
    place = places[1 + back]
    own = slice(pad, pad + cols)
    for y in range(rows):
        put_own(conc, depth + y, conc_own[back, y], y, place, cols, x_low, x_high)
        mob[depth + y, own, :] = mob_core[back - 1, y, own, :]
        chem[1 + y, own, :] = chem_core[back - 1, y, own, :]
        curve[1 + y, own, :] = curve_core[back - 1, y, own, :]
        swing[1 + y, own, :] = swing_core[back - 1, y, own, :]
    for halo, corner, base in zip((from_a, from_b), (corner_a, corner_b), landings(rows, main_first)):
        for at in range(depth):
            first = (1 + back) * depth if back < early else (back - early) * depth
            span = pl.ds((first + at) * cols, cols)
            put_halo(conc, (base + at,), halo[span, :], at, place, cols, corner)

    if more:
        ahead, late_a, late_b = more
        put_ahead(ahead, conc_own, back + 1, x_low, x_high, places, rows, cols)
        for side, base in zip((late_a, late_b), bases(rows, main_first)):
            for after in range(early, steps):
                for at in range(depth):
                    span = pl.ds(((after - early) * depth + at) * cols, cols)
                    side[span, :] = conc_own[after, base + at]
            used = (steps - early) * depth * cols
            side[used:, :] = jnp.zeros((side.shape[0] - used, lanes), f32)

    for y in range(rows):
        for at in (low - 8, pad + cols):
            span = slice(at, at + 16)
            mob[depth + y, span, :] = mobility(conc[depth + y, span, :])
        for at in (low, pad + cols - 8):
            chem_row(row_of(conc, depth + y), set_row(chem, 1 + y), set_row(curve, 1 + y),
                     set_row(swing, 1 + y), at, 16, mask)
    for y, beyond in ((0, -1), (rows - 1, rows)):
        inner = slice(pad + 8, pad + cols - 8)
        chem[1 + y, inner, :] = chem[1 + y, inner, :] - (time_step * grad_energy) * (
            conc[depth + beyond, inner, :]
        )

    for y in (-1, rows):
        for at, size in chunks(low - 8, high + 8):
            mob[depth + y, at : at + size, :] = mobility(conc[depth + y, at : at + size, :])
        for at, size in chunks(low, high):
            chem_row(row_of(conc, depth + y), set_row(chem, 1 + y), lambda *_: None,
                     lambda *_: None, at, size, mask)


def next_interior(rows, cols, nz, final, mob, chem, curve, swing, rate, inner, outer, before, *rest):
    if final:
        out, tiles, grad_out, adj, pot, part, grad, turned, sem = rest
        send = pltpu.make_async_copy(turned, grad_out, sem)
    else:
        edge_before, out, grad, adj, pot, part, sums = rest
        for y in range(rows):
            sums[y] = before[y]
        for s, y in ((0, 0), (1, rows - 1)):
            sums[y] = edge_before[s]
        before = sums
    lanes = adj.shape[2]
    for y in range(depth, rows - depth):
        adj[1 + y] = inner[y]
    for s, k, y in sides_of(rows):
        adj[1 + y] = outer[s, k]
    adj[0] = outer[0, 0]
    adj[1 + rows] = outer[1, 0]

    def send_grad():
        for y in range(rows):
            turned[pl.ds(y, nz, stride=rows), :] = fold(grad[y, pad : pad + cols, :].T, nz)
        send.start()

    all_rows(rows, cols, nz, adj, mob, depth, chem, curve, swing, rate, before, pot, part, out,
             grad, send_grad if final else None)
    if final:
        for y in range(depth, rows - depth):
            tiles[pl.ds(y, lanes, stride=rows), :] = out[y, pad : pad + cols, :].T
        send.wait()


def fold(value, nz):
    total = value[:nz]
    for frame in range(1, value.shape[0] // nz):
        total = total + value[frame * nz : (frame + 1) * nz]
    return total


def next_boundary(rows, cols, nz, final, mob, chem, curve, swing, inside, outer, from_a, from_b,
                  *rest):
    if final:
        tiles, out, halo, delta, result = rest
    else:
        ahead, rate, result, to_a, to_b, halo, delta, open_g = rest
    low, high = reach(cols)
    first, last = sent(cols)
    lanes = mob.shape[2]
    mask = face_mask(lanes, nz)
    to_next = a_is_next("gy", round_first)
    for got, side in ((from_a, jnp.where(to_next, 1, 0)), (from_b, jnp.where(to_next, 0, 1))):
        for k in range(2):
            halo[side, k, first:last, :] = got[k]
    for s in range(2):
        y, beyond = s * (rows - 1), s * (rows + 1) - 1
        for at, size in chunks(low, high):
            span = slice(at, at + size)
            diff = halo[s, 0, span, :] - outer[s, 0, span, :]
            both = mob[depth + beyond, span, :] + mob[depth + y, span, :]
            delta[s, span, :] = both * diff
        for at, size in chunks(low, high):
            span = slice(at, at + size)
            more = delta[s, span, :]
            diff = halo[s, 0, span, :] - outer[s, 0, span, :]
            pair = (chem[1 + beyond, span, :] - chem[1 + y, span, :]) * diff
            step_z = (up(more) - more) * mask
            lap = (
                (delta[s, at + 1 : at + size + 1, :] + delta[s, at - 1 : at + size - 1, :])
                + (halo[s, 1, span, :] - more)
                - 4.0 * more
                + (step_z - down(step_z))
            )
            result[s, 0, span, :] = (
                inside[y, span, :]
                + (swing[1 + y, span, :] * pair + curve[1 + y, span, :] * more)
                - grad_energy * lap
            )
            result[s, 1, span, :] = inside[1 + s * (rows - 3), span, :] - grad_energy * more
    if final:
        out[...] = tiles[...]
        for s, k, y in sides_of(rows):
            out[pl.ds(y, lanes, stride=rows), :] = result[s, k, pad : pad + cols, :].T
    else:
        send_rows(result, ahead, rate, to_a, to_b, open_g, cols, nz)


def call(kernel, outs, scratch, *operands, cost=0, far=False, far_outs=()):
    if far:
        operands = [pltpu.with_memory_space_constraint(value, pltpu.HBM) for value in operands]
    space = pl.ANY if far else pltpu.VMEM
    return pl.pallas_call(
        kernel,
        out_shape=[jax.ShapeDtypeStruct(shape, f32) for shape in outs],
        in_specs=[pl.BlockSpec(memory_space=space)] * len(operands),
        out_specs=[
            pl.BlockSpec(memory_space=pltpu.HBM if i in far_outs else pltpu.VMEM)
            for i in range(len(outs))
        ],
        scratch_shapes=[pltpu.VMEM(s, f32) if isinstance(s, tuple) else s for s in scratch],
        compiler_params=pltpu.CompilerParams(vmem_limit_bytes=vmem_limit),
        cost_estimate=pl.CostEstimate(
            flops=cost * 1_000_000, bytes_accessed=cost * 2_000_000, transcendentals=0
        ),
    )(*operands)


def swap(value_a, value_b, axis, first):
    count = lax.axis_size(axis)
    pairs_a = [(i, (i + 1 - 2 * ((i + first) % 2)) % count) for i in range(count)]
    pairs_b = [(i, (i - 1 + 2 * ((i + first) % 2)) % count) for i in range(count)]
    return lax.ppermute(value_a, axis, pairs_a), lax.ppermute(value_b, axis, pairs_b)


def shards(saved_conc, adjoint_end, rate_field):
    steps, frames, nz, rows, cols = saved_conc.shape
    lanes = frames * nz
    _, total = slots(steps)
    width = cols + 2 * pad
    flat = lanes * rows

    def field(count):
        return (count, width, lanes)

    both = (2, depth, width, lanes)
    edge = (2, cols + 8, lanes)
    open_g = (2, cols + 16, lanes)
    raw = [(steps, flat, cols), (flat, cols), (nz * rows, cols)]
    conc_own, adj_own, rate_own, main_a, main_b, x_a, x_b = call(
        functools.partial(pack_kernel, steps, rows, cols, nz),
        [(steps, rows, cols, lanes), (rows, cols, lanes), (rows, cols, lanes)]
        + [((1 + early) * depth * cols + cols // 2, lanes)] * 2
        + [(rows, total, lanes)] * 2,
        raw + [pltpu.SemaphoreType.DMA((2 + steps, 2))],
        saved_conc.reshape(raw[0]), adjoint_end.reshape(raw[1]), rate_field.reshape(raw[2]),
        cost=3,
        far=True,
    )
    main_a, main_b = swap(main_a, main_b, "gy", main_first)
    x_a, x_b = swap(x_a, x_b, "gx", x_first)
    whole = (steps - 1, rows, width, lanes)
    core = call(
        functools.partial(core_kernel, steps, rows, cols, nz),
        [whole] * 4,
        [field(rows + 2)],
        conc_own,
        cost=2,
    )
    x_low, x_high, corner_a, corner_b = call(
        functools.partial(corner_kernel, rows),
        [(rows, total, lanes)] * 2 + [(2, depth, total, lanes)] * 2,
        [],
        x_a, x_b, core[1],
    )
    corners = swap(corner_a, corner_b, "gy", round_first)
    corner_a, corner_b = corners if main_first == round_first else corners[::-1]

    conc, adj, rate, chem, curve, swing, inner, grad, ahead = call(
        functools.partial(first_interior, steps, rows, cols, nz),
        [field(rows + 2)] * 2 + [field(rows)] + [field(rows + 2)] * 3 + [field(rows)] * 2 + [both],
        [field(rows + 2)] * 2 + [field(rows)],
        conc_own, adj_own, rate_own, x_low, x_high,
        cost=3,
    )
    outer, edge_grad, to_a, to_b = call(
        functools.partial(first_boundary, steps, rows, cols, nz),
        [both, field(2), edge, edge],
        [both, both] + [field(2)] * 5 + [open_g],
        conc, adj, rate, chem, curve, swing, inner, grad, main_a, main_b, corner_b, corner_a, ahead,
        cost=2,
    )
    sums = (grad, edge_grad)
    got = main_a, main_b
    late = (max((steps - early) * depth * cols, 2 * (cols + 8) + 8), lanes)
    for back in range(1, steps):
        adj_a, adj_b = swap(to_a, to_b, "gy", round_first)
        final = back == steps - 1
        fields = call(
            functools.partial(prepare_kernel, steps, rows, cols, nz, back),
            [field(rows + 2 * depth)] + [field(rows + 2)] * 3
            + ([] if final else [both, late, late]),
            [field(rows + 2 * depth)],
            conc_own, *got, x_low, x_high, corner_b, corner_a, *core,
            cost=2,
        )
        fields, ahead, more = fields[:4], fields[4:5], fields[5:]
        if not final:
            got = swap(*more, "gy", main_first)
        work = [field(rows + 2)] * 2 + [field(rows)] * 2
        if final:
            inner, tiles, grad = call(
                functools.partial(next_interior, rows, cols, nz, final),
                [field(rows), (flat, cols), (nz * rows, cols)],
                work + [(nz * rows, cols), pltpu.SemaphoreType.DMA],
                *fields, rate, inner, outer, *sums,
                cost=3,
                far_outs=(2,),
            )
            (adj,) = call(
                functools.partial(next_boundary, rows, cols, nz, final),
                [(flat, cols)],
                [both, field(2), both],
                *fields, inner, outer, adj_a, adj_b, tiles,
                cost=1,
            )
        else:
            inner, grad = call(
                functools.partial(next_interior, rows, cols, nz, final),
                [field(rows)] * 2,
                work,
                *fields, rate, inner, outer, *sums,
                cost=3,
            )
            outer, to_a, to_b = call(
                functools.partial(next_boundary, rows, cols, nz, final),
                [both, edge, edge],
                [both, field(2), open_g],
                *fields, inner, outer, adj_a, adj_b, *ahead, rate,
                cost=1,
            )
            sums = (grad,)
    return adj.reshape(adjoint_end.shape), grad.reshape(rate_field.shape)


def solution(mesh):
    return jax.shard_map(
        shards,
        mesh=mesh,
        in_specs=(P(None, None, None, "gy", "gx"), P(None, None, "gy", "gx"), P(None, "gy", "gx")),
        out_specs=(P(None, None, "gy", "gx"), P(None, "gy", "gx")),
        check_vma=False,
    )
```

```python
import functools

import jax
import jax.numpy as jnp
from jax import lax
from jax.experimental import pallas as pl
from jax.experimental.pallas import tpu as pltpu
from jax.sharding import PartitionSpec as P

mix_energy = 2.5
grad_energy = 1.0
time_step = 0.1
diff_step = 0.03
bath_potential = 0.5

pad = 16
chunk = 72
depth = 2
early = 2
x_first, main_first, round_first = 0, 0, 1
vmem_limit = 20 * 1024 * 1024
f32 = jnp.float32


def slots(steps):
    widths = [2 * steps] + [2 * steps - 2 * back for back in range(steps)] + [2 * steps - 1]
    starts = [sum(widths[:i]) for i in range(len(widths))]
    total = -(-sum(widths) // 8) * 8
    return list(zip(starts, widths)), total


def chunks(low, high):
    return [(at, min(chunk, high - at)) for at in range(low, high, chunk)]


def reach(cols):
    return pad - 8, pad + cols + 8


def sent(cols):
    return pad - 4, pad + cols + 4


def up(value):
    return pltpu.roll(value, value.shape[1] - 1, 1)


def down(value):
    return pltpu.roll(value, 1, 1)


def face_mask(lanes, nz):
    lane = lax.broadcasted_iota(jnp.int32, (1, lanes), 1)
    return jnp.where(lane % nz == nz - 1, 0.0, 1.0).astype(f32)


def row_of(ref, y):
    return lambda dy, cut: ref[y + dy, cut, :]


def laplace(field, at, size, mask):
    span = slice(at, at + size)
    here = field(0, span)
    step_z = (up(here) - here) * mask
    sides = field(0, slice(at + 1, at + size + 1)) + field(0, slice(at - 1, at + size - 1))
    return here, (
        (sides + (field(-1, span) + field(1, span))) - 4.0 * here + (step_z - down(step_z))
    )


def mobility(c):
    return (0.5 * diff_step) * c * (1.0 - c)


def chem_row(conc, chem, curve, swing, at, size, mask):
    c, lap = laplace(conc, at, size, mask)
    inv = 1.0 / (c * (1.0 - c))
    span = slice(at, at + size)
    chem(
        span,
        time_step * (jnp.log(c * c * inv) - grad_energy * lap)
        + (time_step * (mix_energy - bath_potential) - (2.0 * time_step * mix_energy) * c),
    )
    curve(span, inv - 2.0 * mix_energy)
    swing(span, c * (diff_step / time_step) - 0.5 * diff_step / time_step)


def face_sums(adj, mob, chem, at, size, mask, across=(1, -1)):
    span = slice(at, at + size)
    a = adj(0, span)
    m = None if mob is None else mob(0, span)
    mu = None if chem is None else chem(0, span)
    flow = pair = None
    for dy, cut in (
        (0, slice(at + 1, at + size + 1)),
        (0, slice(at - 1, at + size - 1)),
    ) + tuple((dy, span) for dy in across):
        diff = adj(dy, cut) - a
        if mob is not None:
            term = (mob(dy, cut) + m) * diff
            flow = term if flow is None else flow + term
        if chem is not None:
            term = (chem(dy, cut) - mu) * diff
            pair = term if pair is None else pair + term
    diff = (up(a) - a) * mask
    if mob is not None:
        term = (up(m) + m) * diff
        flow = flow + (term - down(term))
    if chem is not None:
        term = (up(mu) - mu) * diff
        pair = pair + (term + down(term))
    return a, mu, flow, pair


def partial(a, swing, pair, curve, g):
    return a + swing * pair + curve * g


def gain(a, chem, before):
    value = a * chem
    return -value if before is None else before - value


def set_row(ref, y):
    def put(span, value):
        ref[y, span, :] = value

    return put


def all_rows(rows, cols, nz, adj, mob, mob_skip, chem, curve, swing, rate, before, pot, part, out,
             grad, between=None):
    low, high = reach(cols)
    mask = face_mask(adj.shape[2], nz)

    def body(y, _):
        for at, size in chunks(low, high):
            span = slice(at, at + size)
            a, mu, flow, pair = face_sums(
                row_of(adj, y + 1), row_of(mob, y + mob_skip), row_of(chem, y + 1), at, size, mask
            )
            g = flow - rate[y, span, :] * a
            pot[y + 1, span, :] = g
            part[y, span, :] = partial(
                a, swing[y + 1, span, :], pair, curve[y + 1, span, :], g
            )
            grad[y, span, :] = gain(a, mu, None if before is None else before[y, span, :])
        return 0

    def close(y, _):
        for at, size in chunks(low, high):
            span = slice(at, at + size)
            _g, lap = laplace(row_of(pot, y + 1), at, size, mask)
            out[y, span, :] = part[y, span, :] - grad_energy * lap
        return 0

    for row in (0, rows + 1):
        pot[row] = jnp.zeros(pot.shape[1:], f32)
    lax.fori_loop(0, rows, body, 0, unroll=2)
    if between is not None:
        between()
    lax.fori_loop(0, rows, close, 0, unroll=4)


def a_is_next(axis, first):
    return lax.rem(lax.axis_index(axis), 2) == first


def bases(rows, first):
    to_next = a_is_next("gy", first)
    top = rows - depth
    return jnp.where(to_next, top, 0), jnp.where(to_next, 0, top)


def landings(rows, first):
    to_next = a_is_next("gy", first)
    top = rows + depth
    return jnp.where(to_next, top, 0), jnp.where(to_next, 0, top)


def sides_of(rows):
    return [(0, 0, 0), (0, 1, 1), (1, 0, rows - 1), (1, 1, rows - 2)]


def pack_kernel(steps, rows, cols, nz, conc_hbm, adj_hbm, rate_hbm, conc_out, adj_out, rate_out,
                main_a, main_b, x_a, x_b, conc_in, adj_in, rate_in, sems):
    places, total = slots(steps)
    lanes = adj_out.shape[2]
    half = cols // 2
    lower = lax.broadcasted_iota(jnp.int32, (half, lanes), 1) < nz
    next_x = a_is_next("gx", x_first)
    sides = list(zip((main_a, main_b), bases(rows, main_first)))
    fetches = [(adj_hbm, adj_in), (rate_hbm, rate_in)] + [
        (conc_hbm.at[steps - 1 - back], conc_in.at[back]) for back in range(steps)
    ]
    copies = []
    for i, (there, here) in enumerate(fetches):
        part = here.shape[0] // 2
        copies.append(
            [
                pltpu.make_async_copy(
                    there.at[pl.ds(k * part, part)], here.at[pl.ds(k * part, part)], sems.at[i, k]
                )
                for k in range(2)
            ]
        )
    for pair in copies:
        for copy in pair:
            copy.start()

    def arrived(i):
        for copy in copies[i]:
            copy.wait()

    def to_x(y, value, place):
        start, width = place
        last, first = value[cols - width :, :], value[:width, :]
        x_a[y, start : start + width, :] = jnp.where(next_x, last, first)
        x_b[y, start : start + width, :] = jnp.where(next_x, first, last)

    used = sum(places[-1])
    arrived(0)
    for y in range(rows):
        adj = adj_in[pl.ds(y, lanes, stride=rows), :].T
        adj_out[y] = adj
        to_x(y, adj, places[0])
    for side, base in sides:
        for at in range(depth):
            side[pl.ds(at * cols, cols), :] = adj_out[base + at]
    arrived(1)
    for y in range(rows):
        rate = turned_rate(rate_in, y, rows, nz, lanes)
        rate_out[y] = rate
        to_x(y, rate, places[steps + 1])
        if used < total:
            x_a[y, used:, :] = jnp.zeros((total - used, lanes), f32)
            x_b[y, used:, :] = jnp.zeros((total - used, lanes), f32)
    for side, base in sides:
        edge = jnp.where(base == 0, 0, rows - 1)
        side[pl.ds((1 + early) * depth * cols, half), :] = jnp.where(
            lower, rate_out[edge, :half, :], rate_out[edge, half:, :]
        )
    for back in range(steps):
        arrived(2 + back)
        for y in range(rows):
            conc = conc_in[back, pl.ds(y, lanes, stride=rows), :].T
            conc_out[back, y] = conc
            to_x(y, conc, places[1 + back])
        if back < early:
            for side, base in sides:
                for at in range(depth):
                    side[pl.ds(((1 + back) * depth + at) * cols, cols), :] = conc_out[
                        back, base + at
                    ]


def turned_rate(rate, y, rows, nz, lanes):
    value = time_step * rate[pl.ds(y, nz, stride=rows), :]
    return jnp.concatenate([value] * (lanes // nz), axis=0).T


def put_own(out, row, value, y, place, cols, x_low, x_high):
    start, width = place
    right = pad + cols
    out[row, pad:right, :] = value
    out[row, pad - width : pad, :] = x_low[y, start : start + width, :]
    out[row, right : right + width, :] = x_high[y, start : start + width, :]


def put_halo(out, index, value, from_row, place, cols, corner):
    start, width = place
    right = pad + cols
    out[(*index, slice(pad, right))] = value
    out[(*index, slice(pad - width, pad))] = corner[0, from_row, start : start + width, :]
    out[(*index, slice(right, right + width))] = corner[1, from_row, start : start + width, :]


def corner_kernel(rows, got_a, got_b, _core, x_low, x_high, corner_a, corner_b):
    next_x = a_is_next("gx", x_first)
    x_low[...] = jnp.where(next_x, got_b[...], got_a[...])
    x_high[...] = jnp.where(next_x, got_a[...], got_b[...])
    for out, base in zip((corner_a, corner_b), bases(rows, round_first)):
        for at in range(depth):
            out[0, at] = x_low[base + at]
            out[1, at] = x_high[base + at]


def first_interior(steps, rows, cols, nz, conc_own, adj_own, rate_own, x_low, x_high,
                   conc, adj, rate, chem, curve, swing, out, grad, ahead, mob, pot, part):
    places, _ = slots(steps)
    low, high = reach(cols)
    lanes = adj.shape[2]
    mask = face_mask(lanes, nz)
    for y in range(rows):
        put_own(conc, 1 + y, conc_own[0, y], y, places[1], cols, x_low, x_high)
        put_own(adj, 1 + y, adj_own[y], y, places[0], cols, x_low, x_high)
        put_own(rate, y, rate_own[y], y, places[steps + 1], cols, x_low, x_high)
    for row, beside in ((0, 1), (rows + 1, rows)):
        adj[row] = adj[beside]
        for ref in (conc, chem, mob):
            ref[row] = jnp.zeros(ref.shape[1:], f32)
    put_ahead(ahead, conc_own, 1, x_low, x_high, places, rows, cols)

    def mob_row(row, _):
        for at, size in chunks(low - 8, high + 8):
            mob[row, at : at + size, :] = mobility(conc[row, at : at + size, :])
        return 0

    def mu_row(row, _):
        for at, size in chunks(low, high):
            chem_row(row_of(conc, row), set_row(chem, row), set_row(curve, row),
                     set_row(swing, row), at, size, mask)
        return 0

    lax.fori_loop(1, rows + 1, mob_row, 0, unroll=4)
    lax.fori_loop(1, rows + 1, mu_row, 0, unroll=2)
    all_rows(rows, cols, nz, adj, mob, 1, chem, curve, swing, rate, None, pot, part, out, grad)


def send_rows(out, ahead, rate, to_a, to_b, open_g, cols, nz):
    low, high = reach(cols)
    first, last = sent(cols)
    rows, lanes = rate.shape[0], rate.shape[2]
    mask = face_mask(lanes, nz)
    for s in range(2):
        for at, size in chunks(low, high):
            a, _mu, flow, _pair = face_sums(
                lambda dy, cut: out[s, dy, cut, :], lambda dy, cut: ahead[s, dy, cut, :], None,
                at, size, mask, (1,)
            )
            open_g[s, at - low : at - low + size, :] = (
                flow - rate[s * (rows - 1), at : at + size, :] * a
            )
    to_next = a_is_next("gy", round_first)
    for to, side in ((to_a, jnp.where(to_next, 1, 0)), (to_b, jnp.where(to_next, 0, 1))):
        to[0] = out[side, 0, first:last, :]
        to[1] = open_g[side, first - low : last - low, :]


def put_ahead(ahead, conc_own, back, x_low, x_high, places, rows, cols):
    for s, k, y in sides_of(rows):
        put_own(ahead.at[s], k, conc_own[back, y], y, places[1 + back], cols, x_low, x_high)
        ahead[s, k] = mobility(ahead[s, k])


def first_boundary(steps, rows, cols, nz, conc, adj, rate, chem, curve, swing, inside, grad,
                   from_a, from_b, corner_b, corner_a, ahead,
                   out, edge_grad, to_a, to_b, far_conc, far_adj, far_rate, far_mob, far_chem,
                   far_pot, delta, open_g):
    places, _ = slots(steps)
    low, high = reach(cols)
    half = cols // 2
    lanes = conc.shape[2]
    mask = face_mask(lanes, nz)
    lower = lax.broadcasted_iota(jnp.int32, (half, lanes), 1) < nz
    to_next = a_is_next("gy", main_first)

    def unpack(side):
        packed = side[pl.ds((1 + early) * depth * cols, half), :]
        turned = pltpu.roll(packed, lanes // 2, 1)
        return jnp.concatenate(
            [jnp.where(lower, packed, turned), jnp.where(lower, turned, packed)], axis=0
        )

    for halo, corner, side in (
        (from_a, corner_a, jnp.where(to_next, 1, 0)),
        (from_b, corner_b, jnp.where(to_next, 0, 1)),
    ):
        for at in range(depth):
            step = jnp.where(side == 1, at, depth - 1 - at)
            for ref, place, first in ((far_adj, places[0], 0), (far_conc, places[1], depth)):
                span = pl.ds((first + at) * cols, cols)
                put_halo(ref, (side, step), halo[span, :], at, place, cols, corner)
        put_halo(far_rate, (side,), unpack(halo), jnp.where(side == 1, 0, depth - 1),
                 places[steps + 1], cols, corner)

    share = time_step * grad_energy
    def side_rows(s, _):
        y, y1 = s * (rows - 1), 1 + s * (rows - 3)
        for at, size in chunks(low - 8, high + 8):
            span = slice(at, at + size)
            far_mob[s, span, :] = mobility(far_conc[s, 0, span, :])

        def conc_at(dy, cut):
            return conc[1 + y, cut, :] if dy == 1 else far_conc[s, -dy, cut, :]

        def adj_at(dy, cut):
            return adj[1 + y, cut, :] if dy == 1 else far_adj[s, -dy, cut, :]

        def mob_at(dy, cut):
            return far_mob[s, cut, :] if dy == 0 else mobility(conc_at(dy, cut))

        for at, size in chunks(low, high):
            span = slice(at, at + size)
            chem_row(conc_at, set_row(far_chem, s), lambda *_: None, lambda *_: None, at, size,
                     mask)
            a, _mu, flow, _pair = face_sums(adj_at, mob_at, None, at, size, mask)
            far_pot[s, span, :] = flow - far_rate[s, span, :] * a
            diff = a - adj[1 + y, span, :]
            delta[s, span, :] = (far_mob[s, span, :] + mobility(conc[1 + y, span, :])) * diff
        for at, size in chunks(low, high):
            span = slice(at, at + size)
            a, c, _flow, spread = face_sums(
                lambda dy, cut: adj[1 + y, cut, :], None, lambda dy, cut: far_conc[s, 0, cut, :],
                at, size, mask, ()
            )
            less = share * c
            inward = less * (adj[1 + y1, span, :] - a)
            pair = (far_chem[s, span, :] - (chem[1 + y, span, :] - less)) * (
                far_adj[s, 0, span, :] - a
            ) + (inward - share * spread)
            more = delta[s, span, :]
            step_z = (up(more) - more) * mask
            lap = (
                (delta[s, at + 1 : at + size + 1, :] + delta[s, at - 1 : at + size - 1, :])
                + (far_pot[s, span, :] - 4.0 * more)
                + (step_z - down(step_z))
            )
            out[s, 0, span, :] = (
                inside[y, span, :]
                + (swing[1 + y, span, :] * pair + curve[1 + y, span, :] * more)
                - grad_energy * lap
            )
            out[s, 1, span, :] = (
                inside[y1, span, :] + swing[1 + y1, span, :] * inward - grad_energy * more
            )
            edge_grad[s, span, :] = grad[y, span, :] + less * a
        return 0

    lax.fori_loop(0, 2, side_rows, 0)
    send_rows(out, ahead, rate, to_a, to_b, open_g, cols, nz)


def core_kernel(steps, rows, cols, nz, conc_own, mob, chem, curve, swing, conc):
    lanes = conc.shape[2]
    mask = face_mask(lanes, nz)
    own = pad, pad + cols
    for row in (0, rows + 1):
        conc[row] = jnp.zeros(conc.shape[1:], f32)
    for i in range(steps - 1):
        for y in range(rows):
            conc[1 + y, pad : pad + cols, :] = conc_own[1 + i, y]

        def row(y, _):
            for at, size in chunks(*own):
                mob[i, y, at : at + size, :] = mobility(conc[1 + y, at : at + size, :])
                chem_row(row_of(conc, 1 + y), set_row(chem.at[i], y), set_row(curve.at[i], y),
                         set_row(swing.at[i], y), at, size, mask)
            return 0

        lax.fori_loop(0, rows, row, 0, unroll=4)


def prepare_kernel(steps, rows, cols, nz, back, conc_own, from_a, from_b, x_low, x_high,
                   corner_b, corner_a, mob_core, chem_core, curve_core, swing_core,
                   mob, chem, curve, swing, *rest):
    *more, conc = rest
    places, _ = slots(steps)
    low, high = reach(cols)
    lanes = conc.shape[2]
    mask = face_mask(lanes, nz)
    place = places[1 + back]
    own = slice(pad, pad + cols)
    for y in range(rows):
        put_own(conc, depth + y, conc_own[back, y], y, place, cols, x_low, x_high)
        mob[depth + y, own, :] = mob_core[back - 1, y, own, :]
        chem[1 + y, own, :] = chem_core[back - 1, y, own, :]
        curve[1 + y, own, :] = curve_core[back - 1, y, own, :]
        swing[1 + y, own, :] = swing_core[back - 1, y, own, :]
    first_swap, corners = main_first, (corner_a, corner_b)
    if back >= early and round_first != main_first:
        first_swap, corners = round_first, (corner_b, corner_a)
    for halo, corner, base in zip((from_a, from_b), corners, landings(rows, first_swap)):
        for at in range(depth):
            first = (1 + back) * depth if back < early else (back - early) * depth
            span = pl.ds((first + at) * cols, cols)
            put_halo(conc, (base + at,), halo[span, :], at, place, cols, corner)

    if more:
        ahead, late_a, late_b = more
        put_ahead(ahead, conc_own, back + 1, x_low, x_high, places, rows, cols)
        for side, base in zip((late_a, late_b), bases(rows, round_first)):
            for after in range(early, steps):
                for at in range(depth):
                    span = pl.ds(((after - early) * depth + at) * cols, cols)
                    side[span, :] = conc_own[after, base + at]
            used = (steps - early) * depth * cols
            side[used:, :] = jnp.zeros((side.shape[0] - used, lanes), f32)

    for y in range(rows):
        for at in (low - 8, pad + cols):
            span = slice(at, at + 16)
            mob[depth + y, span, :] = mobility(conc[depth + y, span, :])
        for at in (low, pad + cols - 8):
            chem_row(row_of(conc, depth + y), set_row(chem, 1 + y), set_row(curve, 1 + y),
                     set_row(swing, 1 + y), at, 16, mask)
    for y, beyond in ((0, -1), (rows - 1, rows)):
        inner = slice(pad + 8, pad + cols - 8)
        chem[1 + y, inner, :] = chem[1 + y, inner, :] - (time_step * grad_energy) * (
            conc[depth + beyond, inner, :]
        )

    for y in (-1, rows):
        for at, size in chunks(low - 8, high + 8):
            mob[depth + y, at : at + size, :] = mobility(conc[depth + y, at : at + size, :])
        for at, size in chunks(low, high):
            chem_row(row_of(conc, depth + y), set_row(chem, 1 + y), lambda *_: None,
                     lambda *_: None, at, size, mask)


def next_interior(rows, cols, nz, final, mob, chem, curve, swing, rate, inner, outer, before, *rest):
    if final:
        out, tiles, grad_out, adj, pot, part, grad, turned, sem = rest
        send = pltpu.make_async_copy(turned, grad_out, sem)
    else:
        edge_before, out, grad, adj, pot, part, sums = rest
        for y in range(rows):
            sums[y] = before[y]
        for s, y in ((0, 0), (1, rows - 1)):
            sums[y] = edge_before[s]
        before = sums
    lanes = adj.shape[2]
    for y in range(depth, rows - depth):
        adj[1 + y] = inner[y]
    for s, k, y in sides_of(rows):
        adj[1 + y] = outer[s, k]
    adj[0] = outer[0, 0]
    adj[1 + rows] = outer[1, 0]

    def send_grad():
        for y in range(rows):
            turned[pl.ds(y, nz, stride=rows), :] = fold(grad[y, pad : pad + cols, :].T, nz)
        send.start()

    all_rows(rows, cols, nz, adj, mob, depth, chem, curve, swing, rate, before, pot, part, out,
             grad, send_grad if final else None)
    if final:
        for y in range(depth, rows - depth):
            tiles[pl.ds(y, lanes, stride=rows), :] = out[y, pad : pad + cols, :].T
        send.wait()


def fold(value, nz):
    total = value[:nz]
    for frame in range(1, value.shape[0] // nz):
        total = total + value[frame * nz : (frame + 1) * nz]
    return total


def next_boundary(rows, cols, nz, final, mob, chem, curve, swing, inside, outer, from_a, from_b,
                  *rest):
    if final:
        tiles, out, halo, delta, result = rest
    else:
        ahead, rate, result, to_a, to_b, halo, delta, open_g = rest
    low, high = reach(cols)
    first, last = sent(cols)
    lanes = mob.shape[2]
    mask = face_mask(lanes, nz)
    to_next = a_is_next("gy", round_first)
    for got, side in ((from_a, jnp.where(to_next, 1, 0)), (from_b, jnp.where(to_next, 0, 1))):
        for k in range(2):
            halo[side, k, first:last, :] = got[k]
    for s in range(2):
        y, beyond = s * (rows - 1), s * (rows + 1) - 1
        for at, size in chunks(low, high):
            span = slice(at, at + size)
            diff = halo[s, 0, span, :] - outer[s, 0, span, :]
            both = mob[depth + beyond, span, :] + mob[depth + y, span, :]
            delta[s, span, :] = both * diff
        for at, size in chunks(low, high):
            span = slice(at, at + size)
            more = delta[s, span, :]
            diff = halo[s, 0, span, :] - outer[s, 0, span, :]
            pair = (chem[1 + beyond, span, :] - chem[1 + y, span, :]) * diff
            step_z = (up(more) - more) * mask
            lap = (
                (delta[s, at + 1 : at + size + 1, :] + delta[s, at - 1 : at + size - 1, :])
                + (halo[s, 1, span, :] - more)
                - 4.0 * more
                + (step_z - down(step_z))
            )
            result[s, 0, span, :] = (
                inside[y, span, :]
                + (swing[1 + y, span, :] * pair + curve[1 + y, span, :] * more)
                - grad_energy * lap
            )
            result[s, 1, span, :] = inside[1 + s * (rows - 3), span, :] - grad_energy * more
    if final:
        out[...] = tiles[...]
        for s, k, y in sides_of(rows):
            out[pl.ds(y, lanes, stride=rows), :] = result[s, k, pad : pad + cols, :].T
    else:
        send_rows(result, ahead, rate, to_a, to_b, open_g, cols, nz)


def call(kernel, outs, scratch, *operands, cost=0, far=False, far_outs=()):
    if far:
        operands = [pltpu.with_memory_space_constraint(value, pltpu.HBM) for value in operands]
    space = pl.ANY if far else pltpu.VMEM
    return pl.pallas_call(
        kernel,
        out_shape=[jax.ShapeDtypeStruct(shape, f32) for shape in outs],
        in_specs=[pl.BlockSpec(memory_space=space)] * len(operands),
        out_specs=[
            pl.BlockSpec(memory_space=pltpu.HBM if i in far_outs else pltpu.VMEM)
            for i in range(len(outs))
        ],
        scratch_shapes=[pltpu.VMEM(s, f32) if isinstance(s, tuple) else s for s in scratch],
        compiler_params=pltpu.CompilerParams(vmem_limit_bytes=vmem_limit),
        cost_estimate=pl.CostEstimate(
            flops=cost * 1_000_000, bytes_accessed=cost * 2_000_000, transcendentals=0
        ),
    )(*operands)


def swap(value_a, value_b, axis, first):
    count = lax.axis_size(axis)
    pairs_a = [(i, (i + 1 - 2 * ((i + first) % 2)) % count) for i in range(count)]
    pairs_b = [(i, (i - 1 + 2 * ((i + first) % 2)) % count) for i in range(count)]
    return lax.ppermute(value_a, axis, pairs_a), lax.ppermute(value_b, axis, pairs_b)


def shards(saved_conc, adjoint_end, rate_field):
    steps, frames, nz, rows, cols = saved_conc.shape
    lanes = frames * nz
    _, total = slots(steps)
    width = cols + 2 * pad
    flat = lanes * rows

    def field(count):
        return (count, width, lanes)

    both = (2, depth, width, lanes)
    edge = (2, cols + 8, lanes)
    open_g = (2, cols + 16, lanes)
    raw = [(steps, flat, cols), (flat, cols), (nz * rows, cols)]
    conc_own, adj_own, rate_own, main_a, main_b, x_a, x_b = call(
        functools.partial(pack_kernel, steps, rows, cols, nz),
        [(steps, rows, cols, lanes), (rows, cols, lanes), (rows, cols, lanes)]
        + [((1 + early) * depth * cols + cols // 2, lanes)] * 2
        + [(rows, total, lanes)] * 2,
        raw + [pltpu.SemaphoreType.DMA((2 + steps, 2))],
        saved_conc.reshape(raw[0]), adjoint_end.reshape(raw[1]), rate_field.reshape(raw[2]),
        cost=3,
        far=True,
    )
    main_a, main_b = swap(main_a, main_b, "gy", main_first)
    x_a, x_b = swap(x_a, x_b, "gx", x_first)
    whole = (steps - 1, rows, width, lanes)
    core = call(
        functools.partial(core_kernel, steps, rows, cols, nz),
        [whole] * 4,
        [field(rows + 2)],
        conc_own,
        cost=2,
    )
    x_low, x_high, corner_a, corner_b = call(
        functools.partial(corner_kernel, rows),
        [(rows, total, lanes)] * 2 + [(2, depth, total, lanes)] * 2,
        [],
        x_a, x_b, core[1],
    )
    corners = swap(corner_a, corner_b, "gy", round_first)
    corner_a, corner_b = corners if main_first == round_first else corners[::-1]

    conc, adj, rate, chem, curve, swing, inner, grad, ahead = call(
        functools.partial(first_interior, steps, rows, cols, nz),
        [field(rows + 2)] * 2 + [field(rows)] + [field(rows + 2)] * 3 + [field(rows)] * 2 + [both],
        [field(rows + 2)] * 2 + [field(rows)],
        conc_own, adj_own, rate_own, x_low, x_high,
        cost=3,
    )
    outer, edge_grad, to_a, to_b = call(
        functools.partial(first_boundary, steps, rows, cols, nz),
        [both, field(2), edge, edge],
        [both, both] + [field(2)] * 5 + [open_g],
        conc, adj, rate, chem, curve, swing, inner, grad, main_a, main_b, corner_b, corner_a, ahead,
        cost=2,
    )
    sums = (grad, edge_grad)
    got = main_a, main_b
    late = (max((steps - early) * depth * cols, 2 * (cols + 8) + 8), lanes)
    for back in range(1, steps):
        adj_a, adj_b = swap(to_a, to_b, "gy", round_first)
        final = back == steps - 1
        fields = call(
            functools.partial(prepare_kernel, steps, rows, cols, nz, back),
            [field(rows + 2 * depth)] + [field(rows + 2)] * 3
            + ([] if final else [both, late, late]),
            [field(rows + 2 * depth)],
            conc_own, *got, x_low, x_high, corner_b, corner_a, *core,
            cost=2,
        )
        fields, ahead, more = fields[:4], fields[4:5], fields[5:]
        if not final:
            got = swap(*more, "gy", round_first)
        work = [field(rows + 2)] * 2 + [field(rows)] * 2
        if final:
            inner, tiles, grad = call(
                functools.partial(next_interior, rows, cols, nz, final),
                [field(rows), (flat, cols), (nz * rows, cols)],
                work + [(nz * rows, cols), pltpu.SemaphoreType.DMA],
                *fields, rate, inner, outer, *sums,
                cost=3,
                far_outs=(2,),
            )
            (adj,) = call(
                functools.partial(next_boundary, rows, cols, nz, final),
                [(flat, cols)],
                [both, field(2), both],
                *fields, inner, outer, adj_a, adj_b, tiles,
                cost=1,
            )
        else:
            inner, grad = call(
                functools.partial(next_interior, rows, cols, nz, final),
                [field(rows)] * 2,
                work,
                *fields, rate, inner, outer, *sums,
                cost=3,
            )
            outer, to_a, to_b = call(
                functools.partial(next_boundary, rows, cols, nz, final),
                [both, edge, edge],
                [both, field(2), open_g],
                *fields, inner, outer, adj_a, adj_b, *ahead, rate,
                cost=1,
            )
            sums = (grad,)
    return adj.reshape(adjoint_end.shape), grad.reshape(rate_field.shape)


def solution(mesh):
    return jax.shard_map(
        shards,
        mesh=mesh,
        in_specs=(P(None, None, None, "gy", "gx"), P(None, None, "gy", "gx"), P(None, "gy", "gx")),
        out_specs=(P(None, None, "gy", "gx"), P(None, "gy", "gx")),
        check_vma=False,
    )
```

```python
import functools

import jax
import jax.numpy as jnp
from jax import lax
from jax.experimental import pallas as pl
from jax.experimental.pallas import tpu as pltpu
from jax.sharding import PartitionSpec as P

mix_energy = 2.5
grad_energy = 1.0
time_step = 0.1
diff_step = 0.03
bath_potential = 0.5

pad = 16
chunk = 72
depth = 2
early = 2
x_first, main_first, round_first = 0, 0, 1
vmem_limit = 20 * 1024 * 1024
f32 = jnp.float32


def slots(steps):
    widths = [2 * steps] + [2 * steps - 2 * back for back in range(steps)] + [2 * steps - 1]
    starts = [sum(widths[:i]) for i in range(len(widths))]
    total = -(-sum(widths) // 8) * 8
    return list(zip(starts, widths)), total


def chunks(low, high):
    return [(at, min(chunk, high - at)) for at in range(low, high, chunk)]


def reach(cols):
    return pad - 8, pad + cols + 8


def sent(cols):
    return pad - 4, pad + cols + 4


def up(value):
    return pltpu.roll(value, value.shape[1] - 1, 1)


def down(value):
    return pltpu.roll(value, 1, 1)


def face_mask(lanes, nz):
    lane = lax.broadcasted_iota(jnp.int32, (1, lanes), 1)
    return jnp.where(lane % nz == nz - 1, 0.0, 1.0).astype(f32)


def row_of(ref, y):
    return lambda dy, cut: ref[y + dy, cut, :]


def laplace(field, at, size, mask):
    span = slice(at, at + size)
    here = field(0, span)
    step_z = (up(here) - here) * mask
    sides = field(0, slice(at + 1, at + size + 1)) + field(0, slice(at - 1, at + size - 1))
    return here, (
        (sides + (field(-1, span) + field(1, span))) - 4.0 * here + (step_z - down(step_z))
    )


def mobility(c):
    return (0.5 * diff_step) * c * (1.0 - c)


def chem_row(conc, chem, curve, swing, at, size, mask):
    c, lap = laplace(conc, at, size, mask)
    inv = 1.0 / (c * (1.0 - c))
    span = slice(at, at + size)
    chem(
        span,
        time_step * (jnp.log(c * c * inv) - grad_energy * lap)
        + (time_step * (mix_energy - bath_potential) - (2.0 * time_step * mix_energy) * c),
    )
    curve(span, inv - 2.0 * mix_energy)
    swing(span, c * (diff_step / time_step) - 0.5 * diff_step / time_step)


def face_sums(adj, mob, chem, at, size, mask, across=(1, -1)):
    span = slice(at, at + size)
    a = adj(0, span)
    m = None if mob is None else mob(0, span)
    mu = None if chem is None else chem(0, span)
    flow = pair = None
    for dy, cut in (
        (0, slice(at + 1, at + size + 1)),
        (0, slice(at - 1, at + size - 1)),
    ) + tuple((dy, span) for dy in across):
        diff = adj(dy, cut) - a
        if mob is not None:
            term = (mob(dy, cut) + m) * diff
            flow = term if flow is None else flow + term
        if chem is not None:
            term = (chem(dy, cut) - mu) * diff
            pair = term if pair is None else pair + term
    diff = (up(a) - a) * mask
    if mob is not None:
        term = (up(m) + m) * diff
        flow = flow + (term - down(term))
    if chem is not None:
        term = (up(mu) - mu) * diff
        pair = pair + (term + down(term))
    return a, mu, flow, pair


def partial(a, swing, pair, curve, g):
    return a + swing * pair + curve * g


def gain(a, chem, before):
    value = a * chem
    return -value if before is None else before - value


def set_row(ref, y):
    def put(span, value):
        ref[y, span, :] = value

    return put


def all_rows(rows, cols, nz, adj, mob, mob_skip, chem, curve, swing, rate, before, pot, part, out,
             grad, between=None):
    low, high = reach(cols)
    mask = face_mask(adj.shape[2], nz)

    def body(y, _):
        for at, size in chunks(low, high):
            span = slice(at, at + size)
            a, mu, flow, pair = face_sums(
                row_of(adj, y + 1), row_of(mob, y + mob_skip), row_of(chem, y + 1), at, size, mask
            )
            g = flow - rate[y, span, :] * a
            pot[y + 1, span, :] = g
            part[y, span, :] = partial(
                a, swing[y + 1, span, :], pair, curve[y + 1, span, :], g
            )
            grad[y, span, :] = gain(a, mu, None if before is None else before[y, span, :])
        return 0

    def close(y, _):
        for at, size in chunks(low, high):
            span = slice(at, at + size)
            _g, lap = laplace(row_of(pot, y + 1), at, size, mask)
            out[y, span, :] = part[y, span, :] - grad_energy * lap
        return 0

    for row in (0, rows + 1):
        pot[row] = jnp.zeros(pot.shape[1:], f32)
    lax.fori_loop(0, rows, body, 0, unroll=2)
    if between is not None:
        between()
    lax.fori_loop(0, rows, close, 0, unroll=2)


def a_is_next(axis, first):
    return lax.rem(lax.axis_index(axis), 2) == first


def bases(rows, first):
    to_next = a_is_next("gy", first)
    top = rows - depth
    return jnp.where(to_next, top, 0), jnp.where(to_next, 0, top)


def landings(rows, first):
    to_next = a_is_next("gy", first)
    top = rows + depth
    return jnp.where(to_next, top, 0), jnp.where(to_next, 0, top)


def sides_of(rows):
    return [(0, 0, 0), (0, 1, 1), (1, 0, rows - 1), (1, 1, rows - 2)]


def pack_kernel(steps, rows, cols, nz, conc_hbm, adj_hbm, rate_hbm, conc_out, adj_out, rate_out,
                main_a, main_b, x_a, x_b, conc_in, adj_in, rate_in, sems):
    places, total = slots(steps)
    lanes = adj_out.shape[2]
    half = cols // 2
    lower = lax.broadcasted_iota(jnp.int32, (half, lanes), 1) < nz
    next_x = a_is_next("gx", x_first)
    sides = list(zip((main_a, main_b), bases(rows, main_first)))
    fetches = [(adj_hbm, adj_in), (rate_hbm, rate_in)] + [
        (conc_hbm.at[steps - 1 - back], conc_in.at[back]) for back in range(steps)
    ]
    copies = []
    for i, (there, here) in enumerate(fetches):
        part = here.shape[0] // 2
        copies.append(
            [
                pltpu.make_async_copy(
                    there.at[pl.ds(k * part, part)], here.at[pl.ds(k * part, part)], sems.at[i, k]
                )
                for k in range(2)
            ]
        )
    for pair in copies:
        for copy in pair:
            copy.start()

    def arrived(i):
        for copy in copies[i]:
            copy.wait()

    def to_x(y, value, place):
        start, width = place
        last, first = value[cols - width :, :], value[:width, :]
        x_a[y, start : start + width, :] = jnp.where(next_x, last, first)
        x_b[y, start : start + width, :] = jnp.where(next_x, first, last)

    used = sum(places[-1])
    arrived(0)
    for y in range(rows):
        adj = adj_in[pl.ds(y, lanes, stride=rows), :].T
        adj_out[y] = adj
        to_x(y, adj, places[0])
    for side, base in sides:
        for at in range(depth):
            side[pl.ds(at * cols, cols), :] = adj_out[base + at]
    arrived(1)
    for y in range(rows):
        rate = turned_rate(rate_in, y, rows, nz, lanes)
        rate_out[y] = rate
        to_x(y, rate, places[steps + 1])
        if used < total:
            x_a[y, used:, :] = jnp.zeros((total - used, lanes), f32)
            x_b[y, used:, :] = jnp.zeros((total - used, lanes), f32)
    for side, base in sides:
        edge = jnp.where(base == 0, 0, rows - 1)
        side[pl.ds((1 + early) * depth * cols, half), :] = jnp.where(
            lower, rate_out[edge, :half, :], rate_out[edge, half:, :]
        )
    for back in range(steps):
        arrived(2 + back)
        for y in range(rows):
            conc = conc_in[back, pl.ds(y, lanes, stride=rows), :].T
            conc_out[back, y] = conc
            to_x(y, conc, places[1 + back])
        if back < early:
            for side, base in sides:
                for at in range(depth):
                    side[pl.ds(((1 + back) * depth + at) * cols, cols), :] = conc_out[
                        back, base + at
                    ]


def turned_rate(rate, y, rows, nz, lanes):
    value = time_step * rate[pl.ds(y, nz, stride=rows), :]
    return jnp.concatenate([value] * (lanes // nz), axis=0).T


def put_own(out, row, value, y, place, cols, x_low, x_high):
    start, width = place
    right = pad + cols
    out[row, pad:right, :] = value
    out[row, pad - width : pad, :] = x_low[y, start : start + width, :]
    out[row, right : right + width, :] = x_high[y, start : start + width, :]


def put_halo(out, index, value, from_row, place, cols, corner):
    start, width = place
    right = pad + cols
    out[(*index, slice(pad, right))] = value
    out[(*index, slice(pad - width, pad))] = corner[0, from_row, start : start + width, :]
    out[(*index, slice(right, right + width))] = corner[1, from_row, start : start + width, :]


def corner_kernel(rows, got_a, got_b, _core, x_low, x_high, corner_a, corner_b):
    next_x = a_is_next("gx", x_first)
    x_low[...] = jnp.where(next_x, got_b[...], got_a[...])
    x_high[...] = jnp.where(next_x, got_a[...], got_b[...])
    for out, base in zip((corner_a, corner_b), bases(rows, round_first)):
        for at in range(depth):
            out[0, at] = x_low[base + at]
            out[1, at] = x_high[base + at]


def first_interior(steps, rows, cols, nz, conc_own, adj_own, rate_own, x_low, x_high,
                   conc, adj, rate, chem, curve, swing, out, grad, ahead, mob, pot, part):
    places, _ = slots(steps)
    low, high = reach(cols)
    lanes = adj.shape[2]
    mask = face_mask(lanes, nz)
    for y in range(rows):
        put_own(conc, 1 + y, conc_own[0, y], y, places[1], cols, x_low, x_high)
        put_own(adj, 1 + y, adj_own[y], y, places[0], cols, x_low, x_high)
        put_own(rate, y, rate_own[y], y, places[steps + 1], cols, x_low, x_high)
    for row, beside in ((0, 1), (rows + 1, rows)):
        adj[row] = adj[beside]
        for ref in (conc, chem, mob):
            ref[row] = jnp.zeros(ref.shape[1:], f32)
    put_ahead(ahead, conc_own, 1, x_low, x_high, places, rows, cols)

    def mob_row(row, _):
        for at, size in chunks(low - 8, high + 8):
            mob[row, at : at + size, :] = mobility(conc[row, at : at + size, :])
        return 0

    def mu_row(row, _):
        for at, size in chunks(low, high):
            chem_row(row_of(conc, row), set_row(chem, row), set_row(curve, row),
                     set_row(swing, row), at, size, mask)
        return 0

    lax.fori_loop(1, rows + 1, mob_row, 0, unroll=4)
    lax.fori_loop(1, rows + 1, mu_row, 0, unroll=2)
    all_rows(rows, cols, nz, adj, mob, 1, chem, curve, swing, rate, None, pot, part, out, grad)


def send_rows(out, ahead, rate, to_a, to_b, open_g, cols, nz):
    low, high = reach(cols)
    first, last = sent(cols)
    rows, lanes = rate.shape[0], rate.shape[2]
    mask = face_mask(lanes, nz)
    for s in range(2):
        for at, size in chunks(low, high):
            a, _mu, flow, _pair = face_sums(
                lambda dy, cut: out[s, dy, cut, :], lambda dy, cut: ahead[s, dy, cut, :], None,
                at, size, mask, (1,)
            )
            open_g[s, at - low : at - low + size, :] = (
                flow - rate[s * (rows - 1), at : at + size, :] * a
            )
    to_next = a_is_next("gy", round_first)
    for to, side in ((to_a, jnp.where(to_next, 1, 0)), (to_b, jnp.where(to_next, 0, 1))):
        to[0] = out[side, 0, first:last, :]
        to[1] = open_g[side, first - low : last - low, :]


def put_ahead(ahead, conc_own, back, x_low, x_high, places, rows, cols):
    for s, k, y in sides_of(rows):
        put_own(ahead.at[s], k, conc_own[back, y], y, places[1 + back], cols, x_low, x_high)
        ahead[s, k] = mobility(ahead[s, k])


def first_boundary(steps, rows, cols, nz, conc, adj, rate, chem, curve, swing, inside, grad,
                   from_a, from_b, corner_b, corner_a, ahead,
                   out, edge_grad, to_a, to_b, far_conc, far_adj, far_rate, far_mob, far_chem,
                   far_pot, delta, open_g):
    places, _ = slots(steps)
    low, high = reach(cols)
    half = cols // 2
    lanes = conc.shape[2]
    mask = face_mask(lanes, nz)
    lower = lax.broadcasted_iota(jnp.int32, (half, lanes), 1) < nz
    to_next = a_is_next("gy", main_first)

    def unpack(side):
        packed = side[pl.ds((1 + early) * depth * cols, half), :]
        turned = pltpu.roll(packed, lanes // 2, 1)
        return jnp.concatenate(
            [jnp.where(lower, packed, turned), jnp.where(lower, turned, packed)], axis=0
        )

    for halo, corner, side in (
        (from_a, corner_a, jnp.where(to_next, 1, 0)),
        (from_b, corner_b, jnp.where(to_next, 0, 1)),
    ):
        for at in range(depth):
            step = jnp.where(side == 1, at, depth - 1 - at)
            for ref, place, first in ((far_adj, places[0], 0), (far_conc, places[1], depth)):
                span = pl.ds((first + at) * cols, cols)
                put_halo(ref, (side, step), halo[span, :], at, place, cols, corner)
        put_halo(far_rate, (side,), unpack(halo), jnp.where(side == 1, 0, depth - 1),
                 places[steps + 1], cols, corner)

    share = time_step * grad_energy
    def side_rows(s, _):
        y, y1 = s * (rows - 1), 1 + s * (rows - 3)
        for at, size in chunks(low - 8, high + 8):
            span = slice(at, at + size)
            far_mob[s, span, :] = mobility(far_conc[s, 0, span, :])

        def conc_at(dy, cut):
            return conc[1 + y, cut, :] if dy == 1 else far_conc[s, -dy, cut, :]

        def adj_at(dy, cut):
            return adj[1 + y, cut, :] if dy == 1 else far_adj[s, -dy, cut, :]

        def mob_at(dy, cut):
            return far_mob[s, cut, :] if dy == 0 else mobility(conc_at(dy, cut))

        for at, size in chunks(low, high):
            span = slice(at, at + size)
            chem_row(conc_at, set_row(far_chem, s), lambda *_: None, lambda *_: None, at, size,
                     mask)
            a, _mu, flow, _pair = face_sums(adj_at, mob_at, None, at, size, mask)
            far_pot[s, span, :] = flow - far_rate[s, span, :] * a
            diff = a - adj[1 + y, span, :]
            delta[s, span, :] = (far_mob[s, span, :] + mobility(conc[1 + y, span, :])) * diff
        for at, size in chunks(low, high):
            span = slice(at, at + size)
            a, c, _flow, spread = face_sums(
                lambda dy, cut: adj[1 + y, cut, :], None, lambda dy, cut: far_conc[s, 0, cut, :],
                at, size, mask, ()
            )
            less = share * c
            inward = less * (adj[1 + y1, span, :] - a)
            pair = (far_chem[s, span, :] - (chem[1 + y, span, :] - less)) * (
                far_adj[s, 0, span, :] - a
            ) + (inward - share * spread)
            more = delta[s, span, :]
            step_z = (up(more) - more) * mask
            lap = (
                (delta[s, at + 1 : at + size + 1, :] + delta[s, at - 1 : at + size - 1, :])
                + (far_pot[s, span, :] - 4.0 * more)
                + (step_z - down(step_z))
            )
            out[s, 0, span, :] = (
                inside[y, span, :]
                + (swing[1 + y, span, :] * pair + curve[1 + y, span, :] * more)
                - grad_energy * lap
            )
            out[s, 1, span, :] = (
                inside[y1, span, :] + swing[1 + y1, span, :] * inward - grad_energy * more
            )
            edge_grad[s, span, :] = grad[y, span, :] + less * a
        return 0

    lax.fori_loop(0, 2, side_rows, 0)
    send_rows(out, ahead, rate, to_a, to_b, open_g, cols, nz)


def core_kernel(steps, rows, cols, nz, conc_own, mob, chem, curve, swing, conc):
    lanes = conc.shape[2]
    mask = face_mask(lanes, nz)
    own = pad, pad + cols
    for row in (0, rows + 1):
        conc[row] = jnp.zeros(conc.shape[1:], f32)
    for i in range(steps - 1):
        for y in range(rows):
            conc[1 + y, pad : pad + cols, :] = conc_own[1 + i, y]

        def row(y, _):
            for at, size in chunks(*own):
                mob[i, y, at : at + size, :] = mobility(conc[1 + y, at : at + size, :])
                chem_row(row_of(conc, 1 + y), set_row(chem.at[i], y), set_row(curve.at[i], y),
                         set_row(swing.at[i], y), at, size, mask)
            return 0

        lax.fori_loop(0, rows, row, 0, unroll=4)


def prepare_kernel(steps, rows, cols, nz, back, conc_own, from_a, from_b, x_low, x_high,
                   corner_b, corner_a, mob_core, chem_core, curve_core, swing_core,
                   mob, chem, curve, swing, *rest):
    *more, conc = rest
    places, _ = slots(steps)
    low, high = reach(cols)
    lanes = conc.shape[2]
    mask = face_mask(lanes, nz)
    place = places[1 + back]
    own = slice(pad, pad + cols)
    for y in range(rows):
        put_own(conc, depth + y, conc_own[back, y], y, place, cols, x_low, x_high)
        mob[depth + y, own, :] = mob_core[back - 1, y, own, :]
        chem[1 + y, own, :] = chem_core[back - 1, y, own, :]
        curve[1 + y, own, :] = curve_core[back - 1, y, own, :]
        swing[1 + y, own, :] = swing_core[back - 1, y, own, :]
    first_swap, corners = main_first, (corner_a, corner_b)
    if back >= early and round_first != main_first:
        first_swap, corners = round_first, (corner_b, corner_a)
    for halo, corner, base in zip((from_a, from_b), corners, landings(rows, first_swap)):
        for at in range(depth):
            first = (1 + back) * depth if back < early else (back - early) * depth
            span = pl.ds((first + at) * cols, cols)
            put_halo(conc, (base + at,), halo[span, :], at, place, cols, corner)

    if more:
        ahead, late_a, late_b = more
        put_ahead(ahead, conc_own, back + 1, x_low, x_high, places, rows, cols)
        for side, base in zip((late_a, late_b), bases(rows, round_first)):
            for after in range(early, steps):
                for at in range(depth):
                    span = pl.ds(((after - early) * depth + at) * cols, cols)
                    side[span, :] = conc_own[after, base + at]
            used = (steps - early) * depth * cols
            side[used:, :] = jnp.zeros((side.shape[0] - used, lanes), f32)

    for y in range(rows):
        for at in (low - 8, pad + cols):
            span = slice(at, at + 16)
            mob[depth + y, span, :] = mobility(conc[depth + y, span, :])
        for at in (low, pad + cols - 8):
            chem_row(row_of(conc, depth + y), set_row(chem, 1 + y), set_row(curve, 1 + y),
                     set_row(swing, 1 + y), at, 16, mask)
    for y, beyond in ((0, -1), (rows - 1, rows)):
        inner = slice(pad + 8, pad + cols - 8)
        chem[1 + y, inner, :] = chem[1 + y, inner, :] - (time_step * grad_energy) * (
            conc[depth + beyond, inner, :]
        )

    for y in (-1, rows):
        for at, size in chunks(low - 8, high + 8):
            mob[depth + y, at : at + size, :] = mobility(conc[depth + y, at : at + size, :])
        for at, size in chunks(low, high):
            chem_row(row_of(conc, depth + y), set_row(chem, 1 + y), lambda *_: None,
                     lambda *_: None, at, size, mask)


def next_interior(rows, cols, nz, final, mob, chem, curve, swing, rate, inner, outer, before, *rest):
    if final:
        out, tiles, grad_out, adj, pot, part, grad, turned, sem = rest
        send = pltpu.make_async_copy(turned, grad_out, sem)
    else:
        edge_before, out, grad, adj, pot, part, sums = rest
        for y in range(rows):
            sums[y] = before[y]
        for s, y in ((0, 0), (1, rows - 1)):
            sums[y] = edge_before[s]
        before = sums
    lanes = adj.shape[2]
    for y in range(depth, rows - depth):
        adj[1 + y] = inner[y]
    for s, k, y in sides_of(rows):
        adj[1 + y] = outer[s, k]
    adj[0] = outer[0, 0]
    adj[1 + rows] = outer[1, 0]

    def send_grad():
        for y in range(rows):
            turned[pl.ds(y, nz, stride=rows), :] = fold(grad[y, pad : pad + cols, :].T, nz)
        send.start()

    all_rows(rows, cols, nz, adj, mob, depth, chem, curve, swing, rate, before, pot, part, out,
             grad, send_grad if final else None)
    if final:
        for y in range(depth, rows - depth):
            tiles[pl.ds(y, lanes, stride=rows), :] = out[y, pad : pad + cols, :].T
        send.wait()


def fold(value, nz):
    total = value[:nz]
    for frame in range(1, value.shape[0] // nz):
        total = total + value[frame * nz : (frame + 1) * nz]
    return total


def next_boundary(rows, cols, nz, final, mob, chem, curve, swing, inside, outer, from_a, from_b,
                  *rest):
    if final:
        tiles, out, halo, delta, result = rest
    else:
        ahead, rate, result, to_a, to_b, halo, delta, open_g = rest
    low, high = reach(cols)
    first, last = sent(cols)
    lanes = mob.shape[2]
    mask = face_mask(lanes, nz)
    to_next = a_is_next("gy", round_first)
    for got, side in ((from_a, jnp.where(to_next, 1, 0)), (from_b, jnp.where(to_next, 0, 1))):
        for k in range(2):
            halo[side, k, first:last, :] = got[k]
    for s in range(2):
        y, beyond = s * (rows - 1), s * (rows + 1) - 1
        for at, size in chunks(low, high):
            span = slice(at, at + size)
            diff = halo[s, 0, span, :] - outer[s, 0, span, :]
            both = mob[depth + beyond, span, :] + mob[depth + y, span, :]
            delta[s, span, :] = both * diff
        for at, size in chunks(low, high):
            span = slice(at, at + size)
            more = delta[s, span, :]
            diff = halo[s, 0, span, :] - outer[s, 0, span, :]
            pair = (chem[1 + beyond, span, :] - chem[1 + y, span, :]) * diff
            step_z = (up(more) - more) * mask
            lap = (
                (delta[s, at + 1 : at + size + 1, :] + delta[s, at - 1 : at + size - 1, :])
                + (halo[s, 1, span, :] - more)
                - 4.0 * more
                + (step_z - down(step_z))
            )
            result[s, 0, span, :] = (
                inside[y, span, :]
                + (swing[1 + y, span, :] * pair + curve[1 + y, span, :] * more)
                - grad_energy * lap
            )
            result[s, 1, span, :] = inside[1 + s * (rows - 3), span, :] - grad_energy * more
    if final:
        out[...] = tiles[...]
        for s, k, y in sides_of(rows):
            out[pl.ds(y, lanes, stride=rows), :] = result[s, k, pad : pad + cols, :].T
    else:
        send_rows(result, ahead, rate, to_a, to_b, open_g, cols, nz)


def call(kernel, outs, scratch, *operands, cost=0, far=False, far_outs=()):
    if far:
        operands = [pltpu.with_memory_space_constraint(value, pltpu.HBM) for value in operands]
    space = pl.ANY if far else pltpu.VMEM
    return pl.pallas_call(
        kernel,
        out_shape=[jax.ShapeDtypeStruct(shape, f32) for shape in outs],
        in_specs=[pl.BlockSpec(memory_space=space)] * len(operands),
        out_specs=[
            pl.BlockSpec(memory_space=pltpu.HBM if i in far_outs else pltpu.VMEM)
            for i in range(len(outs))
        ],
        scratch_shapes=[pltpu.VMEM(s, f32) if isinstance(s, tuple) else s for s in scratch],
        compiler_params=pltpu.CompilerParams(vmem_limit_bytes=vmem_limit),
        cost_estimate=pl.CostEstimate(
            flops=cost * 1_000_000, bytes_accessed=cost * 2_000_000, transcendentals=0
        ),
    )(*operands)


def swap(value_a, value_b, axis, first):
    count = lax.axis_size(axis)
    pairs_a = [(i, (i + 1 - 2 * ((i + first) % 2)) % count) for i in range(count)]
    pairs_b = [(i, (i - 1 + 2 * ((i + first) % 2)) % count) for i in range(count)]
    return lax.ppermute(value_a, axis, pairs_a), lax.ppermute(value_b, axis, pairs_b)


def shards(saved_conc, adjoint_end, rate_field):
    steps, frames, nz, rows, cols = saved_conc.shape
    lanes = frames * nz
    _, total = slots(steps)
    width = cols + 2 * pad
    flat = lanes * rows

    def field(count):
        return (count, width, lanes)

    both = (2, depth, width, lanes)
    edge = (2, cols + 8, lanes)
    open_g = (2, cols + 16, lanes)
    raw = [(steps, flat, cols), (flat, cols), (nz * rows, cols)]
    conc_own, adj_own, rate_own, main_a, main_b, x_a, x_b = call(
        functools.partial(pack_kernel, steps, rows, cols, nz),
        [(steps, rows, cols, lanes), (rows, cols, lanes), (rows, cols, lanes)]
        + [((1 + early) * depth * cols + cols // 2, lanes)] * 2
        + [(rows, total, lanes)] * 2,
        raw + [pltpu.SemaphoreType.DMA((2 + steps, 2))],
        saved_conc.reshape(raw[0]), adjoint_end.reshape(raw[1]), rate_field.reshape(raw[2]),
        cost=3,
        far=True,
    )
    main_a, main_b = swap(main_a, main_b, "gy", main_first)
    x_a, x_b = swap(x_a, x_b, "gx", x_first)
    whole = (steps - 1, rows, width, lanes)
    core = call(
        functools.partial(core_kernel, steps, rows, cols, nz),
        [whole] * 4,
        [field(rows + 2)],
        conc_own,
        cost=2,
    )
    x_low, x_high, corner_a, corner_b = call(
        functools.partial(corner_kernel, rows),
        [(rows, total, lanes)] * 2 + [(2, depth, total, lanes)] * 2,
        [],
        x_a, x_b, core[1],
    )
    corners = swap(corner_a, corner_b, "gy", round_first)
    corner_a, corner_b = corners if main_first == round_first else corners[::-1]

    conc, adj, rate, chem, curve, swing, inner, grad, ahead = call(
        functools.partial(first_interior, steps, rows, cols, nz),
        [field(rows + 2)] * 2 + [field(rows)] + [field(rows + 2)] * 3 + [field(rows)] * 2 + [both],
        [field(rows + 2)] * 2 + [field(rows)],
        conc_own, adj_own, rate_own, x_low, x_high,
        cost=3,
    )
    outer, edge_grad, to_a, to_b = call(
        functools.partial(first_boundary, steps, rows, cols, nz),
        [both, field(2), edge, edge],
        [both, both] + [field(2)] * 5 + [open_g],
        conc, adj, rate, chem, curve, swing, inner, grad, main_a, main_b, corner_b, corner_a, ahead,
        cost=2,
    )
    sums = (grad, edge_grad)
    got = main_a, main_b
    late = (max((steps - early) * depth * cols, 2 * (cols + 8) + 8), lanes)
    for back in range(1, steps):
        adj_a, adj_b = swap(to_a, to_b, "gy", round_first)
        final = back == steps - 1
        fields = call(
            functools.partial(prepare_kernel, steps, rows, cols, nz, back),
            [field(rows + 2 * depth)] + [field(rows + 2)] * 3
            + ([] if final else [both, late, late]),
            [field(rows + 2 * depth)],
            conc_own, *got, x_low, x_high, corner_b, corner_a, *core,
            cost=2,
        )
        fields, ahead, more = fields[:4], fields[4:5], fields[5:]
        if not final:
            got = swap(*more, "gy", round_first)
        work = [field(rows + 2)] * 2 + [field(rows)] * 2
        if final:
            inner, tiles, grad = call(
                functools.partial(next_interior, rows, cols, nz, final),
                [field(rows), (flat, cols), (nz * rows, cols)],
                work + [(nz * rows, cols), pltpu.SemaphoreType.DMA],
                *fields, rate, inner, outer, *sums,
                cost=3,
                far_outs=(2,),
            )
            (adj,) = call(
                functools.partial(next_boundary, rows, cols, nz, final),
                [(flat, cols)],
                [both, field(2), both],
                *fields, inner, outer, adj_a, adj_b, tiles,
                cost=1,
            )
        else:
            inner, grad = call(
                functools.partial(next_interior, rows, cols, nz, final),
                [field(rows)] * 2,
                work,
                *fields, rate, inner, outer, *sums,
                cost=3,
            )
            outer, to_a, to_b = call(
                functools.partial(next_boundary, rows, cols, nz, final),
                [both, edge, edge],
                [both, field(2), open_g],
                *fields, inner, outer, adj_a, adj_b, *ahead, rate,
                cost=1,
            )
            sums = (grad,)
    return adj.reshape(adjoint_end.shape), grad.reshape(rate_field.shape)


def solution(mesh):
    return jax.shard_map(
        shards,
        mesh=mesh,
        in_specs=(P(None, None, None, "gy", "gx"), P(None, None, "gy", "gx"), P(None, "gy", "gx")),
        out_specs=(P(None, None, "gy", "gx"), P(None, "gy", "gx")),
        check_vma=False,
    )
```
